32 devices in a mesh: grp: 4 (over y, x), gx: 2 (over core), gy: 4 (over z).
Axes of the slice: x: 2, y: 2, z: 4, core: 2. Of those that a mesh axis runs over, the one named last changes fastest.
Arguments:
- conserved: float32 [8, 4, 16, 64, 128], P(None, 'grp', 'gx', 'gy'), may hold values from -6 to 6
- velocity: float32 [3, 4, 16, 64, 128], P(None, 'grp', 'gx', 'gy'), may hold values from -0.45 to 0.45
- donor_corner: int32 [4, 2, 4, 4, 8, 32], P('grp', 'gx', 'gy'), may hold values from 0 to 14206, as said below
- donor_fraction: float32 [3, 4, 2, 4, 4, 8, 32], P(None, 'grp', 'gx', 'gy'), may hold values from 0 to 1
- target_cell: int32 [4, 2, 4, 4, 8, 32], P('grp', 'gx', 'gy'), may hold values from 0 to 16384, as said below
Outputs:
- advanced: float32 [8, 4, 16, 64, 128], P(None, 'grp', 'gx', 'gy')
The draws below stay inside these ranges and needn't reach their ends.
Inputs may be any that keep to these rules, and one draw needn't show every extreme that they name: `donor_corner`: each used slot's stencil lies inside the donor device's block (x < 7, y < 15, z < 127); entries of empty slots are 0. Slot s of a pair is used exactly when s is below that pair's count, the same count as in target_cell; a pair's count is at most 32; every device fills 32 slots on the device of the same index in the grid two further on (grid indices modulo 4); devices of one grid fill none on each other, and the two background halves (grids 2 and 3) fill none on each other. `target_cell`: used slots match donor_corner's used slots; on one receiving device the named cells are distinct and lie within 32 layers of either end of the third dimension; empty slots hold 16384.
All inputs are finite; a program needn't handle non-finite values.
Results may differ from the reference program's by a relative error of at most 0.00002.
Values sent between devices are 32-bit elements; how exact they have to be, the bound alone decides.
No kernel may reach another device: no remote copies, remote signals or barrier semaphores. Data moves between devices by JAX's collectives and lax.ppermute only.
A program may use at most 128 MiB of HBM per device.

```python
import jax
import jax.numpy as jnp
from jax import lax

NV = 8
CX = 8
CY = 16
NZ = 128
RIM = 32
S = 32
NP = 8
NX = 16
NY = 64
CELLS = 16384
N_GRP = 4
N_GX = 2
N_GY = 4


def pair_counts(key):
    count_key = jax.random.fold_in(key, 11)
    shape = (N_GRP, NP, N_GRP, NP)
    pair_count = jax.random.randint(count_key, shape, (S + 1) // 2, S + 1)
    src_group = lax.broadcasted_iota(jnp.int32, shape, 0)
    src_device = lax.broadcasted_iota(jnp.int32, shape, 1)
    dst_group = lax.broadcasted_iota(jnp.int32, shape, 2)
    dst_device = lax.broadcasted_iota(jnp.int32, shape, 3)
    forced = (dst_group == (src_group + 2) % N_GRP) & (dst_device == src_device)
    pair_count = jnp.where(forced, S, pair_count)
    pair_count = jnp.where(src_group == dst_group, 0, pair_count)
    pair_count = jnp.where((src_group >= 2) & (dst_group >= 2), 0, pair_count)
    return (pair_count.astype(jnp.int32), forced)


def draw_donor_corner(key, part):
    pair_count, forced = pair_counts(key)
    shape = (N_GRP, NP, N_GRP, NP, S)
    key_x = jax.random.fold_in(key, 21)
    key_y = jax.random.fold_in(key, 22)
    key_z = jax.random.fold_in(key, 23)
    cell_x = jax.random.randint(key_x, shape, 0, CX - 1)
    cell_y = jax.random.randint(key_y, shape, 0, CY - 1)
    cell_z = jax.random.randint(key_z, shape, 0, NZ - 1)
    corner = (cell_x * CY + cell_y) * NZ + cell_z
    slot = lax.broadcasted_iota(jnp.int32, shape, 4)
    corner = jnp.where(slot < pair_count[..., None], corner, 0)
    highest = (CX - 2) * CY * NZ + (CY - 2) * NZ + NZ - 2
    corner = jnp.where(forced[..., None] & (slot == 0), highest, corner)
    return corner.astype(jnp.int32).reshape(N_GRP, N_GX, N_GY, N_GRP, NP, S)


def draw_target_cell(key, part):
    pair_count, forced = pair_counts(key)
    rim_count = CX * CY * 2 * RIM
    perm_keys = jax.random.split(jax.random.fold_in(key, 31), N_GRP * NP)
    orders = jax.vmap(lambda single: jax.random.permutation(single, rim_count))(perm_keys)
    chosen = orders[:, :N_GRP * NP * S].astype(jnp.int32).reshape(N_GRP, NP, N_GRP, NP, S)
    column = chosen // (2 * RIM)
    layer = chosen % (2 * RIM)
    depth = jnp.where(layer < RIM, layer, NZ - 2 * RIM + layer)
    cell = column * NZ + depth
    incoming = pair_count.transpose(2, 3, 0, 1)[..., None]
    slot = lax.broadcasted_iota(jnp.int32, chosen.shape, 4)
    cell = jnp.where(slot < incoming, cell, CELLS)
    return cell.astype(jnp.int32).reshape(N_GRP, N_GX, N_GY, N_GRP, NP, S)


def block_levels(key, extent, cuts, low, high):
    def one(dim, parts):
        draws = jax.random.uniform(jax.random.fold_in(jax.random.fold_in(key, 6), dim), (parts,), jnp.float32, low / len(cuts), high / len(cuts))
        return jnp.repeat(jnp.exp(draws), extent[dim] // parts).reshape((-1,) + (1,) * (len(extent) - dim - 1))

    gain = one(*cuts[0])
    for cut in cuts[1:]:
        gain = gain * one(*cut)
    return gain


def normal_values(rng, dims, deviation, limit, cuts=(), held_as=jnp.bfloat16):
    values = jax.random.normal(rng, dims, jnp.float32) * deviation
    if len(cuts) > 0:
        values = block_levels(rng, dims, cuts, -0.22, 0.18) * values
    return jnp.clip(values, min=-limit, max=limit).astype(held_as)


def setup_inputs(seed: int = 0) -> dict:
    keys = jax.random.split(jax.random.key(seed), 6)
    return {
        "conserved": normal_values(keys[0], (NV, N_GRP, NX, NY, NZ), 1.0, 6.0, ((1, 4), (2, 2), (3, 4)), jnp.float32),
        "velocity": jnp.clip(jax.random.uniform(keys[1], (3, N_GRP, NX, NY, NZ), jnp.float32, -0.45, 0.45) * block_levels(keys[1], (3, N_GRP, NX, NY, NZ), ((1, 4), (2, 2), (3, 4)), -0.4, 0.0), -0.45, 0.45),
        "donor_corner": draw_donor_corner(jax.random.fold_in(keys[5], 71), 0),
        "donor_fraction": jnp.clip(1.0 * jax.random.uniform(keys[3], (3, N_GRP, N_GX, N_GY, N_GRP, NP, S), jnp.float32) ** block_levels(keys[3], (3, N_GRP, N_GX, N_GY, N_GRP, NP, S), ((1, 4), (2, 2), (3, 4)), -0.2, 0.2), 0.0, 1.0),
        "target_cell": draw_target_cell(jax.random.fold_in(keys[5], 71), 0),
    }


signal_speed = 0.5
courant_number = 0.3
corner_shifts = ((0, 0, 0), (0, 0, 1), (0, 1, 0), (0, 1, 1), (1, 0, 0), (1, 0, 1), (1, 1, 0), (1, 1, 1))


def gather_corners(flat_state, corner_base, stride_x, stride_y):
    pieces = [jnp.take(flat_state, corner_base + shift[0] * stride_x + shift[1] * stride_y + shift[2], axis=1) for shift in corner_shifts]
    return jnp.stack(pieces)


def blend_corners(corners, fraction):
    total = jnp.zeros(corners.shape[1:], jnp.float32)
    for number, shift in enumerate(corner_shifts):
        weight_x = fraction[0] if shift[0] else 1.0 - fraction[0]
        weight_y = fraction[1] if shift[1] else 1.0 - fraction[1]
        weight_z = fraction[2] if shift[2] else 1.0 - fraction[2]
        weight = (weight_x * weight_y) * weight_z
        total = total + weight[None] * corners[number]
    return total


def face_pair(array, direction):
    low_index = [slice(None)] + [slice(1, -1)] * 3
    high_index = [slice(None)] + [slice(1, -1)] * 3
    low_index[direction] = slice(0, -1)
    high_index[direction] = slice(1, None)
    return array[tuple(low_index)], array[tuple(high_index)]


def step_diff(array, direction):
    lower = [slice(None)] * 4
    upper = [slice(None)] * 4
    lower[direction] = slice(0, -1)
    upper[direction] = slice(1, None)
    return array[tuple(upper)] - array[tuple(lower)]


def central(field, direction):
    lower = [slice(1, -1)] * 3
    upper = [slice(1, -1)] * 3
    lower[direction] = slice(0, -2)
    upper[direction] = slice(2, None)
    return 0.5 * (field[tuple(upper)] - field[tuple(lower)])


def advance(conserved, speeds):
    hydro = conserved[:5]
    magnetic = conserved[5:]
    change = jnp.zeros(hydro[:, 1:-1, 1:-1, 1:-1].shape, jnp.float32)
    for direction in (1, 2, 3):
        state_low, state_high = face_pair(hydro, direction)
        speed_low, speed_high = face_pair(speeds[direction - 1:direction], direction)
        wave_low = jnp.minimum(jnp.minimum(speed_low, speed_high) - signal_speed, 0.0)
        wave_high = jnp.maximum(jnp.maximum(speed_low, speed_high) + signal_speed, 0.0)
        flux = (wave_high * speed_low * state_low - wave_low * speed_high * state_high + wave_low * wave_high * (state_high - state_low)) / (wave_high - wave_low)
        change = change + step_diff(flux, direction)
    hydro_next = hydro[:, 1:-1, 1:-1, 1:-1] - courant_number * change
    elec_x = -(speeds[1] * magnetic[2] - speeds[2] * magnetic[1])
    elec_y = -(speeds[2] * magnetic[0] - speeds[0] * magnetic[2])
    elec_z = -(speeds[0] * magnetic[1] - speeds[1] * magnetic[0])
    curl_x = central(elec_z, 1) - central(elec_y, 2)
    curl_y = central(elec_x, 2) - central(elec_z, 0)
    curl_z = central(elec_y, 0) - central(elec_x, 1)
    magnetic_next = magnetic[:, 1:-1, 1:-1, 1:-1] - courant_number * jnp.stack([curl_x, curl_y, curl_z])
    return jnp.concatenate([hydro_next, magnetic_next], axis=0)


def reference(conserved, velocity, donor_corner, donor_fraction, target_cell):
    devices = N_GRP * NP
    blocks = conserved.reshape(NV, N_GRP, N_GX, CX, N_GY, CY, NZ).transpose(1, 2, 4, 0, 3, 5, 6).reshape(devices, NV, CELLS)
    bases = donor_corner.reshape(devices, N_GRP, NP, S)
    fractions = donor_fraction.reshape(3, devices, N_GRP, NP, S).transpose(1, 0, 2, 3, 4)

    def donate(packed):
        return blend_corners(gather_corners(packed[0], packed[1], CY * NZ, NZ), packed[2])

    sent = lax.map(donate, (blocks, bases, fractions))
    received = sent.reshape(devices, NV, devices, S).transpose(2, 1, 0, 3).reshape(devices, NV, devices * S)
    targets = target_cell.reshape(devices, devices * S)

    def place(packed):
        return packed[0].at[:, packed[2]].set(packed[1], mode="drop")

    filled = lax.map(place, (blocks, received, targets))
    grid = filled.reshape(N_GRP, N_GX, N_GY, NV, CX, CY, NZ).transpose(0, 3, 1, 4, 2, 5, 6).reshape(N_GRP, NV, NX, NY, NZ)
    speeds = velocity.transpose(1, 0, 2, 3, 4)
    widths = ((0, 0), (1, 1), (1, 1), (1, 1))

    def update(packed):
        return advance(jnp.pad(packed[0], widths), jnp.pad(packed[1], widths))

    result = lax.map(update, (grid, speeds))
    return result.transpose(1, 0, 2, 3, 4)
```

```python
import functools

import jax
import jax.numpy as jnp
from jax import lax
from jax.experimental import pallas as pl
from jax.experimental.pallas import tpu as pltpu
from jax.sharding import PartitionSpec as P

signal_speed = 0.5
courant_number = 0.3
fluid_count = 5
block = 8


def neighbours(ngx, ngy):
    kinds = []
    if ngx == 2:
        kinds.append(("xs", lambda i, j: (1 - i, j)))
    elif ngx > 2:
        kinds.append(("xl", lambda i, j: (max(i - 1, 0), j)))
        kinds.append(("xh", lambda i, j: (min(i + 1, ngx - 1), j)))
    if ngy == 2:
        kinds.append(("ys", lambda i, j: (i, 1 - j)))
    elif ngy > 2:
        kinds.append(("yl", lambda i, j: (i, max(j - 1, 0))))
        kinds.append(("yh", lambda i, j: (i, min(j + 1, ngy - 1))))
    return kinds


def split(value):
    high = value.astype(jnp.bfloat16)
    low = (value - high.astype(jnp.float32)).astype(jnp.bfloat16)
    return high, low


def blend_kernel(ngx, ngy, cons, vel, corner, fraction, target, out, *rest):
    kinds = neighbours(ngx, ngy)
    pays = rest[: len(kinds)]
    uhl, base, fx, fy, fz, packed, moved = rest[len(kinds) :]
    nv, cx, cy, nz = cons.shape
    ng, nq, slots = corner.shape
    lanes = ng * slots
    rows = cx * cy
    per = lanes // slots

    for g in range(ng):
        cols = slice(g * slots, (g + 1) * slots)
        base[:, cols] = corner[g]
        fx[:, cols] = fraction[0, g]
        fy[:, cols] = fraction[1, g]
        fz[:, cols] = fraction[2, g]
        packed[:, cols] = target[g]

    aim = (packed[...] - rows * nz).astype(jnp.float32)
    side_x = lax.axis_index("gx")
    side_y = lax.axis_index("gy")
    for (name, _), pay in zip(kinds, pays):
        along = cy if name[0] == "x" else cx
        for count, source, start in ((nv, cons, 0), (3, vel, nv * along)):
            if name[0] == "x":
                at = {"xl": 0, "xh": cx - 1, "xs": (1 - side_x) * (cx - 1)}[name]
                layer = source[:, pl.ds(at, 1)]
            else:
                at = {"yl": 0, "yh": cy - 1, "ys": (1 - side_y) * (cy - 1)}[name]
                layer = source[:, :, pl.ds(at, 1)]
            pay[start : start + count * along] = layer.reshape(count * along, nz)
        pay[(nv + 3) * along :] = aim

    high, low = split(cons[...].reshape(nv * rows, nz))
    uhl[:, :nz] = high
    uhl[:, nz:] = low

    depth = lax.broadcasted_iota(jnp.int32, (nz, lanes), 0)
    row_x = lax.broadcasted_iota(jnp.int32, (rows, lanes), 0) // cy
    row_y = lax.broadcasted_iota(jnp.int32, (rows, lanes), 0) % cy

    def weight(place, at, upper):
        return jnp.where(place == at, 1.0 - upper, jnp.where(place == at + 1, upper, 0.0))

    def blend(start):
        def one(q):
            row = pl.ds(start + q, 1)
            cell = base[row]
            wz = weight(depth, cell % nz, fz[row])
            wx = weight(row_x, cell // (nz * cy), fx[row])
            wy = weight(row_y, (cell // nz) % cy, fy[row])
            return split(wz) + (wx * wy,)

        for q in range(0, block, 2):
            h0, l0, w0 = one(q)
            h1, l1, w1 = one(q + 1)
            wh = jnp.concatenate([h0, h1], axis=1)
            wl = jnp.concatenate([l0, l1], axis=1)
            along = jnp.dot(
                uhl[...], jnp.concatenate([wh, wh], axis=0), preferred_element_type=jnp.float32
            ) + jnp.dot(uhl[:, :nz], wl, preferred_element_type=jnp.float32)
            wxy = jnp.concatenate([w0, w1], axis=1)
            values = jnp.sum(along.reshape(nv, rows, 2 * lanes) * wxy[None], axis=1)
            for half in range(2):
                value = values[:, half * lanes : (half + 1) * lanes]
                for turn in range(per):
                    moved[turn, start + q + half] = (
                        pltpu.roll(value, turn * slots, 1) if turn else value
                    )

    if nq == block:
        blend(0)
    else:
        lax.fori_loop(0, nq // block, lambda n, c: (blend(n * block), c)[1], 0)

    lane = lax.broadcasted_iota(jnp.int32, (nv, lanes), 1) // slots
    for h in range(ng):
        for q in range(nq):
            i, j = q // ngy, q % ngy
            owners = [q] + [a * ngy + b for a, b in (of(i, j) for _, of in kinds)]
            for t in range(0, len(owners), per):
                tile = None
                for k, owner in enumerate(owners[t : t + per]):
                    piece = moved[(k - h) % per, owner]
                    tile = piece if tile is None else jnp.where(lane == k, piece, tile)
                out[h * nq + q, :, t // per * lanes : (t // per + 1) * lanes] = tile


def step_kernel(ngx, ngy, cons, vel, target, received, *rest):
    kinds = neighbours(ngx, ngy)
    pays = rest[: len(kinds)]
    out, ext, own, vals, acc = rest[len(kinds) :]
    nv, cx, cy, nz = cons.shape
    ng, nq, slots = target.shape
    lanes = ng * slots
    rows = cx * cy
    per = lanes // slots
    side_x = lax.axis_index("gx")
    side_y = lax.axis_index("gy")

    for g in range(ng):
        own[:, g * slots : (g + 1) * slots] = target[g]

    lane = lax.broadcasted_iota(jnp.int32, (nv, lanes), 1) // slots
    for k in range(1 + len(kinds)):
        for p in range(nq):
            tile = None
            for g in range(ng):
                t = k // per
                piece = received[g * nq + p, :, t * lanes : (t + 1) * lanes]
                turn = (g - k) % per
                if turn:
                    piece = pltpu.roll(piece, turn * slots, 1)
                tile = piece if tile is None else jnp.where(lane == g, piece, tile)
            vals[k, :, p * lanes : (p + 1) * lanes] = tile

    parts = [(rows, lambda cell: cell // nz)]
    for name, _ in kinds:
        if name[0] == "x":
            at = {"xl": cx - 1, "xh": 0, "xs": side_x * (cx - 1)}[name]
            parts.append((cy, lambda cell, at=at: cell // nz - at * cy))
        else:
            at = {"yl": cy - 1, "yh": 0, "ys": side_y * (cy - 1)}[name]
            parts.append(
                (
                    cx,
                    lambda cell, at=at: jnp.where(
                        (cell // nz) % cy == at, cell // (nz * cy), -1
                    ),
                )
            )

    offsets = [0]
    for count, _ in parts:
        offsets.append(offsets[-1] + (nv + 1) * count)

    def fill(start, first):
        for k, (count, place) in enumerate(parts):
            if k == 0:
                cells = own[pl.ds(start, block)]
            else:
                along = parts[k][0]
                cells = pays[k - 1][pl.ds((nv + 3) * along + start, block)].astype(jnp.int32)
                cells = cells + rows * nz
            at_row = place(cells)
            at_z = cells % nz
            high, low = split(vals[k, :, pl.ds(start * lanes, block * lanes)])
            high = high.astype(jnp.float32)
            low = low.astype(jnp.float32)
            up_rows = lax.broadcasted_iota(jnp.int32, (count, lanes), 0)
            up_z = lax.broadcasted_iota(jnp.int32, (nz, lanes), 0)
            total = None
            for b in range(block):
                cols = slice(b * lanes, (b + 1) * lanes)
                hit = up_rows == at_row[b : b + 1]
                picks = (up_z == at_z[b : b + 1]).astype(jnp.float32).astype(jnp.bfloat16)
                pieces = [jnp.where(hit, high[v : v + 1, cols], 0.0) for v in range(nv)]
                pieces += [jnp.where(hit, 1.0, 0.0)]
                pieces += [jnp.where(hit, low[v : v + 1, cols], 0.0) for v in range(nv)]
                left = jnp.concatenate(pieces, axis=0).astype(jnp.bfloat16)
                term = lax.dot_general(
                    left, picks, (((1,), (1,)), ((), ())), preferred_element_type=jnp.float32
                )
                total = term if total is None else total + term
            filled = total[: nv * count] + total[(nv + 1) * count :]
            span = slice(offsets[k], offsets[k] + nv * count)
            marks = slice(offsets[k] + nv * count, offsets[k + 1])
            if first:
                acc[span] = filled
                acc[marks] = total[nv * count : (nv + 1) * count]
            else:
                acc[span] += filled
                acc[marks] += total[nv * count : (nv + 1) * count]

    if nq == block:
        fill(0, True)
    else:
        acc[...] = jnp.zeros_like(acc)
        lax.fori_loop(0, nq // block, lambda n, c: (fill(n * block, False), c)[1], 0)

    def merged(k, before):
        count = parts[k][0]
        new = acc[offsets[k] : offsets[k] + nv * count].reshape(nv, count, nz)
        mark = acc[offsets[k] + nv * count : offsets[k + 1]]
        return jnp.where(mark[None] > 0.5, new, before.reshape(nv, count, nz))

    top = 8
    ext[:nv, 1 : cx + 1, top : top + cy] = merged(0, cons[...]).reshape(nv, cx, cy, nz)
    ext[nv:, 1 : cx + 1, top : top + cy] = vel[...]
    none_x = jnp.zeros((nv + 3, cy, nz), jnp.float32)
    none_y = jnp.zeros((nv + 3, cx, nz), jnp.float32)
    sides = {"xl": none_x, "xh": none_x, "yl": none_y, "yh": none_y}
    for k, (name, _) in enumerate(kinds):
        count = parts[k + 1][0]
        pay = pays[k]
        halo = jnp.concatenate(
            [
                merged(k + 1, pay[: nv * count]),
                pay[nv * count : (nv + 3) * count].reshape(3, count, nz),
            ],
            axis=0,
        )
        if name[1] == "s":
            side = side_x if name[0] == "x" else side_y
            sides[name[0] + "l"] = jnp.where(side == 1, halo, 0.0)
            sides[name[0] + "h"] = jnp.where(side == 0, halo, 0.0)
        else:
            sides[name] = halo
    ext[:, 0, top : top + cy] = sides["xl"]
    ext[:, cx + 1, top : top + cy] = sides["xh"]
    ext[:, 1 : cx + 1, top - 1] = sides["yl"]
    ext[:, 1 : cx + 1, top + cy] = sides["yh"]

    at_z = lax.broadcasted_iota(jnp.int32, (1, cy, nz), 2)

    def inner(v):
        return ext[v, 1 : 1 + cx, top : top + cy]

    def shifted(v, d, by):
        if by == 0:
            return inner(v)
        if d == 0:
            return ext[v, 1 + by : 1 + by + cx, top : top + cy]
        if d == 1:
            return ext[v, 1 : 1 + cx, top + by : top + by + cy]
        return along_z(inner(v), by)

    def along_z(value, by):
        edge = 0 if by < 0 else nz - 1
        return jnp.where(at_z == edge, 0.0, pltpu.roll(value, (-by) % nz, 2))

    def face(low, high):
        wave_low = jnp.minimum(jnp.minimum(low, high) - signal_speed, 0.0)
        wave_high = jnp.maximum(jnp.maximum(low, high) + signal_speed, 0.0)
        scale = courant_number / (wave_high - wave_low)
        return (
            scale * wave_high * (low - wave_low),
            scale * wave_low * (wave_high - high),
        )

    centre = jnp.ones((cx, cy, nz), jnp.float32)
    sums = [None] * fluid_count
    for d in range(3):
        speed = inner(nv + d)
        up_low, up_high = face(speed, shifted(nv + d, d, 1))
        down_low, down_high = face(shifted(nv + d, d, -1), speed)
        centre = centre - up_low + down_high
        for v in range(fluid_count):
            term = down_low * shifted(v, d, -1) - up_high * shifted(v, d, 1)
            sums[v] = term if sums[v] is None else sums[v] + term
    for v in range(fluid_count):
        out[v] = sums[v] + centre * inner(v)

    def electric(n, d, by):
        a, b = (n + 1) % 3, (n + 2) % 3
        if d == 2 and by:
            return along_z(electric(n, 2, 0), by)
        return shifted(nv + b, d, by) * shifted(fluid_count + a, d, by) - shifted(
            nv + a, d, by
        ) * shifted(fluid_count + b, d, by)

    def central(n, d):
        return electric(n, d, 1) - electric(n, d, -1)

    for n in range(3):
        a, b = (n + 1) % 3, (n + 2) % 3
        curl = central(b, a) - central(a, b)
        out[fluid_count + n] = inner(fluid_count + n) - (0.5 * courant_number) * curl


def per_device(ngx, ngy, conserved, velocity, donor_corner, donor_fraction, target_cell):
    kinds = neighbours(ngx, ngy)
    cons = conserved[:, 0]
    vel = velocity[:, 0]
    corner = donor_corner[0, 0, 0]
    fraction = donor_fraction[:, 0, 0, 0]
    target = target_cell[0, 0, 0]
    nv, cx, cy, nz = cons.shape
    ng, nq, slots = corner.shape
    lanes = ng * slots
    rows = cx * cy
    tiles = -(-(1 + len(kinds)) * slots // lanes)
    f32 = jnp.float32

    pay_shapes = []
    for name, _ in kinds:
        along = cy if name[0] == "x" else cx
        pay_shapes.append(jax.ShapeDtypeStruct(((nv + 3) * along + nq, nz), f32))
    params = pltpu.CompilerParams(vmem_limit_bytes=48 * 1024 * 1024)
    outs = pl.pallas_call(
        functools.partial(blend_kernel, ngx, ngy),
        out_shape=[jax.ShapeDtypeStruct((ng * nq, nv, tiles * lanes), f32)] + pay_shapes,
        scratch_shapes=[
            pltpu.VMEM((nv * rows, 2 * nz), jnp.bfloat16),
            pltpu.VMEM((nq, lanes), jnp.int32),
            pltpu.VMEM((nq, lanes), f32),
            pltpu.VMEM((nq, lanes), f32),
            pltpu.VMEM((nq, lanes), f32),
            pltpu.VMEM((nq, lanes), jnp.int32),
            pltpu.VMEM((lanes // slots, nq, nv, lanes), f32),
        ],
        compiler_params=params,
        name="blend",
    )(cons, vel, corner, fraction, target)
    blended, pays = outs[0], outs[1:]

    received = lax.all_to_all(
        blended, ("grp", "gx", "gy"), split_axis=0, concat_axis=0, tiled=True
    )
    arrived = []
    for (name, _), pay in zip(kinds, pays):
        axis, count = ("gx", ngx) if name[0] == "x" else ("gy", ngy)
        pairs = {
            "s": [(0, 1), (1, 0)],
            "l": [(n + 1, n) for n in range(count - 1)],
            "h": [(n, n + 1) for n in range(count - 1)],
        }[name[1]]
        arrived.append((name, lax.ppermute(pay, axis, pairs)))
    found = dict(arrived)
    flip = {"xl": "xh", "xh": "xl", "yl": "yh", "yh": "yl", "xs": "xs", "ys": "ys"}
    halos = [found[flip[name]] for name, _ in kinds]

    count = sum((nv + 1) * (cy if name[0] == "x" else cx) for name, _ in kinds)
    result = pl.pallas_call(
        functools.partial(step_kernel, ngx, ngy),
        out_shape=jax.ShapeDtypeStruct((nv, cx, cy, nz), f32),
        scratch_shapes=[
            pltpu.VMEM((nv + 3, cx + 2, cy + 16, nz), f32),
            pltpu.VMEM((nq, lanes), jnp.int32),
            pltpu.VMEM((1 + len(kinds), nv, nq * lanes), f32),
            pltpu.VMEM(((nv + 1) * rows + count, nz), f32),
        ],
        compiler_params=params,
        name="step",
    )(cons, vel, target, received, *halos)
    return result[:, None]


def solution(mesh):
    return jax.shard_map(
        functools.partial(per_device, mesh.shape["gx"], mesh.shape["gy"]),
        mesh=mesh,
        in_specs=(
            P(None, "grp", "gx", "gy", None),
            P(None, "grp", "gx", "gy", None),
            P("grp", "gx", "gy", None, None, None),
            P(None, "grp", "gx", "gy", None, None, None),
            P("grp", "gx", "gy", None, None, None),
        ),
        out_specs=P(None, "grp", "gx", "gy", None),
        check_vma=False,
    )
```

```python
import functools

import jax
import jax.numpy as jnp
from jax import lax
from jax.experimental import pallas as pl
from jax.experimental.pallas import tpu as pltpu
from jax.sharding import PartitionSpec as P

signal_speed = 0.5
courant_number = 0.3
fluid_count = 5
block = 8


def neighbours(ngx, ngy):
    kinds = []
    if ngx == 2:
        kinds.append(("xs", lambda i, j: (1 - i, j)))
    elif ngx > 2:
        kinds.append(("xl", lambda i, j: (max(i - 1, 0), j)))
        kinds.append(("xh", lambda i, j: (min(i + 1, ngx - 1), j)))
    if ngy == 2:
        kinds.append(("ys", lambda i, j: (i, 1 - j)))
    elif ngy > 2:
        kinds.append(("yl", lambda i, j: (i, max(j - 1, 0))))
        kinds.append(("yh", lambda i, j: (i, min(j + 1, ngy - 1))))
    return kinds


def split(value):
    high = value.astype(jnp.bfloat16)
    low = (value - high.astype(jnp.float32)).astype(jnp.bfloat16)
    return high, low


def edge_kernel(ngx, ngy, cons, vel, target, *rest):
    kinds = neighbours(ngx, ngy)
    pays = rest[: len(kinds)]
    state, aims, sems = rest[len(kinds) :]
    nv, cx, cy, nz = cons.shape
    ng, nq, slots = target.shape
    copies = [
        pltpu.make_async_copy(cons, state.at[:nv], sems.at[0]),
        pltpu.make_async_copy(vel, state.at[nv:], sems.at[1]),
        pltpu.make_async_copy(target, aims, sems.at[2]),
    ]
    for copy in copies:
        copy.start()
    for copy in copies:
        copy.wait()
    side_x = lax.axis_index("gx")
    side_y = lax.axis_index("gy")
    for (name, _), pay in zip(kinds, pays):
        if name[0] == "x":
            at = {"xl": 0, "xh": cx - 1, "xs": (1 - side_x) * (cx - 1)}[name]
            layer = state[:, pl.ds(at, 1)]
        else:
            at = {"yl": 0, "yh": cy - 1, "ys": (1 - side_y) * (cy - 1)}[name]
            layer = state[:, :, pl.ds(at, 1)]
        along = cy if name[0] == "x" else cx
        cells = (nv + 3) * along
        pay[:cells] = layer.reshape(cells, nz)
        for g in range(ng):
            pay[cells:, g * slots : (g + 1) * slots] = (aims[g] - cx * cy * nz).astype(jnp.float32)


def each(count, body):
    if count == 1:
        body(0)
    else:
        lax.fori_loop(0, count, lambda n, c: (body(n), c)[1], 0)


def blend_kernel(ngx, ngy, cons, corner, fraction, out, uhl, base, fx, fy, fz, moved):
    kinds = neighbours(ngx, ngy)
    nv, cx, cy, nz = cons.shape
    ng, nq, slots = corner.shape
    lanes = ng * slots
    rows = cx * cy
    per = lanes // slots

    for g in range(ng):
        cols = slice(g * slots, (g + 1) * slots)
        base[:, cols] = corner[g]
        fx[:, cols] = fraction[0, g]
        fy[:, cols] = fraction[1, g]
        fz[:, cols] = fraction[2, g]

    high, low = split(cons[...].reshape(nv * rows, nz))
    uhl[:, :nz] = high
    uhl[:, nz:] = low

    depth = lax.broadcasted_iota(jnp.int32, (nz, lanes), 0)
    row_x = lax.broadcasted_iota(jnp.int32, (rows, lanes), 0) // cy
    row_y = lax.broadcasted_iota(jnp.int32, (rows, lanes), 0) % cy

    def weight(place, at, upper):
        return jnp.where(place == at, 1.0 - upper, jnp.where(place == at + 1, upper, 0.0))

    def blend(n):
        start = n * block

        def one(q):
            row = pl.ds(start + q, 1)
            cell = base[row]
            wz = weight(depth, cell % nz, fz[row])
            wx = weight(row_x, cell // (nz * cy), fx[row])
            wy = weight(row_y, (cell // nz) % cy, fy[row])
            return split(wz) + (wx * wy,)

        for q in range(0, block, 2):
            h0, l0, w0 = one(q)
            h1, l1, w1 = one(q + 1)
            wh = jnp.concatenate([h0, h1], axis=1)
            wl = jnp.concatenate([l0, l1], axis=1)
            along = jnp.dot(
                uhl[...], jnp.concatenate([wh, wh], axis=0), preferred_element_type=jnp.float32
            ) + jnp.dot(uhl[:, :nz], wl, preferred_element_type=jnp.float32)
            wxy = jnp.concatenate([w0, w1], axis=1)
            values = jnp.sum(along.reshape(nv, rows, 2 * lanes) * wxy[None], axis=1)
            for half in range(2):
                value = values[:, half * lanes : (half + 1) * lanes]
                for turn in range(per):
                    moved[turn, start + q + half] = (
                        pltpu.roll(value, turn * slots, 1) if turn else value
                    )

    each(nq // block, blend)

    lane = lax.broadcasted_iota(jnp.int32, (nv, lanes), 1) // slots
    for h in range(ng):
        for q in range(nq):
            i, j = q // ngy, q % ngy
            owners = [q] + [a * ngy + b for a, b in (of(i, j) for _, of in kinds)]
            for t in range(0, len(owners), per):
                tile = None
                for k, owner in enumerate(owners[t : t + per]):
                    piece = moved[(k - h) % per, owner]
                    tile = piece if tile is None else jnp.where(lane == k, piece, tile)
                out[h * nq + q, :, t // per * lanes : (t // per + 1) * lanes] = tile


def fills(kinds, cx, cy):
    spread = 4 if cx % 4 == 0 else 1
    return [(cx * cy // spread, spread)] + [(cy if k[0] == "x" else cx, 1) for k, _ in kinds]


def prepare_kernel(ngx, ngy, cons, vel, target, sent, *rest):
    del sent
    kinds = neighbours(ngx, ngy)
    pays = rest[: len(kinds)]
    coefs, ext = rest[len(kinds) : len(kinds) + 2]
    parts = fills(kinds, *cons.shape[1:3])
    hits = rest[len(kinds) + 2 : len(kinds) + 2 + len(parts)]
    picks = rest[len(kinds) + 2 + len(parts) : len(kinds) + 2 + 2 * len(parts)]
    own, marks = rest[len(kinds) + 2 + 2 * len(parts) :][:2]
    nv, cx, cy, nz = cons.shape
    ng, nq, slots = target.shape
    lanes = ng * slots
    side_x = lax.axis_index("gx")
    side_y = lax.axis_index("gy")

    for g in range(ng):
        own[:, g * slots : (g + 1) * slots] = target[g]

    def column(cell, spread):
        if spread == 1:
            return cell % nz
        return (cell // (nz * cy)) % spread * nz + cell % nz

    def row(k, cell):
        x, y = cell // (nz * cy), (cell // nz) % cy
        if k == 0:
            return x // parts[0][1] * cy + y
        name = kinds[k - 1][0]
        if name[0] == "x":
            at = {"xl": cx - 1, "xh": 0, "xs": side_x * (cx - 1)}[name]
            return jnp.where(x == at, y, -1)
        at = {"yl": cy - 1, "yh": 0, "ys": side_y * (cy - 1)}[name]
        return jnp.where(y == at, x, -1)

    marks[...] = jnp.zeros_like(marks)
    starts = [0]
    for count, spread in parts:
        starts.append(starts[-1] + count * spread)

    def pick(n):
        start = n * block
        for k, (count, spread) in enumerate(parts):
            if k == 0:
                cells = own[pl.ds(start, block)]
            else:
                cells = pays[k - 1][pl.ds((nv + 3) * count + start, block)].astype(jnp.int32)
                cells = cells + cx * cy * nz
            at_row = row(k, cells)
            at_column = column(cells, spread).T
            up = lax.broadcasted_iota(jnp.int32, (count, lanes), 0)
            along = lax.broadcasted_iota(jnp.int32, (lanes, spread * nz), 1)
            for b in range(block):
                hit = jnp.where(up == at_row[b : b + 1], 1.0, 0.0)
                here = pl.ds(pl.multiple_of((start + b) * lanes, lanes), lanes)
                hits[k][:, here] = hit
                picks[k][here] = jnp.where(at_column[:, b : b + 1] == along, 1.0, 0.0).astype(
                    jnp.bfloat16
                )
            here = pl.ds(pl.multiple_of(start * lanes, lanes), block * lanes)
            seen = jnp.dot(
                hits[k][:, here].astype(jnp.bfloat16),
                picks[k][here],
                preferred_element_type=jnp.float32,
            )
            for s in range(spread):
                at = slice(starts[k] + s * count, starts[k] + (s + 1) * count)
                marks[at] += seen[:, s * nz : (s + 1) * nz]

    each(nq // block, pick)

    def cleared(k, s, values):
        count = parts[k][0]
        mark = marks[starts[k] + s * count : starts[k] + (s + 1) * count]
        return jnp.where(mark[None] > 0.5, 0.0, values)

    top = 8
    count, spread = parts[0]
    for s in range(spread):
        for x in range(s, cx, spread):
            mark = marks[s * count + x // spread * cy : s * count + (x // spread + 1) * cy]
            ext[:nv, 1 + x, top : top + cy] = jnp.where(mark[None] > 0.5, 0.0, cons[:, x])
    ext[nv:, 1 : cx + 1, top : top + cy] = vel[...]
    none_x = jnp.zeros((nv + 3, cy, nz), jnp.float32)
    none_y = jnp.zeros((nv + 3, cx, nz), jnp.float32)
    sides = {"xl": none_x, "xh": none_x, "yl": none_y, "yh": none_y}
    for k, (name, _) in enumerate(kinds):
        count = parts[k + 1][0]
        halo = pays[k][: (nv + 3) * count].reshape(nv + 3, count, nz)
        halo = jnp.concatenate([cleared(k + 1, 0, halo[:nv]), halo[nv:]], axis=0)
        if name[1] == "s":
            side = side_x if name[0] == "x" else side_y
            sides[name[0] + "l"] = jnp.where(side == 1, halo, 0.0)
            sides[name[0] + "h"] = jnp.where(side == 0, halo, 0.0)
        else:
            sides[name] = halo
    ext[:, 0, top : top + cy] = sides["xl"]
    ext[:, cx + 1, top : top + cy] = sides["xh"]
    ext[:, 1 : cx + 1, top - 1] = sides["yl"]
    ext[:, 1 : cx + 1, top + cy] = sides["yh"]

    def face(low, high):
        wave_low = jnp.minimum(jnp.minimum(low, high) - signal_speed, 0.0)
        wave_high = jnp.maximum(jnp.maximum(low, high) + signal_speed, 0.0)
        scale = courant_number / (wave_high - wave_low)
        return (
            scale * wave_high * (low - wave_low),
            scale * wave_low * (wave_high - high),
        )

    centre = jnp.ones((cx, cy, nz), jnp.float32)
    for d in range(3):
        speed = window(ext, nv + d, cx, cy)
        up_low, up_high = face(speed, shifted(ext, nv + d, cx, cy, d, 1))
        down_low, down_high = face(shifted(ext, nv + d, cx, cy, d, -1), speed)
        centre = centre - up_low + down_high
        coefs[2 * d] = down_low
        coefs[2 * d + 1] = -up_high
    coefs[6] = centre


def window(ext, v, cx, cy, move_x=0, move_y=0):
    return ext[v, 1 + move_x : 1 + move_x + cx, 8 + move_y : 8 + move_y + cy]


def along_z(value, by):
    nz = value.shape[-1]
    at = lax.broadcasted_iota(jnp.int32, (1,) + value.shape[1:], 2)
    edge = 0 if by < 0 else nz - 1
    return jnp.where(at == edge, 0.0, pltpu.roll(value, (-by) % nz, 2))


def shifted(ext, v, cx, cy, d, by):
    if d == 2 and by:
        return along_z(window(ext, v, cx, cy), by)
    return window(ext, v, cx, cy, by if d == 0 else 0, by if d == 1 else 0)


def step_kernel(ngx, ngy, received, coefs, before, *rest):
    kinds = neighbours(ngx, ngy)
    parts = fills(kinds, *coefs.shape[1:3])
    hits = rest[: len(parts)]
    picks = rest[len(parts) : 2 * len(parts)]
    out, ext, vals, acc = rest[2 * len(parts) :]
    cx, cy, nz = coefs.shape[1:]
    nv = received.shape[1]
    lanes = received.shape[2] // (-(-len(parts) // 4))
    slots = lanes // 4
    ng = per = lanes // slots
    nq = received.shape[0] // ng

    ext[...] = before[...]

    lane = lax.broadcasted_iota(jnp.int32, (nv, lanes), 1) // slots
    for k in range(len(parts)):
        for p in range(nq):
            tile = None
            for g in range(ng):
                t = k // per
                piece = received[g * nq + p, :, t * lanes : (t + 1) * lanes]
                turn = (g - k) % per
                if turn:
                    piece = pltpu.roll(piece, turn * slots, 1)
                tile = piece if tile is None else jnp.where(lane == g, piece, tile)
            vals[k, :, p * lanes : (p + 1) * lanes] = tile

    starts = [0]
    for count, spread in parts:
        starts.append(starts[-1] + nv * count * spread)

    def fill(n):
        here = pl.ds(pl.multiple_of(n * block * lanes, lanes), block * lanes)
        for k, (count, spread) in enumerate(parts):
            high, low = split(vals[k, :, here])
            hit = hits[k][:, here]
            pieces = [hit * high[v : v + 1].astype(jnp.float32) for v in range(nv)]
            pieces += [hit * low[v : v + 1].astype(jnp.float32) for v in range(nv)]
            left = jnp.concatenate(pieces, axis=0).astype(jnp.bfloat16)
            total = jnp.dot(left, picks[k][here], preferred_element_type=jnp.float32)
            total = total[: nv * count] + total[nv * count :]
            for s in range(spread):
                at = slice(starts[k] + s * nv * count, starts[k] + (s + 1) * nv * count)
                value = total[:, s * nz : (s + 1) * nz]
                if nq == block:
                    acc[at] = value
                else:
                    acc[at] += value

    if nq != block:
        acc[...] = jnp.zeros_like(acc)
    each(nq // block, fill)

    top = 8
    count, spread = parts[0]
    for s in range(spread):
        new = acc[starts[0] + s * nv * count : starts[0] + (s + 1) * nv * count]
        new = new.reshape(nv, cx // spread, cy, nz)
        for x in range(s, cx, spread):
            ext[:nv, 1 + x, top : top + cy] += new[:, x // spread]
    side_x = lax.axis_index("gx")
    side_y = lax.axis_index("gy")
    for k, (name, _) in enumerate(kinds):
        new = acc[starts[k + 1] : starts[k + 2]].reshape(nv, parts[k + 1][0], nz)
        if name[0] == "x":
            at = {"xl": 0, "xh": cx + 1, "xs": (1 - side_x) * (cx + 1)}[name]
            ext[:nv, pl.ds(at, 1), top : top + cy] += new[:, None]
        elif name[1] == "s":
            ext[:nv, 1 : cx + 1, top - 1] += jnp.where(side_y == 1, new, 0.0)
            ext[:nv, 1 : cx + 1, top + cy] += jnp.where(side_y == 0, new, 0.0)
        else:
            ext[:nv, 1 : cx + 1, {"yl": top - 1, "yh": top + cy}[name]] += new

    for v in range(fluid_count):
        total = coefs[6] * window(ext, v, cx, cy)
        for d in range(3):
            for n, by in enumerate((-1, 1)):
                total = total + coefs[2 * d + n] * shifted(ext, v, cx, cy, d, by)
        out[v] = total

    def electric(n, d, by):
        a, b = (n + 1) % 3, (n + 2) % 3
        if d == 2 and by:
            return along_z(electric(n, 2, 0), by)

        def at(v):
            return shifted(ext, v, cx, cy, d, by)

        return at(nv + b) * at(fluid_count + a) - at(nv + a) * at(fluid_count + b)

    def central(n, d):
        return electric(n, d, 1) - electric(n, d, -1)

    for n in range(3):
        a, b = (n + 1) % 3, (n + 2) % 3
        curl = central(b, a) - central(a, b)
        out[fluid_count + n] = window(ext, fluid_count + n, cx, cy) - (0.5 * courant_number) * curl


def per_device(ngx, ngy, conserved, velocity, donor_corner, donor_fraction, target_cell):
    kinds = neighbours(ngx, ngy)
    cons = conserved[:, 0]
    vel = velocity[:, 0]
    corner = donor_corner[0, 0, 0]
    fraction = donor_fraction[:, 0, 0, 0]
    target = target_cell[0, 0, 0]
    nv, cx, cy, nz = cons.shape
    ng, nq, slots = corner.shape
    lanes = ng * slots
    rows = cx * cy
    tiles = -(-(1 + len(kinds)) * slots // lanes)
    f32 = jnp.float32
    params = pltpu.CompilerParams(vmem_limit_bytes=56 * 1024 * 1024)

    pay_shapes = []
    for name, _ in kinds:
        along = cy if name[0] == "x" else cx
        pay_shapes.append(jax.ShapeDtypeStruct(((nv + 3) * along + nq, nz), f32))
    pays = pl.pallas_call(
        functools.partial(edge_kernel, ngx, ngy),
        out_shape=pay_shapes,
        in_specs=[pl.BlockSpec(memory_space=pl.ANY)] * 3,
        scratch_shapes=[
            pltpu.VMEM((nv + 3, cx, cy, nz), f32),
            pltpu.VMEM((ng, nq, slots), jnp.int32),
            pltpu.SemaphoreType.DMA((3,)),
        ],
        compiler_params=params,
        name="edge",
    )(cons, vel, target)

    arrived = []
    for (name, _), pay in zip(kinds, pays):
        axis, count = ("gx", ngx) if name[0] == "x" else ("gy", ngy)
        pairs = {
            "s": [(0, 1), (1, 0)],
            "l": [(n + 1, n) for n in range(count - 1)],
            "h": [(n, n + 1) for n in range(count - 1)],
        }[name[1]]
        arrived.append((name, lax.ppermute(pay, axis, pairs)))
    found = dict(arrived)
    flip = {"xl": "xh", "xh": "xl", "yl": "yh", "yh": "yl", "xs": "xs", "ys": "ys"}
    halos = [found[flip[name]] for name, _ in kinds]

    blended = pl.pallas_call(
        functools.partial(blend_kernel, ngx, ngy),
        out_shape=jax.ShapeDtypeStruct((ng * nq, nv, tiles * lanes), f32),
        scratch_shapes=[
            pltpu.VMEM((nv * rows, 2 * nz), jnp.bfloat16),
            pltpu.VMEM((nq, lanes), jnp.int32),
            pltpu.VMEM((nq, lanes), f32),
            pltpu.VMEM((nq, lanes), f32),
            pltpu.VMEM((nq, lanes), f32),
            pltpu.VMEM((lanes // slots, nq, nv, lanes), f32),
        ],
        compiler_params=params,
        name="blend",
    )(cons, corner, fraction)

    received = lax.all_to_all(
        blended, ("grp", "gx", "gy"), split_axis=0, concat_axis=0, tiled=True
    )

    parts = fills(kinds, cx, cy)
    ext_shape = (nv + 3, cx + 2, cy + 16, nz)
    vmem = pl.BlockSpec(memory_space=pltpu.VMEM)
    prepared = pl.pallas_call(
        functools.partial(prepare_kernel, ngx, ngy),
        out_shape=[
            jax.ShapeDtypeStruct((7, cx, cy, nz), f32),
            jax.ShapeDtypeStruct(ext_shape, f32),
        ]
        + [jax.ShapeDtypeStruct((count, nq * lanes), f32) for count, _ in parts]
        + [jax.ShapeDtypeStruct((nq * lanes, spread * nz), jnp.bfloat16) for _, spread in parts],
        in_specs=[vmem] * 3 + [pl.BlockSpec(memory_space=pl.ANY)] + [vmem] * len(kinds),
        scratch_shapes=[
            pltpu.VMEM((nq, lanes), jnp.int32),
            pltpu.VMEM((sum(count * spread for count, spread in parts), nz), f32),
        ],
        compiler_params=params,
        name="prepare",
    )(cons, vel, target, blended, *halos)

    result = pl.pallas_call(
        functools.partial(step_kernel, ngx, ngy),
        out_shape=jax.ShapeDtypeStruct((nv, cx, cy, nz), f32),
        scratch_shapes=[
            pltpu.VMEM(ext_shape, f32),
            pltpu.VMEM((len(parts), nv, nq * lanes), f32),
            pltpu.VMEM((nv * sum(count * spread for count, spread in parts), nz), f32),
        ],
        compiler_params=params,
        name="step",
    )(received, *prepared)
    return result[:, None]


def solution(mesh):
    return jax.shard_map(
        functools.partial(per_device, mesh.shape["gx"], mesh.shape["gy"]),
        mesh=mesh,
        in_specs=(
            P(None, "grp", "gx", "gy", None),
            P(None, "grp", "gx", "gy", None),
            P("grp", "gx", "gy", None, None, None),
            P(None, "grp", "gx", "gy", None, None, None),
            P("grp", "gx", "gy", None, None, None),
        ),
        out_specs=P(None, "grp", "gx", "gy", None),
        check_vma=False,
    )
```

```python
import functools

import jax
import jax.numpy as jnp
from jax import lax
from jax.experimental import pallas as pl
from jax.experimental.pallas import tpu as pltpu
from jax.sharding import PartitionSpec as P

signal_speed = 0.5
courant_number = 0.3
fluid_count = 5
block = 8


def neighbours(ngx, ngy):
    kinds = []
    if ngx == 2:
        kinds.append(("xs", lambda i, j: (1 - i, j)))
    elif ngx > 2:
        kinds.append(("xl", lambda i, j: (max(i - 1, 0), j)))
        kinds.append(("xh", lambda i, j: (min(i + 1, ngx - 1), j)))
    if ngy == 2:
        kinds.append(("ys", lambda i, j: (i, 1 - j)))
    elif ngy > 2:
        kinds.append(("yl", lambda i, j: (i, max(j - 1, 0))))
        kinds.append(("yh", lambda i, j: (i, min(j + 1, ngy - 1))))
    return kinds


def split(value):
    high = value.astype(jnp.bfloat16)
    low = (value - high.astype(jnp.float32)).astype(jnp.bfloat16)
    return high, low


def edge_kernel(ngx, ngy, cons, vel, corner, fraction, target, cells, parts, *rest):
    kinds = neighbours(ngx, ngy)
    pays = rest[: len(kinds)]
    layers = rest[len(kinds) : 2 * len(kinds)]
    at_cells, at_parts, sems = rest[2 * len(kinds) :]
    nv, cx, cy, nz = cons.shape
    ng, nq, slots = target.shape
    side_x = lax.axis_index("gx")
    side_y = lax.axis_index("gy")
    tile = 8
    moves = [(corner, at_cells.at[0]), (target, at_cells.at[1]), (fraction, at_parts)]
    rows = []
    for (name, _), layer in zip(kinds, layers):
        if name[0] == "x":
            at = {"xl": 0, "xh": cx - 1, "xs": (1 - side_x) * (cx - 1)}[name]
            rows.append(None)
            for source, to in ((cons, layer.at[:nv]), (vel, layer.at[nv:])):
                moves.append((source.at[:, pl.ds(at, 1)], to))
        else:
            high = {"yl": 0, "yh": 1, "ys": 1 - side_y}[name]
            rows.append(high * (tile - 1))
            start = pl.multiple_of(high * (cy - tile), tile)
            for source, to in ((cons, layer.at[:nv]), (vel, layer.at[nv:])):
                moves.append((source.at[:, :, pl.ds(start, tile)], to))
    copies = [pltpu.make_async_copy(a, b, sems.at[n]) for n, (a, b) in enumerate(moves)]
    for copy in copies:
        copy.start()
    for copy in copies:
        copy.wait()
    for g in range(ng):
        cells[:, :, g * slots : (g + 1) * slots] = at_cells[:, g]
        parts[:, :, g * slots : (g + 1) * slots] = at_parts[:, g]
    aim = (cells[1] - cx * cy * nz).astype(jnp.float32)
    for row, layer, pay in zip(rows, layers, pays):
        size = pay.shape[0] - nq
        edge = layer[...] if row is None else layer[:, :, pl.ds(row, 1)]
        pay[:size] = edge.reshape(size, nz)
        pay[size:] = aim


def each(count, body):
    if count == 1:
        body(0)
    else:
        lax.fori_loop(0, count, lambda n, c: (body(n), c)[1], 0)


def blend_kernel(cons, cells, parts, moved, uhl):
    per, nq, nv, lanes = moved.shape
    cx, cy, nz = cons.shape[1:]
    slots = lanes // per
    rows = cx * cy

    high, low = split(cons[...].reshape(nv * rows, nz))
    uhl[:, :nz] = high
    uhl[:, nz:] = low

    depth = lax.broadcasted_iota(jnp.int32, (nz, lanes), 0)
    row_x = lax.broadcasted_iota(jnp.int32, (rows, lanes), 0) // cy
    row_y = lax.broadcasted_iota(jnp.int32, (rows, lanes), 0) % cy

    def weight(place, at, upper):
        return jnp.where(place == at, 1.0 - upper, jnp.where(place == at + 1, upper, 0.0))

    def blend(n):
        start = n * block

        def one(q):
            row = pl.ds(start + q, 1)
            cell = cells[0, row]
            wz = weight(depth, cell % nz, parts[2, row])
            wx = weight(row_x, cell // (nz * cy), parts[0, row])
            wy = weight(row_y, (cell // nz) % cy, parts[1, row])
            return split(wz) + (wx * wy,)

        for q in range(0, block, 2):
            h0, l0, w0 = one(q)
            h1, l1, w1 = one(q + 1)
            wh = jnp.concatenate([h0, h1], axis=1)
            wl = jnp.concatenate([l0, l1], axis=1)
            along = jnp.dot(
                uhl[...], jnp.concatenate([wh, wh], axis=0), preferred_element_type=jnp.float32
            ) + jnp.dot(uhl[:, :nz], wl, preferred_element_type=jnp.float32)
            wxy = jnp.concatenate([w0, w1], axis=1)
            values = jnp.sum(along.reshape(nv, rows, 2 * lanes) * wxy[None], axis=1)
            for half in range(2):
                value = values[:, half * lanes : (half + 1) * lanes]
                for turn in range(per):
                    moved[turn, start + q + half] = (
                        pltpu.roll(value, turn * slots, 1) if turn else value
                    )

    each(nq // block, blend)


def assemble_kernel(ngx, ngy, moved, *rest):
    kinds = neighbours(ngx, ngy)
    out = rest[-1]
    per, nq, nv, lanes = moved.shape
    ng, slots = out.shape[0] // nq, lanes // per
    lane = lax.broadcasted_iota(jnp.int32, (nv, lanes), 1) // slots
    for h in range(ng):
        for q in range(nq):
            i, j = q // ngy, q % ngy
            owners = [q] + [a * ngy + b for a, b in (of(i, j) for _, of in kinds)]
            for t in range(0, len(owners), per):
                tile = None
                for k, owner in enumerate(owners[t : t + per]):
                    piece = moved[(k - h) % per, owner]
                    tile = piece if tile is None else jnp.where(lane == k, piece, tile)
                out[h * nq + q, :, t // per * lanes : (t // per + 1) * lanes] = tile


def fills(kinds, cx, cy):
    spread = 4 if cx % 4 == 0 else 1
    return [(cx * cy // spread, spread)] + [(cy if k[0] == "x" else cx, 1) for k, _ in kinds]


def prepare_kernel(ngx, ngy, cons, vel, cells, sent, *rest):
    del sent
    kinds = neighbours(ngx, ngy)
    pays = rest[: len(kinds)]
    coefs, ext = rest[len(kinds) : len(kinds) + 2]
    parts = fills(kinds, *cons.shape[1:3])
    hits = rest[len(kinds) + 2 : len(kinds) + 2 + len(parts)]
    picks = rest[len(kinds) + 2 + len(parts) : len(kinds) + 2 + 2 * len(parts)]
    marks = rest[-1]
    nv, cx, cy, nz = cons.shape
    nq, lanes = cells.shape[1:]
    side_x = lax.axis_index("gx")
    side_y = lax.axis_index("gy")

    def column(cell, spread):
        if spread == 1:
            return cell % nz
        return (cell // (nz * cy)) % spread * nz + cell % nz

    def row(k, cell):
        x, y = cell // (nz * cy), (cell // nz) % cy
        if k == 0:
            return x // parts[0][1] * cy + y
        name = kinds[k - 1][0]
        if name[0] == "x":
            at = {"xl": cx - 1, "xh": 0, "xs": side_x * (cx - 1)}[name]
            return jnp.where(x == at, y, -1)
        at = {"yl": cy - 1, "yh": 0, "ys": side_y * (cy - 1)}[name]
        return jnp.where(y == at, x, -1)

    marks[...] = jnp.zeros_like(marks)
    starts = [0]
    for count, spread in parts:
        starts.append(starts[-1] + count * spread)

    def pick(n):
        start = n * block
        for k, (count, spread) in enumerate(parts):
            if k == 0:
                cell = cells[1, pl.ds(start, block)]
            else:
                cell = pays[k - 1][pl.ds((nv + 3) * count + start, block)].astype(jnp.int32)
                cell = cell + cx * cy * nz
            at_row = row(k, cell)
            at_column = column(cell, spread).T
            up = lax.broadcasted_iota(jnp.int32, (count, lanes), 0)
            along = lax.broadcasted_iota(jnp.int32, (lanes, spread * nz), 1)
            for b in range(block):
                hit = jnp.where(up == at_row[b : b + 1], 1.0, 0.0)
                here = pl.ds(pl.multiple_of((start + b) * lanes, lanes), lanes)
                hits[k][:, here] = hit
                picks[k][here] = jnp.where(at_column[:, b : b + 1] == along, 1.0, 0.0).astype(
                    jnp.bfloat16
                )
            here = pl.ds(pl.multiple_of(start * lanes, lanes), block * lanes)
            seen = jnp.dot(
                hits[k][:, here].astype(jnp.bfloat16),
                picks[k][here],
                preferred_element_type=jnp.float32,
            )
            for s in range(spread):
                at = slice(starts[k] + s * count, starts[k] + (s + 1) * count)
                marks[at] += seen[:, s * nz : (s + 1) * nz]

    each(nq // block, pick)

    def cleared(k, s, values):
        count = parts[k][0]
        mark = marks[starts[k] + s * count : starts[k] + (s + 1) * count]
        return jnp.where(mark[None] > 0.5, 0.0, values)

    top = 8
    count, spread = parts[0]
    for s in range(spread):
        for x in range(s, cx, spread):
            mark = marks[s * count + x // spread * cy : s * count + (x // spread + 1) * cy]
            ext[:nv, 1 + x, top : top + cy] = jnp.where(mark[None] > 0.5, 0.0, cons[:, x])
    ext[nv:, 1 : cx + 1, top : top + cy] = vel[...]
    none_x = jnp.zeros((nv + 3, cy, nz), jnp.float32)
    none_y = jnp.zeros((nv + 3, cx, nz), jnp.float32)
    sides = {"xl": none_x, "xh": none_x, "yl": none_y, "yh": none_y}
    for k, (name, _) in enumerate(kinds):
        count = parts[k + 1][0]
        halo = pays[k][: (nv + 3) * count].reshape(nv + 3, count, nz)
        halo = jnp.concatenate([cleared(k + 1, 0, halo[:nv]), halo[nv:]], axis=0)
        if name[1] == "s":
            side = side_x if name[0] == "x" else side_y
            sides[name[0] + "l"] = jnp.where(side == 1, halo, 0.0)
            sides[name[0] + "h"] = jnp.where(side == 0, halo, 0.0)
        else:
            sides[name] = halo
    ext[:, 0, top : top + cy] = sides["xl"]
    ext[:, cx + 1, top : top + cy] = sides["xh"]
    ext[:, 1 : cx + 1, top - 1] = sides["yl"]
    ext[:, 1 : cx + 1, top + cy] = sides["yh"]

    def face(low, high):
        wave_low = jnp.minimum(jnp.minimum(low, high) - signal_speed, 0.0)
        wave_high = jnp.maximum(jnp.maximum(low, high) + signal_speed, 0.0)
        scale = courant_number / (wave_high - wave_low)
        return (
            scale * wave_high * (low - wave_low),
            scale * wave_low * (wave_high - high),
        )

    centre = jnp.ones((cx, cy, nz), jnp.float32)
    for d in range(3):
        speed = window(ext, nv + d, cx, cy)
        up_low, up_high = face(speed, shifted(ext, nv + d, cx, cy, d, 1))
        down_low, down_high = face(shifted(ext, nv + d, cx, cy, d, -1), speed)
        centre = centre - up_low + down_high
        coefs[2 * d] = down_low
        coefs[2 * d + 1] = -up_high
    coefs[6] = centre


def window(ext, v, cx, cy, move_x=0, move_y=0):
    return ext[v, 1 + move_x : 1 + move_x + cx, 8 + move_y : 8 + move_y + cy]


def along_z(value, by):
    nz = value.shape[-1]
    at = lax.broadcasted_iota(jnp.int32, (1,) + value.shape[1:], 2)
    edge = 0 if by < 0 else nz - 1
    return jnp.where(at == edge, 0.0, pltpu.roll(value, (-by) % nz, 2))


def shifted(ext, v, cx, cy, d, by):
    if d == 2 and by:
        return along_z(window(ext, v, cx, cy), by)
    return window(ext, v, cx, cy, by if d == 0 else 0, by if d == 1 else 0)


def step_kernel(ngx, ngy, received, coefs, before, *rest):
    kinds = neighbours(ngx, ngy)
    parts = fills(kinds, *coefs.shape[1:3])
    hits = rest[: len(parts)]
    picks = rest[len(parts) : 2 * len(parts)]
    out, ext, vals, acc = rest[2 * len(parts) :]
    cx, cy, nz = coefs.shape[1:]
    nv = received.shape[1]
    lanes = received.shape[2] // (-(-len(parts) // 4))
    slots = lanes // 4
    ng = per = lanes // slots
    nq = received.shape[0] // ng

    lane = lax.broadcasted_iota(jnp.int32, (nv, lanes), 1) // slots
    for k in range(len(parts)):
        for p in range(nq):
            tile = None
            for g in range(ng):
                t = k // per
                piece = received[g * nq + p, :, t * lanes : (t + 1) * lanes]
                turn = (g - k) % per
                if turn:
                    piece = pltpu.roll(piece, turn * slots, 1)
                tile = piece if tile is None else jnp.where(lane == g, piece, tile)
            vals[k, :, p * lanes : (p + 1) * lanes] = tile

    starts = [0]
    for count, spread in parts:
        starts.append(starts[-1] + nv * count * spread)

    def fill(n):
        here = pl.ds(pl.multiple_of(n * block * lanes, lanes), block * lanes)
        for k, (count, spread) in enumerate(parts):
            high, low = split(vals[k, :, here])
            hit = hits[k][:, here]
            pieces = [hit * high[v : v + 1].astype(jnp.float32) for v in range(nv)]
            pieces += [hit * low[v : v + 1].astype(jnp.float32) for v in range(nv)]
            left = jnp.concatenate(pieces, axis=0).astype(jnp.bfloat16)
            total = jnp.dot(left, picks[k][here], preferred_element_type=jnp.float32)
            total = total[: nv * count] + total[nv * count :]
            for s in range(spread):
                at = slice(starts[k] + s * nv * count, starts[k] + (s + 1) * nv * count)
                value = total[:, s * nz : (s + 1) * nz]
                if nq == block:
                    acc[at] = value
                else:
                    acc[at] += value

    if nq != block:
        acc[...] = jnp.zeros_like(acc)
    each(nq // block, fill)

    top = 8
    count, spread = parts[0]
    for s in range(spread):
        new = acc[starts[0] + s * nv * count : starts[0] + (s + 1) * nv * count]
        new = new.reshape(nv, cx // spread, cy, nz)
        for x in range(s, cx, spread):
            span = slice(top, top + cy)
            ext[:, 1 + x, span] = before[:nv, 1 + x, span] + new[:, x // spread]
    side_x = lax.axis_index("gx")
    side_y = lax.axis_index("gy")
    sides = {"xl": 0.0, "xh": 0.0, "yl": 0.0, "yh": 0.0}
    for k, (name, _) in enumerate(kinds):
        new = acc[starts[k + 1] : starts[k + 2]].reshape(nv, parts[k + 1][0], nz)
        if name[1] == "s":
            side = side_x if name[0] == "x" else side_y
            sides[name[0] + "l"] = jnp.where(side == 1, new, 0.0)
            sides[name[0] + "h"] = jnp.where(side == 0, new, 0.0)
        else:
            sides[name] = new
    for name, at in (("xl", 0), ("xh", cx + 1)):
        ext[:, at, top : top + cy] = before[:nv, at, top : top + cy] + sides[name]
    for name, at in (("yl", top - 1), ("yh", top + cy)):
        ext[:, 1 : cx + 1, at] = before[:nv, 1 : cx + 1, at] + sides[name]

    for v in range(fluid_count):
        total = coefs[6] * window(ext, v, cx, cy)
        for d in range(3):
            for n, by in enumerate((-1, 1)):
                total = total + coefs[2 * d + n] * shifted(ext, v, cx, cy, d, by)
        out[v] = total

    def electric(n, d, by):
        a, b = (n + 1) % 3, (n + 2) % 3
        if d == 2 and by:
            return along_z(electric(n, 2, 0), by)

        def at(v):
            return shifted(ext if v < nv else before, v, cx, cy, d, by)

        return at(nv + b) * at(fluid_count + a) - at(nv + a) * at(fluid_count + b)

    def central(n, d):
        return electric(n, d, 1) - electric(n, d, -1)

    for n in range(3):
        a, b = (n + 1) % 3, (n + 2) % 3
        curl = central(b, a) - central(a, b)
        out[fluid_count + n] = window(ext, fluid_count + n, cx, cy) - (0.5 * courant_number) * curl


def per_device(ngx, ngy, conserved, velocity, donor_corner, donor_fraction, target_cell):
    kinds = neighbours(ngx, ngy)
    cons = conserved[:, 0]
    vel = velocity[:, 0]
    corner = donor_corner[0, 0, 0]
    fraction = donor_fraction[:, 0, 0, 0]
    target = target_cell[0, 0, 0]
    nv, cx, cy, nz = cons.shape
    ng, nq, slots = corner.shape
    lanes = ng * slots
    rows = cx * cy
    tiles = -(-(1 + len(kinds)) * slots // lanes)
    f32 = jnp.float32
    params = pltpu.CompilerParams(vmem_limit_bytes=min(56, 10 + 6 * nq // block) << 20)

    pay_shapes = []
    layer_shapes = []
    for name, _ in kinds:
        along = cy if name[0] == "x" else cx
        pay_shapes.append(jax.ShapeDtypeStruct(((nv + 3) * along + nq, nz), f32))
        layer = (nv + 3, 1, cy, nz) if name[0] == "x" else (nv + 3, cx, 8, nz)
        layer_shapes.append(pltpu.VMEM(layer, f32))
    copies = 3 + 2 * len(kinds)
    whole = pltpu.CompilerParams(vmem_limit_bytes=56 << 20)
    cells, fractions, *pays = pl.pallas_call(
        functools.partial(edge_kernel, ngx, ngy),
        out_shape=[
            jax.ShapeDtypeStruct((2, nq, lanes), jnp.int32),
            jax.ShapeDtypeStruct((3, nq, lanes), f32),
        ]
        + pay_shapes,
        in_specs=[pl.BlockSpec(memory_space=pltpu.HBM)] * 5,
        scratch_shapes=layer_shapes
        + [
            pltpu.VMEM((2, ng, nq, slots), jnp.int32),
            pltpu.VMEM((3, ng, nq, slots), f32),
            pltpu.SemaphoreType.DMA((copies,)),
        ],
        compiler_params=whole,
        name="edge",
    )(cons, vel, corner, fraction, target)

    arrived = []
    for (name, _), pay in zip(kinds, pays):
        axis, count = ("gx", ngx) if name[0] == "x" else ("gy", ngy)
        pairs = {
            "s": [(0, 1), (1, 0)],
            "l": [(n + 1, n) for n in range(count - 1)],
            "h": [(n, n + 1) for n in range(count - 1)],
        }[name[1]]
        arrived.append((name, lax.ppermute(pay, axis, pairs)))
    found = dict(arrived)
    flip = {"xl": "xh", "xh": "xl", "yl": "yh", "yh": "yl", "xs": "xs", "ys": "ys"}
    halos = [found[flip[name]] for name, _ in kinds]

    vmem = pl.BlockSpec(memory_space=pltpu.VMEM)
    unread = pl.BlockSpec(memory_space=pl.ANY)
    moved = pl.pallas_call(
        blend_kernel,
        out_shape=jax.ShapeDtypeStruct((lanes // slots, nq, nv, lanes), f32),
        scratch_shapes=[pltpu.VMEM((nv * rows, 2 * nz), jnp.bfloat16)],
        compiler_params=params,
        name="blend",
    )(cons, cells, fractions)
    blended = pl.pallas_call(
        functools.partial(assemble_kernel, ngx, ngy),
        out_shape=jax.ShapeDtypeStruct((ng * nq, nv, tiles * lanes), f32),
        in_specs=[vmem] + [unread] * len(kinds),
        compiler_params=params,
        name="assemble",
    )(moved, *halos)

    received = lax.all_to_all(
        blended, ("grp", "gx", "gy"), split_axis=0, concat_axis=0, tiled=True
    )

    parts = fills(kinds, cx, cy)
    ext_shape = (nv + 3, cx + 2, cy + 16, nz)
    prepared = pl.pallas_call(
        functools.partial(prepare_kernel, ngx, ngy),
        out_shape=[
            jax.ShapeDtypeStruct((7, cx, cy, nz), f32),
            jax.ShapeDtypeStruct(ext_shape, f32),
        ]
        + [jax.ShapeDtypeStruct((count, nq * lanes), f32) for count, _ in parts]
        + [jax.ShapeDtypeStruct((nq * lanes, spread * nz), jnp.bfloat16) for _, spread in parts],
        in_specs=[vmem] * 3 + [unread] + [vmem] * len(kinds),
        scratch_shapes=[
            pltpu.VMEM((sum(count * spread for count, spread in parts), nz), f32),
        ],
        compiler_params=params,
        name="prepare",
    )(cons, vel, cells, blended, *halos)

    result = pl.pallas_call(
        functools.partial(step_kernel, ngx, ngy),
        out_shape=jax.ShapeDtypeStruct((nv, cx, cy, nz), f32),
        scratch_shapes=[
            pltpu.VMEM((nv,) + ext_shape[1:], f32),
            pltpu.VMEM((len(parts), nv, nq * lanes), f32),
            pltpu.VMEM((nv * sum(count * spread for count, spread in parts), nz), f32),
        ],
        compiler_params=params,
        name="step",
    )(received, *prepared)
    return result[:, None]


def solution(mesh):
    return jax.shard_map(
        functools.partial(per_device, mesh.shape["gx"], mesh.shape["gy"]),
        mesh=mesh,
        in_specs=(
            P(None, "grp", "gx", "gy", None),
            P(None, "grp", "gx", "gy", None),
            P("grp", "gx", "gy", None, None, None),
            P(None, "grp", "gx", "gy", None, None, None),
            P("grp", "gx", "gy", None, None, None),
        ),
        out_specs=P(None, "grp", "gx", "gy", None),
        check_vma=False,
    )
```

```python
import functools

import jax
import jax.numpy as jnp
from jax import lax
from jax.experimental import pallas as pl
from jax.experimental.pallas import tpu as pltpu
from jax.sharding import PartitionSpec as P

signal_speed = 0.5
courant_number = 0.3
fluid_count = 5
block = 8


def neighbours(ngx, ngy):
    def partner(count, phase, n):
        other = n + 1 if (n + phase) % 2 == 0 else n - 1
        return other if 0 <= other < count else n

    kinds = []
    for phase in range(min(ngx - 1, 2)):
        kinds.append(("gx", phase, lambda i, j, phase=phase: (partner(ngx, phase, i), j)))
    for phase in range(min(ngy - 1, 2)):
        kinds.append(("gy", phase, lambda i, j, phase=phase: (i, partner(ngy, phase, j))))
    return kinds


def partner_above(axis, phase):
    return (lax.axis_index(axis) + phase) % 2 == 0


def split(value):
    high = value.astype(jnp.bfloat16)
    low = (value - high.astype(jnp.float32)).astype(jnp.bfloat16)
    return high, low


def blend_kernel(ngx, ngy, cons, vel, corner, fraction, target, out, *rest):
    kinds = neighbours(ngx, ngy)
    pays = rest[: len(kinds)]
    uhl, base, fx, fy, fz, packed, moved = rest[len(kinds) :]
    nv, cx, cy, nz = cons.shape
    ng, nq, slots = corner.shape
    lanes = ng * slots
    rows = cx * cy
    per = lanes // slots

    for g in range(ng):
        cols = slice(g * slots, (g + 1) * slots)
        base[:, cols] = corner[g]
        fx[:, cols] = fraction[0, g]
        fy[:, cols] = fraction[1, g]
        fz[:, cols] = fraction[2, g]
        packed[:, cols] = target[g]

    aim = (packed[...] - rows * nz).astype(jnp.float32)
    for (axis, phase, _), pay in zip(kinds, pays):
        along = cy if axis == "gx" else cx
        above = partner_above(axis, phase)
        for count, source, start in ((nv, cons, 0), (3, vel, nv * along)):
            if axis == "gx":
                layer = source[:, pl.ds(jnp.where(above, cx - 1, 0), 1)]
            else:
                layer = source[:, :, pl.ds(jnp.where(above, cy - 1, 0), 1)]
            pay[start : start + count * along] = layer.reshape(count * along, nz)
        pay[(nv + 3) * along :] = aim

    high, low = split(cons[...].reshape(nv * rows, nz))
    uhl[:, :nz] = high
    uhl[:, nz:] = low

    depth = lax.broadcasted_iota(jnp.int32, (nz, lanes), 0)
    row_x = lax.broadcasted_iota(jnp.int32, (rows, lanes), 0) // cy
    row_y = lax.broadcasted_iota(jnp.int32, (rows, lanes), 0) % cy

    def weight(place, at, upper):
        return jnp.where(place == at, 1.0 - upper, jnp.where(place == at + 1, upper, 0.0))

    def blend(start):
        def one(q):
            row = pl.ds(start + q, 1)
            cell = base[row]
            wz = weight(depth, cell % nz, fz[row])
            wx = weight(row_x, cell // (nz * cy), fx[row])
            wy = weight(row_y, (cell // nz) % cy, fy[row])
            return split(wz) + (wx * wy,)

        for q in range(0, block, 2):
            h0, l0, w0 = one(q)
            h1, l1, w1 = one(q + 1)
            wh = jnp.concatenate([h0, h1], axis=1)
            wl = jnp.concatenate([l0, l1], axis=1)
            along = jnp.dot(
                uhl[...], jnp.concatenate([wh, wh], axis=0), preferred_element_type=jnp.float32
            ) + jnp.dot(uhl[:, :nz], wl, preferred_element_type=jnp.float32)
            wxy = jnp.concatenate([w0, w1], axis=1)
            values = jnp.sum(along.reshape(nv, rows, 2 * lanes) * wxy[None], axis=1)
            for half in range(2):
                value = values[:, half * lanes : (half + 1) * lanes]
                for turn in range(per):
                    moved[turn, start + q + half] = (
                        pltpu.roll(value, turn * slots, 1) if turn else value
                    )

    if nq == block:
        blend(0)
    else:
        lax.fori_loop(0, nq // block, lambda n, c: (blend(n * block), c)[1], 0)

    lane = lax.broadcasted_iota(jnp.int32, (nv, lanes), 1) // slots
    for h in range(ng):
        for q in range(nq):
            i, j = q // ngy, q % ngy
            owners = [q] + [a * ngy + b for a, b in (of(i, j) for _, _, of in kinds)]
            for t in range(0, len(owners), per):
                tile = None
                for k, owner in enumerate(owners[t : t + per]):
                    piece = moved[(k - h) % per, owner]
                    tile = piece if tile is None else jnp.where(lane == k, piece, tile)
                out[h * nq + q, :, t // per * lanes : (t // per + 1) * lanes] = tile


def step_kernel(ngx, ngy, cons, vel, target, received, *rest):
    kinds = neighbours(ngx, ngy)
    pays = rest[: len(kinds)]
    out, ext, own, vals, acc = rest[len(kinds) :]
    nv, cx, cy, nz = cons.shape
    ng, nq, slots = target.shape
    lanes = ng * slots
    rows = cx * cy
    per = lanes // slots

    for g in range(ng):
        own[:, g * slots : (g + 1) * slots] = target[g]

    lane = lax.broadcasted_iota(jnp.int32, (nv, lanes), 1) // slots
    for k in range(1 + len(kinds)):
        for p in range(nq):
            tile = None
            for g in range(ng):
                t = k // per
                piece = received[g * nq + p, :, t * lanes : (t + 1) * lanes]
                turn = (g - k) % per
                if turn:
                    piece = pltpu.roll(piece, turn * slots, 1)
                tile = piece if tile is None else jnp.where(lane == g, piece, tile)
            vals[k, :, p * lanes : (p + 1) * lanes] = tile

    parts = [(rows, lambda cell: cell // nz)]
    for axis, phase, _ in kinds:
        above = partner_above(axis, phase)
        if axis == "gx":
            at = jnp.where(above, 0, cx - 1)
            parts.append((cy, lambda cell, at=at: cell // nz - at * cy))
        else:
            at = jnp.where(above, 0, cy - 1)
            parts.append(
                (
                    cx,
                    lambda cell, at=at: jnp.where(
                        (cell // nz) % cy == at, cell // (nz * cy), -1
                    ),
                )
            )

    offsets = [0]
    for count, _ in parts:
        offsets.append(offsets[-1] + (nv + 1) * count)

    def fill(start, first):
        for k, (count, place) in enumerate(parts):
            if k == 0:
                cells = own[pl.ds(start, block)]
            else:
                along = parts[k][0]
                cells = pays[k - 1][pl.ds((nv + 3) * along + start, block)].astype(jnp.int32)
                cells = cells + rows * nz
            at_row = place(cells)
            at_z = cells % nz
            high, low = split(vals[k, :, pl.ds(start * lanes, block * lanes)])
            high = high.astype(jnp.float32)
            low = low.astype(jnp.float32)
            up_rows = lax.broadcasted_iota(jnp.int32, (count, lanes), 0)
            up_z = lax.broadcasted_iota(jnp.int32, (nz, lanes), 0)
            total = None
            for b in range(block):
                cols = slice(b * lanes, (b + 1) * lanes)
                hit = up_rows == at_row[b : b + 1]
                picks = (up_z == at_z[b : b + 1]).astype(jnp.float32).astype(jnp.bfloat16)
                pieces = [jnp.where(hit, high[v : v + 1, cols], 0.0) for v in range(nv)]
                pieces += [jnp.where(hit, 1.0, 0.0)]
                pieces += [jnp.where(hit, low[v : v + 1, cols], 0.0) for v in range(nv)]
                left = jnp.concatenate(pieces, axis=0).astype(jnp.bfloat16)
                term = lax.dot_general(
                    left, picks, (((1,), (1,)), ((), ())), preferred_element_type=jnp.float32
                )
                total = term if total is None else total + term
            filled = total[: nv * count] + total[(nv + 1) * count :]
            span = slice(offsets[k], offsets[k] + nv * count)
            marks = slice(offsets[k] + nv * count, offsets[k + 1])
            if first:
                acc[span] = filled
                acc[marks] = total[nv * count : (nv + 1) * count]
            else:
                acc[span] += filled
                acc[marks] += total[nv * count : (nv + 1) * count]

    if nq == block:
        fill(0, True)
    else:
        acc[...] = jnp.zeros_like(acc)
        lax.fori_loop(0, nq // block, lambda n, c: (fill(n * block, False), c)[1], 0)

    def merged(k, before):
        count = parts[k][0]
        new = acc[offsets[k] : offsets[k] + nv * count].reshape(nv, count, nz)
        mark = acc[offsets[k] + nv * count : offsets[k + 1]]
        return jnp.where(mark[None] > 0.5, new, before.reshape(nv, count, nz))

    top = 8
    ext[:nv, 1 : cx + 1, top : top + cy] = merged(0, cons[...]).reshape(nv, cx, cy, nz)
    ext[nv:, 1 : cx + 1, top : top + cy] = vel[...]
    sides = {("gx", True): 0.0, ("gx", False): 0.0, ("gy", True): 0.0, ("gy", False): 0.0}
    for k, (axis, phase, _) in enumerate(kinds):
        count = parts[k + 1][0]
        pay = pays[k]
        halo = jnp.concatenate(
            [
                merged(k + 1, pay[: nv * count]),
                pay[nv * count : (nv + 3) * count].reshape(3, count, nz),
            ],
            axis=0,
        )
        above = partner_above(axis, phase)
        sides[axis, True] += jnp.where(above, halo, 0.0)
        sides[axis, False] += jnp.where(above, 0.0, halo)
    for (axis, above), halo in sides.items():
        count = cy if axis == "gx" else cx
        halo = jnp.broadcast_to(halo, (nv + 3, count, nz))
        if axis == "gx":
            ext[:, cx + 1 if above else 0, top : top + cy] = halo
        else:
            ext[:, 1 : cx + 1, top + cy if above else top - 1] = halo

    at_z = lax.broadcasted_iota(jnp.int32, (1, cy, nz), 2)

    def inner(v):
        return ext[v, 1 : 1 + cx, top : top + cy]

    def shifted(v, d, by):
        if by == 0:
            return inner(v)
        if d == 0:
            return ext[v, 1 + by : 1 + by + cx, top : top + cy]
        if d == 1:
            return ext[v, 1 : 1 + cx, top + by : top + by + cy]
        return along_z(inner(v), by)

    def along_z(value, by):
        edge = 0 if by < 0 else nz - 1
        return jnp.where(at_z == edge, 0.0, pltpu.roll(value, (-by) % nz, 2))

    def face(low, high):
        wave_low = jnp.minimum(jnp.minimum(low, high) - signal_speed, 0.0)
        wave_high = jnp.maximum(jnp.maximum(low, high) + signal_speed, 0.0)
        scale = courant_number / (wave_high - wave_low)
        return (
            scale * wave_high * (low - wave_low),
            scale * wave_low * (wave_high - high),
        )

    centre = jnp.ones((cx, cy, nz), jnp.float32)
    sums = [None] * fluid_count
    for d in range(3):
        speed = inner(nv + d)
        up_low, up_high = face(speed, shifted(nv + d, d, 1))
        down_low, down_high = face(shifted(nv + d, d, -1), speed)
        centre = centre - up_low + down_high
        for v in range(fluid_count):
            term = down_low * shifted(v, d, -1) - up_high * shifted(v, d, 1)
            sums[v] = term if sums[v] is None else sums[v] + term
    for v in range(fluid_count):
        out[v] = sums[v] + centre * inner(v)

    def electric(n, d, by):
        a, b = (n + 1) % 3, (n + 2) % 3
        if d == 2 and by:
            return along_z(electric(n, 2, 0), by)
        return shifted(nv + b, d, by) * shifted(fluid_count + a, d, by) - shifted(
            nv + a, d, by
        ) * shifted(fluid_count + b, d, by)

    def central(n, d):
        return electric(n, d, 1) - electric(n, d, -1)

    for n in range(3):
        a, b = (n + 1) % 3, (n + 2) % 3
        curl = central(b, a) - central(a, b)
        out[fluid_count + n] = inner(fluid_count + n) - (0.5 * courant_number) * curl


def per_device(ngx, ngy, conserved, velocity, donor_corner, donor_fraction, target_cell):
    kinds = neighbours(ngx, ngy)
    cons = conserved[:, 0]
    vel = velocity[:, 0]
    corner = donor_corner[0, 0, 0]
    fraction = donor_fraction[:, 0, 0, 0]
    target = target_cell[0, 0, 0]
    nv, cx, cy, nz = cons.shape
    ng, nq, slots = corner.shape
    lanes = ng * slots
    rows = cx * cy
    tiles = -(-(1 + len(kinds)) * slots // lanes)
    f32 = jnp.float32

    pay_shapes = []
    for axis, _, _ in kinds:
        along = cy if axis == "gx" else cx
        pay_shapes.append(jax.ShapeDtypeStruct(((nv + 3) * along + nq, nz), f32))
    params = pltpu.CompilerParams(vmem_limit_bytes=48 * 1024 * 1024)
    outs = pl.pallas_call(
        functools.partial(blend_kernel, ngx, ngy),
        out_shape=[jax.ShapeDtypeStruct((ng * nq, nv, tiles * lanes), f32)] + pay_shapes,
        scratch_shapes=[
            pltpu.VMEM((nv * rows, 2 * nz), jnp.bfloat16),
            pltpu.VMEM((nq, lanes), jnp.int32),
            pltpu.VMEM((nq, lanes), f32),
            pltpu.VMEM((nq, lanes), f32),
            pltpu.VMEM((nq, lanes), f32),
            pltpu.VMEM((nq, lanes), jnp.int32),
            pltpu.VMEM((lanes // slots, nq, nv, lanes), f32),
        ],
        compiler_params=pltpu.CompilerParams(vmem_limit_bytes=56 << 20),
        name="blend",
    )(cons, vel, corner, fraction, target)
    blended, pays = outs[0], outs[1:]

    received = lax.all_to_all(
        blended, ("grp", "gx", "gy"), split_axis=0, concat_axis=0, tiled=True
    )
    halos = []
    for (axis, phase, _), pay in zip(kinds, pays):
        count = ngx if axis == "gx" else ngy
        pairs = []
        for low in range(phase, count - 1, 2):
            pairs += [(low, low + 1), (low + 1, low)]
        halos.append(lax.ppermute(pay, axis, pairs))

    count = sum((nv + 1) * (cy if axis == "gx" else cx) for axis, _, _ in kinds)
    result = pl.pallas_call(
        functools.partial(step_kernel, ngx, ngy),
        out_shape=jax.ShapeDtypeStruct((nv, cx, cy, nz), f32),
        scratch_shapes=[
            pltpu.VMEM((nv + 3, cx + 2, cy + 16, nz), f32),
            pltpu.VMEM((nq, lanes), jnp.int32),
            pltpu.VMEM((1 + len(kinds), nv, nq * lanes), f32),
            pltpu.VMEM(((nv + 1) * rows + count, nz), f32),
        ],
        compiler_params=params,
        name="step",
    )(cons, vel, target, received, *halos)
    return result[:, None]


def solution(mesh):
    return jax.shard_map(
        functools.partial(per_device, mesh.shape["gx"], mesh.shape["gy"]),
        mesh=mesh,
        in_specs=(
            P(None, "grp", "gx", "gy", None),
            P(None, "grp", "gx", "gy", None),
            P("grp", "gx", "gy", None, None, None),
            P(None, "grp", "gx", "gy", None, None, None),
            P("grp", "gx", "gy", None, None, None),
        ),
        out_specs=P(None, "grp", "gx", "gy", None),
        check_vma=False,
    )
```

```python
import functools

import jax
import jax.numpy as jnp
from jax import lax
from jax.experimental import pallas as pl
from jax.experimental.pallas import tpu as pltpu
from jax.sharding import PartitionSpec as P

signal_speed = 0.5
courant_number = 0.3
fluid_count = 5
block = 8


def exchanges(ngx, ngy):
    kinds = [("gx", phase) for phase in range(min(ngx - 1, 2))]
    return kinds + [("gy", phase) for phase in range(min(ngy - 1, 2))]


def partner_above(axis, phase):
    return (lax.axis_index(axis) + phase) % 2 == 0


def split(value):
    high = value.astype(jnp.bfloat16)
    low = (value - high.astype(jnp.float32)).astype(jnp.bfloat16)
    return high, low


def each(count, body):
    if count == 1:
        body(0)
    else:
        lax.fori_loop(0, count, lambda n, c: (body(n), c)[1], 0)


def block_transpose(value, slots):
    rows, lanes = value.shape
    count = lanes // slots
    each_rows = rows // count
    at_row = lax.broadcasted_iota(jnp.int32, value.shape, 0) // each_rows
    at_lane = lax.broadcasted_iota(jnp.int32, value.shape, 1) // slots
    result = value
    for d in range(1, count):
        turned = pltpu.roll(value, d * each_rows, 0)
        turned = pltpu.roll(turned, lanes - d * slots, 1)
        result = jnp.where((at_row - at_lane) % count == d, turned, result)
    return result


def blend_kernel(cons, corner, fraction, out, uhl, cells, parts):
    nv, cx, cy, nz = cons.shape
    ng, nq, slots = corner.shape
    lanes = nz
    per = lanes // slots
    chunks = block // per
    rows = cx * cy
    me = lax.axis_index("grp")

    high, low = split(cons[...].reshape(nv * rows, nz))
    uhl[:, :nz] = high
    uhl[:, nz:] = low

    depth = lax.broadcasted_iota(jnp.int32, (nz, lanes), 0)
    row_x = lax.broadcasted_iota(jnp.int32, (rows, lanes), 0) // cy
    row_y = lax.broadcasted_iota(jnp.int32, (rows, lanes), 0) % cy

    def weight(place, at, upper):
        return jnp.where(place == at, 1.0 - upper, jnp.where(place == at + 1, upper, 0.0))

    def blend(n):
        out[pl.ds(me * nq + n * block, block)] = jnp.zeros((block,) + out.shape[1:], jnp.float32)
        for away in range(1, ng):
            h = (me + away) % ng
            for c in range(chunks):
                at = (away - 1) * chunks + c
                for q in range(per):
                    row = pl.ds(n * block + c * per + q, 1)
                    cols = slice(q * slots, (q + 1) * slots)
                    cells[at : at + 1, cols] = corner[h, row]
                    for d in range(3):
                        parts[d, at : at + 1, cols] = fraction[d, h, row]

        def one(at):
            cell = cells[at : at + 1]
            wz = weight(depth, cell % nz, parts[2, at : at + 1])
            wx = weight(row_x, cell // (nz * cy), parts[0, at : at + 1])
            wy = weight(row_y, (cell // nz) % cy, parts[1, at : at + 1])
            return split(wz) + (wx * wy,)

        for away in range(1, ng):
            h = (me + away) % ng
            made = [one((away - 1) * chunks + c) for c in range(chunks)]
            wh = jnp.concatenate([m[0] for m in made], axis=1)
            wl = jnp.concatenate([m[1] for m in made], axis=1)
            wxy = jnp.concatenate([m[2] for m in made], axis=1)
            along = jnp.dot(
                uhl[...], jnp.concatenate([wh, wh], axis=0), preferred_element_type=jnp.float32
            ) + jnp.dot(uhl[:, :nz], wl, preferred_element_type=jnp.float32)
            values = jnp.sum(along.reshape(nv, rows, chunks * lanes) * wxy[None], axis=1)
            for c in range(chunks):
                value = block_transpose(values[:, c * lanes : (c + 1) * lanes], slots)
                start = h * nq + n * block + c * per
                out[pl.ds(start, per)] = value.reshape(per, nv // per, lanes)

    each(nq // block, blend)


def fill_kernel(kinds, cons, vel, target, received, filled, *rest):
    pays = rest[: len(kinds)]
    cells, acc = rest[len(kinds) :]
    nv, cx, cy, nz = cons.shape
    ng, nq, slots = target.shape
    lanes = nz
    per = lanes // slots
    chunks = block // per
    spread = 4 if cx % 4 == 0 else 1
    count = cx // spread * cy
    me = lax.axis_index("grp")

    up = lax.broadcasted_iota(jnp.int32, (count, lanes), 0)
    along = lax.broadcasted_iota(jnp.int32, (lanes, spread * nz), 1)
    cells[...] = jnp.full(cells.shape, cx * cy * nz, jnp.int32)

    def fill(n):
        for away in range(1, ng):
            g = (me + away) % ng
            for c in range(chunks):
                at = (away - 1) * chunks + c
                for q in range(per):
                    row = pl.ds(n * block + c * per + q, 1)
                    cells[at : at + 1, q * slots : (q + 1) * slots] = target[g, row]
        cell = cells[...]
        x, y, z = cell // (nz * cy), (cell // nz) % cy, cell % nz
        at_row = x // spread * cy + y
        at_column = (x % spread * nz + z).T
        total = None
        for away in range(1, ng):
            g = (me + away) % ng
            lefts, picks = [], []
            for c in range(chunks):
                at = (away - 1) * chunks + c
                start = g * nq + n * block + c * per
                value = received[pl.ds(start, per)].reshape(nv, lanes)
                value = block_transpose(value, slots)
                high = value.astype(jnp.bfloat16).astype(jnp.float32)
                low = value - high
                hit = up == at_row[at : at + 1]
                pieces = [jnp.where(hit, high[v : v + 1], 0.0) for v in range(nv)]
                pieces += [jnp.where(hit, low[v : v + 1], 0.0) for v in range(nv)]
                pieces += [jnp.where(hit, 1.0, 0.0)]
                lefts.append(jnp.concatenate(pieces, axis=0).astype(jnp.bfloat16))
                pick = jnp.where(at_column[:, at : at + 1] == along, 1.0, 0.0)
                picks.append(pick.astype(jnp.bfloat16))
            term = jnp.dot(
                jnp.concatenate(lefts, axis=1),
                jnp.concatenate(picks, axis=0),
                preferred_element_type=jnp.float32,
            )
            total = term if total is None else total + term
        if nq == block:
            acc[...] = total
        else:
            acc[...] += total

    if nq != block:
        acc[...] = jnp.zeros_like(acc)
    each(nq // block, fill)

    size = nv * count
    for s in range(spread):
        cols = slice(s * nz, (s + 1) * nz)
        value = (acc[:size, cols] + acc[size : 2 * size, cols]).reshape(nv, cx // spread, cy, nz)
        mark = acc[2 * size :, cols].reshape(cx // spread, cy, nz) > 0.5
        for x in range(cx // spread):
            at = x * spread + s
            filled[:, at] = jnp.where(mark[x][None], value[:, x], cons[:, at])

    for (axis, phase), pay in zip(kinds, pays):
        above = partner_above(axis, phase)
        d = 0 if axis == "gx" else 1

        def layer(array, v):
            if d == 0:
                return array[v, pl.ds(jnp.where(above, cx - 1, 0), 1)].reshape(cy, nz)
            return array[v, :, pl.ds(jnp.where(above, cy - 1, 0), 1)].reshape(cx, nz)

        speeds = [layer(vel, n) for n in range(3)]
        field = [layer(filled, fluid_count + n) for n in range(3)]
        sent = [layer(filled, v) for v in range(fluid_count)] + [speeds[d]]
        for n in (1 - d, 2):
            a, b = (n + 1) % 3, (n + 2) % 3
            sent.append(speeds[b] * field[a] - speeds[a] * field[b])
        size = sent[0].shape[0]
        for n, value in enumerate(sent):
            pay[n * size : (n + 1) * size] = value


top = 8


def window(ext, v, cx, cy, move_x=0, move_y=0):
    return ext[v, 1 + move_x : 1 + move_x + cx, top + move_y : top + move_y + cy]


def along_z(value, by):
    nz = value.shape[-1]
    at = lax.broadcasted_iota(jnp.int32, (1,) + value.shape[1:], 2)
    edge = 0 if by < 0 else nz - 1
    return jnp.where(at == edge, 0.0, pltpu.roll(value, (-by) % nz, 2))


def shifted(ext, v, cx, cy, d, by):
    if d == 2 and by:
        return along_z(window(ext, v, cx, cy), by)
    return window(ext, v, cx, cy, by if d == 0 else 0, by if d == 1 else 0)


def face(low, high):
    wave_low = jnp.minimum(jnp.minimum(low, high) - signal_speed, 0.0)
    wave_high = jnp.maximum(jnp.maximum(low, high) + signal_speed, 0.0)
    scale = courant_number / (wave_high - wave_low)
    return (
        scale * wave_high * (low - wave_low),
        scale * wave_low * (wave_high - high),
    )


def step_kernel(kinds, filled, vel, *rest):
    pays = rest[: len(kinds)]
    out, ext, speeds = rest[len(kinds) :]
    nv, cx, cy, nz = filled.shape
    inside = (slice(1, cx + 1), slice(top, top + cy))

    ext[(slice(0, fluid_count),) + inside] = filled[:fluid_count]
    speeds[(slice(None),) + inside] = vel[...]
    for n in range(3):
        a, b = (n + 1) % 3, (n + 2) % 3
        ext[(fluid_count + n,) + inside] = (
            vel[b] * filled[fluid_count + a] - vel[a] * filled[fluid_count + b]
        )

    sides = {("gx", True): 0.0, ("gx", False): 0.0, ("gy", True): 0.0, ("gy", False): 0.0}
    for (axis, phase), pay in zip(kinds, pays):
        above = partner_above(axis, phase)
        halo = pay[...].reshape(fluid_count + 3, -1, nz)
        sides[axis, True] += jnp.where(above, halo, 0.0)
        sides[axis, False] += jnp.where(above, 0.0, halo)
    for (axis, above), halo in sides.items():
        halo = jnp.broadcast_to(halo, (fluid_count + 3, cy if axis == "gx" else cx, nz))
        if axis == "gx":
            at = (cx + 1 if above else 0, slice(top, top + cy))
            d = 0
        else:
            at = (slice(1, cx + 1), top + cy if above else top - 1)
            d = 1
        ext[(slice(0, fluid_count),) + at] = halo[:fluid_count]
        speeds[(d,) + at] = halo[fluid_count]
        ext[(fluid_count + 1 - d,) + at] = halo[fluid_count + 1]
        ext[(fluid_count + 2,) + at] = halo[fluid_count + 2]

    factors = []
    centre = jnp.ones((cx, cy, nz), jnp.float32)
    for d in range(3):
        speed = window(speeds, d, cx, cy)
        up_low, up_high = face(speed, shifted(speeds, d, cx, cy, d, 1))
        down_low, down_high = face(shifted(speeds, d, cx, cy, d, -1), speed)
        centre = centre - up_low + down_high
        factors.append((down_low, up_high))
    for v in range(fluid_count):
        total = centre * window(ext, v, cx, cy)
        for d, (down_low, up_high) in enumerate(factors):
            total = total + down_low * shifted(ext, v, cx, cy, d, -1)
            total = total - up_high * shifted(ext, v, cx, cy, d, 1)
        out[v] = total

    def central(n, d):
        v = fluid_count + n
        return shifted(ext, v, cx, cy, d, 1) - shifted(ext, v, cx, cy, d, -1)

    for n in range(3):
        a, b = (n + 1) % 3, (n + 2) % 3
        curl = central(b, a) - central(a, b)
        out[fluid_count + n] = filled[fluid_count + n] - (0.5 * courant_number) * curl


def per_device(ngx, ngy, conserved, velocity, donor_corner, donor_fraction, target_cell):
    kinds = exchanges(ngx, ngy)
    cons = conserved[:, 0]
    vel = velocity[:, 0]
    corner = donor_corner[0, 0, 0]
    fraction = donor_fraction[:, 0, 0, 0]
    target = target_cell[0, 0, 0]
    nv, cx, cy, nz = cons.shape
    ng, nq, slots = corner.shape
    rows = cx * cy
    per = nz // slots
    chunks = (ng - 1) * block // per
    padded_chunks = -(-chunks // 8) * 8
    spread = 4 if cx % 4 == 0 else 1
    f32 = jnp.float32
    params = pltpu.CompilerParams(vmem_limit_bytes=24 << 20)

    blended = pl.pallas_call(
        blend_kernel,
        out_shape=jax.ShapeDtypeStruct((ng * nq, nv // per, nz), f32),
        scratch_shapes=[
            pltpu.VMEM((nv * rows, 2 * nz), jnp.bfloat16),
            pltpu.VMEM((padded_chunks, nz), jnp.int32),
            pltpu.VMEM((3, padded_chunks, nz), f32),
        ],
        compiler_params=pltpu.CompilerParams(vmem_limit_bytes=56 << 20),
        name="blend",
    )(cons, corner, fraction)

    received = lax.all_to_all(
        blended, ("grp", "gx", "gy"), split_axis=0, concat_axis=0, tiled=True
    )

    pay_shapes = []
    for axis, _ in kinds:
        along = cy if axis == "gx" else cx
        pay_shapes.append(jax.ShapeDtypeStruct(((fluid_count + 3) * along, nz), f32))
    filled, *pays = pl.pallas_call(
        functools.partial(fill_kernel, kinds),
        out_shape=[jax.ShapeDtypeStruct((nv, cx, cy, nz), f32)] + pay_shapes,
        scratch_shapes=[
            pltpu.VMEM((padded_chunks, nz), jnp.int32),
            pltpu.VMEM(((2 * nv + 1) * rows // spread, spread * nz), f32),
        ],
        compiler_params=params,
        name="fill",
    )(cons, vel, target, received)

    halos = []
    for (axis, phase), pay in zip(kinds, pays):
        count = ngx if axis == "gx" else ngy
        pairs = []
        for low in range(phase, count - 1, 2):
            pairs += [(low, low + 1), (low + 1, low)]
        halos.append(lax.ppermute(pay, axis, pairs))

    result = pl.pallas_call(
        functools.partial(step_kernel, kinds),
        out_shape=jax.ShapeDtypeStruct((nv, cx, cy, nz), f32),
        scratch_shapes=[
            pltpu.VMEM((fluid_count + 3, cx + 2, cy + 2 * top, nz), f32),
            pltpu.VMEM((3, cx + 2, cy + 2 * top, nz), f32),
        ],
        compiler_params=params,
        name="step",
    )(filled, vel, *halos)
    return result[:, None]


def solution(mesh):
    return jax.shard_map(
        functools.partial(per_device, mesh.shape["gx"], mesh.shape["gy"]),
        mesh=mesh,
        in_specs=(
            P(None, "grp", "gx", "gy", None),
            P(None, "grp", "gx", "gy", None),
            P("grp", "gx", "gy", None, None, None),
            P(None, "grp", "gx", "gy", None, None, None),
            P("grp", "gx", "gy", None, None, None),
        ),
        out_specs=P(None, "grp", "gx", "gy", None),
        check_vma=False,
    )
```

```python
import functools

import jax
import jax.numpy as jnp
from jax import lax
from jax.experimental import pallas as pl
from jax.experimental.pallas import tpu as pltpu
from jax.sharding import PartitionSpec as P

signal_speed = 0.5
courant_number = 0.3
fluid_count = 5
block = 8


def exchanges(ngx, ngy):
    kinds = [("gx", phase) for phase in range(min(ngx - 1, 2))]
    return kinds + [("gy", phase) for phase in range(min(ngy - 1, 2))]


def partner_above(axis, phase):
    return (lax.axis_index(axis) + phase) % 2 == 0


def split(value):
    high = value.astype(jnp.bfloat16)
    low = (value - high.astype(jnp.float32)).astype(jnp.bfloat16)
    return high, low


def each(count, body):
    if count == 1:
        body(0)
    else:
        lax.fori_loop(0, count, lambda n, c: (body(n), c)[1], 0)


def block_transpose(value, slots):
    rows, lanes = value.shape
    count = lanes // slots
    each_rows = rows // count
    at_row = lax.broadcasted_iota(jnp.int32, value.shape, 0) // each_rows
    at_lane = lax.broadcasted_iota(jnp.int32, value.shape, 1) // slots
    result = value
    for d in range(1, count):
        turned = pltpu.roll(value, d * each_rows, 0)
        turned = pltpu.roll(turned, lanes - d * slots, 1)
        result = jnp.where((at_row - at_lane) % count == d, turned, result)
    return result


def blend_kernel(cons, corner, fraction, out, uhl, cells, parts):
    nv, cx, cy, nz = cons.shape
    ng, nq, slots = corner.shape
    lanes = nz
    per = lanes // slots
    chunks = block // per
    rows = cx * cy
    me = lax.axis_index("grp")

    high, low = split(cons[...].reshape(nv * rows, nz))
    uhl[:, :nz] = high
    uhl[:, nz:] = low

    depth = lax.broadcasted_iota(jnp.int32, (nz, lanes), 0)
    row_x = lax.broadcasted_iota(jnp.int32, (rows, lanes), 0) // cy
    row_y = lax.broadcasted_iota(jnp.int32, (rows, lanes), 0) % cy

    def weight(place, at, upper):
        return jnp.where(place == at, 1.0 - upper, jnp.where(place == at + 1, upper, 0.0))

    def blend(n):
        out[pl.ds(me * nq + n * block, block)] = jnp.zeros((block,) + out.shape[1:], jnp.float32)
        for away in range(1, ng):
            h = (me + away) % ng
            for c in range(chunks):
                at = (away - 1) * chunks + c
                for q in range(per):
                    row = pl.ds(n * block + c * per + q, 1)
                    cols = slice(q * slots, (q + 1) * slots)
                    cells[at : at + 1, cols] = corner[h, row]
                    for d in range(3):
                        parts[d, at : at + 1, cols] = fraction[d, h, row]

        def one(at):
            cell = cells[at : at + 1]
            wz = weight(depth, cell % nz, parts[2, at : at + 1])
            wx = weight(row_x, cell // (nz * cy), parts[0, at : at + 1])
            wy = weight(row_y, (cell // nz) % cy, parts[1, at : at + 1])
            return split(wz) + (wx * wy,)

        for away in range(1, ng):
            h = (me + away) % ng
            made = [one((away - 1) * chunks + c) for c in range(chunks)]
            wh = jnp.concatenate([m[0] for m in made], axis=1)
            wl = jnp.concatenate([m[1] for m in made], axis=1)
            wxy = jnp.concatenate([m[2] for m in made], axis=1)
            along = jnp.dot(
                uhl[...], jnp.concatenate([wh, wh], axis=0), preferred_element_type=jnp.float32
            ) + jnp.dot(uhl[:, :nz], wl, preferred_element_type=jnp.float32)
            values = jnp.sum(along.reshape(nv, rows, chunks * lanes) * wxy[None], axis=1)
            for c in range(chunks):
                value = block_transpose(values[:, c * lanes : (c + 1) * lanes], slots)
                start = h * nq + n * block + c * per
                out[pl.ds(start, per)] = value.reshape(per, nv // per, lanes)

    each(nq // block, blend)


def fill_kernel(kinds, ngy, cons, vel, target, gathered, filled, *rest):
    pays = rest[: len(kinds)]
    cells, acc, received, sem = rest[len(kinds) :]
    nv, cx, cy, nz = cons.shape
    ng, nq, slots = target.shape
    lanes = nz
    per = lanes // slots
    chunks = block // per
    spread = 4 if cx % 4 == 0 else 1
    count = cx // spread * cy
    me = lax.axis_index("grp")
    mine = me * nq + lax.axis_index("gx") * ngy + lax.axis_index("gy")
    copy = pltpu.make_async_copy(gathered.at[:, mine], received, sem)
    copy.start()

    up = lax.broadcasted_iota(jnp.int32, (count, lanes), 0)
    along = lax.broadcasted_iota(jnp.int32, (lanes, spread * nz), 1)
    cells[...] = jnp.full(cells.shape, cx * cy * nz, jnp.int32)

    def fill(n):
        for away in range(1, ng):
            g = (me + away) % ng
            for c in range(chunks):
                at = (away - 1) * chunks + c
                for q in range(per):
                    row = pl.ds(n * block + c * per + q, 1)
                    cells[at : at + 1, q * slots : (q + 1) * slots] = target[g, row]
        cell = cells[...]
        x, y, z = cell // (nz * cy), (cell // nz) % cy, cell % nz
        at_row = x // spread * cy + y
        at_column = (x % spread * nz + z).T
        if nq == block:
            copy.wait()
        total = None
        for away in range(1, ng):
            g = (me + away) % ng
            lefts, picks = [], []
            for c in range(chunks):
                at = (away - 1) * chunks + c
                start = g * nq + n * block + c * per
                value = received[pl.ds(start, per)].reshape(nv, lanes)
                value = block_transpose(value, slots)
                high = value.astype(jnp.bfloat16).astype(jnp.float32)
                low = value - high
                hit = up == at_row[at : at + 1]
                pieces = [jnp.where(hit, high[v : v + 1], 0.0) for v in range(nv)]
                pieces += [jnp.where(hit, low[v : v + 1], 0.0) for v in range(nv)]
                pieces += [jnp.where(hit, 1.0, 0.0)]
                lefts.append(jnp.concatenate(pieces, axis=0).astype(jnp.bfloat16))
                pick = jnp.where(at_column[:, at : at + 1] == along, 1.0, 0.0)
                picks.append(pick.astype(jnp.bfloat16))
            term = jnp.dot(
                jnp.concatenate(lefts, axis=1),
                jnp.concatenate(picks, axis=0),
                preferred_element_type=jnp.float32,
            )
            total = term if total is None else total + term
        if nq == block:
            acc[...] = total
        else:
            acc[...] += total

    if nq != block:
        acc[...] = jnp.zeros_like(acc)
        copy.wait()
    each(nq // block, fill)

    size = nv * count
    for s in range(spread):
        cols = slice(s * nz, (s + 1) * nz)
        value = (acc[:size, cols] + acc[size : 2 * size, cols]).reshape(nv, cx // spread, cy, nz)
        mark = acc[2 * size :, cols].reshape(cx // spread, cy, nz) > 0.5
        for x in range(cx // spread):
            at = x * spread + s
            filled[:, at] = jnp.where(mark[x][None], value[:, x], cons[:, at])

    for (axis, phase), pay in zip(kinds, pays):
        above = partner_above(axis, phase)
        d = 0 if axis == "gx" else 1

        def layer(array, v):
            if d == 0:
                return array[v, pl.ds(jnp.where(above, cx - 1, 0), 1)].reshape(cy, nz)
            return array[v, :, pl.ds(jnp.where(above, cy - 1, 0), 1)].reshape(cx, nz)

        speeds = [layer(vel, n) for n in range(3)]
        field = [layer(filled, fluid_count + n) for n in range(3)]
        sent = [layer(filled, v) for v in range(fluid_count)] + [speeds[d]]
        for n in (1 - d, 2):
            a, b = (n + 1) % 3, (n + 2) % 3
            sent.append(speeds[b] * field[a] - speeds[a] * field[b])
        size = sent[0].shape[0]
        for n, value in enumerate(sent):
            pay[n * size : (n + 1) * size] = value


top = 8


def window(ext, v, cx, cy, move_x=0, move_y=0):
    return ext[v, 1 + move_x : 1 + move_x + cx, top + move_y : top + move_y + cy]


def along_z(value, by):
    nz = value.shape[-1]
    at = lax.broadcasted_iota(jnp.int32, (1,) + value.shape[1:], 2)
    edge = 0 if by < 0 else nz - 1
    return jnp.where(at == edge, 0.0, pltpu.roll(value, (-by) % nz, 2))


def shifted(ext, v, cx, cy, d, by):
    if d == 2 and by:
        return along_z(window(ext, v, cx, cy), by)
    return window(ext, v, cx, cy, by if d == 0 else 0, by if d == 1 else 0)


def face(low, high):
    wave_low = jnp.minimum(jnp.minimum(low, high) - signal_speed, 0.0)
    wave_high = jnp.maximum(jnp.maximum(low, high) + signal_speed, 0.0)
    scale = courant_number / (wave_high - wave_low)
    return (
        scale * wave_high * (low - wave_low),
        scale * wave_low * (wave_high - high),
    )


def step_kernel(kinds, filled, vel, *rest):
    pays = rest[: len(kinds)]
    out, ext, speeds = rest[len(kinds) :]
    nv, cx, cy, nz = filled.shape
    inside = (slice(1, cx + 1), slice(top, top + cy))

    ext[(slice(0, fluid_count),) + inside] = filled[:fluid_count]
    speeds[(slice(None),) + inside] = vel[...]
    for n in range(3):
        a, b = (n + 1) % 3, (n + 2) % 3
        ext[(fluid_count + n,) + inside] = (
            vel[b] * filled[fluid_count + a] - vel[a] * filled[fluid_count + b]
        )

    sides = {("gx", True): 0.0, ("gx", False): 0.0, ("gy", True): 0.0, ("gy", False): 0.0}
    for (axis, phase), pay in zip(kinds, pays):
        above = partner_above(axis, phase)
        halo = pay[...].reshape(fluid_count + 3, -1, nz)
        sides[axis, True] += jnp.where(above, halo, 0.0)
        sides[axis, False] += jnp.where(above, 0.0, halo)
    for (axis, above), halo in sides.items():
        halo = jnp.broadcast_to(halo, (fluid_count + 3, cy if axis == "gx" else cx, nz))
        if axis == "gx":
            at = (cx + 1 if above else 0, slice(top, top + cy))
            d = 0
        else:
            at = (slice(1, cx + 1), top + cy if above else top - 1)
            d = 1
        ext[(slice(0, fluid_count),) + at] = halo[:fluid_count]
        speeds[(d,) + at] = halo[fluid_count]
        ext[(fluid_count + 1 - d,) + at] = halo[fluid_count + 1]
        ext[(fluid_count + 2,) + at] = halo[fluid_count + 2]

    factors = []
    centre = jnp.ones((cx, cy, nz), jnp.float32)
    for d in range(3):
        speed = window(speeds, d, cx, cy)
        up_low, up_high = face(speed, shifted(speeds, d, cx, cy, d, 1))
        down_low, down_high = face(shifted(speeds, d, cx, cy, d, -1), speed)
        centre = centre - up_low + down_high
        factors.append((down_low, up_high))
    for v in range(fluid_count):
        total = centre * window(ext, v, cx, cy)
        for d, (down_low, up_high) in enumerate(factors):
            total = total + down_low * shifted(ext, v, cx, cy, d, -1)
            total = total - up_high * shifted(ext, v, cx, cy, d, 1)
        out[v] = total

    def central(n, d):
        v = fluid_count + n
        return shifted(ext, v, cx, cy, d, 1) - shifted(ext, v, cx, cy, d, -1)

    for n in range(3):
        a, b = (n + 1) % 3, (n + 2) % 3
        curl = central(b, a) - central(a, b)
        out[fluid_count + n] = filled[fluid_count + n] - (0.5 * courant_number) * curl


def per_device(ngx, ngy, conserved, velocity, donor_corner, donor_fraction, target_cell):
    kinds = exchanges(ngx, ngy)
    cons = conserved[:, 0]
    vel = velocity[:, 0]
    corner = donor_corner[0, 0, 0]
    fraction = donor_fraction[:, 0, 0, 0]
    target = target_cell[0, 0, 0]
    nv, cx, cy, nz = cons.shape
    ng, nq, slots = corner.shape
    rows = cx * cy
    per = nz // slots
    chunks = (ng - 1) * block // per
    padded_chunks = -(-chunks // 8) * 8
    spread = 4 if cx % 4 == 0 else 1
    f32 = jnp.float32
    params = pltpu.CompilerParams(vmem_limit_bytes=24 << 20)

    blended = pl.pallas_call(
        blend_kernel,
        out_shape=jax.ShapeDtypeStruct((ng * nq, nv // per, nz), f32),
        scratch_shapes=[
            pltpu.VMEM((nv * rows, 2 * nz), jnp.bfloat16),
            pltpu.VMEM((padded_chunks, nz), jnp.int32),
            pltpu.VMEM((3, padded_chunks, nz), f32),
        ],
        compiler_params=pltpu.CompilerParams(vmem_limit_bytes=56 << 20),
        name="blend",
    )(cons, corner, fraction)

    gathered = lax.all_gather(blended, ("grp", "gx", "gy"), axis=0, tiled=False)

    pay_shapes = []
    for axis, _ in kinds:
        along = cy if axis == "gx" else cx
        pay_shapes.append(jax.ShapeDtypeStruct(((fluid_count + 3) * along, nz), f32))
    filled, *pays = pl.pallas_call(
        functools.partial(fill_kernel, kinds, ngy),
        out_shape=[jax.ShapeDtypeStruct((nv, cx, cy, nz), f32)] + pay_shapes,
        scratch_shapes=[
            pltpu.VMEM((padded_chunks, nz), jnp.int32),
            pltpu.VMEM(((2 * nv + 1) * rows // spread, spread * nz), f32),
            pltpu.VMEM(blended.shape, f32),
            pltpu.SemaphoreType.DMA(()),
        ],
        in_specs=[pl.BlockSpec(memory_space=pltpu.VMEM)] * 3
        + [pl.BlockSpec(memory_space=pl.ANY)],
        compiler_params=params,
        name="fill",
    )(cons, vel, target, gathered)

    halos = []
    for (axis, phase), pay in zip(kinds, pays):
        count = ngx if axis == "gx" else ngy
        pairs = []
        for low in range(phase, count - 1, 2):
            pairs += [(low, low + 1), (low + 1, low)]
        halos.append(lax.ppermute(pay, axis, pairs))

    result = pl.pallas_call(
        functools.partial(step_kernel, kinds),
        out_shape=jax.ShapeDtypeStruct((nv, cx, cy, nz), f32),
        scratch_shapes=[
            pltpu.VMEM((fluid_count + 3, cx + 2, cy + 2 * top, nz), f32),
            pltpu.VMEM((3, cx + 2, cy + 2 * top, nz), f32),
        ],
        compiler_params=params,
        name="step",
    )(filled, vel, *halos)
    return result[:, None]


def solution(mesh):
    return jax.shard_map(
        functools.partial(per_device, mesh.shape["gx"], mesh.shape["gy"]),
        mesh=mesh,
        in_specs=(
            P(None, "grp", "gx", "gy", None),
            P(None, "grp", "gx", "gy", None),
            P("grp", "gx", "gy", None, None, None),
            P(None, "grp", "gx", "gy", None, None, None),
            P("grp", "gx", "gy", None, None, None),
        ),
        out_specs=P(None, "grp", "gx", "gy", None),
        check_vma=False,
    )
```

```python
import functools

import jax
import jax.numpy as jnp
from jax import lax
from jax.experimental import pallas as pl
from jax.experimental.pallas import tpu as pltpu
from jax.sharding import PartitionSpec as P

signal_speed = 0.5
courant_number = 0.3
fluid_count = 5
block = 8


def exchanges(ngx, ngy):
    kinds = [("gx", phase, ngx) for phase in range(min(ngx - 1, 2))]
    return kinds + [("gy", phase, ngy) for phase in range(min(ngy - 1, 2))]


def joined(kind):
    axis, phase, count = kind
    if axis == "gx":
        return 0
    if phase == 0:
        return 1
    return 3 if count == 4 else 0


def partner(kind, at):
    _, phase, count = kind
    above = (at + phase) % 2 == 0
    other = jnp.where(above, at + 1, at - 1)
    valid = (other >= 0) & (other < count)
    return above, jnp.where(valid, other, at), valid


def swap(value, axis, count, k):
    return lax.ppermute(value, axis, [(n, n ^ k) for n in range(count)])


def split(value):
    high = value.astype(jnp.bfloat16)
    low = (value - high.astype(jnp.float32)).astype(jnp.bfloat16)
    return high, low


def each(count, body):
    if count == 1:
        body(0)
    else:
        lax.fori_loop(0, count, lambda n, c: (body(n), c)[1], 0)


def block_transpose(value, slots):
    rows, lanes = value.shape
    count = lanes // slots
    each_rows = rows // count
    at_row = lax.broadcasted_iota(jnp.int32, value.shape, 0) // each_rows
    at_lane = lax.broadcasted_iota(jnp.int32, value.shape, 1) // slots
    result = value
    for d in range(1, count):
        turned = pltpu.roll(value, d * each_rows, 0)
        turned = pltpu.roll(turned, lanes - d * slots, 1)
        result = jnp.where((at_row - at_lane) % count == d, turned, result)
    return result


def blend_kernel(kinds, cons, vel, corner, fraction, target, *rest):
    nv, cx, cy, nz = cons.shape
    ng, nq, slots = corner.shape
    outs = rest[: ng - 1]
    pays = rest[ng - 1 : ng - 1 + len(kinds)]
    uhl, cells, parts = rest[ng - 1 + len(kinds) :]
    lanes = nz
    per = lanes // slots
    chunks = block // per
    rows = cx * cy
    me = lax.axis_index("grp")

    for kind, pay in zip(kinds, pays):
        above, _, _ = partner(kind, lax.axis_index(kind[0]))
        along = cy if kind[0] == "gx" else cx
        for count, source, start in ((nv, cons, 0), (3, vel, nv * along)):
            if kind[0] == "gx":
                layer = source[:, pl.ds(jnp.where(above, cx - 1, 0), 1)]
            else:
                layer = source[:, :, pl.ds(jnp.where(above, cy - 1, 0), 1)]
            pay[start : start + count * along] = layer.reshape(count * along, nz)
        start = (nv + 3) * along
        pay[start:] = jnp.zeros((ng * nq, nz), jnp.float32)
        aim = (target[...] - rows * nz).astype(jnp.float32)
        pay[start:, :slots] = aim.reshape(ng * nq, slots)

    high, low = split(cons[...].reshape(nv * rows, nz))
    uhl[:, :nz] = high
    uhl[:, nz:] = low

    depth = lax.broadcasted_iota(jnp.int32, (nz, lanes), 0)
    row_x = lax.broadcasted_iota(jnp.int32, (rows, lanes), 0) // cy
    row_y = lax.broadcasted_iota(jnp.int32, (rows, lanes), 0) % cy

    def weight(place, at, upper):
        return jnp.where(place == at, 1.0 - upper, jnp.where(place == at + 1, upper, 0.0))

    def blend(n):
        for k in range(1, ng):
            h = me ^ k
            for c in range(chunks):
                at = (k - 1) * chunks + c
                for q in range(per):
                    row = pl.ds(n * block + c * per + q, 1)
                    cols = slice(q * slots, (q + 1) * slots)
                    cells[at : at + 1, cols] = corner[h, row]
                    for d in range(3):
                        parts[d, at : at + 1, cols] = fraction[d, h, row]

        def one(at):
            cell = cells[at : at + 1]
            wz = weight(depth, cell % nz, parts[2, at : at + 1])
            wx = weight(row_x, cell // (nz * cy), parts[0, at : at + 1])
            wy = weight(row_y, (cell // nz) % cy, parts[1, at : at + 1])
            return split(wz) + (wx * wy,)

        for k in range(1, ng):
            made = [one((k - 1) * chunks + c) for c in range(chunks)]
            wh = jnp.concatenate([m[0] for m in made], axis=1)
            wl = jnp.concatenate([m[1] for m in made], axis=1)
            wxy = jnp.concatenate([m[2] for m in made], axis=1)
            along = jnp.dot(
                uhl[...], jnp.concatenate([wh, wh], axis=0), preferred_element_type=jnp.float32
            ) + jnp.dot(uhl[:, :nz], wl, preferred_element_type=jnp.float32)
            values = jnp.sum(along.reshape(nv, rows, chunks * lanes) * wxy[None], axis=1)
            for c in range(chunks):
                start = pl.multiple_of((n * chunks + c) * nv, nv)
                outs[k - 1][pl.ds(start, nv)] = block_transpose(
                    values[:, c * lanes : (c + 1) * lanes], slots
                )

    each(nq // block, blend)


def join_kernel(others, riders, *refs):
    arrived, pays, outs = refs[:others], refs[others : others + len(riders)], refs[others + len(riders) :]
    size = arrived[0].shape[0]
    for k, out in enumerate(outs, 1):
        for n, ref in enumerate(arrived):
            out[n * size : (n + 1) * size] = ref[...]
        for rider, pay in zip(riders, pays):
            if rider == k:
                out[others * size :] = pay[...]


def sort_kernel(kinds, ngx, ngy, others, *refs):
    sources, outs = refs[:ngy], refs[ngy:]
    group = outs[0].shape[0] // (others * ngy)
    units = 1 + sum(kind[0] == "gx" for kind in kinds)
    size = group // units
    for k, out in enumerate(outs):
        at = lax.axis_index("gx") ^ k
        rows = [at] + [partner(kind, at)[1] for kind in kinds if kind[0] == "gx"]
        for g in range(others):
            for kj, source in enumerate(sources):
                for u, i in enumerate(rows):
                    start = ((g * ngy + kj) * units + u) * size
                    out[start : start + size] = source[
                        pl.ds(pl.multiple_of((g * ngx + i) * size, size), size)
                    ]


top = 8


def window(ext, v, cx, cy, move_x=0, move_y=0):
    return ext[v, 1 + move_x : 1 + move_x + cx, top + move_y : top + move_y + cy]


def along_z(value, by):
    nz = value.shape[-1]
    at = lax.broadcasted_iota(jnp.int32, (1,) + value.shape[1:], 2)
    edge = 0 if by < 0 else nz - 1
    return jnp.where(at == edge, 0.0, pltpu.roll(value, (-by) % nz, 2))


def shifted(ext, v, cx, cy, d, by):
    if d == 2 and by:
        return along_z(window(ext, v, cx, cy), by)
    return window(ext, v, cx, cy, by if d == 0 else 0, by if d == 1 else 0)


def face(low, high):
    wave_low = jnp.minimum(jnp.minimum(low, high) - signal_speed, 0.0)
    wave_high = jnp.maximum(jnp.maximum(low, high) + signal_speed, 0.0)
    scale = courant_number / (wave_high - wave_low)
    return (
        scale * wave_high * (low - wave_low),
        scale * wave_low * (wave_high - high),
    )


def step_kernel(kinds, ngx, ngy, places, cons, vel, target, *rest):
    margins, halos = rest[:ngx], rest[ngx : ngx + len(kinds)]
    out, ext, every, cells, acc = rest[ngx + len(kinds) :]
    nv, cx, cy, nz = cons.shape
    ng, nq, slots = target.shape
    lanes = nz
    per = lanes // slots
    two = nv // per
    spread = 4 if cx % 4 == 0 else 1
    my_g, my_i, my_j = (lax.axis_index(name) for name in ("grp", "gx", "gy"))
    units = 1 + sum(kind[0] == "gx" for kind in kinds)

    size = margins[0].shape[0]
    for k, margin in enumerate(margins):
        every[k * size : (k + 1) * size] = margin[...]

    parts = [(cx // spread * cy, spread, 0, my_j)]
    for kind in kinds:
        if kind[0] == "gx":
            parts.append((cy, 1, sum(p[2] > 0 for p in parts) + 1, my_j))
        else:
            parts.append((cx, 1, 0, partner(kind, my_j)[1]))
    states = [partner(kind, lax.axis_index(kind[0])) for kind in kinds]

    starts = [0]
    for count, groups, _, _ in parts:
        starts.append(starts[-1] + (2 * nv + 1) * count * groups)
    step_i = min(ngx, 2)
    cells[...] = jnp.full(cells.shape, cx * cy * nz, jnp.int32)

    def fill(n):
        for part, (count, groups, unit, j) in enumerate(parts):
            for k in range(1, ng):
                for c in range(step_i):
                    at = (k - 1) * step_i + c
                    for kj in range(ngy):
                        g, p = my_g ^ k, (my_i ^ (n * step_i + c)) * ngy + (my_j ^ kj)
                        cols = slice(kj * slots, (kj + 1) * slots)
                        if part == 0:
                            cells[at : at + 1, cols] = target[g, pl.ds(p, 1)]
                        else:
                            ref, place = halos[part - 1], places[part - 1]
                            along = cy if kinds[part - 1][0] == "gx" else cx
                            row = place + (nv + 3) * along + g * nq + p
                            aim = ref[pl.ds(row, 1), :slots].astype(jnp.int32)
                            aim = jnp.where(states[part - 1][2], aim, 0)
                            cells[at : at + 1, cols] = aim + cx * cy * nz
            cell = cells[...]
            x, y, z = cell // (nz * cy), (cell // nz) % cy, cell % nz
            if part == 0:
                at_row = x // spread * cy + y
                at_column = x % spread * nz + z
            else:
                above = states[part - 1][0]
                if kinds[part - 1][0] == "gx":
                    at_row = jnp.where(x == jnp.where(above, 0, cx - 1), y, -1)
                else:
                    at_row = jnp.where(y == jnp.where(above, 0, cy - 1), x, -1)
                at_column = z
            at_column = at_column.T
            up = lax.broadcasted_iota(jnp.int32, (count, lanes), 0)
            along = lax.broadcasted_iota(jnp.int32, (lanes, groups * nz), 1)
            total = None
            for k in range(1, ng):
                lefts, picks = [], []
                for c in range(step_i):
                    at = (k - 1) * step_i + c
                    pieces = []
                    for kj in range(ngy):
                        start = (n * step_i + c) * size
                        start = start + (((k - 1) * ngy + kj) * units + unit) * two * ngy + two * j
                        pieces.append(every[pl.ds(start, two)])
                    value = block_transpose(jnp.concatenate(pieces, axis=0), slots)
                    high = value.astype(jnp.bfloat16).astype(jnp.float32)
                    low = value - high
                    hit = up == at_row[at : at + 1]
                    pieces = [jnp.where(hit, high[v : v + 1], 0.0) for v in range(nv)]
                    pieces += [jnp.where(hit, low[v : v + 1], 0.0) for v in range(nv)]
                    pieces += [jnp.where(hit, 1.0, 0.0)]
                    lefts.append(jnp.concatenate(pieces, axis=0).astype(jnp.bfloat16))
                    pick = jnp.where(at_column[:, at : at + 1] == along, 1.0, 0.0)
                    picks.append(pick.astype(jnp.bfloat16))
                term = jnp.dot(
                    jnp.concatenate(lefts, axis=1),
                    jnp.concatenate(picks, axis=0),
                    preferred_element_type=jnp.float32,
                )
                total = term if total is None else total + term
            rows = (2 * nv + 1) * count
            for s in range(groups):
                here = slice(starts[part] + s * rows, starts[part] + (s + 1) * rows)
                value = total[:, s * nz : (s + 1) * nz]
                if ngx <= 2:
                    acc[here] = value
                else:
                    acc[here] += value

    if ngx > 2:
        acc[...] = jnp.zeros_like(acc)
    each(ngx // step_i, fill)

    def filled(part, s, before):
        count = parts[part][0]
        start = starts[part] + s * (2 * nv + 1) * count
        new = acc[start : start + nv * count] + acc[start + nv * count : start + 2 * nv * count]
        mark = acc[start + 2 * nv * count : start + (2 * nv + 1) * count]
        return jnp.where(mark[None] > 0.5, new.reshape(nv, count, nz), before)

    inside = slice(top, top + cy)
    for s in range(spread):
        before = jnp.concatenate([cons[:, x] for x in range(s, cx, spread)], axis=1)
        new = filled(0, s, before)
        for n, x in enumerate(range(s, cx, spread)):
            ext[:nv, 1 + x, inside] = new[:, n * cy : (n + 1) * cy]
    ext[nv:, 1 : cx + 1, inside] = vel[...]

    sides = {("gx", True): 0.0, ("gx", False): 0.0, ("gy", True): 0.0, ("gy", False): 0.0}
    for n, kind in enumerate(kinds):
        above, _, valid = states[n]
        along = cy if kind[0] == "gx" else cx
        halo = halos[n][places[n] : places[n] + (nv + 3) * along].reshape(nv + 3, along, nz)
        halo = jnp.concatenate([filled(n + 1, 0, halo[:nv]), halo[nv:]], axis=0)
        sides[kind[0], True] += jnp.where(above & valid, halo, 0.0)
        sides[kind[0], False] += jnp.where(above | ~valid, 0.0, halo)
    for (axis, above), halo in sides.items():
        halo = jnp.broadcast_to(halo, (nv + 3, cy if axis == "gx" else cx, nz))
        if axis == "gx":
            ext[:, cx + 1 if above else 0, inside] = halo
        else:
            ext[:, 1 : cx + 1, top + cy if above else top - 1] = halo

    factors = []
    centre = jnp.ones((cx, cy, nz), jnp.float32)
    for d in range(3):
        speed = window(ext, nv + d, cx, cy)
        up_low, up_high = face(speed, shifted(ext, nv + d, cx, cy, d, 1))
        down_low, down_high = face(shifted(ext, nv + d, cx, cy, d, -1), speed)
        centre = centre - up_low + down_high
        factors.append((down_low, up_high))
    for v in range(fluid_count):
        total = centre * window(ext, v, cx, cy)
        for d, (down_low, up_high) in enumerate(factors):
            total = total + down_low * shifted(ext, v, cx, cy, d, -1)
            total = total - up_high * shifted(ext, v, cx, cy, d, 1)
        out[v] = total

    def electric(n, d, by):
        a, b = (n + 1) % 3, (n + 2) % 3
        if d == 2 and by:
            return along_z(electric(n, 2, 0), by)

        def at(v):
            return shifted(ext, v, cx, cy, d, by)

        return at(nv + b) * at(fluid_count + a) - at(nv + a) * at(fluid_count + b)

    def central(n, d):
        return electric(n, d, 1) - electric(n, d, -1)

    for n in range(3):
        a, b = (n + 1) % 3, (n + 2) % 3
        curl = central(b, a) - central(a, b)
        out[fluid_count + n] = window(ext, fluid_count + n, cx, cy) - (0.5 * courant_number) * curl


def per_device(ngx, ngy, conserved, velocity, donor_corner, donor_fraction, target_cell):
    kinds = exchanges(ngx, ngy)
    cons = conserved[:, 0]
    vel = velocity[:, 0]
    corner = donor_corner[0, 0, 0]
    fraction = donor_fraction[:, 0, 0, 0]
    target = target_cell[0, 0, 0]
    nv, cx, cy, nz = cons.shape
    ng, nq, slots = corner.shape
    rows = cx * cy
    per = nz // slots
    two = nv // per
    chunks = (ng - 1) * block // per
    padded_chunks = -(-chunks // 8) * 8
    spread = 4 if cx % 4 == 0 else 1
    f32 = jnp.float32
    params = pltpu.CompilerParams(vmem_limit_bytes=min(56, 16 + nq // 2) << 20)

    def shape(*dims):
        return jax.ShapeDtypeStruct(dims, f32)

    alongs = [cy if kind[0] == "gx" else cx for kind in kinds]
    pay_rows = [(nv + 3) * along + ng * nq for along in alongs]
    outs = pl.pallas_call(
        functools.partial(blend_kernel, kinds),
        out_shape=[shape(two * nq, nz)] * (ng - 1) + [shape(count, nz) for count in pay_rows],
        scratch_shapes=[
            pltpu.VMEM((nv * rows, 2 * nz), jnp.bfloat16),
            pltpu.VMEM((padded_chunks, nz), jnp.int32),
            pltpu.VMEM((3, padded_chunks, nz), f32),
        ],
        compiler_params=pltpu.CompilerParams(vmem_limit_bytes=56 << 20),
        name="blend",
    )(cons, vel, corner, fraction, target)
    blended, pays = list(outs[: ng - 1]), list(outs[ng - 1 :])

    riders = [joined(kind) for kind in kinds]
    halos = {}
    for n, (kind, pay) in enumerate(zip(kinds, pays)):
        if not riders[n]:
            axis, phase, count = kind
            pairs = []
            for low in range(phase, count - 1, 2):
                pairs += [(low, low + 1), (low + 1, low)]
            halos[n] = (lax.ppermute(pay, axis, pairs), 0)

    over_grids = [swap(value, "grp", ng, k) for k, value in enumerate(blended, 1)]
    base = (ng - 1) * two * nq
    extra = {k: count for k, count in zip(riders, pay_rows) if k}
    messages = pl.pallas_call(
        functools.partial(join_kernel, ng - 1, [k for k in riders if k]),
        out_shape=[shape(base + extra.get(k, 0), nz) for k in range(1, ngy)],
        compiler_params=params,
        name="join",
    )(*over_grids, *[pay for k, pay in zip(riders, pays) if k])
    over_y = [swap(value, "gy", ngy, k) for k, value in enumerate(messages, 1)]
    for n, k in enumerate(riders):
        if k:
            halos[n] = (over_y[k - 1], base)

    units = 1 + sum(kind[0] == "gx" for kind in kinds)
    margin_rows = (ng - 1) * ngy * units * two * ngy
    messages = pl.pallas_call(
        functools.partial(sort_kernel, kinds, ngx, ngy, ng - 1),
        out_shape=[shape(margin_rows, nz)] * ngx,
        compiler_params=params,
        name="sort",
    )(messages[0], *over_y)
    margins = [messages[0]] + [swap(messages[k], "gx", ngx, k) for k in range(1, ngx)]

    groups = [rows] + alongs
    result = pl.pallas_call(
        functools.partial(
            step_kernel, kinds, ngx, ngy, [halos[n][1] for n in range(len(kinds))]
        ),
        out_shape=shape(nv, cx, cy, nz),
        scratch_shapes=[
            pltpu.VMEM((nv + 3, cx + 2, cy + 2 * top, nz), f32),
            pltpu.VMEM((ngx * margin_rows, nz), f32),
            pltpu.VMEM((8, nz), jnp.int32),
            pltpu.VMEM(((2 * nv + 1) * sum(groups), nz), f32),
        ],
        compiler_params=params,
        name="step",
    )(cons, vel, target, *margins, *[halos[n][0] for n in range(len(kinds))])
    return result[:, None]


def solution(mesh):
    return jax.shard_map(
        functools.partial(per_device, mesh.shape["gx"], mesh.shape["gy"]),
        mesh=mesh,
        in_specs=(
            P(None, "grp", "gx", "gy", None),
            P(None, "grp", "gx", "gy", None),
            P("grp", "gx", "gy", None, None, None),
            P(None, "grp", "gx", "gy", None, None, None),
            P("grp", "gx", "gy", None, None, None),
        ),
        out_specs=P(None, "grp", "gx", "gy", None),
        check_vma=False,
    )
```

```python
import functools

import jax
import jax.numpy as jnp
from jax import lax
from jax.experimental import pallas as pl
from jax.experimental.pallas import tpu as pltpu
from jax.sharding import PartitionSpec as P

signal_speed = 0.5
courant_number = 0.3
fluid_count = 5
block = 8


def exchanges(ngx, ngy):
    def partner(count, phase, n):
        other = n + 1 if (n + phase) % 2 == 0 else n - 1
        return other if 0 <= other < count else n

    kinds = []
    for phase in range(min(ngx - 1, 2)):
        kinds.append(("gx", phase, lambda i, j, phase=phase: (partner(ngx, phase, i), j)))
    for phase in range(min(ngy - 1, 2)):
        kinds.append(("gy", phase, lambda i, j, phase=phase: (i, partner(ngy, phase, j))))
    return kinds


def partner_above(axis, phase):
    return (lax.axis_index(axis) + phase) % 2 == 0


def split(value):
    high = value.astype(jnp.bfloat16)
    low = (value - high.astype(jnp.float32)).astype(jnp.bfloat16)
    return high, low


def each(count, body):
    if count == 1:
        body(0)
    else:
        lax.fori_loop(0, count, lambda n, c: (body(n), c)[1], 0)


def blend_kernel(ngy, kinds, cons, vel, corner, fraction, target, out, aims, *rest):
    pays = rest[: len(kinds)]
    uhl, cells, parts, moved = rest[len(kinds) :]
    nv, cx, cy, nz = cons.shape
    ng, nq, slots = corner.shape
    lanes = nz
    per = lanes // slots
    chunks = block // per
    rows = cx * cy
    me = lax.axis_index("grp")

    aims[...] = jnp.zeros(aims.shape, jnp.float32)
    for n in range(nq // block):
        for away in range(1, ng):
            h = (me + away) % ng
            for c in range(chunks):
                at = n * block + (away - 1) * chunks + c
                for q in range(per):
                    row = n * block + c * per + q
                    cols = slice(q * slots, (q + 1) * slots)
                    cells[at : at + 1, cols] = corner[h, row : row + 1]
                    for d in range(3):
                        parts[d, at : at + 1, cols] = fraction[d, h, row : row + 1]
                    aim = target[h, row : row + 1] - rows * nz
                    aims[at : at + 1, cols] = aim.astype(jnp.float32)

    for (axis, phase, _), pay in zip(kinds, pays):
        above = partner_above(axis, phase)
        along = cy if axis == "gx" else cx
        for count, source, start in ((nv, cons, 0), (3, vel, nv * along)):
            if axis == "gx":
                layer = source[:, pl.ds(jnp.where(above, cx - 1, 0), 1)]
            else:
                layer = source[:, :, pl.ds(jnp.where(above, cy - 1, 0), 1)]
            pay[start : start + count * along] = layer.reshape(count * along, nz)
        pay[(nv + 3) * along :] = aims[...]

    high, low = split(cons[...].reshape(nv * rows, nz))
    uhl[:, :nz] = high
    uhl[:, nz : 2 * nz] = low
    uhl[:, 2 * nz :] = high

    depth = lax.broadcasted_iota(jnp.int32, (nz, lanes), 0)
    row_x = lax.broadcasted_iota(jnp.int32, (rows, lanes), 0) // cy
    row_y = lax.broadcasted_iota(jnp.int32, (rows, lanes), 0) % cy

    def weight(place, at, upper):
        return jnp.where(place == at, 1.0 - upper, jnp.where(place == at + 1, upper, 0.0))

    def blend(n):
        def one(at):
            row = pl.ds(n * block + at, 1)
            cell = cells[row]
            wz = weight(depth, cell % nz, parts[2, row])
            wx = weight(row_x, cell // (nz * cy), parts[0, row])
            wy = weight(row_y, (cell // nz) % cy, parts[1, row])
            return split(wz) + (wx * wy,)

        for away in range(1, ng):
            made = [one((away - 1) * chunks + c) for c in range(chunks)]
            wh = jnp.concatenate([m[0] for m in made], axis=1)
            wl = jnp.concatenate([m[1] for m in made], axis=1)
            wxy = jnp.concatenate([m[2] for m in made], axis=1)
            along = jnp.dot(
                uhl[...],
                jnp.concatenate([wh, wh, wl], axis=0),
                preferred_element_type=jnp.float32,
            )
            values = jnp.sum(along.reshape(nv, rows, chunks * lanes) * wxy[None], axis=1)
            for c in range(chunks):
                value = values[:, c * lanes : (c + 1) * lanes]
                for turn in range(per):
                    moved[away - 1, turn, n * chunks + c] = (
                        pltpu.roll(value, turn * slots, 1) if turn else value
                    )

    each(nq // block, blend)

    out[pl.ds(me * nq, nq)] = jnp.zeros((nq,) + out.shape[1:], jnp.float32)
    lane = lax.broadcasted_iota(jnp.int32, (nv, lanes), 1) // slots
    for away in range(1, ng):
        h = (me + away) % ng
        for q in range(nq):
            i, j = q // ngy, q % ngy
            owners = [q] + [a * ngy + b for a, b in (of(i, j) for _, _, of in kinds)]
            for t in range(0, len(owners), per):
                tile = None
                for k, owner in enumerate(owners[t : t + per]):
                    piece = moved[away - 1, (k - owner) % per, owner // per]
                    tile = piece if tile is None else jnp.where(lane == k, piece, tile)
                cols = slice(t // per * lanes, (t // per + 1) * lanes)
                out[pl.ds(h * nq + q, 1), :, cols] = tile[None]


top = 8


def window(ext, v, cx, cy, move_x=0, move_y=0):
    return ext[v, 1 + move_x : 1 + move_x + cx, top + move_y : top + move_y + cy]


def along_z(value, by):
    nz = value.shape[-1]
    at = lax.broadcasted_iota(jnp.int32, (1,) + value.shape[1:], 2)
    edge = 0 if by < 0 else nz - 1
    return jnp.where(at == edge, 0.0, pltpu.roll(value, (-by) % nz, 2))


def shifted(ext, v, cx, cy, d, by):
    if d == 2 and by:
        return along_z(window(ext, v, cx, cy), by)
    return window(ext, v, cx, cy, by if d == 0 else 0, by if d == 1 else 0)


def face(low, high):
    wave_low = jnp.minimum(jnp.minimum(low, high) - signal_speed, 0.0)
    wave_high = jnp.maximum(jnp.maximum(low, high) + signal_speed, 0.0)
    scale = courant_number / (wave_high - wave_low)
    return (
        scale * wave_high * (low - wave_low),
        scale * wave_low * (wave_high - high),
    )


def step_kernel(kinds, slots, ng, cons, vel, aims, received, *rest):
    halos = rest[: len(kinds)]
    out, ext, acc, result, sems = rest[len(kinds) :]
    nv, cx, cy, nz = cons.shape
    lanes = nz
    nq = received.shape[0] // ng
    per = lanes // slots
    chunks = block // per
    spread = 4 if cx % 4 == 0 else 1
    me = lax.axis_index("grp")
    lane = lax.broadcasted_iota(jnp.int32, (nv, lanes), 1) // slots
    above = [partner_above(axis, phase) for axis, phase, _ in kinds]

    parts = [(cx // spread * cy, spread)]
    parts += [(cy if axis == "gx" else cx, 1) for axis, _, _ in kinds]
    starts = [0]
    for count, groups in parts:
        starts.append(starts[-1] + (2 * nv + 1) * count * groups)

    def fill(n):
        for part, (count, groups) in enumerate(parts):
            if part == 0:
                cell = aims[pl.ds(n * block, block)]
            else:
                cell = halos[part - 1][pl.ds((nv + 3) * count + n * block, block)]
            cell = cell.astype(jnp.int32) + cx * cy * nz
            x, y, z = cell // (nz * cy), (cell // nz) % cy, cell % nz
            if part == 0:
                at_row = x // spread * cy + y
                at_column = x % spread * nz + z
            elif kinds[part - 1][0] == "gx":
                at_row = jnp.where(x == jnp.where(above[part - 1], 0, cx - 1), y, -1)
                at_column = z
            else:
                at_row = jnp.where(y == jnp.where(above[part - 1], 0, cy - 1), x, -1)
                at_column = z
            at_column = at_column.T
            up = lax.broadcasted_iota(jnp.int32, (count, lanes), 0)
            along = lax.broadcasted_iota(jnp.int32, (lanes, groups * nz), 1)
            here = slice(part // per * lanes, (part // per + 1) * lanes)
            total = None
            for away in range(1, ng):
                g = (me + away) % ng
                lefts, picks = [], []
                for c in range(chunks):
                    at = (away - 1) * chunks + c
                    value = None
                    for p in range(per):
                        piece = received[g * nq + n * block + c * per + p, :, here]
                        turn = (p - part) % per
                        if turn:
                            piece = pltpu.roll(piece, turn * slots, 1)
                        value = piece if value is None else jnp.where(lane == p, piece, value)
                    high = value.astype(jnp.bfloat16).astype(jnp.float32)
                    low = value - high
                    hit = up == at_row[at : at + 1]
                    pieces = [jnp.where(hit, high[v : v + 1], 0.0) for v in range(nv)]
                    pieces += [jnp.where(hit, low[v : v + 1], 0.0) for v in range(nv)]
                    pieces += [jnp.where(hit, 1.0, 0.0)]
                    lefts.append(jnp.concatenate(pieces, axis=0).astype(jnp.bfloat16))
                    pick = jnp.where(at_column[:, at : at + 1] == along, 1.0, 0.0)
                    picks.append(pick.astype(jnp.bfloat16))
                term = jnp.dot(
                    jnp.concatenate(lefts, axis=1),
                    jnp.concatenate(picks, axis=0),
                    preferred_element_type=jnp.float32,
                )
                total = term if total is None else total + term
            rows = (2 * nv + 1) * count
            for s in range(groups):
                to = slice(starts[part] + s * rows, starts[part] + (s + 1) * rows)
                value = total[:, s * nz : (s + 1) * nz]
                if nq == block:
                    acc[to] = value
                else:
                    acc[to] += value

    if nq != block:
        acc[...] = jnp.zeros_like(acc)
    each(nq // block, fill)

    def filled(part, s, before):
        count = parts[part][0]
        start = starts[part] + s * (2 * nv + 1) * count
        new = acc[start : start + nv * count] + acc[start + nv * count : start + 2 * nv * count]
        mark = acc[start + 2 * nv * count : start + (2 * nv + 1) * count]
        return jnp.where(mark[None] > 0.5, new.reshape(nv, count, nz), before)

    inside = slice(top, top + cy)
    for s in range(spread):
        before = jnp.concatenate([cons[:, x] for x in range(s, cx, spread)], axis=1)
        new = filled(0, s, before)
        for n, x in enumerate(range(s, cx, spread)):
            ext[:nv, 1 + x, inside] = new[:, n * cy : (n + 1) * cy]
    ext[nv:, 1 : cx + 1, inside] = vel[...]

    sides = {("gx", True): 0.0, ("gx", False): 0.0, ("gy", True): 0.0, ("gy", False): 0.0}
    for n, (axis, _, _) in enumerate(kinds):
        count = parts[n + 1][0]
        halo = halos[n][: (nv + 3) * count].reshape(nv + 3, count, nz)
        halo = jnp.concatenate([filled(n + 1, 0, halo[:nv]), halo[nv:]], axis=0)
        sides[axis, True] += jnp.where(above[n], halo, 0.0)
        sides[axis, False] += jnp.where(above[n], 0.0, halo)
    for (axis, high), halo in sides.items():
        halo = jnp.broadcast_to(halo, (nv + 3, cy if axis == "gx" else cx, nz))
        if axis == "gx":
            ext[:, cx + 1 if high else 0, inside] = halo
        else:
            ext[:, 1 : cx + 1, top + cy if high else top - 1] = halo

    copies = []

    def finish(v, value):
        result[v] = value
        copies.append(pltpu.make_async_copy(result.at[v], out.at[v], sems.at[v]))
        copies[-1].start()

    def electric(n, d, by):
        a, b = (n + 1) % 3, (n + 2) % 3
        if d == 2 and by:
            return along_z(electric(n, 2, 0), by)

        def at(v):
            return shifted(ext, v, cx, cy, d, by)

        return at(nv + b) * at(fluid_count + a) - at(nv + a) * at(fluid_count + b)

    def central(n, d):
        return electric(n, d, 1) - electric(n, d, -1)

    for n in range(3):
        v = fluid_count + n
        a, b = (n + 1) % 3, (n + 2) % 3
        curl = central(b, a) - central(a, b)
        finish(v, window(ext, v, cx, cy) - (0.5 * courant_number) * curl)

    factors = []
    centre = jnp.ones((cx, cy, nz), jnp.float32)
    for d in range(3):
        speed = window(ext, nv + d, cx, cy)
        up_low, up_high = face(speed, shifted(ext, nv + d, cx, cy, d, 1))
        down_low, down_high = face(shifted(ext, nv + d, cx, cy, d, -1), speed)
        centre = centre - up_low + down_high
        factors.append((down_low, up_high))
    for v in range(fluid_count):
        total = centre * window(ext, v, cx, cy)
        for d, (down_low, up_high) in enumerate(factors):
            total = total + down_low * shifted(ext, v, cx, cy, d, -1)
            total = total - up_high * shifted(ext, v, cx, cy, d, 1)
        finish(v, total)
    for copy in copies:
        copy.wait()


def per_device(ngx, ngy, conserved, velocity, donor_corner, donor_fraction, target_cell):
    kinds = exchanges(ngx, ngy)
    cons = conserved[:, 0]
    vel = velocity[:, 0]
    corner = donor_corner[0, 0, 0]
    fraction = donor_fraction[:, 0, 0, 0]
    target = target_cell[0, 0, 0]
    nv, cx, cy, nz = cons.shape
    ng, nq, slots = corner.shape
    rows = cx * cy
    per = nz // slots
    tiles = -(-(1 + len(kinds)) // per)
    f32 = jnp.float32

    def shape(*dims):
        return jax.ShapeDtypeStruct(dims, f32)

    alongs = [cy if axis == "gx" else cx for axis, _, _ in kinds]
    blended, aims, *pays = pl.pallas_call(
        functools.partial(blend_kernel, ngy, kinds),
        out_shape=[shape(ng * nq, nv, tiles * nz), shape(nq, nz)]
        + [shape((nv + 3) * along + nq, nz) for along in alongs],
        scratch_shapes=[
            pltpu.VMEM((nv * rows, 3 * nz), jnp.bfloat16),
            pltpu.VMEM((nq, nz), jnp.int32),
            pltpu.VMEM((3, nq, nz), f32),
            pltpu.VMEM((ng - 1, per, nq // per, nv, nz), f32),
        ],
        compiler_params=pltpu.CompilerParams(vmem_limit_bytes=56 << 20),
        name="blend",
    )(cons, vel, corner, fraction, target)

    received = lax.all_to_all(
        blended, ("grp", "gx", "gy"), split_axis=0, concat_axis=0, tiled=True
    )
    halos = []
    for (axis, phase, _), pay in zip(kinds, pays):
        count = ngx if axis == "gx" else ngy
        pairs = []
        for low in range(phase, count - 1, 2):
            pairs += [(low, low + 1), (low + 1, low)]
        halos.append(lax.ppermute(pay, axis, pairs))

    result = pl.pallas_call(
        functools.partial(step_kernel, kinds, slots, ng),
        out_shape=shape(nv, cx, cy, nz),
        out_specs=pl.BlockSpec(memory_space=pl.ANY),
        scratch_shapes=[
            pltpu.VMEM((nv + 3, cx + 2, cy + 2 * top, nz), f32),
            pltpu.VMEM(((2 * nv + 1) * (rows + sum(alongs)), nz), f32),
            pltpu.VMEM((nv, cx, cy, nz), f32),
            pltpu.SemaphoreType.DMA((nv,)),
        ],
        compiler_params=pltpu.CompilerParams(vmem_limit_bytes=min(48, 16 + nq // 2) << 20),
        name="step",
    )(cons, vel, aims, received, *halos)
    return result[:, None]


def solution(mesh):
    return jax.shard_map(
        functools.partial(per_device, mesh.shape["gx"], mesh.shape["gy"]),
        mesh=mesh,
        in_specs=(
            P(None, "grp", "gx", "gy", None),
            P(None, "grp", "gx", "gy", None),
            P("grp", "gx", "gy", None, None, None),
            P(None, "grp", "gx", "gy", None, None, None),
            P("grp", "gx", "gy", None, None, None),
        ),
        out_specs=P(None, "grp", "gx", "gy", None),
        check_vma=False,
    )
```

```python
import functools

import jax
import jax.numpy as jnp
from jax import lax
from jax.experimental import pallas as pl
from jax.experimental.pallas import tpu as pltpu
from jax.sharding import PartitionSpec as P

signal_speed = 0.5
courant_number = 0.3
fluid_count = 5
block = 8


def exchanges(ngx, ngy):
    def partner(count, phase, n):
        other = n + 1 if (n + phase) % 2 == 0 else n - 1
        return other if 0 <= other < count else n

    kinds = []
    for phase in range(min(ngx - 1, 2)):
        kinds.append(("gx", phase, lambda i, j, phase=phase: (partner(ngx, phase, i), j)))
    for phase in range(min(ngy - 1, 2)):
        kinds.append(("gy", phase, lambda i, j, phase=phase: (i, partner(ngy, phase, j))))
    return kinds


def partner_above(axis, phase):
    return (lax.axis_index(axis) + phase) % 2 == 0


def split(value):
    high = value.astype(jnp.bfloat16)
    low = (value - high.astype(jnp.float32)).astype(jnp.bfloat16)
    return high, low


def over(value, n):
    return value >> (n.bit_length() - 1) if n & (n - 1) == 0 else value // n


def rest_of(value, n):
    return value & (n - 1) if n & (n - 1) == 0 else value % n


def each(count, body):
    if count == 1:
        body(0)
    else:
        lax.fori_loop(0, count, lambda n, c: (body(n), c)[1], 0)


def blend_kernel(ngy, kinds, cons, vel, corner, fraction, target, out, aims, *rest):
    pays_out = rest[: len(kinds)]
    pays = rest[len(kinds) : 2 * len(kinds)]
    (at_cons, at_vel, at_corner, at_fraction, at_target, uhl, cells, parts, aimed, moved, tiles) = rest[
        2 * len(kinds) : -2
    ]
    arrive, leave = rest[-2:]
    nv, cx, cy, nz = cons.shape
    ng, nq, slots = corner.shape
    lanes = nz
    per = lanes // slots
    chunks = block // per
    rows = cx * cy
    me = lax.axis_index("grp")

    moves = [(corner, at_corner), (fraction, at_fraction), (target, at_target)]
    moves += [(cons, at_cons), (vel, at_vel)]
    ins = [pltpu.make_async_copy(a, b, arrive.at[n]) for n, (a, b) in enumerate(moves)]
    outs = []

    def send(source, to):
        outs.append(pltpu.make_async_copy(source, to, leave.at[len(outs)]))
        outs[-1].start()

    for copy in ins:
        copy.start()

    tiles[0] = jnp.zeros(tiles.shape[1:], jnp.float32)
    send(tiles.at[0], out.at[pl.ds(me * nq, nq)])

    for copy in ins[:3]:
        copy.wait()
    aimed[...] = jnp.zeros(aimed.shape, jnp.float32)
    for n in range(nq // block):
        for away in range(1, ng):
            h = (me + away) % ng
            for c in range(chunks):
                at = n * block + (away - 1) * chunks + c
                for q in range(per):
                    row = n * block + c * per + q
                    cols = slice(q * slots, (q + 1) * slots)
                    cells[at : at + 1, cols] = at_corner[h, row : row + 1]
                    for d in range(3):
                        parts[d, at : at + 1, cols] = at_fraction[d, h, row : row + 1]
                    aim = at_target[h, row : row + 1] - rows * nz
                    aimed[at : at + 1, cols] = aim.astype(jnp.float32)
    send(aimed, aims)

    for copy in ins[3:]:
        copy.wait()
    for (axis, phase, _), pay, to in zip(kinds, pays, pays_out):
        above = partner_above(axis, phase)
        along = cy if axis == "gx" else cx
        for count, source, start in ((nv, at_cons, 0), (3, at_vel, nv * along)):
            if axis == "gx":
                layer = source[:, pl.ds(jnp.where(above, cx - 1, 0), 1)]
            else:
                layer = source[:, :, pl.ds(jnp.where(above, cy - 1, 0), 1)]
            pay[start : start + count * along] = layer.reshape(count * along, nz)
        pay[(nv + 3) * along :] = aimed[...]
        send(pay, to)

    high, low = split(at_cons[...].reshape(nv * rows, nz))
    uhl[:, :nz] = high
    uhl[:, nz : 2 * nz] = low
    uhl[:, 2 * nz :] = high

    def weight(count, at, upper):
        place = lax.broadcasted_iota(jnp.int32, (count, lanes), 0)
        return jnp.where(place == at, 1.0 - upper, jnp.where(place == at + 1, upper, 0.0))

    def blend(n):
        here = pl.ds(n * block, block)
        cell = cells[here]
        at_x, at_y, at_z = over(cell, nz * cy), rest_of(over(cell, nz), cy), rest_of(cell, nz)
        fx, fy, fz = parts[0, here], parts[1, here], parts[2, here]

        def one(at):
            row = slice(at, at + 1)
            wx = weight(cx, at_x[row], fx[row])
            wy = weight(cy, at_y[row], fy[row])
            wxy = jnp.concatenate([wx[x : x + 1] * wy for x in range(cx)], axis=0)
            return split(weight(nz, at_z[row], fz[row])) + (wxy,)

        for away in range(1, ng):
            made = [one((away - 1) * chunks + c) for c in range(chunks)]
            wh = jnp.concatenate([m[0] for m in made], axis=1)
            wl = jnp.concatenate([m[1] for m in made], axis=1)
            wxy = jnp.concatenate([m[2] for m in made], axis=1)
            along = jnp.dot(
                uhl[...],
                jnp.concatenate([wh, wh, wl], axis=0),
                preferred_element_type=jnp.float32,
            )
            values = jnp.sum(along.reshape(nv, rows, chunks * lanes) * wxy[None], axis=1)
            for c in range(chunks):
                value = values[:, c * lanes : (c + 1) * lanes]
                for turn in range(per):
                    moved[away - 1, turn, n * chunks + c] = (
                        pltpu.roll(value, turn * slots, 1) if turn else value
                    )
            if nq == block:
                assemble(away)

    lane = lax.broadcasted_iota(jnp.int32, (nv, lanes), 1) // slots

    def assemble(away):
        for q in range(nq):
            i, j = q // ngy, q % ngy
            owners = [q] + [a * ngy + b for a, b in (of(i, j) for _, _, of in kinds)]
            for t in range(0, len(owners), per):
                tile = None
                for k, owner in enumerate(owners[t : t + per]):
                    piece = moved[away - 1, (k - owner) % per, owner // per]
                    tile = piece if tile is None else jnp.where(lane == k, piece, tile)
                tiles[away, q, :, t // per * lanes : (t // per + 1) * lanes] = tile
        send(tiles.at[away], out.at[pl.ds((me + away) % ng * nq, nq)])

    each(nq // block, blend)
    if nq != block:
        for away in range(1, ng):
            assemble(away)
    for copy in outs:
        copy.wait()


top = 8


def window(ext, v, cx, cy, move_x=0, move_y=0):
    return ext[v, 1 + move_x : 1 + move_x + cx, top + move_y : top + move_y + cy]


def along_z(value, by):
    nz = value.shape[-1]
    at = lax.broadcasted_iota(jnp.int32, (1,) + value.shape[1:], 2)
    edge = 0 if by < 0 else nz - 1
    return jnp.where(at == edge, 0.0, pltpu.roll(value, (-by) % nz, 2))


def shifted(ext, v, cx, cy, d, by):
    if d == 2 and by:
        return along_z(window(ext, v, cx, cy), by)
    return window(ext, v, cx, cy, by if d == 0 else 0, by if d == 1 else 0)


def face(low, high):
    wave_low = jnp.minimum(jnp.minimum(low, high) - signal_speed, 0.0)
    wave_high = jnp.maximum(jnp.maximum(low, high) + signal_speed, 0.0)
    scale = courant_number / (wave_high - wave_low)
    return (
        scale * wave_high * (low - wave_low),
        scale * wave_low * (wave_high - high),
    )


def step_kernel(kinds, slots, ng, cons, vel, aims, received, *rest):
    halos = rest[: len(kinds)]
    out, ext, acc, result, sems = rest[len(kinds) :]
    nv, cx, cy, nz = cons.shape
    lanes = nz
    nq = received.shape[0] // ng
    per = lanes // slots
    chunks = block // per
    spread = 4 if cx % 4 == 0 else 1
    me = lax.axis_index("grp")
    lane = lax.broadcasted_iota(jnp.int32, (nv, lanes), 1) // slots
    above = [partner_above(axis, phase) for axis, phase, _ in kinds]

    parts = [(cx // spread * cy, spread)]
    parts += [(cy if axis == "gx" else cx, 1) for axis, _, _ in kinds]
    starts = [0]
    for count, groups in parts:
        starts.append(starts[-1] + (2 * nv + 1) * count * groups)

    def fill(n):
        for part, (count, groups) in enumerate(parts):
            if part == 0:
                cell = aims[pl.ds(n * block, block)]
            else:
                cell = halos[part - 1][pl.ds((nv + 3) * count + n * block, block)]
            cell = cell.astype(jnp.int32) + cx * cy * nz
            x, y, z = over(cell, nz * cy), rest_of(over(cell, nz), cy), rest_of(cell, nz)
            if part == 0:
                at_row = over(x, spread) * cy + y
                at_column = rest_of(x, spread) * nz + z
            elif kinds[part - 1][0] == "gx":
                at_row = jnp.where(x == jnp.where(above[part - 1], 0, cx - 1), y, -1)
                at_column = z
            else:
                at_row = jnp.where(y == jnp.where(above[part - 1], 0, cy - 1), x, -1)
                at_column = z
            at_column = at_column.T
            up = lax.broadcasted_iota(jnp.int32, (count, lanes), 0)
            along = lax.broadcasted_iota(jnp.int32, (lanes, groups * nz), 1)
            here = slice(part // per * lanes, (part // per + 1) * lanes)
            total = None
            for away in range(1, ng):
                g = (me + away) % ng
                lefts, picks = [], []
                for c in range(chunks):
                    at = (away - 1) * chunks + c
                    value = None
                    for p in range(per):
                        piece = received[g * nq + n * block + c * per + p, :, here]
                        turn = (p - part) % per
                        if turn:
                            piece = pltpu.roll(piece, turn * slots, 1)
                        value = piece if value is None else jnp.where(lane == p, piece, value)
                    high = value.astype(jnp.bfloat16).astype(jnp.float32)
                    low = value - high
                    hit = up == at_row[at : at + 1]
                    pieces = [jnp.where(hit, high[v : v + 1], 0.0) for v in range(nv)]
                    pieces += [jnp.where(hit, low[v : v + 1], 0.0) for v in range(nv)]
                    pieces += [jnp.where(hit, 1.0, 0.0)]
                    lefts.append(jnp.concatenate(pieces, axis=0).astype(jnp.bfloat16))
                    pick = jnp.where(at_column[:, at : at + 1] == along, 1.0, 0.0)
                    picks.append(pick.astype(jnp.bfloat16))
                term = jnp.dot(
                    jnp.concatenate(lefts, axis=1),
                    jnp.concatenate(picks, axis=0),
                    preferred_element_type=jnp.float32,
                )
                total = term if total is None else total + term
            rows = (2 * nv + 1) * count
            for s in range(groups):
                to = slice(starts[part] + s * rows, starts[part] + (s + 1) * rows)
                value = total[:, s * nz : (s + 1) * nz]
                if nq == block:
                    acc[to] = value
                else:
                    acc[to] += value

    if nq != block:
        acc[...] = jnp.zeros_like(acc)
    each(nq // block, fill)

    def filled(part, s, before):
        count = parts[part][0]
        start = starts[part] + s * (2 * nv + 1) * count
        new = acc[start : start + nv * count] + acc[start + nv * count : start + 2 * nv * count]
        mark = acc[start + 2 * nv * count : start + (2 * nv + 1) * count]
        return jnp.where(mark[None] > 0.5, new.reshape(nv, count, nz), before)

    inside = slice(top, top + cy)
    for s in range(spread):
        before = jnp.concatenate([cons[:, x] for x in range(s, cx, spread)], axis=1)
        new = filled(0, s, before)
        for n, x in enumerate(range(s, cx, spread)):
            ext[:nv, 1 + x, inside] = new[:, n * cy : (n + 1) * cy]
    ext[nv:, 1 : cx + 1, inside] = vel[...]

    sides = {("gx", True): 0.0, ("gx", False): 0.0, ("gy", True): 0.0, ("gy", False): 0.0}
    for n, (axis, _, _) in enumerate(kinds):
        count = parts[n + 1][0]
        halo = halos[n][: (nv + 3) * count].reshape(nv + 3, count, nz)
        halo = jnp.concatenate([filled(n + 1, 0, halo[:nv]), halo[nv:]], axis=0)
        sides[axis, True] += jnp.where(above[n], halo, 0.0)
        sides[axis, False] += jnp.where(above[n], 0.0, halo)
    for (axis, high), halo in sides.items():
        halo = jnp.broadcast_to(halo, (nv + 3, cy if axis == "gx" else cx, nz))
        if axis == "gx":
            ext[:, cx + 1 if high else 0, inside] = halo
        else:
            ext[:, 1 : cx + 1, top + cy if high else top - 1] = halo

    copies = []

    def finish(v, value):
        result[v] = value
        copies.append(pltpu.make_async_copy(result.at[v], out.at[v], sems.at[v]))
        copies[-1].start()

    def electric(n, d, by):
        a, b = (n + 1) % 3, (n + 2) % 3
        if d == 2 and by:
            return along_z(electric(n, 2, 0), by)

        def at(v):
            return shifted(ext, v, cx, cy, d, by)

        return at(nv + b) * at(fluid_count + a) - at(nv + a) * at(fluid_count + b)

    def central(n, d):
        return electric(n, d, 1) - electric(n, d, -1)

    for n in range(3):
        v = fluid_count + n
        a, b = (n + 1) % 3, (n + 2) % 3
        curl = central(b, a) - central(a, b)
        finish(v, window(ext, v, cx, cy) - (0.5 * courant_number) * curl)

    factors = []
    centre = jnp.ones((cx, cy, nz), jnp.float32)
    for d in range(3):
        speed = window(ext, nv + d, cx, cy)
        up_low, up_high = face(speed, shifted(ext, nv + d, cx, cy, d, 1))
        down_low, down_high = face(shifted(ext, nv + d, cx, cy, d, -1), speed)
        centre = centre - up_low + down_high
        factors.append((down_low, up_high))
    for v in range(fluid_count):
        total = centre * window(ext, v, cx, cy)
        for d, (down_low, up_high) in enumerate(factors):
            total = total + down_low * shifted(ext, v, cx, cy, d, -1)
            total = total - up_high * shifted(ext, v, cx, cy, d, 1)
        finish(v, total)
    for copy in copies:
        copy.wait()


def per_device(ngx, ngy, conserved, velocity, donor_corner, donor_fraction, target_cell):
    kinds = exchanges(ngx, ngy)
    cons = conserved[:, 0]
    vel = velocity[:, 0]
    corner = donor_corner[0, 0, 0]
    fraction = donor_fraction[:, 0, 0, 0]
    target = target_cell[0, 0, 0]
    nv, cx, cy, nz = cons.shape
    ng, nq, slots = corner.shape
    rows = cx * cy
    per = nz // slots
    tiles = -(-(1 + len(kinds)) // per)
    f32 = jnp.float32

    def shape(*dims):
        return jax.ShapeDtypeStruct(dims, f32)

    alongs = [cy if axis == "gx" else cx for axis, _, _ in kinds]
    pay_shapes = [((nv + 3) * along + nq, nz) for along in alongs]
    anywhere = pl.BlockSpec(memory_space=pl.ANY)
    blended, aims, *pays = pl.pallas_call(
        functools.partial(blend_kernel, ngy, kinds),
        out_shape=[shape(ng * nq, nv, tiles * nz), shape(nq, nz)]
        + [shape(*dims) for dims in pay_shapes],
        in_specs=[anywhere] * 5,
        out_specs=[anywhere] * (2 + len(kinds)),
        scratch_shapes=[pltpu.VMEM(dims, f32) for dims in pay_shapes]
        + [
            pltpu.VMEM(cons.shape, f32),
            pltpu.VMEM(vel.shape, f32),
            pltpu.VMEM(corner.shape, jnp.int32),
            pltpu.VMEM(fraction.shape, f32),
            pltpu.VMEM(target.shape, jnp.int32),
            pltpu.VMEM((nv * rows, 3 * nz), jnp.bfloat16),
            pltpu.VMEM((nq, nz), jnp.int32),
            pltpu.VMEM((3, nq, nz), f32),
            pltpu.VMEM((nq, nz), f32),
            pltpu.VMEM((ng - 1, per, nq // per, nv, nz), f32),
            pltpu.VMEM((ng, nq, nv, tiles * nz), f32),
            pltpu.SemaphoreType.DMA((5,)),
            pltpu.SemaphoreType.DMA((1 + ng + len(kinds),)),
        ],
        compiler_params=pltpu.CompilerParams(vmem_limit_bytes=56 << 20),
        name="blend",
    )(cons, vel, corner, fraction, target)

    received = lax.all_to_all(
        blended, ("grp", "gx", "gy"), split_axis=0, concat_axis=0, tiled=True
    )
    halos = []
    for (axis, phase, _), pay in zip(kinds, pays):
        count = ngx if axis == "gx" else ngy
        pairs = []
        for low in range(phase, count - 1, 2):
            pairs += [(low, low + 1), (low + 1, low)]
        halos.append(lax.ppermute(pay, axis, pairs))

    result = pl.pallas_call(
        functools.partial(step_kernel, kinds, slots, ng),
        out_shape=shape(nv, cx, cy, nz),
        out_specs=pl.BlockSpec(memory_space=pl.ANY),
        scratch_shapes=[
            pltpu.VMEM((nv + 3, cx + 2, cy + 2 * top, nz), f32),
            pltpu.VMEM(((2 * nv + 1) * (rows + sum(alongs)), nz), f32),
            pltpu.VMEM((nv, cx, cy, nz), f32),
            pltpu.SemaphoreType.DMA((nv,)),
        ],
        compiler_params=pltpu.CompilerParams(vmem_limit_bytes=min(48, 16 + nq // 2) << 20),
        name="step",
    )(cons, vel, aims, received, *halos)
    return result[:, None]


def solution(mesh):
    return jax.shard_map(
        functools.partial(per_device, mesh.shape["gx"], mesh.shape["gy"]),
        mesh=mesh,
        in_specs=(
            P(None, "grp", "gx", "gy", None),
            P(None, "grp", "gx", "gy", None),
            P("grp", "gx", "gy", None, None, None),
            P(None, "grp", "gx", "gy", None, None, None),
            P("grp", "gx", "gy", None, None, None),
        ),
        out_specs=P(None, "grp", "gx", "gy", None),
        check_vma=False,
    )
```

```python
import functools

import jax
import jax.numpy as jnp
from jax import lax
from jax.experimental import pallas as pl
from jax.experimental.pallas import tpu as pltpu
from jax.sharding import PartitionSpec as P

signal_speed = 0.5
courant_number = 0.3
fluid_count = 5
block = 8


def exchanges(ngx, ngy):
    def partner(count, phase, n):
        other = n + 1 if (n + phase) % 2 == 0 else n - 1
        return other if 0 <= other < count else n

    kinds = []
    for phase in range(min(ngx - 1, 2)):
        kinds.append(("gx", phase, lambda i, j, phase=phase: (partner(ngx, phase, i), j)))
    for phase in range(min(ngy - 1, 2)):
        kinds.append(("gy", phase, lambda i, j, phase=phase: (i, partner(ngy, phase, j))))
    return kinds


def partner_above(axis, phase):
    return (lax.axis_index(axis) + phase) % 2 == 0


def split(value):
    high = value.astype(jnp.bfloat16)
    low = (value - high.astype(jnp.float32)).astype(jnp.bfloat16)
    return high, low


def over(value, n):
    return value >> (n.bit_length() - 1) if n & (n - 1) == 0 else value // n


def rest_of(value, n):
    return value & (n - 1) if n & (n - 1) == 0 else value % n


def each(count, body):
    if count == 1:
        body(0)
    else:
        lax.fori_loop(0, count, lambda n, c: (body(n), c)[1], 0)


def blend_kernel(ngy, kinds, cons, vel, corner, fraction, target, out, aims, *rest):
    pays_out = rest[: len(kinds)]
    pays = rest[len(kinds) : 2 * len(kinds)]
    (at_cons, at_vel, at_corner, at_fraction, at_target, uhl, cells, parts, aimed, moved, tiles) = rest[
        2 * len(kinds) : -2
    ]
    arrive, leave = rest[-2:]
    nv, cx, cy, nz = cons.shape
    ng, nq, slots = corner.shape
    lanes = nz
    per = lanes // slots
    chunks = block // per
    rows = cx * cy
    me = lax.axis_index("grp")

    moves = [(corner, at_corner), (fraction, at_fraction), (target, at_target)]
    moves += [(cons, at_cons), (vel, at_vel)]
    ins = [pltpu.make_async_copy(a, b, arrive.at[n]) for n, (a, b) in enumerate(moves)]
    outs = []

    def send(source, to):
        outs.append(pltpu.make_async_copy(source, to, leave.at[len(outs)]))
        outs[-1].start()

    for copy in ins:
        copy.start()

    tiles[0] = jnp.zeros(tiles.shape[1:], jnp.float32)
    send(tiles.at[0], out.at[pl.ds(me * nq, nq)])

    for copy in ins[:3]:
        copy.wait()
    aimed[...] = jnp.zeros(aimed.shape, jnp.float32)
    for n in range(nq // block):
        for away in range(1, ng):
            h = (me + away) % ng
            for c in range(chunks):
                at = n * block + (away - 1) * chunks + c
                for q in range(per):
                    row = n * block + c * per + q
                    cols = slice(q * slots, (q + 1) * slots)
                    cells[at : at + 1, cols] = at_corner[h, row : row + 1]
                    for d in range(3):
                        parts[d, at : at + 1, cols] = at_fraction[d, h, row : row + 1]
                    aim = at_target[h, row : row + 1] - rows * nz
                    aimed[at : at + 1, cols] = aim.astype(jnp.float32)
    send(aimed, aims)

    for copy in ins[3:]:
        copy.wait()
    for (axis, phase, _), pay, to in zip(kinds, pays, pays_out):
        above = partner_above(axis, phase)
        along = cy if axis == "gx" else cx
        for count, source, start in ((nv, at_cons, 0), (3, at_vel, nv * along)):
            if axis == "gx":
                layer = source[:, pl.ds(jnp.where(above, cx - 1, 0), 1)]
            else:
                layer = source[:, :, pl.ds(jnp.where(above, cy - 1, 0), 1)]
            pay[start : start + count * along] = layer.reshape(count * along, nz)
        pay[(nv + 3) * along :] = aimed[...]
        send(pay, to)

    high, low = split(at_cons[...].reshape(nv * rows, nz))
    uhl[:, :nz] = high
    uhl[:, nz : 2 * nz] = low
    uhl[:, 2 * nz :] = high

    def weight(count, at, upper):
        place = lax.broadcasted_iota(jnp.int32, (count, lanes), 0)
        return jnp.where(place == at, 1.0 - upper, jnp.where(place == at + 1, upper, 0.0))

    def blend(n):
        here = pl.ds(n * block, block)
        cell = cells[here]
        at_x, at_y, at_z = over(cell, nz * cy), rest_of(over(cell, nz), cy), rest_of(cell, nz)
        fx, fy, fz = parts[0, here], parts[1, here], parts[2, here]

        def one(at):
            row = slice(at, at + 1)
            wx = weight(cx, at_x[row], fx[row])
            wy = weight(cy, at_y[row], fy[row])
            wxy = jnp.concatenate([wx[x : x + 1] * wy for x in range(cx)], axis=0)
            return split(weight(nz, at_z[row], fz[row])) + (wxy,)

        for away in range(1, ng):
            made = [one((away - 1) * chunks + c) for c in range(chunks)]
            wh = jnp.concatenate([m[0] for m in made], axis=1)
            wl = jnp.concatenate([m[1] for m in made], axis=1)
            wxy = jnp.concatenate([m[2] for m in made], axis=1)
            along = jnp.dot(
                uhl[...],
                jnp.concatenate([wh, wh, wl], axis=0),
                preferred_element_type=jnp.float32,
            )
            values = jnp.sum(along.reshape(nv, rows, chunks * lanes) * wxy[None], axis=1)
            for c in range(chunks):
                value = values[:, c * lanes : (c + 1) * lanes]
                for turn in range(per):
                    moved[away - 1, turn, n * chunks + c] = (
                        pltpu.roll(value, turn * slots, 1) if turn else value
                    )
            if nq == block:
                assemble(away)

    lane = lax.broadcasted_iota(jnp.int32, (nv, lanes), 1) // slots

    def assemble(away):
        for q in range(nq):
            i, j = q // ngy, q % ngy
            owners = [q] + [a * ngy + b for a, b in (of(i, j) for _, _, of in kinds)]
            for t in range(0, len(owners), per):
                tile = None
                for k, owner in enumerate(owners[t : t + per]):
                    piece = moved[away - 1, (k - owner) % per, owner // per]
                    tile = piece if tile is None else jnp.where(lane == k, piece, tile)
                tiles[away, q, :, t // per * lanes : (t // per + 1) * lanes] = tile
        send(tiles.at[away], out.at[pl.ds((me + away) % ng * nq, nq)])

    each(nq // block, blend)
    if nq != block:
        for away in range(1, ng):
            assemble(away)
    for copy in outs:
        copy.wait()


top = 8


def window(ext, v, cx, cy, move_x=0, move_y=0):
    return ext[v, 1 + move_x : 1 + move_x + cx, top + move_y : top + move_y + cy]


def along_z(value, by):
    nz = value.shape[-1]
    at = lax.broadcasted_iota(jnp.int32, (1,) + value.shape[1:], 2)
    edge = 0 if by < 0 else nz - 1
    return jnp.where(at == edge, 0.0, pltpu.roll(value, (-by) % nz, 2))


def shifted(ext, v, cx, cy, d, by):
    if d == 2 and by:
        return along_z(window(ext, v, cx, cy), by)
    return window(ext, v, cx, cy, by if d == 0 else 0, by if d == 1 else 0)


def face(low, high):
    wave_low = jnp.minimum(jnp.minimum(low, high) - signal_speed, 0.0)
    wave_high = jnp.maximum(jnp.maximum(low, high) + signal_speed, 0.0)
    scale = courant_number / (wave_high - wave_low)
    return (
        scale * wave_high * (low - wave_low),
        scale * wave_low * (wave_high - high),
    )


def prepare_kernel(slots, ng, cons, vel, aims, coefs, base, picks, marks):
    nv, cx, cy, nz = cons.shape
    lanes = nz
    per = lanes // slots
    chunks = block // per
    nq = aims.shape[0]
    spread = 4 if cx % 4 == 0 else 1
    count = cx // spread * cy
    used = (ng - 1) * chunks

    def pick(n):
        cell = aims[pl.ds(n * block, block)].astype(jnp.int32) + cx * cy * nz
        x, y, z = over(cell, nz * cy), rest_of(over(cell, nz), cy), rest_of(cell, nz)
        at_row = over(x, spread) * cy + y
        at_column = (rest_of(x, spread) * nz + z).T
        up = lax.broadcasted_iota(jnp.int32, (count, lanes), 0)
        along = lax.broadcasted_iota(jnp.int32, (lanes, spread * nz), 1)
        total = None
        for at in range(0, used, chunks):
            hits = []
            for c in range(chunks):
                hits.append(jnp.where(up == at_row[at + c : at + c + 1], 1.0, 0.0))
                to = pl.ds(pl.multiple_of((n * used + at + c) * lanes, lanes), lanes)
                chosen = at_column[:, at + c : at + c + 1] == along
                picks[to] = jnp.where(chosen, 1.0, 0.0).astype(jnp.bfloat16)
            to = pl.ds(pl.multiple_of((n * used + at) * lanes, lanes), chunks * lanes)
            term = jnp.dot(
                jnp.concatenate(hits, axis=1).astype(jnp.bfloat16),
                picks[to],
                preferred_element_type=jnp.float32,
            )
            total = term if total is None else total + term
        if nq == block:
            marks[...] = total
        else:
            marks[...] += total

    if nq != block:
        marks[...] = jnp.zeros_like(marks)
    each(nq // block, pick)
    for x in range(cx):
        rows = slice(x // spread * cy, (x // spread + 1) * cy)
        mark = marks[rows, x % spread * nz : (x % spread + 1) * nz]
        base[:, x] = jnp.where(mark[None] > 0.5, 0.0, cons[:, x])

    centre = jnp.ones((cx, cy, nz), jnp.float32)
    none = jnp.zeros((1, cy, nz), jnp.float32)
    low, high = face(vel[0, : cx - 1], vel[0, 1:])
    coefs[0] = jnp.concatenate([none, low], axis=0)
    coefs[1] = -jnp.concatenate([high, none], axis=0)
    centre += jnp.concatenate([none, high], axis=0) - jnp.concatenate([low, none], axis=0)

    at_y = lax.broadcasted_iota(jnp.int32, (1, cy, nz), 1)
    speed = vel[1]
    low, high = face(speed, pltpu.roll(speed, cy - 1, 1))
    low = jnp.where(at_y == cy - 1, 0.0, low)
    high = jnp.where(at_y == cy - 1, 0.0, high)
    coefs[2] = pltpu.roll(low, 1, 1)
    coefs[3] = -high
    centre += pltpu.roll(high, 1, 1) - low

    speed = vel[2]
    up_low, up_high = face(speed, along_z(speed, 1))
    down_low, down_high = face(along_z(speed, -1), speed)
    coefs[4] = down_low
    coefs[5] = -up_high
    coefs[6] = centre + down_high - up_low


def step_kernel(kinds, slots, ng, vel, aims, given, base, picks, received, *rest):
    halos = rest[: len(kinds)]
    out, coefs, ext, field, acc, result, sems = rest[len(kinds) :]
    nv, cx, cy, nz = base.shape
    lanes = nz
    nq = received.shape[0] // ng
    per = lanes // slots
    chunks = block // per
    used = (ng - 1) * chunks
    spread = 4 if cx % 4 == 0 else 1
    me = lax.axis_index("grp")
    lane = lax.broadcasted_iota(jnp.int32, (nv, lanes), 1) // slots
    above = [partner_above(axis, phase) for axis, phase, _ in kinds]

    parts = [(cx // spread * cy, spread)]
    parts += [(cy if axis == "gx" else cx, 1) for axis, _, _ in kinds]
    starts = [0]
    for count, groups in parts:
        starts.append(starts[-1] + (2 * nv + 1) * count * groups)

    def fill(n):
        for part, (count, groups) in enumerate(parts):
            if part == 0:
                cell = aims[pl.ds(n * block, block)]
            else:
                cell = halos[part - 1][pl.ds((nv + 3) * count + n * block, block)]
            cell = cell.astype(jnp.int32) + cx * cy * nz
            x, y, z = over(cell, nz * cy), rest_of(over(cell, nz), cy), rest_of(cell, nz)
            if part == 0:
                at_row = over(x, spread) * cy + y
            elif kinds[part - 1][0] == "gx":
                at_row = jnp.where(x == jnp.where(above[part - 1], 0, cx - 1), y, -1)
            else:
                at_row = jnp.where(y == jnp.where(above[part - 1], 0, cy - 1), x, -1)
            at_column = z.T
            up = lax.broadcasted_iota(jnp.int32, (count, lanes), 0)
            along = lax.broadcasted_iota(jnp.int32, (lanes, nz), 1)
            here = slice(part // per * lanes, (part // per + 1) * lanes)
            total = None
            for away in range(1, ng):
                g = (me + away) % ng
                lefts, chosen = [], []
                for c in range(chunks):
                    at = (away - 1) * chunks + c
                    value = None
                    for p in range(per):
                        piece = received[g * nq + n * block + c * per + p, :, here]
                        turn = (p - part) % per
                        if turn:
                            piece = pltpu.roll(piece, turn * slots, 1)
                        value = piece if value is None else jnp.where(lane == p, piece, value)
                    high = value.astype(jnp.bfloat16).astype(jnp.float32)
                    low = value - high
                    hit = up == at_row[at : at + 1]
                    pieces = [jnp.where(hit, high[v : v + 1], 0.0) for v in range(nv)]
                    pieces += [jnp.where(hit, low[v : v + 1], 0.0) for v in range(nv)]
                    if part:
                        pieces += [jnp.where(hit, 1.0, 0.0)]
                        pick = jnp.where(at_column[:, at : at + 1] == along, 1.0, 0.0)
                        chosen.append(pick.astype(jnp.bfloat16))
                    lefts.append(jnp.concatenate(pieces, axis=0).astype(jnp.bfloat16))
                if part:
                    chosen = jnp.concatenate(chosen, axis=0)
                else:
                    start = (n * used + (away - 1) * chunks) * lanes
                    chosen = picks[pl.ds(pl.multiple_of(start, lanes), chunks * lanes)]
                term = jnp.dot(
                    jnp.concatenate(lefts, axis=1), chosen, preferred_element_type=jnp.float32
                )
                total = term if total is None else total + term
            rows = total.shape[0]
            for s in range(groups):
                start = starts[part] + s * (2 * nv + 1) * count
                value = total[:, s * nz : (s + 1) * nz]
                if nq == block:
                    acc[start : start + rows] = value
                else:
                    acc[start : start + rows] += value

    if nq != block:
        acc[...] = jnp.zeros_like(acc)
    each(nq // block, fill)

    def brought(part, s):
        count = parts[part][0]
        start = starts[part] + s * (2 * nv + 1) * count
        new = acc[start : start + nv * count] + acc[start + nv * count : start + 2 * nv * count]
        return new.reshape(nv, count, nz)

    def crossed(n, speeds, fields):
        a, b = (n + 1) % 3, (n + 2) % 3
        return speeds[b] * fields[a] - speeds[a] * fields[b]

    inside = slice(top, top + cy)
    for s in range(spread):
        new = brought(0, s)
        for n, x in enumerate(range(s, cx, spread)):
            state = base[:, x] + new[:, n * cy : (n + 1) * cy]
            ext[:fluid_count, 1 + x, inside] = state[:fluid_count]
            field[:, x] = state[fluid_count:]
            for d in range(3):
                ext[fluid_count + d, 1 + x, inside] = crossed(d, vel[:, x], state[fluid_count:])

    sides = {("gx", True): 0.0, ("gx", False): 0.0, ("gy", True): 0.0, ("gy", False): 0.0}
    for n, (axis, _, _) in enumerate(kinds):
        count = parts[n + 1][0]
        d = 0 if axis == "gx" else 1
        halo = halos[n][: (nv + 3) * count].reshape(nv + 3, count, nz)
        mark = acc[starts[n + 1] + 2 * nv * count : starts[n + 1] + (2 * nv + 1) * count]
        state = jnp.where(mark[None] > 0.5, brought(n + 1, 0), halo[:nv])
        electric = [crossed(m, halo[nv:], state[fluid_count:])[None] for m in (1 - d, 2)]
        halo = jnp.concatenate([state[:fluid_count], halo[nv + d : nv + d + 1]] + electric, axis=0)
        sides[axis, True] += jnp.where(above[n], halo, 0.0)
        sides[axis, False] += jnp.where(above[n], 0.0, halo)

    coefs[...] = given[...]
    for (axis, high), halo in sides.items():
        d = 0 if axis == "gx" else 1
        halo = jnp.broadcast_to(halo, (fluid_count + 3, cx if d else cy, nz))
        if d == 0:
            at = (cx + 1 if high else 0, inside)
            edge = (cx - 1 if high else 0,)
        else:
            at = (slice(1, cx + 1), top + cy if high else top - 1)
            edge = (slice(None), cy - 1 if high else 0)
        ext[(slice(0, fluid_count),) + at] = halo[:fluid_count]
        ext[(fluid_count + 1 - d,) + at] = halo[fluid_count + 1]
        ext[(fluid_count + 2,) + at] = halo[fluid_count + 2]
        speed = vel[(d,) + edge]
        if high:
            of_low, of_high = face(speed, halo[fluid_count])
            coefs[(2 * d + 1,) + edge] = -of_high
            coefs[(6,) + edge] -= of_low
        else:
            of_low, of_high = face(halo[fluid_count], speed)
            coefs[(2 * d,) + edge] = of_low
            coefs[(6,) + edge] += of_high

    copies = []

    def finish(v, value):
        result[v] = value
        copies.append(pltpu.make_async_copy(result.at[v], out.at[v], sems.at[v]))
        copies[-1].start()

    def central(n, d):
        v = fluid_count + n
        return shifted(ext, v, cx, cy, d, 1) - shifted(ext, v, cx, cy, d, -1)

    for n in range(3):
        a, b = (n + 1) % 3, (n + 2) % 3
        curl = central(b, a) - central(a, b)
        finish(fluid_count + n, field[n] - (0.5 * courant_number) * curl)
    for v in range(fluid_count):
        total = coefs[6] * window(ext, v, cx, cy)
        for d in range(3):
            total = total + coefs[2 * d] * shifted(ext, v, cx, cy, d, -1)
            total = total + coefs[2 * d + 1] * shifted(ext, v, cx, cy, d, 1)
        finish(v, total)
    for copy in copies:
        copy.wait()


def per_device(ngx, ngy, conserved, velocity, donor_corner, donor_fraction, target_cell):
    kinds = exchanges(ngx, ngy)
    cons = conserved[:, 0]
    vel = velocity[:, 0]
    corner = donor_corner[0, 0, 0]
    fraction = donor_fraction[:, 0, 0, 0]
    target = target_cell[0, 0, 0]
    nv, cx, cy, nz = cons.shape
    ng, nq, slots = corner.shape
    rows = cx * cy
    per = nz // slots
    tiles = -(-(1 + len(kinds)) // per)
    f32 = jnp.float32

    def shape(*dims):
        return jax.ShapeDtypeStruct(dims, f32)

    alongs = [cy if axis == "gx" else cx for axis, _, _ in kinds]
    pay_shapes = [((nv + 3) * along + nq, nz) for along in alongs]
    anywhere = pl.BlockSpec(memory_space=pl.ANY)
    blended, aims, *pays = pl.pallas_call(
        functools.partial(blend_kernel, ngy, kinds),
        out_shape=[shape(ng * nq, nv, tiles * nz), shape(nq, nz)]
        + [shape(*dims) for dims in pay_shapes],
        in_specs=[anywhere] * 5,
        out_specs=[anywhere] * (2 + len(kinds)),
        scratch_shapes=[pltpu.VMEM(dims, f32) for dims in pay_shapes]
        + [
            pltpu.VMEM(cons.shape, f32),
            pltpu.VMEM(vel.shape, f32),
            pltpu.VMEM(corner.shape, jnp.int32),
            pltpu.VMEM(fraction.shape, f32),
            pltpu.VMEM(target.shape, jnp.int32),
            pltpu.VMEM((nv * rows, 3 * nz), jnp.bfloat16),
            pltpu.VMEM((nq, nz), jnp.int32),
            pltpu.VMEM((3, nq, nz), f32),
            pltpu.VMEM((nq, nz), f32),
            pltpu.VMEM((ng - 1, per, nq // per, nv, nz), f32),
            pltpu.VMEM((ng, nq, nv, tiles * nz), f32),
            pltpu.SemaphoreType.DMA((5,)),
            pltpu.SemaphoreType.DMA((1 + ng + len(kinds),)),
        ],
        compiler_params=pltpu.CompilerParams(vmem_limit_bytes=56 << 20),
        name="blend",
    )(cons, vel, corner, fraction, target)

    received = lax.all_to_all(
        blended, ("grp", "gx", "gy"), split_axis=0, concat_axis=0, tiled=True
    )
    halos = []
    for (axis, phase, _), pay in zip(kinds, pays):
        count = ngx if axis == "gx" else ngy
        pairs = []
        for low in range(phase, count - 1, 2):
            pairs += [(low, low + 1), (low + 1, low)]
        halos.append(lax.ppermute(pay, axis, pairs))

    spread = 4 if cx % 4 == 0 else 1
    coefs, base, picks = pl.pallas_call(
        functools.partial(prepare_kernel, slots, ng),
        out_shape=[
            shape(7, cx, cy, nz),
            shape(nv, cx, cy, nz),
            jax.ShapeDtypeStruct(((ng - 1) * nq * slots, spread * nz), jnp.bfloat16),
        ],
        scratch_shapes=[pltpu.VMEM((rows // spread, spread * nz), f32)],
        compiler_params=pltpu.CompilerParams(vmem_limit_bytes=56 << 20),
        name="prepare",
    )(cons, vel, aims)

    result = pl.pallas_call(
        functools.partial(step_kernel, kinds, slots, ng),
        out_shape=shape(nv, cx, cy, nz),
        out_specs=pl.BlockSpec(memory_space=pl.ANY),
        scratch_shapes=[
            pltpu.VMEM((7, cx, cy, nz), f32),
            pltpu.VMEM((fluid_count + 3, cx + 2, cy + 2 * top, nz), f32),
            pltpu.VMEM((nv - fluid_count, cx, cy, nz), f32),
            pltpu.VMEM(((2 * nv + 1) * (rows + sum(alongs)), nz), f32),
            pltpu.VMEM((nv, cx, cy, nz), f32),
            pltpu.SemaphoreType.DMA((nv,)),
        ],
        compiler_params=pltpu.CompilerParams(vmem_limit_bytes=min(48, 16 + nq // 2) << 20),
        name="step",
    )(vel, aims, coefs, base, picks, received, *halos)
    return result[:, None]


def solution(mesh):
    return jax.shard_map(
        functools.partial(per_device, mesh.shape["gx"], mesh.shape["gy"]),
        mesh=mesh,
        in_specs=(
            P(None, "grp", "gx", "gy", None),
            P(None, "grp", "gx", "gy", None),
            P("grp", "gx", "gy", None, None, None),
            P(None, "grp", "gx", "gy", None, None, None),
            P("grp", "gx", "gy", None, None, None),
        ),
        out_specs=P(None, "grp", "gx", "gy", None),
        check_vma=False,
    )
```

```python
import functools

import jax
import jax.numpy as jnp
from jax import lax
from jax.experimental import pallas as pl
from jax.experimental.pallas import tpu as pltpu
from jax.sharding import PartitionSpec as P

signal_speed = 0.5
courant_number = 0.3
fluid_count = 5
block = 8


def exchanges(ngx, ngy):
    def partner(count, phase, n):
        other = n + 1 if (n + phase) % 2 == 0 else n - 1
        return other if 0 <= other < count else n

    kinds = []
    for phase in range(min(ngx - 1, 2)):
        kinds.append(("gx", phase, lambda i, j, phase=phase: (partner(ngx, phase, i), j)))
    for phase in range(min(ngy - 1, 2)):
        kinds.append(("gy", phase, lambda i, j, phase=phase: (i, partner(ngy, phase, j))))
    return kinds


def partner_above(axis, phase):
    return (lax.axis_index(axis) + phase) % 2 == 0


def split(value):
    high = value.astype(jnp.bfloat16)
    low = (value - high.astype(jnp.float32)).astype(jnp.bfloat16)
    return high, low


def over(value, n):
    return value >> (n.bit_length() - 1) if n & (n - 1) == 0 else value // n


def rest_of(value, n):
    return value & (n - 1) if n & (n - 1) == 0 else value % n


def each(count, body):
    if count == 1:
        body(0)
    else:
        lax.fori_loop(0, count, lambda n, c: (body(n), c)[1], 0)


def blend_kernel(ngy, kinds, cons, vel, corner, fraction, target, out, aims, *rest):
    pays_out = rest[: len(kinds)]
    pays = rest[len(kinds) : 2 * len(kinds)]
    (at_cons, at_vel, at_corner, at_fraction, at_target, uhl, cells, parts, aimed, moved, tiles) = rest[
        2 * len(kinds) : -2
    ]
    arrive, leave = rest[-2:]
    nv, cx, cy, nz = cons.shape
    ng, nq, slots = corner.shape
    lanes = nz
    per = lanes // slots
    chunks = block // per
    rows = cx * cy
    me = lax.axis_index("grp")

    moves = [(corner, at_corner), (fraction, at_fraction), (target, at_target)]
    moves += [(cons, at_cons), (vel, at_vel)]
    ins = [pltpu.make_async_copy(a, b, arrive.at[n]) for n, (a, b) in enumerate(moves)]
    outs = []

    def send(source, to):
        outs.append(pltpu.make_async_copy(source, to, leave.at[len(outs)]))
        outs[-1].start()

    for copy in ins:
        copy.start()

    tiles[0] = jnp.zeros(tiles.shape[1:], jnp.float32)
    send(tiles.at[0], out.at[pl.ds(me * nq, nq)])

    for copy in ins[:3]:
        copy.wait()
    aimed[...] = jnp.zeros(aimed.shape, jnp.float32)
    for n in range(nq // block):
        for away in range(1, ng):
            h = (me + away) % ng
            for c in range(chunks):
                at = n * block + (away - 1) * chunks + c
                for q in range(per):
                    row = n * block + c * per + q
                    cols = slice(q * slots, (q + 1) * slots)
                    cells[at : at + 1, cols] = at_corner[h, row : row + 1]
                    for d in range(3):
                        parts[d, at : at + 1, cols] = at_fraction[d, h, row : row + 1]
                    aim = at_target[h, row : row + 1] - rows * nz
                    aimed[at : at + 1, cols] = aim.astype(jnp.float32)
    send(aimed, aims)

    for copy in ins[3:]:
        copy.wait()
    for (axis, phase, _), pay, to in zip(kinds, pays, pays_out):
        above = partner_above(axis, phase)
        along = cy if axis == "gx" else cx
        for count, source, start in ((nv, at_cons, 0), (3, at_vel, nv * along)):
            if axis == "gx":
                layer = source[:, pl.ds(jnp.where(above, cx - 1, 0), 1)]
            else:
                layer = source[:, :, pl.ds(jnp.where(above, cy - 1, 0), 1)]
            pay[start : start + count * along] = layer.reshape(count * along, nz)
        pay[(nv + 3) * along :] = aimed[...]
        send(pay, to)

    high, low = split(at_cons[...].reshape(nv * rows, nz))
    uhl[:, :nz] = high
    uhl[:, nz : 2 * nz] = low
    uhl[:, 2 * nz :] = high

    def weight(count, at, upper):
        place = lax.broadcasted_iota(jnp.int32, (count, lanes), 0)
        return jnp.where(place == at, 1.0 - upper, jnp.where(place == at + 1, upper, 0.0))

    def blend(n):
        here = pl.ds(n * block, block)
        cell = cells[here]
        at_x, at_y, at_z = over(cell, nz * cy), rest_of(over(cell, nz), cy), rest_of(cell, nz)
        fx, fy, fz = parts[0, here], parts[1, here], parts[2, here]

        def one(at):
            row = slice(at, at + 1)
            wx = weight(cx, at_x[row], fx[row])
            wy = weight(cy, at_y[row], fy[row])
            wxy = jnp.concatenate([wx[x : x + 1] * wy for x in range(cx)], axis=0)
            return split(weight(nz, at_z[row], fz[row])) + (wxy,)

        for away in range(1, ng):
            made = [one((away - 1) * chunks + c) for c in range(chunks)]
            wh = jnp.concatenate([m[0] for m in made], axis=1)
            wl = jnp.concatenate([m[1] for m in made], axis=1)
            wxy = jnp.concatenate([m[2] for m in made], axis=1)
            along = jnp.dot(
                uhl[...],
                jnp.concatenate([wh, wh, wl], axis=0),
                preferred_element_type=jnp.float32,
            )
            values = jnp.sum(along.reshape(nv, rows, chunks * lanes) * wxy[None], axis=1)
            for c in range(chunks):
                value = values[:, c * lanes : (c + 1) * lanes]
                for turn in range(per):
                    moved[away - 1, turn, n * chunks + c] = (
                        pltpu.roll(value, turn * slots, 1) if turn else value
                    )
            if nq == block:
                assemble(away)

    lane = lax.broadcasted_iota(jnp.int32, (nv, lanes), 1) // slots

    def assemble(away):
        for q in range(nq):
            i, j = q // ngy, q % ngy
            owners = [q] + [a * ngy + b for a, b in (of(i, j) for _, _, of in kinds)]
            for t in range(0, len(owners), per):
                tile = None
                for k, owner in enumerate(owners[t : t + per]):
                    piece = moved[away - 1, (k - owner) % per, owner // per]
                    tile = piece if tile is None else jnp.where(lane == k, piece, tile)
                tiles[away, q, :, t // per * lanes : (t // per + 1) * lanes] = tile
        send(tiles.at[away], out.at[pl.ds((me + away) % ng * nq, nq)])

    each(nq // block, blend)
    if nq != block:
        for away in range(1, ng):
            assemble(away)
    for copy in outs:
        copy.wait()


top = 8


def window(ext, v, cx, cy, move_x=0, move_y=0):
    return ext[v, 1 + move_x : 1 + move_x + cx, top + move_y : top + move_y + cy]


def along_z(value, by):
    nz = value.shape[-1]
    at = lax.broadcasted_iota(jnp.int32, (1,) + value.shape[1:], 2)
    edge = 0 if by < 0 else nz - 1
    return jnp.where(at == edge, 0.0, pltpu.roll(value, (-by) % nz, 2))


def shifted(ext, v, cx, cy, d, by):
    if d == 2 and by:
        return along_z(window(ext, v, cx, cy), by)
    return window(ext, v, cx, cy, by if d == 0 else 0, by if d == 1 else 0)


def face(low, high):
    wave_low = jnp.minimum(jnp.minimum(low, high) - signal_speed, 0.0)
    wave_high = jnp.maximum(jnp.maximum(low, high) + signal_speed, 0.0)
    scale = courant_number / (wave_high - wave_low)
    return (
        scale * wave_high * (low - wave_low),
        scale * wave_low * (wave_high - high),
    )


def prepare_kernel(slots, ng, cons, vel, aims, coefs, base, picks, marks):
    nv, cx, cy, nz = cons.shape
    lanes = nz
    per = lanes // slots
    chunks = block // per
    nq = aims.shape[0]
    spread = 4 if cx % 4 == 0 else 1
    count = cx // spread * cy
    used = (ng - 1) * chunks

    def pick(n):
        cell = aims[pl.ds(n * block, block)].astype(jnp.int32) + cx * cy * nz
        x, y, z = over(cell, nz * cy), rest_of(over(cell, nz), cy), rest_of(cell, nz)
        at_row = over(x, spread) * cy + y
        at_column = (rest_of(x, spread) * nz + z).T
        up = lax.broadcasted_iota(jnp.int32, (count, lanes), 0)
        along = lax.broadcasted_iota(jnp.int32, (lanes, spread * nz), 1)
        total = None
        for at in range(0, used, chunks):
            hits = []
            for c in range(chunks):
                hits.append(jnp.where(up == at_row[at + c : at + c + 1], 1.0, 0.0))
                to = pl.ds(pl.multiple_of((n * used + at + c) * lanes, lanes), lanes)
                chosen = at_column[:, at + c : at + c + 1] == along
                picks[to] = jnp.where(chosen, 1.0, 0.0).astype(jnp.bfloat16)
            to = pl.ds(pl.multiple_of((n * used + at) * lanes, lanes), chunks * lanes)
            term = jnp.dot(
                jnp.concatenate(hits, axis=1).astype(jnp.bfloat16),
                picks[to],
                preferred_element_type=jnp.float32,
            )
            total = term if total is None else total + term
        if nq == block:
            marks[...] = total
        else:
            marks[...] += total

    if nq != block:
        marks[...] = jnp.zeros_like(marks)
    each(nq // block, pick)
    for x in range(cx):
        rows = slice(x // spread * cy, (x // spread + 1) * cy)
        mark = marks[rows, x % spread * nz : (x % spread + 1) * nz]
        base[:, x] = jnp.where(mark[None] > 0.5, 0.0, cons[:, x])

    centre = jnp.ones((cx, cy, nz), jnp.float32)
    none = jnp.zeros((1, cy, nz), jnp.float32)
    low, high = face(vel[0, : cx - 1], vel[0, 1:])
    coefs[0] = jnp.concatenate([none, low], axis=0)
    coefs[1] = -jnp.concatenate([high, none], axis=0)
    centre += jnp.concatenate([none, high], axis=0) - jnp.concatenate([low, none], axis=0)

    at_y = lax.broadcasted_iota(jnp.int32, (1, cy, nz), 1)
    speed = vel[1]
    low, high = face(speed, pltpu.roll(speed, cy - 1, 1))
    low = jnp.where(at_y == cy - 1, 0.0, low)
    high = jnp.where(at_y == cy - 1, 0.0, high)
    coefs[2] = pltpu.roll(low, 1, 1)
    coefs[3] = -high
    centre += pltpu.roll(high, 1, 1) - low

    speed = vel[2]
    up_low, up_high = face(speed, along_z(speed, 1))
    down_low, down_high = face(along_z(speed, -1), speed)
    coefs[4] = down_low
    coefs[5] = -up_high
    coefs[6] = centre + down_high - up_low


def step_kernel(kinds, slots, ng, vel, aims, given, base, picks, received, *rest):
    halos = rest[: len(kinds)]
    out, coefs, ext, field, acc, result, sems = rest[len(kinds) :]
    nv, cx, cy, nz = base.shape
    lanes = nz
    nq = received.shape[0] // ng
    per = lanes // slots
    chunks = block // per
    used = (ng - 1) * chunks
    spread = 4 if cx % 4 == 0 else 1
    me = lax.axis_index("grp")
    lane = lax.broadcasted_iota(jnp.int32, (nv, lanes), 1) // slots
    above = [partner_above(axis, phase) for axis, phase, _ in kinds]

    parts = [(cx // spread * cy, spread)]
    parts += [(cy if axis == "gx" else cx, 1) for axis, _, _ in kinds]
    starts = [0]
    for count, groups in parts:
        starts.append(starts[-1] + (2 * nv + 1) * count * groups)

    def fill(n):
        for part, (count, groups) in enumerate(parts):
            if part == 0:
                cell = aims[pl.ds(n * block, block)]
            else:
                cell = halos[part - 1][pl.ds((nv + 3) * count + n * block, block)]
            cell = cell.astype(jnp.int32) + cx * cy * nz
            x, y, z = over(cell, nz * cy), rest_of(over(cell, nz), cy), rest_of(cell, nz)
            if part == 0:
                at_row = over(x, spread) * cy + y
            elif kinds[part - 1][0] == "gx":
                at_row = jnp.where(x == jnp.where(above[part - 1], 0, cx - 1), y, -1)
            else:
                at_row = jnp.where(y == jnp.where(above[part - 1], 0, cy - 1), x, -1)
            at_column = z.T
            up = lax.broadcasted_iota(jnp.int32, (count, lanes), 0)
            along = lax.broadcasted_iota(jnp.int32, (lanes, nz), 1)
            here = slice(part // per * lanes, (part // per + 1) * lanes)
            total = None
            for away in range(1, ng):
                g = (me + away) % ng
                lefts, chosen = [], []
                for c in range(chunks):
                    at = (away - 1) * chunks + c
                    value = None
                    for p in range(per):
                        piece = received[g * nq + n * block + c * per + p, :, here]
                        turn = (p - part) % per
                        if turn:
                            piece = pltpu.roll(piece, turn * slots, 1)
                        value = piece if value is None else jnp.where(lane == p, piece, value)
                    high = value.astype(jnp.bfloat16).astype(jnp.float32)
                    low = value - high
                    hit = up == at_row[at : at + 1]
                    pieces = [jnp.where(hit, high[v : v + 1], 0.0) for v in range(nv)]
                    pieces += [jnp.where(hit, low[v : v + 1], 0.0) for v in range(nv)]
                    if part:
                        pieces += [jnp.where(hit, 1.0, 0.0)]
                        pick = jnp.where(at_column[:, at : at + 1] == along, 1.0, 0.0)
                        chosen.append(pick.astype(jnp.bfloat16))
                    lefts.append(jnp.concatenate(pieces, axis=0).astype(jnp.bfloat16))
                if part:
                    chosen = jnp.concatenate(chosen, axis=0)
                else:
                    start = (n * used + (away - 1) * chunks) * lanes
                    chosen = picks[pl.ds(pl.multiple_of(start, lanes), chunks * lanes)]
                term = jnp.dot(
                    jnp.concatenate(lefts, axis=1), chosen, preferred_element_type=jnp.float32
                )
                total = term if total is None else total + term
            rows = total.shape[0]
            for s in range(groups):
                start = starts[part] + s * (2 * nv + 1) * count
                value = total[:, s * nz : (s + 1) * nz]
                if nq == block:
                    acc[start : start + rows] = value
                else:
                    acc[start : start + rows] += value

    if nq != block:
        acc[...] = jnp.zeros_like(acc)
    each(nq // block, fill)

    def brought(part, s):
        count = parts[part][0]
        start = starts[part] + s * (2 * nv + 1) * count
        new = acc[start : start + nv * count] + acc[start + nv * count : start + 2 * nv * count]
        return new.reshape(nv, count, nz)

    def crossed(n, speeds, fields):
        a, b = (n + 1) % 3, (n + 2) % 3
        return speeds[b] * fields[a] - speeds[a] * fields[b]

    inside = slice(top, top + cy)
    for s in range(spread):
        new = brought(0, s)
        for n, x in enumerate(range(s, cx, spread)):
            state = base[:, x] + new[:, n * cy : (n + 1) * cy]
            ext[:fluid_count, 1 + x, inside] = state[:fluid_count]
            field[:, x] = state[fluid_count:]
            for d in range(3):
                ext[fluid_count + d, 1 + x, inside] = crossed(d, vel[:, x], state[fluid_count:])

    sides = {("gx", True): 0.0, ("gx", False): 0.0, ("gy", True): 0.0, ("gy", False): 0.0}
    for n, (axis, _, _) in enumerate(kinds):
        count = parts[n + 1][0]
        d = 0 if axis == "gx" else 1
        halo = halos[n][: (nv + 3) * count].reshape(nv + 3, count, nz)
        mark = acc[starts[n + 1] + 2 * nv * count : starts[n + 1] + (2 * nv + 1) * count]
        state = jnp.where(mark[None] > 0.5, brought(n + 1, 0), halo[:nv])
        electric = [crossed(m, halo[nv:], state[fluid_count:])[None] for m in (1 - d, 2)]
        halo = jnp.concatenate([state[:fluid_count], halo[nv + d : nv + d + 1]] + electric, axis=0)
        sides[axis, True] += jnp.where(above[n], halo, 0.0)
        sides[axis, False] += jnp.where(above[n], 0.0, halo)

    coefs[...] = given[...]
    for (axis, high), halo in sides.items():
        d = 0 if axis == "gx" else 1
        halo = jnp.broadcast_to(halo, (fluid_count + 3, cx if d else cy, nz))
        if d == 0:
            at = (cx + 1 if high else 0, inside)
            edge = (cx - 1 if high else 0,)
        else:
            at = (slice(1, cx + 1), top + cy if high else top - 1)
            edge = (slice(None), cy - 1 if high else 0)
        ext[(slice(0, fluid_count),) + at] = halo[:fluid_count]
        ext[(fluid_count + 1 - d,) + at] = halo[fluid_count + 1]
        ext[(fluid_count + 2,) + at] = halo[fluid_count + 2]
        speed = vel[(d,) + edge]
        if high:
            of_low, of_high = face(speed, halo[fluid_count])
            coefs[(2 * d + 1,) + edge] = -of_high
            coefs[(6,) + edge] -= of_low
        else:
            of_low, of_high = face(halo[fluid_count], speed)
            coefs[(2 * d,) + edge] = of_low
            coefs[(6,) + edge] += of_high

    copies = []

    def finish(v, value):
        result[v] = value
        copies.append(pltpu.make_async_copy(result.at[v], out.at[v], sems.at[v]))
        copies[-1].start()

    def central(n, d):
        v = fluid_count + n
        return shifted(ext, v, cx, cy, d, 1) - shifted(ext, v, cx, cy, d, -1)

    for n in range(3):
        a, b = (n + 1) % 3, (n + 2) % 3
        curl = central(b, a) - central(a, b)
        finish(fluid_count + n, field[n] - (0.5 * courant_number) * curl)
    for v in range(fluid_count):
        total = coefs[6] * window(ext, v, cx, cy)
        for d in range(3):
            total = total + coefs[2 * d] * shifted(ext, v, cx, cy, d, -1)
            total = total + coefs[2 * d + 1] * shifted(ext, v, cx, cy, d, 1)
        finish(v, total)
    for copy in copies:
        copy.wait()


def per_device(ngx, ngy, conserved, velocity, donor_corner, donor_fraction, target_cell):
    kinds = exchanges(ngx, ngy)
    cons = conserved[:, 0]
    vel = velocity[:, 0]
    corner = donor_corner[0, 0, 0]
    fraction = donor_fraction[:, 0, 0, 0]
    target = target_cell[0, 0, 0]
    nv, cx, cy, nz = cons.shape
    ng, nq, slots = corner.shape
    rows = cx * cy
    per = nz // slots
    tiles = -(-(1 + len(kinds)) // per)
    f32 = jnp.float32

    def shape(*dims):
        return jax.ShapeDtypeStruct(dims, f32)

    params = pltpu.CompilerParams(vmem_limit_bytes=(12 + nq // 2) << 20)
    alongs = [cy if axis == "gx" else cx for axis, _, _ in kinds]
    pay_shapes = [((nv + 3) * along + nq, nz) for along in alongs]
    anywhere = pl.BlockSpec(memory_space=pl.ANY)
    blended, aims, *pays = pl.pallas_call(
        functools.partial(blend_kernel, ngy, kinds),
        out_shape=[shape(ng * nq, nv, tiles * nz), shape(nq, nz)]
        + [shape(*dims) for dims in pay_shapes],
        in_specs=[anywhere] * 5,
        out_specs=[anywhere] * (2 + len(kinds)),
        scratch_shapes=[pltpu.VMEM(dims, f32) for dims in pay_shapes]
        + [
            pltpu.VMEM(cons.shape, f32),
            pltpu.VMEM(vel.shape, f32),
            pltpu.VMEM(corner.shape, jnp.int32),
            pltpu.VMEM(fraction.shape, f32),
            pltpu.VMEM(target.shape, jnp.int32),
            pltpu.VMEM((nv * rows, 3 * nz), jnp.bfloat16),
            pltpu.VMEM((nq, nz), jnp.int32),
            pltpu.VMEM((3, nq, nz), f32),
            pltpu.VMEM((nq, nz), f32),
            pltpu.VMEM((ng - 1, per, nq // per, nv, nz), f32),
            pltpu.VMEM((ng, nq, nv, tiles * nz), f32),
            pltpu.SemaphoreType.DMA((5,)),
            pltpu.SemaphoreType.DMA((1 + ng + len(kinds),)),
        ],
        compiler_params=pltpu.CompilerParams(vmem_limit_bytes=56 << 20),
        name="blend",
    )(cons, vel, corner, fraction, target)

    received = lax.all_to_all(
        blended, ("grp", "gx", "gy"), split_axis=0, concat_axis=0, tiled=True
    )
    halos = []
    for (axis, phase, _), pay in zip(kinds, pays):
        count = ngx if axis == "gx" else ngy
        pairs = []
        for low in range(phase, count - 1, 2):
            pairs += [(low, low + 1), (low + 1, low)]
        halos.append(lax.ppermute(pay, axis, pairs))

    spread = 4 if cx % 4 == 0 else 1
    coefs, base, picks = pl.pallas_call(
        functools.partial(prepare_kernel, slots, ng),
        out_shape=[
            pltpu.VMEM((7, cx, cy, nz), f32),
            pltpu.VMEM((nv, cx, cy, nz), f32),
            pltpu.VMEM(((ng - 1) * nq * slots, spread * nz), jnp.bfloat16),
        ],
        scratch_shapes=[pltpu.VMEM((rows // spread, spread * nz), f32)],
        compiler_params=params,
        name="prepare",
    )(cons, vel, aims)
    coefs, base, picks = (
        pltpu.with_memory_space_constraint(value, pltpu.VMEM) for value in (coefs, base, picks)
    )

    result = pl.pallas_call(
        functools.partial(step_kernel, kinds, slots, ng),
        out_shape=shape(nv, cx, cy, nz),
        out_specs=pl.BlockSpec(memory_space=pl.ANY),
        scratch_shapes=[
            pltpu.VMEM((7, cx, cy, nz), f32),
            pltpu.VMEM((fluid_count + 3, cx + 2, cy + 2 * top, nz), f32),
            pltpu.VMEM((nv - fluid_count, cx, cy, nz), f32),
            pltpu.VMEM(((2 * nv + 1) * (rows + sum(alongs)), nz), f32),
            pltpu.VMEM((nv, cx, cy, nz), f32),
            pltpu.SemaphoreType.DMA((nv,)),
        ],
        compiler_params=params,
        name="step",
    )(vel, aims, coefs, base, picks, received, *halos)
    return result[:, None]


def solution(mesh):
    return jax.shard_map(
        functools.partial(per_device, mesh.shape["gx"], mesh.shape["gy"]),
        mesh=mesh,
        in_specs=(
            P(None, "grp", "gx", "gy", None),
            P(None, "grp", "gx", "gy", None),
            P("grp", "gx", "gy", None, None, None),
            P(None, "grp", "gx", "gy", None, None, None),
            P("grp", "gx", "gy", None, None, None),
        ),
        out_specs=P(None, "grp", "gx", "gy", None),
        check_vma=False,
    )
```

```python
import functools

import jax
import jax.numpy as jnp
from jax import lax
from jax.experimental import pallas as pl
from jax.experimental.pallas import tpu as pltpu
from jax.sharding import PartitionSpec as P

signal_speed = 0.5
courant_number = 0.3
fluid_count = 5
block = 8


def exchanges(ngx, ngy):
    def partner(count, phase, n):
        other = n + 1 if (n + phase) % 2 == 0 else n - 1
        return other if 0 <= other < count else n

    kinds = []
    for phase in range(min(ngx - 1, 2)):
        kinds.append(("gx", phase, lambda i, j, phase=phase: (partner(ngx, phase, i), j)))
    for phase in range(min(ngy - 1, 2)):
        kinds.append(("gy", phase, lambda i, j, phase=phase: (i, partner(ngy, phase, j))))
    return kinds


def partner_above(axis, phase):
    return (lax.axis_index(axis) + phase) % 2 == 0


def split(value):
    high = value.astype(jnp.bfloat16)
    low = (value - high.astype(jnp.float32)).astype(jnp.bfloat16)
    return high, low


def over(value, n):
    return value >> (n.bit_length() - 1) if n & (n - 1) == 0 else value // n


def rest_of(value, n):
    return value & (n - 1) if n & (n - 1) == 0 else value % n


def each(count, body):
    if count == 1:
        body(0)
    else:
        lax.fori_loop(0, count, lambda n, c: (body(n), c)[1], 0)


def blend_kernel(ngy, kinds, cons, vel, corner, fraction, target, out, aims, *rest):
    pays = rest[: len(kinds)]
    at_cons, at_vel, at_corner, at_fraction, at_target, uhl, cells, parts, moved, arrive = rest[
        len(kinds) :
    ]
    nv, cx, cy, nz = cons.shape
    ng, nq, slots = corner.shape
    lanes = nz
    per = lanes // slots
    chunks = block // per
    rows = cx * cy
    me = lax.axis_index("grp")

    moves = [(corner, at_corner), (fraction, at_fraction), (target, at_target)]
    moves += [(cons, at_cons), (vel, at_vel)]
    ins = [pltpu.make_async_copy(a, b, arrive.at[n]) for n, (a, b) in enumerate(moves)]
    for copy in ins:
        copy.start()

    out[pl.ds(me * nq, nq)] = jnp.zeros((nq,) + out.shape[1:], jnp.float32)

    for copy in ins[:3]:
        copy.wait()
    aims[...] = jnp.zeros(aims.shape, jnp.float32)
    for n in range(nq // block):
        for away in range(1, ng):
            h = (me + away) % ng
            for c in range(chunks):
                at = n * block + (away - 1) * chunks + c
                for q in range(per):
                    row = n * block + c * per + q
                    cols = slice(q * slots, (q + 1) * slots)
                    cells[at : at + 1, cols] = at_corner[h, row : row + 1]
                    for d in range(3):
                        parts[d, at : at + 1, cols] = at_fraction[d, h, row : row + 1]
                    aim = at_target[h, row : row + 1] - rows * nz
                    aims[at : at + 1, cols] = aim.astype(jnp.float32)

    for copy in ins[3:]:
        copy.wait()
    for (axis, phase, _), pay in zip(kinds, pays):
        above = partner_above(axis, phase)
        along = cy if axis == "gx" else cx
        for count, source, start in ((nv, at_cons, 0), (3, at_vel, nv * along)):
            if axis == "gx":
                layer = source[:, pl.ds(jnp.where(above, cx - 1, 0), 1)]
            else:
                layer = source[:, :, pl.ds(jnp.where(above, cy - 1, 0), 1)]
            pay[start : start + count * along] = layer.reshape(count * along, nz)
        pay[(nv + 3) * along :] = aims[...]

    high, low = split(at_cons[...].reshape(nv * rows, nz))
    uhl[:, :nz] = high
    uhl[:, nz : 2 * nz] = low
    uhl[:, 2 * nz :] = high

    def weight(count, at, upper):
        place = lax.broadcasted_iota(jnp.int32, (count, lanes), 0)
        return jnp.where(place == at, 1.0 - upper, jnp.where(place == at + 1, upper, 0.0))

    def blend(n):
        here = pl.ds(n * block, block)
        cell = cells[here]
        at_x, at_y, at_z = over(cell, nz * cy), rest_of(over(cell, nz), cy), rest_of(cell, nz)
        fx, fy, fz = parts[0, here], parts[1, here], parts[2, here]

        def one(at):
            row = slice(at, at + 1)
            wx = weight(cx, at_x[row], fx[row])
            wy = weight(cy, at_y[row], fy[row])
            wxy = jnp.concatenate([wx[x : x + 1] * wy for x in range(cx)], axis=0)
            return split(weight(nz, at_z[row], fz[row])) + (wxy,)

        for away in range(1, ng):
            made = [one((away - 1) * chunks + c) for c in range(chunks)]
            wh = jnp.concatenate([m[0] for m in made], axis=1)
            wl = jnp.concatenate([m[1] for m in made], axis=1)
            wxy = jnp.concatenate([m[2] for m in made], axis=1)
            along = jnp.dot(
                uhl[...],
                jnp.concatenate([wh, wh, wl], axis=0),
                preferred_element_type=jnp.float32,
            )
            values = jnp.sum(along.reshape(nv, rows, chunks * lanes) * wxy[None], axis=1)
            for c in range(chunks):
                value = values[:, c * lanes : (c + 1) * lanes]
                for turn in range(per):
                    moved[away - 1, turn, n * chunks + c] = (
                        pltpu.roll(value, turn * slots, 1) if turn else value
                    )
            if nq == block:
                assemble(away)

    lane = lax.broadcasted_iota(jnp.int32, (nv, lanes), 1) // slots

    def assemble(away):
        for q in range(nq):
            i, j = q // ngy, q % ngy
            owners = [q] + [a * ngy + b for a, b in (of(i, j) for _, _, of in kinds)]
            for t in range(0, len(owners), per):
                tile = None
                for k, owner in enumerate(owners[t : t + per]):
                    piece = moved[away - 1, (k - owner) % per, owner // per]
                    tile = piece if tile is None else jnp.where(lane == k, piece, tile)
                cols = slice(t // per * lanes, (t // per + 1) * lanes)
                out[pl.ds((me + away) % ng * nq + q, 1), :, cols] = tile[None]

    each(nq // block, blend)
    if nq != block:
        for away in range(1, ng):
            assemble(away)


top = 8


def window(ext, v, cx, cy, move_x=0, move_y=0):
    return ext[v, 1 + move_x : 1 + move_x + cx, top + move_y : top + move_y + cy]


def along_z(value, by):
    nz = value.shape[-1]
    at = lax.broadcasted_iota(jnp.int32, (1,) + value.shape[1:], 2)
    edge = 0 if by < 0 else nz - 1
    return jnp.where(at == edge, 0.0, pltpu.roll(value, (-by) % nz, 2))


def shifted(ext, v, cx, cy, d, by):
    if d == 2 and by:
        return along_z(window(ext, v, cx, cy), by)
    return window(ext, v, cx, cy, by if d == 0 else 0, by if d == 1 else 0)


def face(low, high):
    wave_low = jnp.minimum(jnp.minimum(low, high) - signal_speed, 0.0)
    wave_high = jnp.maximum(jnp.maximum(low, high) + signal_speed, 0.0)
    scale = courant_number / (wave_high - wave_low)
    return (
        scale * wave_high * (low - wave_low),
        scale * wave_low * (wave_high - high),
    )


def prepare_kernel(slots, ng, cons, vel, aims, coefs, base, picks, marks):
    nv, cx, cy, nz = cons.shape
    lanes = nz
    per = lanes // slots
    chunks = block // per
    nq = aims.shape[0]
    spread = 4 if cx % 4 == 0 else 1
    count = cx // spread * cy
    used = (ng - 1) * chunks

    def pick(n):
        cell = aims[pl.ds(n * block, block)].astype(jnp.int32) + cx * cy * nz
        x, y, z = over(cell, nz * cy), rest_of(over(cell, nz), cy), rest_of(cell, nz)
        at_row = over(x, spread) * cy + y
        at_column = (rest_of(x, spread) * nz + z).T
        up = lax.broadcasted_iota(jnp.int32, (count, lanes), 0)
        along = lax.broadcasted_iota(jnp.int32, (lanes, spread * nz), 1)
        total = None
        for at in range(0, used, chunks):
            hits = []
            for c in range(chunks):
                hits.append(jnp.where(up == at_row[at + c : at + c + 1], 1.0, 0.0))
                to = pl.ds(pl.multiple_of((n * used + at + c) * lanes, lanes), lanes)
                chosen = at_column[:, at + c : at + c + 1] == along
                picks[to] = jnp.where(chosen, 1.0, 0.0).astype(jnp.bfloat16)
            to = pl.ds(pl.multiple_of((n * used + at) * lanes, lanes), chunks * lanes)
            term = jnp.dot(
                jnp.concatenate(hits, axis=1).astype(jnp.bfloat16),
                picks[to],
                preferred_element_type=jnp.float32,
            )
            total = term if total is None else total + term
        if nq == block:
            marks[...] = total
        else:
            marks[...] += total

    if nq != block:
        marks[...] = jnp.zeros_like(marks)
    each(nq // block, pick)
    for x in range(cx):
        rows = slice(x // spread * cy, (x // spread + 1) * cy)
        mark = marks[rows, x % spread * nz : (x % spread + 1) * nz]
        base[:, x] = jnp.where(mark[None] > 0.5, 0.0, cons[:, x])

    centre = jnp.ones((cx, cy, nz), jnp.float32)
    none = jnp.zeros((1, cy, nz), jnp.float32)
    low, high = face(vel[0, : cx - 1], vel[0, 1:])
    coefs[0] = jnp.concatenate([none, low], axis=0)
    coefs[1] = -jnp.concatenate([high, none], axis=0)
    centre += jnp.concatenate([none, high], axis=0) - jnp.concatenate([low, none], axis=0)

    at_y = lax.broadcasted_iota(jnp.int32, (1, cy, nz), 1)
    speed = vel[1]
    low, high = face(speed, pltpu.roll(speed, cy - 1, 1))
    low = jnp.where(at_y == cy - 1, 0.0, low)
    high = jnp.where(at_y == cy - 1, 0.0, high)
    coefs[2] = pltpu.roll(low, 1, 1)
    coefs[3] = -high
    centre += pltpu.roll(high, 1, 1) - low

    speed = vel[2]
    up_low, up_high = face(speed, along_z(speed, 1))
    down_low, down_high = face(along_z(speed, -1), speed)
    coefs[4] = down_low
    coefs[5] = -up_high
    coefs[6] = centre + down_high - up_low


def step_kernel(kinds, slots, ng, vel, aims, given, base, picks, received, *rest):
    halos = rest[: len(kinds)]
    out, coefs, ext, field, acc, result, sems = rest[len(kinds) :]
    nv, cx, cy, nz = base.shape
    lanes = nz
    nq = received.shape[0] // ng
    per = lanes // slots
    chunks = block // per
    used = (ng - 1) * chunks
    spread = 4 if cx % 4 == 0 else 1
    me = lax.axis_index("grp")
    lane = lax.broadcasted_iota(jnp.int32, (nv, lanes), 1) // slots
    above = [partner_above(axis, phase) for axis, phase, _ in kinds]

    parts = [(cx // spread * cy, spread)]
    parts += [(cy if axis == "gx" else cx, 1) for axis, _, _ in kinds]
    starts = [0]
    for count, groups in parts:
        starts.append(starts[-1] + (2 * nv + 1) * count * groups)

    def fill(n):
        for part, (count, groups) in enumerate(parts):
            if part == 0:
                cell = aims[pl.ds(n * block, block)]
            else:
                cell = halos[part - 1][pl.ds((nv + 3) * count + n * block, block)]
            cell = cell.astype(jnp.int32) + cx * cy * nz
            x, y, z = over(cell, nz * cy), rest_of(over(cell, nz), cy), rest_of(cell, nz)
            if part == 0:
                at_row = over(x, spread) * cy + y
            elif kinds[part - 1][0] == "gx":
                at_row = jnp.where(x == jnp.where(above[part - 1], 0, cx - 1), y, -1)
            else:
                at_row = jnp.where(y == jnp.where(above[part - 1], 0, cy - 1), x, -1)
            at_column = z.T
            up = lax.broadcasted_iota(jnp.int32, (count, lanes), 0)
            along = lax.broadcasted_iota(jnp.int32, (lanes, nz), 1)
            here = slice(part // per * lanes, (part // per + 1) * lanes)
            total = None
            for away in range(1, ng):
                g = (me + away) % ng
                lefts, chosen = [], []
                for c in range(chunks):
                    at = (away - 1) * chunks + c
                    value = None
                    for p in range(per):
                        piece = received[g * nq + n * block + c * per + p, :, here]
                        turn = (p - part) % per
                        if turn:
                            piece = pltpu.roll(piece, turn * slots, 1)
                        value = piece if value is None else jnp.where(lane == p, piece, value)
                    high = value.astype(jnp.bfloat16).astype(jnp.float32)
                    low = value - high
                    hit = up == at_row[at : at + 1]
                    pieces = [jnp.where(hit, high[v : v + 1], 0.0) for v in range(nv)]
                    pieces += [jnp.where(hit, low[v : v + 1], 0.0) for v in range(nv)]
                    if part:
                        pieces += [jnp.where(hit, 1.0, 0.0)]
                        pick = jnp.where(at_column[:, at : at + 1] == along, 1.0, 0.0)
                        chosen.append(pick.astype(jnp.bfloat16))
                    lefts.append(jnp.concatenate(pieces, axis=0).astype(jnp.bfloat16))
                if part:
                    chosen = jnp.concatenate(chosen, axis=0)
                else:
                    start = (n * used + (away - 1) * chunks) * lanes
                    chosen = picks[pl.ds(pl.multiple_of(start, lanes), chunks * lanes)]
                term = jnp.dot(
                    jnp.concatenate(lefts, axis=1), chosen, preferred_element_type=jnp.float32
                )
                total = term if total is None else total + term
            rows = total.shape[0]
            for s in range(groups):
                start = starts[part] + s * (2 * nv + 1) * count
                value = total[:, s * nz : (s + 1) * nz]
                if nq == block:
                    acc[start : start + rows] = value
                else:
                    acc[start : start + rows] += value

    if nq != block:
        acc[...] = jnp.zeros_like(acc)
    each(nq // block, fill)

    def brought(part, s):
        count = parts[part][0]
        start = starts[part] + s * (2 * nv + 1) * count
        new = acc[start : start + nv * count] + acc[start + nv * count : start + 2 * nv * count]
        return new.reshape(nv, count, nz)

    def crossed(n, speeds, fields):
        a, b = (n + 1) % 3, (n + 2) % 3
        return speeds[b] * fields[a] - speeds[a] * fields[b]

    inside = slice(top, top + cy)
    for s in range(spread):
        new = brought(0, s)
        for n, x in enumerate(range(s, cx, spread)):
            state = base[:, x] + new[:, n * cy : (n + 1) * cy]
            ext[:fluid_count, 1 + x, inside] = state[:fluid_count]
            field[:, x] = state[fluid_count:]
            for d in range(3):
                ext[fluid_count + d, 1 + x, inside] = crossed(d, vel[:, x], state[fluid_count:])

    sides = {("gx", True): 0.0, ("gx", False): 0.0, ("gy", True): 0.0, ("gy", False): 0.0}
    for n, (axis, _, _) in enumerate(kinds):
        count = parts[n + 1][0]
        d = 0 if axis == "gx" else 1
        halo = halos[n][: (nv + 3) * count].reshape(nv + 3, count, nz)
        mark = acc[starts[n + 1] + 2 * nv * count : starts[n + 1] + (2 * nv + 1) * count]
        state = jnp.where(mark[None] > 0.5, brought(n + 1, 0), halo[:nv])
        electric = [crossed(m, halo[nv:], state[fluid_count:])[None] for m in (1 - d, 2)]
        halo = jnp.concatenate([state[:fluid_count], halo[nv + d : nv + d + 1]] + electric, axis=0)
        sides[axis, True] += jnp.where(above[n], halo, 0.0)
        sides[axis, False] += jnp.where(above[n], 0.0, halo)

    coefs[...] = given[...]
    for (axis, high), halo in sides.items():
        d = 0 if axis == "gx" else 1
        halo = jnp.broadcast_to(halo, (fluid_count + 3, cx if d else cy, nz))
        if d == 0:
            at = (cx + 1 if high else 0, inside)
            edge = (cx - 1 if high else 0,)
        else:
            at = (slice(1, cx + 1), top + cy if high else top - 1)
            edge = (slice(None), cy - 1 if high else 0)
        ext[(slice(0, fluid_count),) + at] = halo[:fluid_count]
        ext[(fluid_count + 1 - d,) + at] = halo[fluid_count + 1]
        ext[(fluid_count + 2,) + at] = halo[fluid_count + 2]
        speed = vel[(d,) + edge]
        if high:
            of_low, of_high = face(speed, halo[fluid_count])
            coefs[(2 * d + 1,) + edge] = -of_high
            coefs[(6,) + edge] -= of_low
        else:
            of_low, of_high = face(halo[fluid_count], speed)
            coefs[(2 * d,) + edge] = of_low
            coefs[(6,) + edge] += of_high

    copies = []

    def finish(v, value):
        result[v] = value
        copies.append(pltpu.make_async_copy(result.at[v], out.at[v], sems.at[v]))
        copies[-1].start()

    def central(n, d):
        v = fluid_count + n
        return shifted(ext, v, cx, cy, d, 1) - shifted(ext, v, cx, cy, d, -1)

    for n in range(3):
        a, b = (n + 1) % 3, (n + 2) % 3
        curl = central(b, a) - central(a, b)
        finish(fluid_count + n, field[n] - (0.5 * courant_number) * curl)
    for v in range(fluid_count):
        total = coefs[6] * window(ext, v, cx, cy)
        for d in range(3):
            total = total + coefs[2 * d] * shifted(ext, v, cx, cy, d, -1)
            total = total + coefs[2 * d + 1] * shifted(ext, v, cx, cy, d, 1)
        finish(v, total)
    for copy in copies:
        copy.wait()


def per_device(ngx, ngy, conserved, velocity, donor_corner, donor_fraction, target_cell):
    kinds = exchanges(ngx, ngy)
    cons = conserved[:, 0]
    vel = velocity[:, 0]
    corner = donor_corner[0, 0, 0]
    fraction = donor_fraction[:, 0, 0, 0]
    target = target_cell[0, 0, 0]
    nv, cx, cy, nz = cons.shape
    ng, nq, slots = corner.shape
    rows = cx * cy
    per = nz // slots
    tiles = -(-(1 + len(kinds)) // per)
    f32 = jnp.float32

    def shape(*dims):
        return jax.ShapeDtypeStruct(dims, f32)

    params = pltpu.CompilerParams(vmem_limit_bytes=(12 + nq // 2) << 20)
    alongs = [cy if axis == "gx" else cx for axis, _, _ in kinds]
    pay_shapes = [((nv + 3) * along + nq, nz) for along in alongs]
    arguments = [
        pltpu.with_memory_space_constraint(value, pltpu.HBM)
        for value in (cons, vel, corner, fraction, target)
    ]
    blended, aims, *pays = pl.pallas_call(
        functools.partial(blend_kernel, ngy, kinds),
        out_shape=[pltpu.VMEM((ng * nq, nv, tiles * nz), f32), pltpu.VMEM((nq, nz), f32)]
        + [pltpu.VMEM(dims, f32) for dims in pay_shapes],
        in_specs=[pl.BlockSpec(memory_space=pl.ANY)] * 5,
        scratch_shapes=[
            pltpu.VMEM(cons.shape, f32),
            pltpu.VMEM(vel.shape, f32),
            pltpu.VMEM(corner.shape, jnp.int32),
            pltpu.VMEM(fraction.shape, f32),
            pltpu.VMEM(target.shape, jnp.int32),
            pltpu.VMEM((nv * rows, 3 * nz), jnp.bfloat16),
            pltpu.VMEM((nq, nz), jnp.int32),
            pltpu.VMEM((3, nq, nz), f32),
            pltpu.VMEM((ng - 1, per, nq // per, nv, nz), f32),
            pltpu.SemaphoreType.DMA((5,)),
        ],
        compiler_params=params,
        name="blend",
    )(*arguments)

    received = lax.all_to_all(
        blended, ("grp", "gx", "gy"), split_axis=0, concat_axis=0, tiled=True
    )
    halos = []
    for (axis, phase, _), pay in zip(kinds, pays):
        count = ngx if axis == "gx" else ngy
        pairs = []
        for low in range(phase, count - 1, 2):
            pairs += [(low, low + 1), (low + 1, low)]
        halos.append(lax.ppermute(pay, axis, pairs))

    spread = 4 if cx % 4 == 0 else 1
    coefs, base, picks = pl.pallas_call(
        functools.partial(prepare_kernel, slots, ng),
        out_shape=[
            pltpu.VMEM((7, cx, cy, nz), f32),
            pltpu.VMEM((nv, cx, cy, nz), f32),
            pltpu.VMEM(((ng - 1) * nq * slots, spread * nz), jnp.bfloat16),
        ],
        scratch_shapes=[pltpu.VMEM((rows // spread, spread * nz), f32)],
        compiler_params=params,
        name="prepare",
    )(cons, vel, aims)
    coefs, base, picks = (
        pltpu.with_memory_space_constraint(value, pltpu.VMEM) for value in (coefs, base, picks)
    )

    result = pl.pallas_call(
        functools.partial(step_kernel, kinds, slots, ng),
        out_shape=shape(nv, cx, cy, nz),
        out_specs=pl.BlockSpec(memory_space=pl.ANY),
        scratch_shapes=[
            pltpu.VMEM((7, cx, cy, nz), f32),
            pltpu.VMEM((fluid_count + 3, cx + 2, cy + 2 * top, nz), f32),
            pltpu.VMEM((nv - fluid_count, cx, cy, nz), f32),
            pltpu.VMEM(((2 * nv + 1) * (rows + sum(alongs)), nz), f32),
            pltpu.VMEM((nv, cx, cy, nz), f32),
            pltpu.SemaphoreType.DMA((nv,)),
        ],
        compiler_params=params,
        name="step",
    )(vel, aims, coefs, base, picks, received, *halos)
    return result[:, None]


def solution(mesh):
    return jax.shard_map(
        functools.partial(per_device, mesh.shape["gx"], mesh.shape["gy"]),
        mesh=mesh,
        in_specs=(
            P(None, "grp", "gx", "gy", None),
            P(None, "grp", "gx", "gy", None),
            P("grp", "gx", "gy", None, None, None),
            P(None, "grp", "gx", "gy", None, None, None),
            P("grp", "gx", "gy", None, None, None),
        ),
        out_specs=P(None, "grp", "gx", "gy", None),
        check_vma=False,
    )
```

```python
import functools

import jax
import jax.numpy as jnp
from jax import lax
from jax.experimental import pallas as pl
from jax.experimental.pallas import tpu as pltpu
from jax.sharding import PartitionSpec as P

signal_speed = 0.5
courant_number = 0.3
fluid_count = 5
block = 8


def exchanges(ngx, ngy):
    def partner(count, phase, n):
        other = n + 1 if (n + phase) % 2 == 0 else n - 1
        return other if 0 <= other < count else n

    kinds = []
    for phase in range(min(ngx - 1, 2)):
        kinds.append(("gx", phase, lambda i, j, phase=phase: (partner(ngx, phase, i), j)))
    for phase in range(min(ngy - 1, 2)):
        kinds.append(("gy", phase, lambda i, j, phase=phase: (i, partner(ngy, phase, j))))
    return kinds


def partner_above(axis, phase):
    return (lax.axis_index(axis) + phase) % 2 == 0


def split(value):
    high = value.astype(jnp.bfloat16)
    low = (value - high.astype(jnp.float32)).astype(jnp.bfloat16)
    return high, low


def over(value, n):
    return value >> (n.bit_length() - 1) if n & (n - 1) == 0 else value // n


def rest_of(value, n):
    return value & (n - 1) if n & (n - 1) == 0 else value % n


def each(count, body):
    if count == 1:
        body(0)
    else:
        lax.fori_loop(0, count, lambda n, c: (body(n), c)[1], 0)


def block_transpose(value, slots):
    rows, lanes = value.shape
    count = lanes // slots
    each_rows = rows // count
    at_row = lax.broadcasted_iota(jnp.int32, value.shape, 0) // each_rows
    at_lane = lax.broadcasted_iota(jnp.int32, value.shape, 1) // slots
    result = value
    for d in range(1, count):
        turned = pltpu.roll(value, d * each_rows, 0)
        turned = pltpu.roll(turned, lanes - d * slots, 1)
        result = jnp.where((at_row - at_lane) % count == d, turned, result)
    return result


def packed(tiles, slots):
    empty = jnp.zeros(tiles[0].shape, tiles[0].dtype)
    return block_transpose(jnp.concatenate(tiles + [empty], axis=1), slots)


def blend_kernel(ngy, kinds, cons, corner, fraction, out, *scratch):
    at_cons, at_corner, at_fraction, uhl, wzs, wxys, moved, arrive = scratch
    nv, cx, cy, nz = cons.shape
    ng, nq, slots = corner.shape
    lanes = nz
    per = lanes // slots
    chunks = block // per
    rows = cx * cy
    me = lax.axis_index("grp")

    moves = [(corner, at_corner), (fraction, at_fraction), (cons, at_cons)]
    ins = [pltpu.make_async_copy(a, b, arrive.at[n]) for n, (a, b) in enumerate(moves)]
    for copy in ins:
        copy.start()

    out[pl.ds(me * nq, nq)] = jnp.zeros((nq,) + out.shape[1:], jnp.float32)

    def weight(count, at, upper):
        place = lax.broadcasted_iota(jnp.int32, (count, lanes), 0)
        return jnp.where(place == at, 1.0 - upper, jnp.where(place == at + 1, upper, 0.0))

    def weigh(n):
        here = pl.ds(n * block, block)
        grids = [(me + away) % ng for away in range(1, ng)]
        cell = packed([at_corner[h, here] for h in grids], slots)
        at_x, at_y, at_z = over(cell, nz * cy), rest_of(over(cell, nz), cy), rest_of(cell, nz)
        fx, fy, fz = (packed([at_fraction[d, h, here] for h in grids], slots) for d in range(3))
        for away in range(1, ng):
            for c in range(chunks):
                row = slice((away - 1) * chunks + c, (away - 1) * chunks + c + 1)
                cols = slice(c * lanes, (c + 1) * lanes)
                wx = weight(cx, at_x[row], fx[row])
                wy = weight(cy, at_y[row], fy[row])
                for x in range(cx):
                    wxys[away - 1, x * cy : (x + 1) * cy, cols] = wx[x : x + 1] * wy
                high, low = split(weight(nz, at_z[row], fz[row]))
                wzs[away - 1, :nz, cols] = high
                wzs[away - 1, nz : 2 * nz, cols] = high
                wzs[away - 1, 2 * nz :, cols] = low

    def blend(n):
        for away in range(1, ng):
            along = jnp.dot(uhl[...], wzs[away - 1], preferred_element_type=jnp.float32)
            along = along.reshape(nv, rows, chunks * lanes)
            values = jnp.sum(along * wxys[away - 1][None], axis=1)
            for c in range(chunks):
                value = values[:, c * lanes : (c + 1) * lanes]
                for turn in range(per):
                    moved[away - 1, turn, n * chunks + c] = (
                        pltpu.roll(value, turn * slots, 1) if turn else value
                    )
            if nq == block:
                assemble(away)

    lane = lax.broadcasted_iota(jnp.int32, (nv, lanes), 1) // slots

    def assemble(away):
        for q in range(nq):
            i, j = q // ngy, q % ngy
            owners = [q] + [a * ngy + b for a, b in (of(i, j) for _, _, of in kinds)]
            for t in range(0, len(owners), per):
                tile = None
                for k, owner in enumerate(owners[t : t + per]):
                    chunk = owner // block * chunks + owner % chunks
                    piece = moved[away - 1, (k - owner % block // chunks) % per, chunk]
                    tile = piece if tile is None else jnp.where(lane == k, piece, tile)
                cols = slice(t // per * lanes, (t // per + 1) * lanes)
                out[pl.ds((me + away) % ng * nq + q, 1), :, cols] = tile[None]

    for copy in ins[:2]:
        copy.wait()
    if nq == block:
        weigh(0)
    ins[2].wait()
    high, low = split(at_cons[...].reshape(nv * rows, nz))
    uhl[:, :nz] = high
    uhl[:, nz : 2 * nz] = low
    uhl[:, 2 * nz :] = high
    if nq == block:
        blend(0)
    else:

        def both(n):
            weigh(n)
            blend(n)

        each(nq // block, both)
        for away in range(1, ng):
            assemble(away)


def edge_kernel(kinds, cons, vel, target, sent, aims, *pays):
    del sent
    nv, cx, cy, nz = cons.shape
    ng, nq, slots = target.shape
    me = lax.axis_index("grp")
    for n in range(nq // block):
        here = slice(n * block, (n + 1) * block)
        tiles = [target[(me + away) % ng, here] - cx * cy * nz for away in range(1, ng)]
        aims[here] = packed(tiles, slots).astype(jnp.float32)
    for (axis, phase, _), pay in zip(kinds, pays):
        above = partner_above(axis, phase)
        along = cy if axis == "gx" else cx
        for count, source, start in ((nv, cons, 0), (3, vel, nv * along)):
            if axis == "gx":
                layer = source[:, pl.ds(jnp.where(above, cx - 1, 0), 1)]
            else:
                layer = source[:, :, pl.ds(jnp.where(above, cy - 1, 0), 1)]
            pay[start : start + count * along] = layer.reshape(count * along, nz)
        pay[(nv + 3) * along :] = aims[...]


top = 8


def window(ext, v, cx, cy, move_x=0, move_y=0):
    return ext[v, 1 + move_x : 1 + move_x + cx, top + move_y : top + move_y + cy]


def along_z(value, by):
    nz = value.shape[-1]
    at = lax.broadcasted_iota(jnp.int32, (1,) + value.shape[1:], 2)
    edge = 0 if by < 0 else nz - 1
    return jnp.where(at == edge, 0.0, pltpu.roll(value, (-by) % nz, 2))


def shifted(ext, v, cx, cy, d, by):
    if d == 2 and by:
        return along_z(window(ext, v, cx, cy), by)
    return window(ext, v, cx, cy, by if d == 0 else 0, by if d == 1 else 0)


def face(low, high):
    wave_low = jnp.minimum(jnp.minimum(low, high) - signal_speed, 0.0)
    wave_high = jnp.maximum(jnp.maximum(low, high) + signal_speed, 0.0)
    scale = courant_number / (wave_high - wave_low)
    return (
        scale * wave_high * (low - wave_low),
        scale * wave_low * (wave_high - high),
    )


def prepare_kernel(slots, ng, cons, vel, aims, coefs, base, picks, marks):
    nv, cx, cy, nz = cons.shape
    lanes = nz
    per = lanes // slots
    chunks = block // per
    nq = aims.shape[0]
    spread = 4 if cx % 4 == 0 else 1
    count = cx // spread * cy
    used = (ng - 1) * chunks

    def pick(n):
        cell = aims[pl.ds(n * block, block)].astype(jnp.int32) + cx * cy * nz
        x, y, z = over(cell, nz * cy), rest_of(over(cell, nz), cy), rest_of(cell, nz)
        at_row = over(x, spread) * cy + y
        at_column = (rest_of(x, spread) * nz + z).T
        up = lax.broadcasted_iota(jnp.int32, (count, lanes), 0)
        along = lax.broadcasted_iota(jnp.int32, (lanes, spread * nz), 1)
        total = None
        for at in range(0, used, chunks):
            hits = []
            for c in range(chunks):
                hits.append(jnp.where(up == at_row[at + c : at + c + 1], 1.0, 0.0))
                to = pl.ds(pl.multiple_of((n * used + at + c) * lanes, lanes), lanes)
                chosen = at_column[:, at + c : at + c + 1] == along
                picks[to] = jnp.where(chosen, 1.0, 0.0).astype(jnp.bfloat16)
            to = pl.ds(pl.multiple_of((n * used + at) * lanes, lanes), chunks * lanes)
            term = jnp.dot(
                jnp.concatenate(hits, axis=1).astype(jnp.bfloat16),
                picks[to],
                preferred_element_type=jnp.float32,
            )
            total = term if total is None else total + term
        if nq == block:
            marks[...] = total
        else:
            marks[...] += total

    if nq != block:
        marks[...] = jnp.zeros_like(marks)
    each(nq // block, pick)
    for x in range(cx):
        rows = slice(x // spread * cy, (x // spread + 1) * cy)
        mark = marks[rows, x % spread * nz : (x % spread + 1) * nz]
        base[:, x] = jnp.where(mark[None] > 0.5, 0.0, cons[:, x])

    centre = jnp.ones((cx, cy, nz), jnp.float32)
    none = jnp.zeros((1, cy, nz), jnp.float32)
    low, high = face(vel[0, : cx - 1], vel[0, 1:])
    coefs[0] = jnp.concatenate([none, low], axis=0)
    coefs[1] = -jnp.concatenate([high, none], axis=0)
    centre += jnp.concatenate([none, high], axis=0) - jnp.concatenate([low, none], axis=0)

    at_y = lax.broadcasted_iota(jnp.int32, (1, cy, nz), 1)
    speed = vel[1]
    low, high = face(speed, pltpu.roll(speed, cy - 1, 1))
    low = jnp.where(at_y == cy - 1, 0.0, low)
    high = jnp.where(at_y == cy - 1, 0.0, high)
    coefs[2] = pltpu.roll(low, 1, 1)
    coefs[3] = -high
    centre += pltpu.roll(high, 1, 1) - low

    speed = vel[2]
    up_low, up_high = face(speed, along_z(speed, 1))
    down_low, down_high = face(along_z(speed, -1), speed)
    coefs[4] = down_low
    coefs[5] = -up_high
    coefs[6] = centre + down_high - up_low


def step_kernel(kinds, slots, ng, vel, aims, given, base, picks, received, *rest):
    halos = rest[: len(kinds)]
    out, coefs, ext, field, acc, result, sems = rest[len(kinds) :]
    nv, cx, cy, nz = base.shape
    lanes = nz
    nq = received.shape[0] // ng
    per = lanes // slots
    chunks = block // per
    used = (ng - 1) * chunks
    spread = 4 if cx % 4 == 0 else 1
    me = lax.axis_index("grp")
    lane = lax.broadcasted_iota(jnp.int32, (nv, lanes), 1) // slots
    above = [partner_above(axis, phase) for axis, phase, _ in kinds]

    parts = [(cx // spread * cy, spread)]
    parts += [(cy if axis == "gx" else cx, 1) for axis, _, _ in kinds]
    starts = [0]
    for count, groups in parts:
        starts.append(starts[-1] + (2 * nv + 1) * count * groups)

    def fill(n):
        for part, (count, groups) in enumerate(parts):
            if part == 0:
                cell = aims[pl.ds(n * block, block)]
            else:
                cell = halos[part - 1][pl.ds((nv + 3) * count + n * block, block)]
            cell = cell.astype(jnp.int32) + cx * cy * nz
            x, y, z = over(cell, nz * cy), rest_of(over(cell, nz), cy), rest_of(cell, nz)
            if part == 0:
                at_row = over(x, spread) * cy + y
            elif kinds[part - 1][0] == "gx":
                at_row = jnp.where(x == jnp.where(above[part - 1], 0, cx - 1), y, -1)
            else:
                at_row = jnp.where(y == jnp.where(above[part - 1], 0, cy - 1), x, -1)
            at_column = z.T
            up = lax.broadcasted_iota(jnp.int32, (count, lanes), 0)
            along = lax.broadcasted_iota(jnp.int32, (lanes, nz), 1)
            here = slice(part // per * lanes, (part // per + 1) * lanes)
            total = None
            for away in range(1, ng):
                g = (me + away) % ng
                lefts, chosen = [], []
                for c in range(chunks):
                    at = (away - 1) * chunks + c
                    value = None
                    for p in range(per):
                        piece = received[g * nq + n * block + p * chunks + c, :, here]
                        turn = (p - part) % per
                        if turn:
                            piece = pltpu.roll(piece, turn * slots, 1)
                        value = piece if value is None else jnp.where(lane == p, piece, value)
                    high = value.astype(jnp.bfloat16).astype(jnp.float32)
                    low = value - high
                    hit = up == at_row[at : at + 1]
                    pieces = [jnp.where(hit, high[v : v + 1], 0.0) for v in range(nv)]
                    pieces += [jnp.where(hit, low[v : v + 1], 0.0) for v in range(nv)]
                    if part:
                        pieces += [jnp.where(hit, 1.0, 0.0)]
                        pick = jnp.where(at_column[:, at : at + 1] == along, 1.0, 0.0)
                        chosen.append(pick.astype(jnp.bfloat16))
                    lefts.append(jnp.concatenate(pieces, axis=0).astype(jnp.bfloat16))
                if part:
                    chosen = jnp.concatenate(chosen, axis=0)
                else:
                    start = (n * used + (away - 1) * chunks) * lanes
                    chosen = picks[pl.ds(pl.multiple_of(start, lanes), chunks * lanes)]
                term = jnp.dot(
                    jnp.concatenate(lefts, axis=1), chosen, preferred_element_type=jnp.float32
                )
                total = term if total is None else total + term
            rows = total.shape[0]
            for s in range(groups):
                start = starts[part] + s * (2 * nv + 1) * count
                value = total[:, s * nz : (s + 1) * nz]
                if nq == block:
                    acc[start : start + rows] = value
                else:
                    acc[start : start + rows] += value

    if nq != block:
        acc[...] = jnp.zeros_like(acc)
    each(nq // block, fill)

    def brought(part, s):
        count = parts[part][0]
        start = starts[part] + s * (2 * nv + 1) * count
        new = acc[start : start + nv * count] + acc[start + nv * count : start + 2 * nv * count]
        return new.reshape(nv, count, nz)

    def crossed(n, speeds, fields):
        a, b = (n + 1) % 3, (n + 2) % 3
        return speeds[b] * fields[a] - speeds[a] * fields[b]

    inside = slice(top, top + cy)
    for s in range(spread):
        new = brought(0, s)
        for n, x in enumerate(range(s, cx, spread)):
            state = base[:, x] + new[:, n * cy : (n + 1) * cy]
            ext[:fluid_count, 1 + x, inside] = state[:fluid_count]
            field[:, x] = state[fluid_count:]
            for d in range(3):
                ext[fluid_count + d, 1 + x, inside] = crossed(d, vel[:, x], state[fluid_count:])

    sides = {("gx", True): 0.0, ("gx", False): 0.0, ("gy", True): 0.0, ("gy", False): 0.0}
    for n, (axis, _, _) in enumerate(kinds):
        count = parts[n + 1][0]
        d = 0 if axis == "gx" else 1
        halo = halos[n][: (nv + 3) * count].reshape(nv + 3, count, nz)
        mark = acc[starts[n + 1] + 2 * nv * count : starts[n + 1] + (2 * nv + 1) * count]
        state = jnp.where(mark[None] > 0.5, brought(n + 1, 0), halo[:nv])
        electric = [crossed(m, halo[nv:], state[fluid_count:])[None] for m in (1 - d, 2)]
        halo = jnp.concatenate([state[:fluid_count], halo[nv + d : nv + d + 1]] + electric, axis=0)
        sides[axis, True] += jnp.where(above[n], halo, 0.0)
        sides[axis, False] += jnp.where(above[n], 0.0, halo)

    coefs[...] = given[...]
    for (axis, high), halo in sides.items():
        d = 0 if axis == "gx" else 1
        halo = jnp.broadcast_to(halo, (fluid_count + 3, cx if d else cy, nz))
        if d == 0:
            at = (cx + 1 if high else 0, inside)
            edge = (cx - 1 if high else 0,)
        else:
            at = (slice(1, cx + 1), top + cy if high else top - 1)
            edge = (slice(None), cy - 1 if high else 0)
        ext[(slice(0, fluid_count),) + at] = halo[:fluid_count]
        ext[(fluid_count + 1 - d,) + at] = halo[fluid_count + 1]
        ext[(fluid_count + 2,) + at] = halo[fluid_count + 2]
        speed = vel[(d,) + edge]
        if high:
            of_low, of_high = face(speed, halo[fluid_count])
            coefs[(2 * d + 1,) + edge] = -of_high
            coefs[(6,) + edge] -= of_low
        else:
            of_low, of_high = face(halo[fluid_count], speed)
            coefs[(2 * d,) + edge] = of_low
            coefs[(6,) + edge] += of_high

    copies = []

    def finish(v, value):
        result[v] = value
        copies.append(pltpu.make_async_copy(result.at[v], out.at[v], sems.at[v]))
        copies[-1].start()

    def central(n, d):
        v = fluid_count + n
        return shifted(ext, v, cx, cy, d, 1) - shifted(ext, v, cx, cy, d, -1)

    for n in range(3):
        a, b = (n + 1) % 3, (n + 2) % 3
        curl = central(b, a) - central(a, b)
        finish(fluid_count + n, field[n] - (0.5 * courant_number) * curl)
    for v in range(fluid_count):
        total = coefs[6] * window(ext, v, cx, cy)
        for d in range(3):
            total = total + coefs[2 * d] * shifted(ext, v, cx, cy, d, -1)
            total = total + coefs[2 * d + 1] * shifted(ext, v, cx, cy, d, 1)
        finish(v, total)
    for copy in copies:
        copy.wait()


def per_device(ngx, ngy, conserved, velocity, donor_corner, donor_fraction, target_cell):
    kinds = exchanges(ngx, ngy)
    cons = conserved[:, 0]
    vel = velocity[:, 0]
    corner = donor_corner[0, 0, 0]
    fraction = donor_fraction[:, 0, 0, 0]
    target = target_cell[0, 0, 0]
    nv, cx, cy, nz = cons.shape
    ng, nq, slots = corner.shape
    rows = cx * cy
    per = nz // slots
    tiles = -(-(1 + len(kinds)) // per)
    f32 = jnp.float32

    def shape(*dims):
        return jax.ShapeDtypeStruct(dims, f32)

    params = pltpu.CompilerParams(vmem_limit_bytes=(12 + nq // 2) << 20)
    alongs = [cy if axis == "gx" else cx for axis, _, _ in kinds]
    pay_shapes = [((nv + 3) * along + nq, nz) for along in alongs]
    blended = pl.pallas_call(
        functools.partial(blend_kernel, ngy, kinds),
        out_shape=pltpu.VMEM((ng * nq, nv, tiles * nz), f32),
        in_specs=[pl.BlockSpec(memory_space=pl.ANY)] * 3,
        scratch_shapes=[
            pltpu.VMEM(cons.shape, f32),
            pltpu.VMEM(corner.shape, jnp.int32),
            pltpu.VMEM(fraction.shape, f32),
            pltpu.VMEM((nv * rows, 3 * nz), jnp.bfloat16),
            pltpu.VMEM((ng - 1, 3 * nz, block * slots), jnp.bfloat16),
            pltpu.VMEM((ng - 1, rows, block * slots), f32),
            pltpu.VMEM((ng - 1, per, nq // per, nv, nz), f32),
            pltpu.SemaphoreType.DMA((3,)),
        ],
        compiler_params=params,
        name="blend",
    )(*(pltpu.with_memory_space_constraint(value, pltpu.HBM) for value in (cons, corner, fraction)))

    aims, *pays = pl.pallas_call(
        functools.partial(edge_kernel, kinds),
        out_shape=[pltpu.VMEM((nq, nz), f32)] + [pltpu.VMEM(dims, f32) for dims in pay_shapes],
        in_specs=[pl.BlockSpec(memory_space=pltpu.VMEM)] * 3 + [pl.BlockSpec(memory_space=pl.ANY)],
        compiler_params=params,
        name="edge",
    )(cons, vel, target, blended)

    received = lax.all_to_all(
        blended, ("grp", "gx", "gy"), split_axis=0, concat_axis=0, tiled=True
    )
    halos = []
    for (axis, phase, _), pay in zip(kinds, pays):
        count = ngx if axis == "gx" else ngy
        pairs = []
        for low in range(phase, count - 1, 2):
            pairs += [(low, low + 1), (low + 1, low)]
        halos.append(lax.ppermute(pay, axis, pairs))

    spread = 4 if cx % 4 == 0 else 1
    coefs, base, picks = pl.pallas_call(
        functools.partial(prepare_kernel, slots, ng),
        out_shape=[
            pltpu.VMEM((7, cx, cy, nz), f32),
            pltpu.VMEM((nv, cx, cy, nz), f32),
            pltpu.VMEM(((ng - 1) * nq * slots, spread * nz), jnp.bfloat16),
        ],
        scratch_shapes=[pltpu.VMEM((rows // spread, spread * nz), f32)],
        compiler_params=params,
        name="prepare",
    )(cons, vel, aims)
    coefs, base, picks = (
        pltpu.with_memory_space_constraint(value, pltpu.VMEM) for value in (coefs, base, picks)
    )

    result = pl.pallas_call(
        functools.partial(step_kernel, kinds, slots, ng),
        out_shape=shape(nv, cx, cy, nz),
        out_specs=pl.BlockSpec(memory_space=pl.ANY),
        scratch_shapes=[
            pltpu.VMEM((7, cx, cy, nz), f32),
            pltpu.VMEM((fluid_count + 3, cx + 2, cy + 2 * top, nz), f32),
            pltpu.VMEM((nv - fluid_count, cx, cy, nz), f32),
            pltpu.VMEM(((2 * nv + 1) * (rows + sum(alongs)), nz), f32),
            pltpu.VMEM((nv, cx, cy, nz), f32),
            pltpu.SemaphoreType.DMA((nv,)),
        ],
        compiler_params=params,
        name="step",
    )(vel, aims, coefs, base, picks, received, *halos)
    return result[:, None]


def solution(mesh):
    return jax.shard_map(
        functools.partial(per_device, mesh.shape["gx"], mesh.shape["gy"]),
        mesh=mesh,
        in_specs=(
            P(None, "grp", "gx", "gy", None),
            P(None, "grp", "gx", "gy", None),
            P("grp", "gx", "gy", None, None, None),
            P(None, "grp", "gx", "gy", None, None, None),
            P("grp", "gx", "gy", None, None, None),
        ),
        out_specs=P(None, "grp", "gx", "gy", None),
        check_vma=False,
    )
```

```python
import functools

import jax
import jax.numpy as jnp
from jax import lax
from jax.experimental import pallas as pl
from jax.experimental.pallas import tpu as pltpu
from jax.sharding import PartitionSpec as P

signal_speed = 0.5
courant_number = 0.3
fluid_count = 5
block = 8


def exchanges(ngx, ngy):
    def partner(count, phase, n):
        other = n + 1 if (n + phase) % 2 == 0 else n - 1
        return other if 0 <= other < count else n

    kinds = []
    for phase in range(min(ngx - 1, 2)):
        kinds.append(("gx", phase, lambda i, j, phase=phase: (partner(ngx, phase, i), j)))
    for phase in range(min(ngy - 1, 2)):
        kinds.append(("gy", phase, lambda i, j, phase=phase: (i, partner(ngy, phase, j))))
    return kinds


def partner_above(axis, phase):
    return (lax.axis_index(axis) + phase) % 2 == 0


def split(value):
    high = value.astype(jnp.bfloat16)
    low = (value - high.astype(jnp.float32)).astype(jnp.bfloat16)
    return high, low


def over(value, n):
    return value >> (n.bit_length() - 1) if n & (n - 1) == 0 else value // n


def rest_of(value, n):
    return value & (n - 1) if n & (n - 1) == 0 else value % n


def each(count, body):
    if count == 1:
        body(0)
    else:
        lax.fori_loop(0, count, lambda n, c: (body(n), c)[1], 0)


def block_transpose(value, slots):
    rows, lanes = value.shape
    count = lanes // slots
    each_rows = rows // count
    at_row = lax.broadcasted_iota(jnp.int32, value.shape, 0) // each_rows
    at_lane = lax.broadcasted_iota(jnp.int32, value.shape, 1) // slots
    result = value
    for d in range(1, count):
        turned = pltpu.roll(value, d * each_rows, 0)
        turned = pltpu.roll(turned, lanes - d * slots, 1)
        result = jnp.where((at_row - at_lane) % count == d, turned, result)
    return result


def packed(tiles, slots):
    empty = jnp.zeros(tiles[0].shape, tiles[0].dtype)
    return block_transpose(jnp.concatenate(tiles + [empty], axis=1), slots)


def blend_kernel(ngy, kinds, cons, corner, fraction, out, at_cons, *scratch):
    at_corner, at_fraction, uhl, wzs, wxys, moved, arrive = scratch
    nv, cx, cy, nz = cons.shape
    ng, nq, slots = corner.shape
    lanes = nz
    per = lanes // slots
    chunks = block // per
    rows = cx * cy
    me = lax.axis_index("grp")

    moves = [(corner, at_corner), (fraction, at_fraction)]
    moves += [(cons.at[v], at_cons.at[v]) for v in range(nv)]
    ins = [pltpu.make_async_copy(a, b, arrive.at[n]) for n, (a, b) in enumerate(moves)]
    for copy in ins:
        copy.start()

    out[pl.ds(me * nq, nq)] = jnp.zeros((nq,) + out.shape[1:], jnp.float32)

    def weight(count, at, upper):
        place = lax.broadcasted_iota(jnp.int32, (count, lanes), 0)
        return jnp.where(place == at, 1.0 - upper, jnp.where(place == at + 1, upper, 0.0))

    def weigh(n):
        here = pl.ds(n * block, block)
        grids = [(me + away) % ng for away in range(1, ng)]
        cell = packed([at_corner[h, here] for h in grids], slots)
        at_x, at_y, at_z = over(cell, nz * cy), rest_of(over(cell, nz), cy), rest_of(cell, nz)
        fx, fy, fz = (packed([at_fraction[d, h, here] for h in grids], slots) for d in range(3))
        for away in range(1, ng):
            for c in range(chunks):
                row = slice((away - 1) * chunks + c, (away - 1) * chunks + c + 1)
                cols = slice(c * lanes, (c + 1) * lanes)
                wx = weight(cx, at_x[row], fx[row])
                wy = weight(cy, at_y[row], fy[row])
                for x in range(cx):
                    wxys[away - 1, x * cy : (x + 1) * cy, cols] = wx[x : x + 1] * wy
                high, low = split(weight(nz, at_z[row], fz[row]))
                wzs[away - 1, :nz, cols] = high
                wzs[away - 1, nz : 2 * nz, cols] = high
                wzs[away - 1, 2 * nz :, cols] = low

    def blend(n):
        for away in range(1, ng):
            along = jnp.dot(uhl[...], wzs[away - 1], preferred_element_type=jnp.float32)
            along = along.reshape(nv, rows, chunks * lanes)
            values = jnp.sum(along * wxys[away - 1][None], axis=1)
            for c in range(chunks):
                value = values[:, c * lanes : (c + 1) * lanes]
                for turn in range(per):
                    moved[away - 1, turn, n * chunks + c] = (
                        pltpu.roll(value, turn * slots, 1) if turn else value
                    )
            if nq == block:
                assemble(away)

    lane = lax.broadcasted_iota(jnp.int32, (nv, lanes), 1) // slots

    def assemble(away):
        for q in range(nq):
            i, j = q // ngy, q % ngy
            owners = [q] + [a * ngy + b for a, b in (of(i, j) for _, _, of in kinds)]
            for t in range(0, len(owners), per):
                tile = None
                for k, owner in enumerate(owners[t : t + per]):
                    chunk = owner // block * chunks + owner % chunks
                    piece = moved[away - 1, (k - owner % block // chunks) % per, chunk]
                    tile = piece if tile is None else jnp.where(lane == k, piece, tile)
                cols = slice(t // per * lanes, (t // per + 1) * lanes)
                out[pl.ds((me + away) % ng * nq + q, 1), :, cols] = tile[None]

    for copy in ins[:2]:
        copy.wait()
    if nq == block:
        weigh(0)
    for v in range(nv):
        ins[2 + v].wait()
        high, low = split(at_cons[v].reshape(rows, nz))
        here = slice(v * rows, (v + 1) * rows)
        uhl[here, :nz] = high
        uhl[here, nz : 2 * nz] = low
        uhl[here, 2 * nz :] = high
    if nq == block:
        blend(0)
    else:

        def both(n):
            weigh(n)
            blend(n)

        each(nq // block, both)
        for away in range(1, ng):
            assemble(away)


def edge_kernel(kinds, cons, vel, target, sent, aims, *pays):
    del sent
    nv, cx, cy, nz = cons.shape
    ng, nq, slots = target.shape
    me = lax.axis_index("grp")
    for n in range(nq // block):
        here = slice(n * block, (n + 1) * block)
        tiles = [target[(me + away) % ng, here] - cx * cy * nz for away in range(1, ng)]
        aims[here] = packed(tiles, slots).astype(jnp.float32)
    for (axis, phase, _), pay in zip(kinds, pays):
        above = partner_above(axis, phase)
        along = cy if axis == "gx" else cx
        for count, source, start in ((nv, cons, 0), (3, vel, nv * along)):
            if axis == "gx":
                layer = source[:, pl.ds(jnp.where(above, cx - 1, 0), 1)]
            else:
                layer = source[:, :, pl.ds(jnp.where(above, cy - 1, 0), 1)]
            pay[start : start + count * along] = layer.reshape(count * along, nz)
        pay[(nv + 3) * along :] = aims[...]


top = 8


def window(ext, v, cx, cy, move_x=0, move_y=0):
    return ext[v, 1 + move_x : 1 + move_x + cx, top + move_y : top + move_y + cy]


def along_z(value, by):
    nz = value.shape[-1]
    at = lax.broadcasted_iota(jnp.int32, (1,) + value.shape[1:], 2)
    edge = 0 if by < 0 else nz - 1
    return jnp.where(at == edge, 0.0, pltpu.roll(value, (-by) % nz, 2))


def shifted(ext, v, cx, cy, d, by):
    if d == 2 and by:
        return along_z(window(ext, v, cx, cy), by)
    return window(ext, v, cx, cy, by if d == 0 else 0, by if d == 1 else 0)


def face(low, high):
    wave_low = jnp.minimum(jnp.minimum(low, high) - signal_speed, 0.0)
    wave_high = jnp.maximum(jnp.maximum(low, high) + signal_speed, 0.0)
    scale = courant_number / (wave_high - wave_low)
    return (
        scale * wave_high * (low - wave_low),
        scale * wave_low * (wave_high - high),
    )


def prepare_kernel(slots, ng, cons, vel, aims, coefs, base, picks, marks):
    nv, cx, cy, nz = cons.shape
    lanes = nz
    per = lanes // slots
    chunks = block // per
    nq = aims.shape[0]
    spread = 4 if cx % 4 == 0 else 1
    count = cx // spread * cy
    used = (ng - 1) * chunks

    def pick(n):
        cell = aims[pl.ds(n * block, block)].astype(jnp.int32) + cx * cy * nz
        x, y, z = over(cell, nz * cy), rest_of(over(cell, nz), cy), rest_of(cell, nz)
        at_row = over(x, spread) * cy + y
        at_column = (rest_of(x, spread) * nz + z).T
        up = lax.broadcasted_iota(jnp.int32, (count, lanes), 0)
        along = lax.broadcasted_iota(jnp.int32, (lanes, spread * nz), 1)
        total = None
        for at in range(0, used, chunks):
            hits = []
            for c in range(chunks):
                hits.append(jnp.where(up == at_row[at + c : at + c + 1], 1.0, 0.0))
                to = pl.ds(pl.multiple_of((n * used + at + c) * lanes, lanes), lanes)
                chosen = at_column[:, at + c : at + c + 1] == along
                picks[to] = jnp.where(chosen, 1.0, 0.0).astype(jnp.bfloat16)
            to = pl.ds(pl.multiple_of((n * used + at) * lanes, lanes), chunks * lanes)
            term = jnp.dot(
                jnp.concatenate(hits, axis=1).astype(jnp.bfloat16),
                picks[to],
                preferred_element_type=jnp.float32,
            )
            total = term if total is None else total + term
        if nq == block:
            marks[...] = total
        else:
            marks[...] += total

    if nq != block:
        marks[...] = jnp.zeros_like(marks)
    each(nq // block, pick)
    for x in range(cx):
        rows = slice(x // spread * cy, (x // spread + 1) * cy)
        mark = marks[rows, x % spread * nz : (x % spread + 1) * nz]
        base[:, x] = jnp.where(mark[None] > 0.5, 0.0, cons[:, x])

    centre = jnp.ones((cx, cy, nz), jnp.float32)
    none = jnp.zeros((1, cy, nz), jnp.float32)
    low, high = face(vel[0, : cx - 1], vel[0, 1:])
    coefs[0] = jnp.concatenate([none, low], axis=0)
    coefs[1] = -jnp.concatenate([high, none], axis=0)
    centre += jnp.concatenate([none, high], axis=0) - jnp.concatenate([low, none], axis=0)

    at_y = lax.broadcasted_iota(jnp.int32, (1, cy, nz), 1)
    speed = vel[1]
    low, high = face(speed, pltpu.roll(speed, cy - 1, 1))
    low = jnp.where(at_y == cy - 1, 0.0, low)
    high = jnp.where(at_y == cy - 1, 0.0, high)
    coefs[2] = pltpu.roll(low, 1, 1)
    coefs[3] = -high
    centre += pltpu.roll(high, 1, 1) - low

    speed = vel[2]
    up_low, up_high = face(speed, along_z(speed, 1))
    down_low, down_high = face(along_z(speed, -1), speed)
    coefs[4] = down_low
    coefs[5] = -up_high
    coefs[6] = centre + down_high - up_low


def step_kernel(kinds, slots, ng, vel, aims, given, base, picks, received, *rest):
    halos = rest[: len(kinds)]
    out, coefs, ext, field, acc, result, sems = rest[len(kinds) :]
    nv, cx, cy, nz = base.shape
    lanes = nz
    nq = received.shape[0] // ng
    per = lanes // slots
    chunks = block // per
    used = (ng - 1) * chunks
    spread = 4 if cx % 4 == 0 else 1
    me = lax.axis_index("grp")
    lane = lax.broadcasted_iota(jnp.int32, (nv, lanes), 1) // slots
    above = [partner_above(axis, phase) for axis, phase, _ in kinds]

    parts = [(cx // spread * cy, spread)]
    parts += [(cy if axis == "gx" else cx, 1) for axis, _, _ in kinds]
    starts = [0]
    for count, groups in parts:
        starts.append(starts[-1] + (2 * nv + 1) * count * groups)

    def fill(n):
        for part, (count, groups) in enumerate(parts):
            if part == 0:
                cell = aims[pl.ds(n * block, block)]
            else:
                cell = halos[part - 1][pl.ds((nv + 3) * count + n * block, block)]
            cell = cell.astype(jnp.int32) + cx * cy * nz
            x, y, z = over(cell, nz * cy), rest_of(over(cell, nz), cy), rest_of(cell, nz)
            if part == 0:
                at_row = over(x, spread) * cy + y
            elif kinds[part - 1][0] == "gx":
                at_row = jnp.where(x == jnp.where(above[part - 1], 0, cx - 1), y, -1)
            else:
                at_row = jnp.where(y == jnp.where(above[part - 1], 0, cy - 1), x, -1)
            at_column = z.T
            up = lax.broadcasted_iota(jnp.int32, (count, lanes), 0)
            along = lax.broadcasted_iota(jnp.int32, (lanes, nz), 1)
            here = slice(part // per * lanes, (part // per + 1) * lanes)
            total = None
            for away in range(1, ng):
                g = (me + away) % ng
                lefts, chosen = [], []
                for c in range(chunks):
                    at = (away - 1) * chunks + c
                    value = None
                    for p in range(per):
                        piece = received[g * nq + n * block + p * chunks + c, :, here]
                        turn = (p - part) % per
                        if turn:
                            piece = pltpu.roll(piece, turn * slots, 1)
                        value = piece if value is None else jnp.where(lane == p, piece, value)
                    high = value.astype(jnp.bfloat16).astype(jnp.float32)
                    low = value - high
                    hit = up == at_row[at : at + 1]
                    pieces = [jnp.where(hit, high[v : v + 1], 0.0) for v in range(nv)]
                    pieces += [jnp.where(hit, low[v : v + 1], 0.0) for v in range(nv)]
                    if part:
                        pieces += [jnp.where(hit, 1.0, 0.0)]
                        pick = jnp.where(at_column[:, at : at + 1] == along, 1.0, 0.0)
                        chosen.append(pick.astype(jnp.bfloat16))
                    lefts.append(jnp.concatenate(pieces, axis=0).astype(jnp.bfloat16))
                if part:
                    chosen = jnp.concatenate(chosen, axis=0)
                else:
                    start = (n * used + (away - 1) * chunks) * lanes
                    chosen = picks[pl.ds(pl.multiple_of(start, lanes), chunks * lanes)]
                term = jnp.dot(
                    jnp.concatenate(lefts, axis=1), chosen, preferred_element_type=jnp.float32
                )
                total = term if total is None else total + term
            rows = total.shape[0]
            for s in range(groups):
                start = starts[part] + s * (2 * nv + 1) * count
                value = total[:, s * nz : (s + 1) * nz]
                if nq == block:
                    acc[start : start + rows] = value
                else:
                    acc[start : start + rows] += value

    if nq != block:
        acc[...] = jnp.zeros_like(acc)
    each(nq // block, fill)

    def brought(part, s):
        count = parts[part][0]
        start = starts[part] + s * (2 * nv + 1) * count
        new = acc[start : start + nv * count] + acc[start + nv * count : start + 2 * nv * count]
        return new.reshape(nv, count, nz)

    def crossed(n, speeds, fields):
        a, b = (n + 1) % 3, (n + 2) % 3
        return speeds[b] * fields[a] - speeds[a] * fields[b]

    inside = slice(top, top + cy)
    for s in range(spread):
        new = brought(0, s)
        for n, x in enumerate(range(s, cx, spread)):
            state = base[:, x] + new[:, n * cy : (n + 1) * cy]
            ext[:fluid_count, 1 + x, inside] = state[:fluid_count]
            field[:, x] = state[fluid_count:]
            for d in range(3):
                ext[fluid_count + d, 1 + x, inside] = crossed(d, vel[:, x], state[fluid_count:])

    sides = {("gx", True): 0.0, ("gx", False): 0.0, ("gy", True): 0.0, ("gy", False): 0.0}
    for n, (axis, _, _) in enumerate(kinds):
        count = parts[n + 1][0]
        d = 0 if axis == "gx" else 1
        halo = halos[n][: (nv + 3) * count].reshape(nv + 3, count, nz)
        mark = acc[starts[n + 1] + 2 * nv * count : starts[n + 1] + (2 * nv + 1) * count]
        state = jnp.where(mark[None] > 0.5, brought(n + 1, 0), halo[:nv])
        electric = [crossed(m, halo[nv:], state[fluid_count:])[None] for m in (1 - d, 2)]
        halo = jnp.concatenate([state[:fluid_count], halo[nv + d : nv + d + 1]] + electric, axis=0)
        sides[axis, True] += jnp.where(above[n], halo, 0.0)
        sides[axis, False] += jnp.where(above[n], 0.0, halo)

    coefs[...] = given[...]
    for (axis, high), halo in sides.items():
        d = 0 if axis == "gx" else 1
        halo = jnp.broadcast_to(halo, (fluid_count + 3, cx if d else cy, nz))
        if d == 0:
            at = (cx + 1 if high else 0, inside)
            edge = (cx - 1 if high else 0,)
        else:
            at = (slice(1, cx + 1), top + cy if high else top - 1)
            edge = (slice(None), cy - 1 if high else 0)
        ext[(slice(0, fluid_count),) + at] = halo[:fluid_count]
        ext[(fluid_count + 1 - d,) + at] = halo[fluid_count + 1]
        ext[(fluid_count + 2,) + at] = halo[fluid_count + 2]
        speed = vel[(d,) + edge]
        if high:
            of_low, of_high = face(speed, halo[fluid_count])
            coefs[(2 * d + 1,) + edge] = -of_high
            coefs[(6,) + edge] -= of_low
        else:
            of_low, of_high = face(halo[fluid_count], speed)
            coefs[(2 * d,) + edge] = of_low
            coefs[(6,) + edge] += of_high

    copies = []

    def finish(v, value):
        result[v] = value
        copies.append(pltpu.make_async_copy(result.at[v], out.at[v], sems.at[v]))
        copies[-1].start()

    def central(n, d):
        v = fluid_count + n
        return shifted(ext, v, cx, cy, d, 1) - shifted(ext, v, cx, cy, d, -1)

    for n in range(3):
        a, b = (n + 1) % 3, (n + 2) % 3
        curl = central(b, a) - central(a, b)
        finish(fluid_count + n, field[n] - (0.5 * courant_number) * curl)
    for v in range(fluid_count):
        total = coefs[6] * window(ext, v, cx, cy)
        for d in range(3):
            total = total + coefs[2 * d] * shifted(ext, v, cx, cy, d, -1)
            total = total + coefs[2 * d + 1] * shifted(ext, v, cx, cy, d, 1)
        finish(v, total)
    for copy in copies:
        copy.wait()


def per_device(ngx, ngy, conserved, velocity, donor_corner, donor_fraction, target_cell):
    kinds = exchanges(ngx, ngy)
    cons = conserved[:, 0]
    vel = velocity[:, 0]
    corner = donor_corner[0, 0, 0]
    fraction = donor_fraction[:, 0, 0, 0]
    target = target_cell[0, 0, 0]
    nv, cx, cy, nz = cons.shape
    ng, nq, slots = corner.shape
    rows = cx * cy
    per = nz // slots
    tiles = -(-(1 + len(kinds)) // per)
    f32 = jnp.float32

    def shape(*dims):
        return jax.ShapeDtypeStruct(dims, f32)

    params = pltpu.CompilerParams(vmem_limit_bytes=(12 + nq // 2) << 20)
    alongs = [cy if axis == "gx" else cx for axis, _, _ in kinds]
    pay_shapes = [((nv + 3) * along + nq, nz) for along in alongs]
    blended, state = pl.pallas_call(
        functools.partial(blend_kernel, ngy, kinds),
        out_shape=[pltpu.VMEM((ng * nq, nv, tiles * nz), f32), pltpu.VMEM(cons.shape, f32)],
        in_specs=[pl.BlockSpec(memory_space=pl.ANY)] * 3,
        scratch_shapes=[
            pltpu.VMEM(corner.shape, jnp.int32),
            pltpu.VMEM(fraction.shape, f32),
            pltpu.VMEM((nv * rows, 3 * nz), jnp.bfloat16),
            pltpu.VMEM((ng - 1, 3 * nz, block * slots), jnp.bfloat16),
            pltpu.VMEM((ng - 1, rows, block * slots), f32),
            pltpu.VMEM((ng - 1, per, nq // per, nv, nz), f32),
            pltpu.SemaphoreType.DMA((2 + nv,)),
        ],
        compiler_params=params,
        name="blend",
    )(*(pltpu.with_memory_space_constraint(value, pltpu.HBM) for value in (cons, corner, fraction)))

    state = pltpu.with_memory_space_constraint(state, pltpu.VMEM)
    aims, *pays = pl.pallas_call(
        functools.partial(edge_kernel, kinds),
        out_shape=[pltpu.VMEM((nq, nz), f32)] + [pltpu.VMEM(dims, f32) for dims in pay_shapes],
        in_specs=[pl.BlockSpec(memory_space=pltpu.VMEM)] * 3 + [pl.BlockSpec(memory_space=pl.ANY)],
        compiler_params=params,
        name="edge",
    )(state, vel, target, blended)

    received = lax.all_to_all(
        blended, ("grp", "gx", "gy"), split_axis=0, concat_axis=0, tiled=True
    )
    halos = []
    for (axis, phase, _), pay in zip(kinds, pays):
        count = ngx if axis == "gx" else ngy
        pairs = []
        for low in range(phase, count - 1, 2):
            pairs += [(low, low + 1), (low + 1, low)]
        halos.append(lax.ppermute(pay, axis, pairs))

    spread = 4 if cx % 4 == 0 else 1
    coefs, base, picks = pl.pallas_call(
        functools.partial(prepare_kernel, slots, ng),
        out_shape=[
            pltpu.VMEM((7, cx, cy, nz), f32),
            pltpu.VMEM((nv, cx, cy, nz), f32),
            pltpu.VMEM(((ng - 1) * nq * slots, spread * nz), jnp.bfloat16),
        ],
        scratch_shapes=[pltpu.VMEM((rows // spread, spread * nz), f32)],
        compiler_params=params,
        name="prepare",
    )(state, vel, aims)
    coefs, base, picks = (
        pltpu.with_memory_space_constraint(value, pltpu.VMEM) for value in (coefs, base, picks)
    )

    result = pl.pallas_call(
        functools.partial(step_kernel, kinds, slots, ng),
        out_shape=shape(nv, cx, cy, nz),
        out_specs=pl.BlockSpec(memory_space=pl.ANY),
        scratch_shapes=[
            pltpu.VMEM((7, cx, cy, nz), f32),
            pltpu.VMEM((fluid_count + 3, cx + 2, cy + 2 * top, nz), f32),
            pltpu.VMEM((nv - fluid_count, cx, cy, nz), f32),
            pltpu.VMEM(((2 * nv + 1) * (rows + sum(alongs)), nz), f32),
            pltpu.VMEM((nv, cx, cy, nz), f32),
            pltpu.SemaphoreType.DMA((nv,)),
        ],
        compiler_params=params,
        name="step",
    )(vel, aims, coefs, base, picks, received, *halos)
    return result[:, None]


def solution(mesh):
    return jax.shard_map(
        functools.partial(per_device, mesh.shape["gx"], mesh.shape["gy"]),
        mesh=mesh,
        in_specs=(
            P(None, "grp", "gx", "gy", None),
            P(None, "grp", "gx", "gy", None),
            P("grp", "gx", "gy", None, None, None),
            P(None, "grp", "gx", "gy", None, None, None),
            P("grp", "gx", "gy", None, None, None),
        ),
        out_specs=P(None, "grp", "gx", "gy", None),
        check_vma=False,
    )
```

```python
import functools

import jax
import jax.numpy as jnp
from jax import lax
from jax.experimental import pallas as pl
from jax.experimental.pallas import tpu as pltpu
from jax.sharding import PartitionSpec as P

signal_speed = 0.5
courant_number = 0.3
fluid_count = 5
block = 8


def exchanges(ngx, ngy):
    def partner(count, phase, n):
        other = n + 1 if (n + phase) % 2 == 0 else n - 1
        return other if 0 <= other < count else n

    kinds = []
    for phase in range(min(ngx - 1, 2)):
        kinds.append(("gx", phase, lambda i, j, phase=phase: (partner(ngx, phase, i), j)))
    for phase in range(min(ngy - 1, 2)):
        kinds.append(("gy", phase, lambda i, j, phase=phase: (i, partner(ngy, phase, j))))
    return kinds


def partner_above(axis, phase):
    return (lax.axis_index(axis) + phase) % 2 == 0


def split(value):
    high = value.astype(jnp.bfloat16)
    low = (value - high.astype(jnp.float32)).astype(jnp.bfloat16)
    return high, low


def over(value, n):
    return value >> (n.bit_length() - 1) if n & (n - 1) == 0 else value // n


def rest_of(value, n):
    return value & (n - 1) if n & (n - 1) == 0 else value % n


def each(count, body):
    if count == 1:
        body(0)
    else:
        lax.fori_loop(0, count, lambda n, c: (body(n), c)[1], 0)


def block_transpose(value, slots):
    rows, lanes = value.shape
    count = lanes // slots
    each_rows = rows // count
    at_row = lax.broadcasted_iota(jnp.int32, value.shape, 0) // each_rows
    at_lane = lax.broadcasted_iota(jnp.int32, value.shape, 1) // slots
    result = value
    for d in range(1, count):
        turned = pltpu.roll(value, d * each_rows, 0)
        turned = pltpu.roll(turned, lanes - d * slots, 1)
        result = jnp.where((at_row - at_lane) % count == d, turned, result)
    return result


def packed(tiles, slots):
    empty = jnp.zeros(tiles[0].shape, tiles[0].dtype)
    return block_transpose(jnp.concatenate(tiles + [empty], axis=1), slots)


def blend_kernel(ngy, kinds, cons, corner, fraction, out, at_cons, *scratch):
    at_corner, at_fraction, at_depth, upper, wxys, moved, arrive = scratch
    nv, cx, cy, nz = cons.shape
    ng, nq, slots = corner.shape
    lanes = nz
    per = lanes // slots
    chunks = block // per
    rows = cx * cy
    me = lax.axis_index("grp")

    moves = [(corner, at_corner), (fraction, at_fraction)]
    moves += [(cons.at[v], at_cons.at[v]) for v in range(nv)]
    ins = [pltpu.make_async_copy(a, b, arrive.at[n]) for n, (a, b) in enumerate(moves)]
    for copy in ins:
        copy.start()

    out[pl.ds(me * nq, nq)] = jnp.zeros((nq,) + out.shape[1:], jnp.float32)

    def weight(count, at, upper):
        place = lax.broadcasted_iota(jnp.int32, (count, lanes), 0)
        return jnp.where(place == at, 1.0 - upper, jnp.where(place == at + 1, upper, 0.0))

    def weigh(n):
        here = pl.ds(n * block, block)
        grids = [(me + away) % ng for away in range(1, ng)]
        cell = packed([at_corner[h, here] for h in grids], slots)
        at_x, at_y, at_z = over(cell, nz * cy), rest_of(over(cell, nz), cy), rest_of(cell, nz)
        fx, fy, fz = (packed([at_fraction[d, h, here] for h in grids], slots) for d in range(3))
        at_depth[...] = jnp.minimum(at_z, nz - 2)
        upper[...] = fz
        for away in range(1, ng):
            for c in range(chunks):
                row = slice((away - 1) * chunks + c, (away - 1) * chunks + c + 1)
                cols = slice(c * lanes, (c + 1) * lanes)
                wx = weight(cx, at_x[row], fx[row])
                wy = weight(cy, at_y[row], fy[row])
                for x in range(cx):
                    wxys[away - 1, x * cy : (x + 1) * cy, cols] = wx[x : x + 1] * wy

    def blend(n):
        for away in range(1, ng):
            values = []
            for c in range(chunks):
                here = pl.ds((away - 1) * chunks + c, 1)
                low = jnp.broadcast_to(at_depth[here], (rows, lanes))
                fz = upper[here]
                wxy = wxys[away - 1, :, c * lanes : (c + 1) * lanes]
                sums = []
                for v in range(nv):
                    layer = at_cons[v].reshape(rows, nz)
                    first = jnp.take_along_axis(layer, low, axis=1, mode="promise_in_bounds")
                    second = jnp.take_along_axis(layer, low + 1, axis=1, mode="promise_in_bounds")
                    along = first * (1.0 - fz) + second * fz
                    sums.append(jnp.sum(along * wxy, axis=0, keepdims=True))
                values.append(jnp.concatenate(sums, axis=0))
            values = jnp.concatenate(values, axis=1)
            for c in range(chunks):
                value = values[:, c * lanes : (c + 1) * lanes]
                for turn in range(per):
                    moved[away - 1, turn, n * chunks + c] = (
                        pltpu.roll(value, turn * slots, 1) if turn else value
                    )
            if nq == block:
                assemble(away)

    lane = lax.broadcasted_iota(jnp.int32, (nv, lanes), 1) // slots

    def assemble(away):
        for q in range(nq):
            i, j = q // ngy, q % ngy
            owners = [q] + [a * ngy + b for a, b in (of(i, j) for _, _, of in kinds)]
            for t in range(0, len(owners), per):
                tile = None
                for k, owner in enumerate(owners[t : t + per]):
                    chunk = owner // block * chunks + owner % chunks
                    piece = moved[away - 1, (k - owner % block // chunks) % per, chunk]
                    tile = piece if tile is None else jnp.where(lane == k, piece, tile)
                cols = slice(t // per * lanes, (t // per + 1) * lanes)
                out[pl.ds((me + away) % ng * nq + q, 1), :, cols] = tile[None]

    for copy in ins[:2]:
        copy.wait()
    if nq == block:
        weigh(0)
    for copy in ins[2:]:
        copy.wait()
    if nq == block:
        blend(0)
    else:

        def both(n):
            weigh(n)
            blend(n)

        each(nq // block, both)
        for away in range(1, ng):
            assemble(away)


def edge_kernel(kinds, cons, vel, target, sent, aims, *pays):
    del sent
    nv, cx, cy, nz = cons.shape
    ng, nq, slots = target.shape
    me = lax.axis_index("grp")
    for n in range(nq // block):
        here = slice(n * block, (n + 1) * block)
        tiles = [target[(me + away) % ng, here] - cx * cy * nz for away in range(1, ng)]
        aims[here] = packed(tiles, slots).astype(jnp.float32)
    for (axis, phase, _), pay in zip(kinds, pays):
        above = partner_above(axis, phase)
        along = cy if axis == "gx" else cx
        for count, source, start in ((nv, cons, 0), (3, vel, nv * along)):
            if axis == "gx":
                layer = source[:, pl.ds(jnp.where(above, cx - 1, 0), 1)]
            else:
                layer = source[:, :, pl.ds(jnp.where(above, cy - 1, 0), 1)]
            pay[start : start + count * along] = layer.reshape(count * along, nz)
        pay[(nv + 3) * along :] = aims[...]


top = 8


def window(ext, v, cx, cy, move_x=0, move_y=0):
    return ext[v, 1 + move_x : 1 + move_x + cx, top + move_y : top + move_y + cy]


def along_z(value, by):
    nz = value.shape[-1]
    at = lax.broadcasted_iota(jnp.int32, (1,) + value.shape[1:], 2)
    edge = 0 if by < 0 else nz - 1
    return jnp.where(at == edge, 0.0, pltpu.roll(value, (-by) % nz, 2))


def shifted(ext, v, cx, cy, d, by):
    if d == 2 and by:
        return along_z(window(ext, v, cx, cy), by)
    return window(ext, v, cx, cy, by if d == 0 else 0, by if d == 1 else 0)


def face(low, high):
    wave_low = jnp.minimum(jnp.minimum(low, high) - signal_speed, 0.0)
    wave_high = jnp.maximum(jnp.maximum(low, high) + signal_speed, 0.0)
    scale = courant_number / (wave_high - wave_low)
    return (
        scale * wave_high * (low - wave_low),
        scale * wave_low * (wave_high - high),
    )


def prepare_kernel(slots, ng, cons, vel, aims, coefs, base, picks, marks):
    nv, cx, cy, nz = cons.shape
    lanes = nz
    per = lanes // slots
    chunks = block // per
    nq = aims.shape[0]
    spread = 4 if cx % 4 == 0 else 1
    count = cx // spread * cy
    used = (ng - 1) * chunks

    def pick(n):
        cell = aims[pl.ds(n * block, block)].astype(jnp.int32) + cx * cy * nz
        x, y, z = over(cell, nz * cy), rest_of(over(cell, nz), cy), rest_of(cell, nz)
        at_row = over(x, spread) * cy + y
        at_column = (rest_of(x, spread) * nz + z).T
        up = lax.broadcasted_iota(jnp.int32, (count, lanes), 0)
        along = lax.broadcasted_iota(jnp.int32, (lanes, spread * nz), 1)
        total = None
        for at in range(0, used, chunks):
            hits = []
            for c in range(chunks):
                hits.append(jnp.where(up == at_row[at + c : at + c + 1], 1.0, 0.0))
                to = pl.ds(pl.multiple_of((n * used + at + c) * lanes, lanes), lanes)
                chosen = at_column[:, at + c : at + c + 1] == along
                picks[to] = jnp.where(chosen, 1.0, 0.0).astype(jnp.bfloat16)
            to = pl.ds(pl.multiple_of((n * used + at) * lanes, lanes), chunks * lanes)
            term = jnp.dot(
                jnp.concatenate(hits, axis=1).astype(jnp.bfloat16),
                picks[to],
                preferred_element_type=jnp.float32,
            )
            total = term if total is None else total + term
        if nq == block:
            marks[...] = total
        else:
            marks[...] += total

    if nq != block:
        marks[...] = jnp.zeros_like(marks)
    each(nq // block, pick)
    for x in range(cx):
        rows = slice(x // spread * cy, (x // spread + 1) * cy)
        mark = marks[rows, x % spread * nz : (x % spread + 1) * nz]
        base[:, x] = jnp.where(mark[None] > 0.5, 0.0, cons[:, x])

    centre = jnp.ones((cx, cy, nz), jnp.float32)
    none = jnp.zeros((1, cy, nz), jnp.float32)
    low, high = face(vel[0, : cx - 1], vel[0, 1:])
    coefs[0] = jnp.concatenate([none, low], axis=0)
    coefs[1] = -jnp.concatenate([high, none], axis=0)
    centre += jnp.concatenate([none, high], axis=0) - jnp.concatenate([low, none], axis=0)

    at_y = lax.broadcasted_iota(jnp.int32, (1, cy, nz), 1)
    speed = vel[1]
    low, high = face(speed, pltpu.roll(speed, cy - 1, 1))
    low = jnp.where(at_y == cy - 1, 0.0, low)
    high = jnp.where(at_y == cy - 1, 0.0, high)
    coefs[2] = pltpu.roll(low, 1, 1)
    coefs[3] = -high
    centre += pltpu.roll(high, 1, 1) - low

    speed = vel[2]
    up_low, up_high = face(speed, along_z(speed, 1))
    down_low, down_high = face(along_z(speed, -1), speed)
    coefs[4] = down_low
    coefs[5] = -up_high
    coefs[6] = centre + down_high - up_low


def step_kernel(kinds, slots, ng, vel, aims, given, base, picks, received, *rest):
    halos = rest[: len(kinds)]
    out, coefs, ext, field, acc, result, sems = rest[len(kinds) :]
    nv, cx, cy, nz = base.shape
    lanes = nz
    nq = received.shape[0] // ng
    per = lanes // slots
    chunks = block // per
    used = (ng - 1) * chunks
    spread = 4 if cx % 4 == 0 else 1
    me = lax.axis_index("grp")
    lane = lax.broadcasted_iota(jnp.int32, (nv, lanes), 1) // slots
    above = [partner_above(axis, phase) for axis, phase, _ in kinds]

    parts = [(cx // spread * cy, spread)]
    parts += [(cy if axis == "gx" else cx, 1) for axis, _, _ in kinds]
    starts = [0]
    for count, groups in parts:
        starts.append(starts[-1] + (2 * nv + 1) * count * groups)

    def fill(n):
        for part, (count, groups) in enumerate(parts):
            if part == 0:
                cell = aims[pl.ds(n * block, block)]
            else:
                cell = halos[part - 1][pl.ds((nv + 3) * count + n * block, block)]
            cell = cell.astype(jnp.int32) + cx * cy * nz
            x, y, z = over(cell, nz * cy), rest_of(over(cell, nz), cy), rest_of(cell, nz)
            if part == 0:
                at_row = over(x, spread) * cy + y
            elif kinds[part - 1][0] == "gx":
                at_row = jnp.where(x == jnp.where(above[part - 1], 0, cx - 1), y, -1)
            else:
                at_row = jnp.where(y == jnp.where(above[part - 1], 0, cy - 1), x, -1)
            at_column = z.T
            up = lax.broadcasted_iota(jnp.int32, (count, lanes), 0)
            along = lax.broadcasted_iota(jnp.int32, (lanes, nz), 1)
            here = slice(part // per * lanes, (part // per + 1) * lanes)
            total = None
            for away in range(1, ng):
                g = (me + away) % ng
                lefts, chosen = [], []
                for c in range(chunks):
                    at = (away - 1) * chunks + c
                    value = None
                    for p in range(per):
                        piece = received[g * nq + n * block + p * chunks + c, :, here]
                        turn = (p - part) % per
                        if turn:
                            piece = pltpu.roll(piece, turn * slots, 1)
                        value = piece if value is None else jnp.where(lane == p, piece, value)
                    high = value.astype(jnp.bfloat16).astype(jnp.float32)
                    low = value - high
                    hit = up == at_row[at : at + 1]
                    pieces = [jnp.where(hit, high[v : v + 1], 0.0) for v in range(nv)]
                    pieces += [jnp.where(hit, low[v : v + 1], 0.0) for v in range(nv)]
                    if part:
                        pieces += [jnp.where(hit, 1.0, 0.0)]
                        pick = jnp.where(at_column[:, at : at + 1] == along, 1.0, 0.0)
                        chosen.append(pick.astype(jnp.bfloat16))
                    lefts.append(jnp.concatenate(pieces, axis=0).astype(jnp.bfloat16))
                if part:
                    chosen = jnp.concatenate(chosen, axis=0)
                else:
                    start = (n * used + (away - 1) * chunks) * lanes
                    chosen = picks[pl.ds(pl.multiple_of(start, lanes), chunks * lanes)]
                term = jnp.dot(
                    jnp.concatenate(lefts, axis=1), chosen, preferred_element_type=jnp.float32
                )
                total = term if total is None else total + term
            rows = total.shape[0]
            for s in range(groups):
                start = starts[part] + s * (2 * nv + 1) * count
                value = total[:, s * nz : (s + 1) * nz]
                if nq == block:
                    acc[start : start + rows] = value
                else:
                    acc[start : start + rows] += value

    if nq != block:
        acc[...] = jnp.zeros_like(acc)
    each(nq // block, fill)

    def brought(part, s):
        count = parts[part][0]
        start = starts[part] + s * (2 * nv + 1) * count
        new = acc[start : start + nv * count] + acc[start + nv * count : start + 2 * nv * count]
        return new.reshape(nv, count, nz)

    def crossed(n, speeds, fields):
        a, b = (n + 1) % 3, (n + 2) % 3
        return speeds[b] * fields[a] - speeds[a] * fields[b]

    inside = slice(top, top + cy)
    for s in range(spread):
        new = brought(0, s)
        for n, x in enumerate(range(s, cx, spread)):
            state = base[:, x] + new[:, n * cy : (n + 1) * cy]
            ext[:fluid_count, 1 + x, inside] = state[:fluid_count]
            field[:, x] = state[fluid_count:]
            for d in range(3):
                ext[fluid_count + d, 1 + x, inside] = crossed(d, vel[:, x], state[fluid_count:])

    sides = {("gx", True): 0.0, ("gx", False): 0.0, ("gy", True): 0.0, ("gy", False): 0.0}
    for n, (axis, _, _) in enumerate(kinds):
        count = parts[n + 1][0]
        d = 0 if axis == "gx" else 1
        halo = halos[n][: (nv + 3) * count].reshape(nv + 3, count, nz)
        mark = acc[starts[n + 1] + 2 * nv * count : starts[n + 1] + (2 * nv + 1) * count]
        state = jnp.where(mark[None] > 0.5, brought(n + 1, 0), halo[:nv])
        electric = [crossed(m, halo[nv:], state[fluid_count:])[None] for m in (1 - d, 2)]
        halo = jnp.concatenate([state[:fluid_count], halo[nv + d : nv + d + 1]] + electric, axis=0)
        sides[axis, True] += jnp.where(above[n], halo, 0.0)
        sides[axis, False] += jnp.where(above[n], 0.0, halo)

    coefs[...] = given[...]
    for (axis, high), halo in sides.items():
        d = 0 if axis == "gx" else 1
        halo = jnp.broadcast_to(halo, (fluid_count + 3, cx if d else cy, nz))
        if d == 0:
            at = (cx + 1 if high else 0, inside)
            edge = (cx - 1 if high else 0,)
        else:
            at = (slice(1, cx + 1), top + cy if high else top - 1)
            edge = (slice(None), cy - 1 if high else 0)
        ext[(slice(0, fluid_count),) + at] = halo[:fluid_count]
        ext[(fluid_count + 1 - d,) + at] = halo[fluid_count + 1]
        ext[(fluid_count + 2,) + at] = halo[fluid_count + 2]
        speed = vel[(d,) + edge]
        if high:
            of_low, of_high = face(speed, halo[fluid_count])
            coefs[(2 * d + 1,) + edge] = -of_high
            coefs[(6,) + edge] -= of_low
        else:
            of_low, of_high = face(halo[fluid_count], speed)
            coefs[(2 * d,) + edge] = of_low
            coefs[(6,) + edge] += of_high

    copies = []

    def finish(v, value):
        result[v] = value
        copies.append(pltpu.make_async_copy(result.at[v], out.at[v], sems.at[v]))
        copies[-1].start()

    def central(n, d):
        v = fluid_count + n
        return shifted(ext, v, cx, cy, d, 1) - shifted(ext, v, cx, cy, d, -1)

    for n in range(3):
        a, b = (n + 1) % 3, (n + 2) % 3
        curl = central(b, a) - central(a, b)
        finish(fluid_count + n, field[n] - (0.5 * courant_number) * curl)
    for v in range(fluid_count):
        total = coefs[6] * window(ext, v, cx, cy)
        for d in range(3):
            total = total + coefs[2 * d] * shifted(ext, v, cx, cy, d, -1)
            total = total + coefs[2 * d + 1] * shifted(ext, v, cx, cy, d, 1)
        finish(v, total)
    for copy in copies:
        copy.wait()


def per_device(ngx, ngy, conserved, velocity, donor_corner, donor_fraction, target_cell):
    kinds = exchanges(ngx, ngy)
    cons = conserved[:, 0]
    vel = velocity[:, 0]
    corner = donor_corner[0, 0, 0]
    fraction = donor_fraction[:, 0, 0, 0]
    target = target_cell[0, 0, 0]
    nv, cx, cy, nz = cons.shape
    ng, nq, slots = corner.shape
    rows = cx * cy
    per = nz // slots
    tiles = -(-(1 + len(kinds)) // per)
    f32 = jnp.float32

    def shape(*dims):
        return jax.ShapeDtypeStruct(dims, f32)

    params = pltpu.CompilerParams(vmem_limit_bytes=(12 + nq // 2) << 20)
    alongs = [cy if axis == "gx" else cx for axis, _, _ in kinds]
    pay_shapes = [((nv + 3) * along + nq, nz) for along in alongs]
    blended, state = pl.pallas_call(
        functools.partial(blend_kernel, ngy, kinds),
        out_shape=[pltpu.VMEM((ng * nq, nv, tiles * nz), f32), pltpu.VMEM(cons.shape, f32)],
        in_specs=[pl.BlockSpec(memory_space=pl.ANY)] * 3,
        scratch_shapes=[
            pltpu.VMEM(corner.shape, jnp.int32),
            pltpu.VMEM(fraction.shape, f32),
            pltpu.VMEM((block, nz), jnp.int32),
            pltpu.VMEM((block, nz), f32),
            pltpu.VMEM((ng - 1, rows, block * slots), f32),
            pltpu.VMEM((ng - 1, per, nq // per, nv, nz), f32),
            pltpu.SemaphoreType.DMA((2 + nv,)),
        ],
        compiler_params=params,
        name="blend",
    )(*(pltpu.with_memory_space_constraint(value, pltpu.HBM) for value in (cons, corner, fraction)))

    state = pltpu.with_memory_space_constraint(state, pltpu.VMEM)
    aims, *pays = pl.pallas_call(
        functools.partial(edge_kernel, kinds),
        out_shape=[pltpu.VMEM((nq, nz), f32)] + [pltpu.VMEM(dims, f32) for dims in pay_shapes],
        in_specs=[pl.BlockSpec(memory_space=pltpu.VMEM)] * 3 + [pl.BlockSpec(memory_space=pl.ANY)],
        compiler_params=params,
        name="edge",
    )(state, vel, target, blended)

    received = lax.all_to_all(
        blended, ("grp", "gx", "gy"), split_axis=0, concat_axis=0, tiled=True
    )
    halos = []
    for (axis, phase, _), pay in zip(kinds, pays):
        count = ngx if axis == "gx" else ngy
        pairs = []
        for low in range(phase, count - 1, 2):
            pairs += [(low, low + 1), (low + 1, low)]
        halos.append(lax.ppermute(pay, axis, pairs))

    spread = 4 if cx % 4 == 0 else 1
    coefs, base, picks = pl.pallas_call(
        functools.partial(prepare_kernel, slots, ng),
        out_shape=[
            pltpu.VMEM((7, cx, cy, nz), f32),
            pltpu.VMEM((nv, cx, cy, nz), f32),
            pltpu.VMEM(((ng - 1) * nq * slots, spread * nz), jnp.bfloat16),
        ],
        scratch_shapes=[pltpu.VMEM((rows // spread, spread * nz), f32)],
        compiler_params=params,
        name="prepare",
    )(state, vel, aims)
    coefs, base, picks = (
        pltpu.with_memory_space_constraint(value, pltpu.VMEM) for value in (coefs, base, picks)
    )

    result = pl.pallas_call(
        functools.partial(step_kernel, kinds, slots, ng),
        out_shape=shape(nv, cx, cy, nz),
        out_specs=pl.BlockSpec(memory_space=pl.ANY),
        scratch_shapes=[
            pltpu.VMEM((7, cx, cy, nz), f32),
            pltpu.VMEM((fluid_count + 3, cx + 2, cy + 2 * top, nz), f32),
            pltpu.VMEM((nv - fluid_count, cx, cy, nz), f32),
            pltpu.VMEM(((2 * nv + 1) * (rows + sum(alongs)), nz), f32),
            pltpu.VMEM((nv, cx, cy, nz), f32),
            pltpu.SemaphoreType.DMA((nv,)),
        ],
        compiler_params=params,
        name="step",
    )(vel, aims, coefs, base, picks, received, *halos)
    return result[:, None]


def solution(mesh):
    return jax.shard_map(
        functools.partial(per_device, mesh.shape["gx"], mesh.shape["gy"]),
        mesh=mesh,
        in_specs=(
            P(None, "grp", "gx", "gy", None),
            P(None, "grp", "gx", "gy", None),
            P("grp", "gx", "gy", None, None, None),
            P(None, "grp", "gx", "gy", None, None, None),
            P("grp", "gx", "gy", None, None, None),
        ),
        out_specs=P(None, "grp", "gx", "gy", None),
        check_vma=False,
    )
```

```python
import functools

import jax
import jax.numpy as jnp
from jax import lax
from jax.experimental import pallas as pl
from jax.experimental.pallas import tpu as pltpu
from jax.sharding import PartitionSpec as P

signal_speed = 0.5
courant_number = 0.3
fluid_count = 5
block = 8


def exchanges(ngx, ngy):
    def partner(count, phase, n):
        other = n + 1 if (n + phase) % 2 == 0 else n - 1
        return other if 0 <= other < count else n

    kinds = []
    for phase in range(min(ngx - 1, 2)):
        kinds.append(("gx", phase, lambda i, j, phase=phase: (partner(ngx, phase, i), j)))
    for phase in range(min(ngy - 1, 2)):
        kinds.append(("gy", phase, lambda i, j, phase=phase: (i, partner(ngy, phase, j))))
    return kinds


def partner_above(axis, phase):
    return (lax.axis_index(axis) + phase) % 2 == 0


def split(value):
    high = value.astype(jnp.bfloat16)
    low = (value - high.astype(jnp.float32)).astype(jnp.bfloat16)
    return high, low


def over(value, n):
    return value >> (n.bit_length() - 1) if n & (n - 1) == 0 else value // n


def rest_of(value, n):
    return value & (n - 1) if n & (n - 1) == 0 else value % n


def each(count, body):
    if count == 1:
        body(0)
    else:
        lax.fori_loop(0, count, lambda n, c: (body(n), c)[1], 0)


def block_transpose(value, slots):
    rows, lanes = value.shape
    count = lanes // slots
    each_rows = rows // count
    at_row = lax.broadcasted_iota(jnp.int32, value.shape, 0) // each_rows
    at_lane = lax.broadcasted_iota(jnp.int32, value.shape, 1) // slots
    result = value
    for d in range(1, count):
        turned = pltpu.roll(value, d * each_rows, 0)
        turned = pltpu.roll(turned, lanes - d * slots, 1)
        result = jnp.where((at_row - at_lane) % count == d, turned, result)
    return result


def packed(tiles, slots):
    empty = jnp.zeros(tiles[0].shape, tiles[0].dtype)
    return block_transpose(jnp.concatenate(tiles + [empty], axis=1), slots)


def blend_kernel(ngy, kinds, cons, corner, fraction, out, at_cons, *scratch):
    at_corner, at_fraction, uhl, wzs, wxys, moved, arrive = scratch
    nv, cx, cy, nz = cons.shape
    ng, nq, slots = corner.shape
    lanes = nz
    per = lanes // slots
    chunks = block // per
    rows = cx * cy
    me = lax.axis_index("grp")

    moves = [(corner, at_corner), (fraction, at_fraction)]
    moves += [(cons.at[v], at_cons.at[v]) for v in range(nv)]
    ins = [pltpu.make_async_copy(a, b, arrive.at[n]) for n, (a, b) in enumerate(moves)]
    for copy in ins:
        copy.start()

    out[pl.ds(me * nq, nq)] = jnp.zeros((nq,) + out.shape[1:], jnp.float32)

    def weight(count, at, upper):
        place = lax.broadcasted_iota(jnp.int32, (count, lanes), 0)
        return jnp.where(place == at, 1.0 - upper, jnp.where(place == at + 1, upper, 0.0))

    def weigh(n):
        here = pl.ds(n * block, block)
        grids = [(me + away) % ng for away in range(1, ng)]
        cell = packed([at_corner[h, here] for h in grids], slots)
        at_x, at_y, at_z = over(cell, nz * cy), rest_of(over(cell, nz), cy), rest_of(cell, nz)
        fx, fy, fz = (packed([at_fraction[d, h, here] for h in grids], slots) for d in range(3))
        for away in range(1, ng):
            for c in range(chunks):
                row = slice((away - 1) * chunks + c, (away - 1) * chunks + c + 1)
                cols = slice(c * lanes, (c + 1) * lanes)
                wx = weight(cx, at_x[row], fx[row])
                wy = weight(cy, at_y[row], fy[row])
                for x in range(cx):
                    wxys[away - 1, x * cy : (x + 1) * cy, cols] = wx[x : x + 1] * wy
                high, low = split(weight(nz, at_z[row], fz[row]))
                wzs[away - 1, :nz, cols] = high
                wzs[away - 1, nz : 2 * nz, cols] = high
                wzs[away - 1, 2 * nz :, cols] = low

    def blend(n):
        for away in range(1, ng):
            both = jnp.dot(uhl[...], wzs[away - 1, : 2 * nz], preferred_element_type=jnp.float32)
            small = jnp.dot(
                uhl[:, :nz], wzs[away - 1, 2 * nz :], preferred_element_type=jnp.float32
            )
            along = (both + small).reshape(nv, rows, chunks * lanes)
            values = jnp.sum(along * wxys[away - 1][None], axis=1)
            for c in range(chunks):
                value = values[:, c * lanes : (c + 1) * lanes]
                for turn in range(per):
                    moved[away - 1, turn, n * chunks + c] = (
                        pltpu.roll(value, turn * slots, 1) if turn else value
                    )
            if nq == block:
                assemble(away)

    lane = lax.broadcasted_iota(jnp.int32, (nv, lanes), 1) // slots

    def assemble(away):
        for q in range(nq):
            i, j = q // ngy, q % ngy
            owners = [q] + [a * ngy + b for a, b in (of(i, j) for _, _, of in kinds)]
            for t in range(0, len(owners), per):
                tile = None
                for k, owner in enumerate(owners[t : t + per]):
                    chunk = owner // block * chunks + owner % chunks
                    piece = moved[away - 1, (k - owner % block // chunks) % per, chunk]
                    tile = piece if tile is None else jnp.where(lane == k, piece, tile)
                cols = slice(t // per * lanes, (t // per + 1) * lanes)
                out[pl.ds((me + away) % ng * nq + q, 1), :, cols] = tile[None]

    for copy in ins[:2]:
        copy.wait()
    if nq == block:
        weigh(0)
    for v in range(nv):
        ins[2 + v].wait()
        high, low = split(at_cons[v].reshape(rows, nz))
        here = slice(v * rows, (v + 1) * rows)
        uhl[here, :nz] = high
        uhl[here, nz:] = low
    if nq == block:
        blend(0)
    else:

        def both(n):
            weigh(n)
            blend(n)

        each(nq // block, both)
        for away in range(1, ng):
            assemble(away)


def edge_kernel(kinds, cons, vel, target, sent, aims, *pays):
    del sent
    nv, cx, cy, nz = cons.shape
    ng, nq, slots = target.shape
    me = lax.axis_index("grp")
    for n in range(nq // block):
        here = slice(n * block, (n + 1) * block)
        tiles = [target[(me + away) % ng, here] - cx * cy * nz for away in range(1, ng)]
        aims[here] = packed(tiles, slots).astype(jnp.float32)
    for (axis, phase, _), pay in zip(kinds, pays):
        above = partner_above(axis, phase)
        along = cy if axis == "gx" else cx
        for count, source, start in ((nv, cons, 0), (3, vel, nv * along)):
            if axis == "gx":
                layer = source[:, pl.ds(jnp.where(above, cx - 1, 0), 1)]
            else:
                layer = source[:, :, pl.ds(jnp.where(above, cy - 1, 0), 1)]
            pay[start : start + count * along] = layer.reshape(count * along, nz)
        pay[(nv + 3) * along :] = aims[...]


top = 8


def window(ext, v, cx, cy, move_x=0, move_y=0):
    return ext[v, 1 + move_x : 1 + move_x + cx, top + move_y : top + move_y + cy]


def along_z(value, by):
    nz = value.shape[-1]
    at = lax.broadcasted_iota(jnp.int32, (1,) + value.shape[1:], 2)
    edge = 0 if by < 0 else nz - 1
    return jnp.where(at == edge, 0.0, pltpu.roll(value, (-by) % nz, 2))


def shifted(ext, v, cx, cy, d, by):
    if d == 2 and by:
        return along_z(window(ext, v, cx, cy), by)
    return window(ext, v, cx, cy, by if d == 0 else 0, by if d == 1 else 0)


def face(low, high):
    wave_low = jnp.minimum(jnp.minimum(low, high) - signal_speed, 0.0)
    wave_high = jnp.maximum(jnp.maximum(low, high) + signal_speed, 0.0)
    scale = courant_number / (wave_high - wave_low)
    return (
        scale * wave_high * (low - wave_low),
        scale * wave_low * (wave_high - high),
    )


def prepare_kernel(slots, ng, cons, vel, aims, coefs, base, picks, marks):
    nv, cx, cy, nz = cons.shape
    lanes = nz
    per = lanes // slots
    chunks = block // per
    nq = aims.shape[0]
    spread = 4 if cx % 4 == 0 else 1
    count = cx // spread * cy
    used = (ng - 1) * chunks

    def pick(n):
        cell = aims[pl.ds(n * block, block)].astype(jnp.int32) + cx * cy * nz
        x, y, z = over(cell, nz * cy), rest_of(over(cell, nz), cy), rest_of(cell, nz)
        at_row = over(x, spread) * cy + y
        at_column = (rest_of(x, spread) * nz + z).T
        up = lax.broadcasted_iota(jnp.int32, (count, lanes), 0)
        along = lax.broadcasted_iota(jnp.int32, (lanes, spread * nz), 1)
        total = None
        for at in range(0, used, chunks):
            hits = []
            for c in range(chunks):
                hits.append(jnp.where(up == at_row[at + c : at + c + 1], 1.0, 0.0))
                to = pl.ds(pl.multiple_of((n * used + at + c) * lanes, lanes), lanes)
                chosen = at_column[:, at + c : at + c + 1] == along
                picks[to] = jnp.where(chosen, 1.0, 0.0).astype(jnp.bfloat16)
            to = pl.ds(pl.multiple_of((n * used + at) * lanes, lanes), chunks * lanes)
            term = jnp.dot(
                jnp.concatenate(hits, axis=1).astype(jnp.bfloat16),
                picks[to],
                preferred_element_type=jnp.float32,
            )
            total = term if total is None else total + term
        if nq == block:
            marks[...] = total
        else:
            marks[...] += total

    if nq != block:
        marks[...] = jnp.zeros_like(marks)
    each(nq // block, pick)
    for x in range(cx):
        rows = slice(x // spread * cy, (x // spread + 1) * cy)
        mark = marks[rows, x % spread * nz : (x % spread + 1) * nz]
        base[:, x] = jnp.where(mark[None] > 0.5, 0.0, cons[:, x])

    centre = jnp.ones((cx, cy, nz), jnp.float32)
    none = jnp.zeros((1, cy, nz), jnp.float32)
    low, high = face(vel[0, : cx - 1], vel[0, 1:])
    coefs[0] = jnp.concatenate([none, low], axis=0)
    coefs[1] = -jnp.concatenate([high, none], axis=0)
    centre += jnp.concatenate([none, high], axis=0) - jnp.concatenate([low, none], axis=0)

    at_y = lax.broadcasted_iota(jnp.int32, (1, cy, nz), 1)
    speed = vel[1]
    low, high = face(speed, pltpu.roll(speed, cy - 1, 1))
    low = jnp.where(at_y == cy - 1, 0.0, low)
    high = jnp.where(at_y == cy - 1, 0.0, high)
    coefs[2] = pltpu.roll(low, 1, 1)
    coefs[3] = -high
    centre += pltpu.roll(high, 1, 1) - low

    speed = vel[2]
    up_low, up_high = face(speed, along_z(speed, 1))
    down_low, down_high = face(along_z(speed, -1), speed)
    coefs[4] = down_low
    coefs[5] = -up_high
    coefs[6] = centre + down_high - up_low


def step_kernel(kinds, slots, ng, vel, aims, given, base, picks, received, *rest):
    halos = rest[: len(kinds)]
    out, coefs, ext, field, acc, result, sems = rest[len(kinds) :]
    nv, cx, cy, nz = base.shape
    lanes = nz
    nq = received.shape[0] // ng
    per = lanes // slots
    chunks = block // per
    used = (ng - 1) * chunks
    spread = 4 if cx % 4 == 0 else 1
    me = lax.axis_index("grp")
    lane = lax.broadcasted_iota(jnp.int32, (nv, lanes), 1) // slots
    above = [partner_above(axis, phase) for axis, phase, _ in kinds]

    parts = [(cx // spread * cy, spread)]
    parts += [(cy if axis == "gx" else cx, 1) for axis, _, _ in kinds]
    starts = [0]
    for count, groups in parts:
        starts.append(starts[-1] + (2 * nv + 1) * count * groups)

    def fill(n):
        for part, (count, groups) in enumerate(parts):
            if part == 0:
                cell = aims[pl.ds(n * block, block)]
            else:
                cell = halos[part - 1][pl.ds((nv + 3) * count + n * block, block)]
            cell = cell.astype(jnp.int32) + cx * cy * nz
            x, y, z = over(cell, nz * cy), rest_of(over(cell, nz), cy), rest_of(cell, nz)
            if part == 0:
                at_row = over(x, spread) * cy + y
            elif kinds[part - 1][0] == "gx":
                at_row = jnp.where(x == jnp.where(above[part - 1], 0, cx - 1), y, -1)
            else:
                at_row = jnp.where(y == jnp.where(above[part - 1], 0, cy - 1), x, -1)
            at_column = z.T
            up = lax.broadcasted_iota(jnp.int32, (count, lanes), 0)
            along = lax.broadcasted_iota(jnp.int32, (lanes, nz), 1)
            here = slice(part // per * lanes, (part // per + 1) * lanes)
            total = None
            for away in range(1, ng):
                g = (me + away) % ng
                lefts, chosen = [], []
                for c in range(chunks):
                    at = (away - 1) * chunks + c
                    value = None
                    for p in range(per):
                        piece = received[g * nq + n * block + p * chunks + c, :, here]
                        turn = (p - part) % per
                        if turn:
                            piece = pltpu.roll(piece, turn * slots, 1)
                        value = piece if value is None else jnp.where(lane == p, piece, value)
                    high = value.astype(jnp.bfloat16).astype(jnp.float32)
                    low = value - high
                    hit = up == at_row[at : at + 1]
                    pieces = [jnp.where(hit, high[v : v + 1], 0.0) for v in range(nv)]
                    pieces += [jnp.where(hit, low[v : v + 1], 0.0) for v in range(nv)]
                    if part:
                        pieces += [jnp.where(hit, 1.0, 0.0)]
                        pick = jnp.where(at_column[:, at : at + 1] == along, 1.0, 0.0)
                        chosen.append(pick.astype(jnp.bfloat16))
                    lefts.append(jnp.concatenate(pieces, axis=0).astype(jnp.bfloat16))
                if part:
                    chosen = jnp.concatenate(chosen, axis=0)
                else:
                    start = (n * used + (away - 1) * chunks) * lanes
                    chosen = picks[pl.ds(pl.multiple_of(start, lanes), chunks * lanes)]
                term = jnp.dot(
                    jnp.concatenate(lefts, axis=1), chosen, preferred_element_type=jnp.float32
                )
                total = term if total is None else total + term
            rows = total.shape[0]
            for s in range(groups):
                start = starts[part] + s * (2 * nv + 1) * count
                value = total[:, s * nz : (s + 1) * nz]
                if nq == block:
                    acc[start : start + rows] = value
                else:
                    acc[start : start + rows] += value

    if nq != block:
        acc[...] = jnp.zeros_like(acc)
    each(nq // block, fill)

    def brought(part, s):
        count = parts[part][0]
        start = starts[part] + s * (2 * nv + 1) * count
        new = acc[start : start + nv * count] + acc[start + nv * count : start + 2 * nv * count]
        return new.reshape(nv, count, nz)

    def crossed(n, speeds, fields):
        a, b = (n + 1) % 3, (n + 2) % 3
        return speeds[b] * fields[a] - speeds[a] * fields[b]

    inside = slice(top, top + cy)
    for s in range(spread):
        new = brought(0, s)
        for n, x in enumerate(range(s, cx, spread)):
            state = base[:, x] + new[:, n * cy : (n + 1) * cy]
            ext[:fluid_count, 1 + x, inside] = state[:fluid_count]
            field[:, x] = state[fluid_count:]
            for d in range(3):
                ext[fluid_count + d, 1 + x, inside] = crossed(d, vel[:, x], state[fluid_count:])

    sides = {("gx", True): 0.0, ("gx", False): 0.0, ("gy", True): 0.0, ("gy", False): 0.0}
    for n, (axis, _, _) in enumerate(kinds):
        count = parts[n + 1][0]
        d = 0 if axis == "gx" else 1
        halo = halos[n][: (nv + 3) * count].reshape(nv + 3, count, nz)
        mark = acc[starts[n + 1] + 2 * nv * count : starts[n + 1] + (2 * nv + 1) * count]
        state = jnp.where(mark[None] > 0.5, brought(n + 1, 0), halo[:nv])
        electric = [crossed(m, halo[nv:], state[fluid_count:])[None] for m in (1 - d, 2)]
        halo = jnp.concatenate([state[:fluid_count], halo[nv + d : nv + d + 1]] + electric, axis=0)
        sides[axis, True] += jnp.where(above[n], halo, 0.0)
        sides[axis, False] += jnp.where(above[n], 0.0, halo)

    coefs[...] = given[...]
    for (axis, high), halo in sides.items():
        d = 0 if axis == "gx" else 1
        halo = jnp.broadcast_to(halo, (fluid_count + 3, cx if d else cy, nz))
        if d == 0:
            at = (cx + 1 if high else 0, inside)
            edge = (cx - 1 if high else 0,)
        else:
            at = (slice(1, cx + 1), top + cy if high else top - 1)
            edge = (slice(None), cy - 1 if high else 0)
        ext[(slice(0, fluid_count),) + at] = halo[:fluid_count]
        ext[(fluid_count + 1 - d,) + at] = halo[fluid_count + 1]
        ext[(fluid_count + 2,) + at] = halo[fluid_count + 2]
        speed = vel[(d,) + edge]
        if high:
            of_low, of_high = face(speed, halo[fluid_count])
            coefs[(2 * d + 1,) + edge] = -of_high
            coefs[(6,) + edge] -= of_low
        else:
            of_low, of_high = face(halo[fluid_count], speed)
            coefs[(2 * d,) + edge] = of_low
            coefs[(6,) + edge] += of_high

    copies = []

    def finish(v, value):
        result[v] = value
        copies.append(pltpu.make_async_copy(result.at[v], out.at[v], sems.at[v]))
        copies[-1].start()

    def central(n, d):
        v = fluid_count + n
        return shifted(ext, v, cx, cy, d, 1) - shifted(ext, v, cx, cy, d, -1)

    for n in range(3):
        a, b = (n + 1) % 3, (n + 2) % 3
        curl = central(b, a) - central(a, b)
        finish(fluid_count + n, field[n] - (0.5 * courant_number) * curl)
    for v in range(fluid_count):
        total = coefs[6] * window(ext, v, cx, cy)
        for d in range(3):
            total = total + coefs[2 * d] * shifted(ext, v, cx, cy, d, -1)
            total = total + coefs[2 * d + 1] * shifted(ext, v, cx, cy, d, 1)
        finish(v, total)
    for copy in copies:
        copy.wait()


def per_device(ngx, ngy, conserved, velocity, donor_corner, donor_fraction, target_cell):
    kinds = exchanges(ngx, ngy)
    cons = conserved[:, 0]
    vel = velocity[:, 0]
    corner = donor_corner[0, 0, 0]
    fraction = donor_fraction[:, 0, 0, 0]
    target = target_cell[0, 0, 0]
    nv, cx, cy, nz = cons.shape
    ng, nq, slots = corner.shape
    rows = cx * cy
    per = nz // slots
    tiles = -(-(1 + len(kinds)) // per)
    f32 = jnp.float32

    def shape(*dims):
        return jax.ShapeDtypeStruct(dims, f32)

    params = pltpu.CompilerParams(vmem_limit_bytes=(12 + nq // 2) << 20)
    alongs = [cy if axis == "gx" else cx for axis, _, _ in kinds]
    pay_shapes = [((nv + 3) * along + nq, nz) for along in alongs]
    blended, state = pl.pallas_call(
        functools.partial(blend_kernel, ngy, kinds),
        out_shape=[pltpu.VMEM((ng * nq, nv, tiles * nz), f32), pltpu.VMEM(cons.shape, f32)],
        in_specs=[pl.BlockSpec(memory_space=pl.ANY)] * 3,
        scratch_shapes=[
            pltpu.VMEM(corner.shape, jnp.int32),
            pltpu.VMEM(fraction.shape, f32),
            pltpu.VMEM((nv * rows, 2 * nz), jnp.bfloat16),
            pltpu.VMEM((ng - 1, 3 * nz, block * slots), jnp.bfloat16),
            pltpu.VMEM((ng - 1, rows, block * slots), f32),
            pltpu.VMEM((ng - 1, per, nq // per, nv, nz), f32),
            pltpu.SemaphoreType.DMA((2 + nv,)),
        ],
        compiler_params=params,
        name="blend",
    )(*(pltpu.with_memory_space_constraint(value, pltpu.HBM) for value in (cons, corner, fraction)))

    state = pltpu.with_memory_space_constraint(state, pltpu.VMEM)
    aims, *pays = pl.pallas_call(
        functools.partial(edge_kernel, kinds),
        out_shape=[pltpu.VMEM((nq, nz), f32)] + [pltpu.VMEM(dims, f32) for dims in pay_shapes],
        in_specs=[pl.BlockSpec(memory_space=pltpu.VMEM)] * 3 + [pl.BlockSpec(memory_space=pl.ANY)],
        compiler_params=params,
        name="edge",
    )(state, vel, target, blended)

    received = lax.all_to_all(
        blended, ("grp", "gx", "gy"), split_axis=0, concat_axis=0, tiled=True
    )
    halos = []
    for (axis, phase, _), pay in zip(kinds, pays):
        count = ngx if axis == "gx" else ngy
        pairs = []
        for low in range(phase, count - 1, 2):
            pairs += [(low, low + 1), (low + 1, low)]
        halos.append(lax.ppermute(pay, axis, pairs))

    spread = 4 if cx % 4 == 0 else 1
    coefs, base, picks = pl.pallas_call(
        functools.partial(prepare_kernel, slots, ng),
        out_shape=[
            pltpu.VMEM((7, cx, cy, nz), f32),
            pltpu.VMEM((nv, cx, cy, nz), f32),
            pltpu.VMEM(((ng - 1) * nq * slots, spread * nz), jnp.bfloat16),
        ],
        scratch_shapes=[pltpu.VMEM((rows // spread, spread * nz), f32)],
        compiler_params=params,
        name="prepare",
    )(state, vel, aims)
    coefs, base, picks = (
        pltpu.with_memory_space_constraint(value, pltpu.VMEM) for value in (coefs, base, picks)
    )

    result = pl.pallas_call(
        functools.partial(step_kernel, kinds, slots, ng),
        out_shape=shape(nv, cx, cy, nz),
        out_specs=pl.BlockSpec(memory_space=pl.ANY),
        scratch_shapes=[
            pltpu.VMEM((7, cx, cy, nz), f32),
            pltpu.VMEM((fluid_count + 3, cx + 2, cy + 2 * top, nz), f32),
            pltpu.VMEM((nv - fluid_count, cx, cy, nz), f32),
            pltpu.VMEM(((2 * nv + 1) * (rows + sum(alongs)), nz), f32),
            pltpu.VMEM((nv, cx, cy, nz), f32),
            pltpu.SemaphoreType.DMA((nv,)),
        ],
        compiler_params=params,
        name="step",
    )(vel, aims, coefs, base, picks, received, *halos)
    return result[:, None]


def solution(mesh):
    return jax.shard_map(
        functools.partial(per_device, mesh.shape["gx"], mesh.shape["gy"]),
        mesh=mesh,
        in_specs=(
            P(None, "grp", "gx", "gy", None),
            P(None, "grp", "gx", "gy", None),
            P("grp", "gx", "gy", None, None, None),
            P(None, "grp", "gx", "gy", None, None, None),
            P("grp", "gx", "gy", None, None, None),
        ),
        out_specs=P(None, "grp", "gx", "gy", None),
        check_vma=False,
    )
```

```python
import functools

import jax
import jax.numpy as jnp
from jax import lax
from jax.experimental import pallas as pl
from jax.experimental.pallas import tpu as pltpu
from jax.sharding import PartitionSpec as P

signal_speed = 0.5
courant_number = 0.3
fluid_count = 5
block = 8


def exchanges(ngx, ngy):
    def partner(count, phase, n):
        other = n + 1 if (n + phase) % 2 == 0 else n - 1
        return other if 0 <= other < count else n

    kinds = []
    for phase in range(min(ngx - 1, 2)):
        kinds.append(("gx", phase, lambda i, j, phase=phase: (partner(ngx, phase, i), j)))
    for phase in range(min(ngy - 1, 2)):
        kinds.append(("gy", phase, lambda i, j, phase=phase: (i, partner(ngy, phase, j))))
    return kinds


def partner_above(axis, phase):
    return (lax.axis_index(axis) + phase) % 2 == 0


def split(value):
    high = value.astype(jnp.bfloat16)
    low = (value - high.astype(jnp.float32)).astype(jnp.bfloat16)
    return high, low


def over(value, n):
    return value >> (n.bit_length() - 1) if n & (n - 1) == 0 else value // n


def rest_of(value, n):
    return value & (n - 1) if n & (n - 1) == 0 else value % n


def each(count, body):
    if count == 1:
        body(0)
    else:
        lax.fori_loop(0, count, lambda n, c: (body(n), c)[1], 0)


def block_transpose(value, slots):
    rows, lanes = value.shape
    count = lanes // slots
    each_rows = rows // count
    at_row = lax.broadcasted_iota(jnp.int32, value.shape, 0) // each_rows
    at_lane = lax.broadcasted_iota(jnp.int32, value.shape, 1) // slots
    result = value
    for d in range(1, count):
        turned = pltpu.roll(value, d * each_rows, 0)
        turned = pltpu.roll(turned, lanes - d * slots, 1)
        result = jnp.where((at_row - at_lane) % count == d, turned, result)
    return result


def packed(tiles, slots):
    empty = jnp.zeros(tiles[0].shape, tiles[0].dtype)
    return block_transpose(jnp.concatenate(tiles + [empty], axis=1), slots)


def blend_kernel(ngy, kinds, cons, corner, fraction, out, at_cons, *scratch):
    at_corner, at_fraction, uhl, places, parts, moved, arrive = scratch
    nv, cx, cy, nz = cons.shape
    ng, nq, slots = corner.shape
    lanes = nz
    per = lanes // slots
    chunks = block // per
    rows = cx * cy
    me = lax.axis_index("grp")

    moves = [(corner, at_corner), (fraction, at_fraction)]
    moves += [(cons.at[v], at_cons.at[v]) for v in range(nv)]
    ins = [pltpu.make_async_copy(a, b, arrive.at[n]) for n, (a, b) in enumerate(moves)]
    for copy in ins:
        copy.start()

    out[pl.ds(me * nq, nq)] = jnp.zeros((nq,) + out.shape[1:], jnp.float32)

    def weight(count, at, upper):
        place = lax.broadcasted_iota(jnp.int32, (count, lanes), 0)
        return jnp.where(place == at, 1.0 - upper, jnp.where(place == at + 1, upper, 0.0))

    def weigh(n):
        here = pl.ds(n * block, block)
        grids = [(me + away) % ng for away in range(1, ng)]
        cell = packed([at_corner[h, here] for h in grids], slots)
        places[0], places[1], places[2] = (
            over(cell, nz * cy),
            rest_of(over(cell, nz), cy),
            rest_of(cell, nz),
        )
        for d in range(3):
            parts[d] = packed([at_fraction[d, h, here] for h in grids], slots)

    def made(at):
        row = pl.ds(at, 1)
        wx = weight(cx, places[0, row], parts[0, row])
        wy = weight(cy, places[1, row], parts[1, row])
        wxy = jnp.concatenate([wx[x : x + 1] * wy for x in range(cx)], axis=0)
        return split(weight(nz, places[2, row], parts[2, row])) + (wxy,)

    def blend(n, away):
        factors = [made((away - 1) * chunks + c) for c in range(chunks)]
        wh, wl, wxy = (jnp.concatenate(group, axis=1) for group in zip(*factors))
        both = jnp.dot(
            uhl[...], jnp.concatenate([wh, wh], axis=0), preferred_element_type=jnp.float32
        )
        small = jnp.dot(uhl[:, :nz], wl, preferred_element_type=jnp.float32)
        along = (both + small).reshape(nv, rows, chunks * lanes)
        values = jnp.sum(along * wxy[None], axis=1)
        for c in range(chunks):
            value = values[:, c * lanes : (c + 1) * lanes]
            for turn in range(per):
                moved[away - 1, turn, n * chunks + c] = (
                    pltpu.roll(value, turn * slots, 1) if turn else value
                )

    lane = lax.broadcasted_iota(jnp.int32, (nv, lanes), 1) // slots

    def assemble(away):
        for q in range(nq):
            i, j = q // ngy, q % ngy
            owners = [q] + [a * ngy + b for a, b in (of(i, j) for _, _, of in kinds)]
            for t in range(0, len(owners), per):
                tile = None
                for k, owner in enumerate(owners[t : t + per]):
                    chunk = owner // block * chunks + owner % chunks
                    piece = moved[away - 1, (k - owner % block // chunks) % per, chunk]
                    tile = piece if tile is None else jnp.where(lane == k, piece, tile)
                cols = slice(t // per * lanes, (t // per + 1) * lanes)
                out[pl.ds((me + away) % ng * nq + q, 1), :, cols] = tile[None]

    for copy in ins[:2]:
        copy.wait()
    if nq == block:
        weigh(0)
    for v in range(nv):
        ins[2 + v].wait()
        high, low = split(at_cons[v].reshape(rows, nz))
        here = slice(v * rows, (v + 1) * rows)
        uhl[here, :nz] = high
        uhl[here, nz:] = low
    if nq == block:

        def grid(away, carry):
            blend(0, away)
            assemble(away)
            return carry

        lax.fori_loop(1, ng, grid, 0)
    else:

        def part(n):
            weigh(n)
            for away in range(1, ng):
                blend(n, away)

        each(nq // block, part)
        for away in range(1, ng):
            assemble(away)


def edge_kernel(kinds, cons, vel, target, sent, aims, *pays):
    del sent
    nv, cx, cy, nz = cons.shape
    ng, nq, slots = target.shape
    me = lax.axis_index("grp")
    for n in range(nq // block):
        here = slice(n * block, (n + 1) * block)
        tiles = [target[(me + away) % ng, here] - cx * cy * nz for away in range(1, ng)]
        aims[here] = packed(tiles, slots).astype(jnp.float32)
    for (axis, phase, _), pay in zip(kinds, pays):
        above = partner_above(axis, phase)
        along = cy if axis == "gx" else cx
        for count, source, start in ((nv, cons, 0), (3, vel, nv * along)):
            if axis == "gx":
                layer = source[:, pl.ds(jnp.where(above, cx - 1, 0), 1)]
            else:
                layer = source[:, :, pl.ds(jnp.where(above, cy - 1, 0), 1)]
            pay[start : start + count * along] = layer.reshape(count * along, nz)
        pay[(nv + 3) * along :] = aims[...]


top = 8


def window(ext, v, cx, cy, move_x=0, move_y=0):
    return ext[v, 1 + move_x : 1 + move_x + cx, top + move_y : top + move_y + cy]


def along_z(value, by):
    nz = value.shape[-1]
    at = lax.broadcasted_iota(jnp.int32, (1,) + value.shape[1:], 2)
    edge = 0 if by < 0 else nz - 1
    return jnp.where(at == edge, 0.0, pltpu.roll(value, (-by) % nz, 2))


def shifted(ext, v, cx, cy, d, by):
    if d == 2 and by:
        return along_z(window(ext, v, cx, cy), by)
    return window(ext, v, cx, cy, by if d == 0 else 0, by if d == 1 else 0)


def face(low, high):
    wave_low = jnp.minimum(jnp.minimum(low, high) - signal_speed, 0.0)
    wave_high = jnp.maximum(jnp.maximum(low, high) + signal_speed, 0.0)
    scale = courant_number / (wave_high - wave_low)
    return (
        scale * wave_high * (low - wave_low),
        scale * wave_low * (wave_high - high),
    )


def prepare_kernel(slots, ng, cons, vel, aims, coefs, base, picks, marks):
    nv, cx, cy, nz = cons.shape
    lanes = nz
    per = lanes // slots
    chunks = block // per
    nq = aims.shape[0]
    spread = 4 if cx % 4 == 0 else 1
    count = cx // spread * cy
    used = (ng - 1) * chunks

    def pick(n):
        cell = aims[pl.ds(n * block, block)].astype(jnp.int32) + cx * cy * nz
        x, y, z = over(cell, nz * cy), rest_of(over(cell, nz), cy), rest_of(cell, nz)
        at_row = over(x, spread) * cy + y
        at_column = (rest_of(x, spread) * nz + z).T
        up = lax.broadcasted_iota(jnp.int32, (count, lanes), 0)
        along = lax.broadcasted_iota(jnp.int32, (lanes, spread * nz), 1)
        total = None
        for at in range(0, used, chunks):
            hits = []
            for c in range(chunks):
                hits.append(jnp.where(up == at_row[at + c : at + c + 1], 1.0, 0.0))
                to = pl.ds(pl.multiple_of((n * used + at + c) * lanes, lanes), lanes)
                chosen = at_column[:, at + c : at + c + 1] == along
                picks[to] = jnp.where(chosen, 1.0, 0.0).astype(jnp.bfloat16)
            to = pl.ds(pl.multiple_of((n * used + at) * lanes, lanes), chunks * lanes)
            term = jnp.dot(
                jnp.concatenate(hits, axis=1).astype(jnp.bfloat16),
                picks[to],
                preferred_element_type=jnp.float32,
            )
            total = term if total is None else total + term
        if nq == block:
            marks[...] = total
        else:
            marks[...] += total

    if nq != block:
        marks[...] = jnp.zeros_like(marks)
    each(nq // block, pick)
    for x in range(cx):
        rows = slice(x // spread * cy, (x // spread + 1) * cy)
        mark = marks[rows, x % spread * nz : (x % spread + 1) * nz]
        base[:, x] = jnp.where(mark[None] > 0.5, 0.0, cons[:, x])

    centre = jnp.ones((cx, cy, nz), jnp.float32)
    none = jnp.zeros((1, cy, nz), jnp.float32)
    low, high = face(vel[0, : cx - 1], vel[0, 1:])
    coefs[0] = jnp.concatenate([none, low], axis=0)
    coefs[1] = -jnp.concatenate([high, none], axis=0)
    centre += jnp.concatenate([none, high], axis=0) - jnp.concatenate([low, none], axis=0)

    at_y = lax.broadcasted_iota(jnp.int32, (1, cy, nz), 1)
    speed = vel[1]
    low, high = face(speed, pltpu.roll(speed, cy - 1, 1))
    low = jnp.where(at_y == cy - 1, 0.0, low)
    high = jnp.where(at_y == cy - 1, 0.0, high)
    coefs[2] = pltpu.roll(low, 1, 1)
    coefs[3] = -high
    centre += pltpu.roll(high, 1, 1) - low

    speed = vel[2]
    up_low, up_high = face(speed, along_z(speed, 1))
    down_low, down_high = face(along_z(speed, -1), speed)
    coefs[4] = down_low
    coefs[5] = -up_high
    coefs[6] = centre + down_high - up_low


def step_kernel(kinds, slots, ng, vel, aims, given, base, picks, received, *rest):
    halos = rest[: len(kinds)]
    out, coefs, ext, field, acc, result, sems = rest[len(kinds) :]
    nv, cx, cy, nz = base.shape
    lanes = nz
    nq = received.shape[0] // ng
    per = lanes // slots
    chunks = block // per
    used = (ng - 1) * chunks
    spread = 4 if cx % 4 == 0 else 1
    me = lax.axis_index("grp")
    lane = lax.broadcasted_iota(jnp.int32, (nv, lanes), 1) // slots
    above = [partner_above(axis, phase) for axis, phase, _ in kinds]

    parts = [(cx // spread * cy, spread)]
    parts += [(cy if axis == "gx" else cx, 1) for axis, _, _ in kinds]
    starts = [0]
    for count, groups in parts:
        starts.append(starts[-1] + (2 * nv + 1) * count * groups)

    def fill(n):
        for part, (count, groups) in enumerate(parts):
            if part == 0:
                cell = aims[pl.ds(n * block, block)]
            else:
                cell = halos[part - 1][pl.ds((nv + 3) * count + n * block, block)]
            cell = cell.astype(jnp.int32) + cx * cy * nz
            x, y, z = over(cell, nz * cy), rest_of(over(cell, nz), cy), rest_of(cell, nz)
            if part == 0:
                at_row = over(x, spread) * cy + y
            elif kinds[part - 1][0] == "gx":
                at_row = jnp.where(x == jnp.where(above[part - 1], 0, cx - 1), y, -1)
            else:
                at_row = jnp.where(y == jnp.where(above[part - 1], 0, cy - 1), x, -1)
            at_column = z.T
            up = lax.broadcasted_iota(jnp.int32, (count, lanes), 0)
            along = lax.broadcasted_iota(jnp.int32, (lanes, nz), 1)
            here = slice(part // per * lanes, (part // per + 1) * lanes)
            total = None
            for away in range(1, ng):
                g = (me + away) % ng
                lefts, chosen = [], []
                for c in range(chunks):
                    at = (away - 1) * chunks + c
                    value = None
                    for p in range(per):
                        piece = received[g * nq + n * block + p * chunks + c, :, here]
                        turn = (p - part) % per
                        if turn:
                            piece = pltpu.roll(piece, turn * slots, 1)
                        value = piece if value is None else jnp.where(lane == p, piece, value)
                    high = value.astype(jnp.bfloat16).astype(jnp.float32)
                    low = value - high
                    hit = up == at_row[at : at + 1]
                    pieces = [jnp.where(hit, high[v : v + 1], 0.0) for v in range(nv)]
                    pieces += [jnp.where(hit, low[v : v + 1], 0.0) for v in range(nv)]
                    if part:
                        pieces += [jnp.where(hit, 1.0, 0.0)]
                        pick = jnp.where(at_column[:, at : at + 1] == along, 1.0, 0.0)
                        chosen.append(pick.astype(jnp.bfloat16))
                    lefts.append(jnp.concatenate(pieces, axis=0).astype(jnp.bfloat16))
                if part:
                    chosen = jnp.concatenate(chosen, axis=0)
                else:
                    start = (n * used + (away - 1) * chunks) * lanes
                    chosen = picks[pl.ds(pl.multiple_of(start, lanes), chunks * lanes)]
                term = jnp.dot(
                    jnp.concatenate(lefts, axis=1), chosen, preferred_element_type=jnp.float32
                )
                total = term if total is None else total + term
            rows = total.shape[0]
            for s in range(groups):
                start = starts[part] + s * (2 * nv + 1) * count
                value = total[:, s * nz : (s + 1) * nz]
                if nq == block:
                    acc[start : start + rows] = value
                else:
                    acc[start : start + rows] += value

    if nq != block:
        acc[...] = jnp.zeros_like(acc)
    each(nq // block, fill)

    def brought(part, s):
        count = parts[part][0]
        start = starts[part] + s * (2 * nv + 1) * count
        new = acc[start : start + nv * count] + acc[start + nv * count : start + 2 * nv * count]
        return new.reshape(nv, count, nz)

    def crossed(n, speeds, fields):
        a, b = (n + 1) % 3, (n + 2) % 3
        return speeds[b] * fields[a] - speeds[a] * fields[b]

    inside = slice(top, top + cy)
    for s in range(spread):
        new = brought(0, s)
        for n, x in enumerate(range(s, cx, spread)):
            state = base[:, x] + new[:, n * cy : (n + 1) * cy]
            ext[:fluid_count, 1 + x, inside] = state[:fluid_count]
            field[:, x] = state[fluid_count:]
            for d in range(3):
                ext[fluid_count + d, 1 + x, inside] = crossed(d, vel[:, x], state[fluid_count:])

    sides = {("gx", True): 0.0, ("gx", False): 0.0, ("gy", True): 0.0, ("gy", False): 0.0}
    for n, (axis, _, _) in enumerate(kinds):
        count = parts[n + 1][0]
        d = 0 if axis == "gx" else 1
        halo = halos[n][: (nv + 3) * count].reshape(nv + 3, count, nz)
        mark = acc[starts[n + 1] + 2 * nv * count : starts[n + 1] + (2 * nv + 1) * count]
        state = jnp.where(mark[None] > 0.5, brought(n + 1, 0), halo[:nv])
        electric = [crossed(m, halo[nv:], state[fluid_count:])[None] for m in (1 - d, 2)]
        halo = jnp.concatenate([state[:fluid_count], halo[nv + d : nv + d + 1]] + electric, axis=0)
        sides[axis, True] += jnp.where(above[n], halo, 0.0)
        sides[axis, False] += jnp.where(above[n], 0.0, halo)

    coefs[...] = given[...]
    for (axis, high), halo in sides.items():
        d = 0 if axis == "gx" else 1
        halo = jnp.broadcast_to(halo, (fluid_count + 3, cx if d else cy, nz))
        if d == 0:
            at = (cx + 1 if high else 0, inside)
            edge = (cx - 1 if high else 0,)
        else:
            at = (slice(1, cx + 1), top + cy if high else top - 1)
            edge = (slice(None), cy - 1 if high else 0)
        ext[(slice(0, fluid_count),) + at] = halo[:fluid_count]
        ext[(fluid_count + 1 - d,) + at] = halo[fluid_count + 1]
        ext[(fluid_count + 2,) + at] = halo[fluid_count + 2]
        speed = vel[(d,) + edge]
        if high:
            of_low, of_high = face(speed, halo[fluid_count])
            coefs[(2 * d + 1,) + edge] = -of_high
            coefs[(6,) + edge] -= of_low
        else:
            of_low, of_high = face(halo[fluid_count], speed)
            coefs[(2 * d,) + edge] = of_low
            coefs[(6,) + edge] += of_high

    copies = []

    def finish(v, value):
        result[v] = value
        copies.append(pltpu.make_async_copy(result.at[v], out.at[v], sems.at[v]))
        copies[-1].start()

    def central(n, d):
        v = fluid_count + n
        return shifted(ext, v, cx, cy, d, 1) - shifted(ext, v, cx, cy, d, -1)

    for n in range(3):
        a, b = (n + 1) % 3, (n + 2) % 3
        curl = central(b, a) - central(a, b)
        finish(fluid_count + n, field[n] - (0.5 * courant_number) * curl)
    for v in range(fluid_count):
        total = coefs[6] * window(ext, v, cx, cy)
        for d in range(3):
            total = total + coefs[2 * d] * shifted(ext, v, cx, cy, d, -1)
            total = total + coefs[2 * d + 1] * shifted(ext, v, cx, cy, d, 1)
        finish(v, total)
    for copy in copies:
        copy.wait()


def per_device(ngx, ngy, conserved, velocity, donor_corner, donor_fraction, target_cell):
    kinds = exchanges(ngx, ngy)
    cons = conserved[:, 0]
    vel = velocity[:, 0]
    corner = donor_corner[0, 0, 0]
    fraction = donor_fraction[:, 0, 0, 0]
    target = target_cell[0, 0, 0]
    nv, cx, cy, nz = cons.shape
    ng, nq, slots = corner.shape
    rows = cx * cy
    per = nz // slots
    tiles = -(-(1 + len(kinds)) // per)
    f32 = jnp.float32

    def shape(*dims):
        return jax.ShapeDtypeStruct(dims, f32)

    params = pltpu.CompilerParams(vmem_limit_bytes=(12 + nq // 2) << 20)
    alongs = [cy if axis == "gx" else cx for axis, _, _ in kinds]
    pay_shapes = [((nv + 3) * along + nq, nz) for along in alongs]
    blended, state = pl.pallas_call(
        functools.partial(blend_kernel, ngy, kinds),
        out_shape=[pltpu.VMEM((ng * nq, nv, tiles * nz), f32), pltpu.VMEM(cons.shape, f32)],
        in_specs=[pl.BlockSpec(memory_space=pl.ANY)] * 3,
        scratch_shapes=[
            pltpu.VMEM(corner.shape, jnp.int32),
            pltpu.VMEM(fraction.shape, f32),
            pltpu.VMEM((nv * rows, 2 * nz), jnp.bfloat16),
            pltpu.VMEM((3, block, nz), jnp.int32),
            pltpu.VMEM((3, block, nz), f32),
            pltpu.VMEM((ng - 1, per, nq // per, nv, nz), f32),
            pltpu.SemaphoreType.DMA((2 + nv,)),
        ],
        compiler_params=params,
        name="blend",
    )(*(pltpu.with_memory_space_constraint(value, pltpu.HBM) for value in (cons, corner, fraction)))

    state = pltpu.with_memory_space_constraint(state, pltpu.VMEM)
    aims, *pays = pl.pallas_call(
        functools.partial(edge_kernel, kinds),
        out_shape=[pltpu.VMEM((nq, nz), f32)] + [pltpu.VMEM(dims, f32) for dims in pay_shapes],
        in_specs=[pl.BlockSpec(memory_space=pltpu.VMEM)] * 3 + [pl.BlockSpec(memory_space=pl.ANY)],
        compiler_params=params,
        name="edge",
    )(state, vel, target, blended)

    received = lax.all_to_all(
        blended, ("grp", "gx", "gy"), split_axis=0, concat_axis=0, tiled=True
    )
    halos = []
    for (axis, phase, _), pay in zip(kinds, pays):
        count = ngx if axis == "gx" else ngy
        pairs = []
        for low in range(phase, count - 1, 2):
            pairs += [(low, low + 1), (low + 1, low)]
        halos.append(lax.ppermute(pay, axis, pairs))

    spread = 4 if cx % 4 == 0 else 1
    coefs, base, picks = pl.pallas_call(
        functools.partial(prepare_kernel, slots, ng),
        out_shape=[
            pltpu.VMEM((7, cx, cy, nz), f32),
            pltpu.VMEM((nv, cx, cy, nz), f32),
            pltpu.VMEM(((ng - 1) * nq * slots, spread * nz), jnp.bfloat16),
        ],
        scratch_shapes=[pltpu.VMEM((rows // spread, spread * nz), f32)],
        compiler_params=params,
        name="prepare",
    )(state, vel, aims)
    coefs, base, picks = (
        pltpu.with_memory_space_constraint(value, pltpu.VMEM) for value in (coefs, base, picks)
    )

    result = pl.pallas_call(
        functools.partial(step_kernel, kinds, slots, ng),
        out_shape=shape(nv, cx, cy, nz),
        out_specs=pl.BlockSpec(memory_space=pl.ANY),
        scratch_shapes=[
            pltpu.VMEM((7, cx, cy, nz), f32),
            pltpu.VMEM((fluid_count + 3, cx + 2, cy + 2 * top, nz), f32),
            pltpu.VMEM((nv - fluid_count, cx, cy, nz), f32),
            pltpu.VMEM(((2 * nv + 1) * (rows + sum(alongs)), nz), f32),
            pltpu.VMEM((nv, cx, cy, nz), f32),
            pltpu.SemaphoreType.DMA((nv,)),
        ],
        compiler_params=params,
        name="step",
    )(vel, aims, coefs, base, picks, received, *halos)
    return result[:, None]


def solution(mesh):
    return jax.shard_map(
        functools.partial(per_device, mesh.shape["gx"], mesh.shape["gy"]),
        mesh=mesh,
        in_specs=(
            P(None, "grp", "gx", "gy", None),
            P(None, "grp", "gx", "gy", None),
            P("grp", "gx", "gy", None, None, None),
            P(None, "grp", "gx", "gy", None, None, None),
            P("grp", "gx", "gy", None, None, None),
        ),
        out_specs=P(None, "grp", "gx", "gy", None),
        check_vma=False,
    )
```

```python
import functools

import jax
import jax.numpy as jnp
from jax import lax
from jax.experimental import pallas as pl
from jax.experimental.pallas import tpu as pltpu
from jax.sharding import PartitionSpec as P

signal_speed = 0.5
courant_number = 0.3
fluid_count = 5
block = 8


def exchanges(ngx, ngy):
    def partner(count, phase, n):
        other = n + 1 if (n + phase) % 2 == 0 else n - 1
        return other if 0 <= other < count else n

    kinds = []
    for phase in range(min(ngx - 1, 2)):
        kinds.append(("gx", phase, lambda i, j, phase=phase: (partner(ngx, phase, i), j)))
    for phase in range(min(ngy - 1, 2)):
        kinds.append(("gy", phase, lambda i, j, phase=phase: (i, partner(ngy, phase, j))))
    return kinds


def partner_above(axis, phase):
    return (lax.axis_index(axis) + phase) % 2 == 0


def split(value):
    high = value.astype(jnp.bfloat16)
    low = (value - high.astype(jnp.float32)).astype(jnp.bfloat16)
    return high, low


def over(value, n):
    return value >> (n.bit_length() - 1) if n & (n - 1) == 0 else value // n


def rest_of(value, n):
    return value & (n - 1) if n & (n - 1) == 0 else value % n


def each(count, body):
    if count == 1:
        body(0)
    else:
        lax.fori_loop(0, count, lambda n, c: (body(n), c)[1], 0)


def block_transpose(value, slots):
    rows, lanes = value.shape
    count = lanes // slots
    each_rows = rows // count
    at_row = lax.broadcasted_iota(jnp.int32, value.shape, 0) // each_rows
    at_lane = lax.broadcasted_iota(jnp.int32, value.shape, 1) // slots
    result = value
    for d in range(1, count):
        turned = pltpu.roll(value, d * each_rows, 0)
        turned = pltpu.roll(turned, lanes - d * slots, 1)
        result = jnp.where((at_row - at_lane) % count == d, turned, result)
    return result


def place(ng, ngx, ngy, grid, q):
    return (q % ngy * ng + grid) * ngx + q // ngy


def packed(tiles, slots):
    empty = jnp.zeros(tiles[0].shape, tiles[0].dtype)
    return block_transpose(jnp.concatenate(tiles + [empty], axis=1), slots)


def blend_kernel(ngy, kinds, cons, corner, fraction, out, *scratch):
    at_cons, at_corner, at_fraction, uhl, wzs, wxys, moved, arrive = scratch
    nv, cx, cy, nz = cons.shape
    ng, nq, slots = corner.shape
    lanes = nz
    per = lanes // slots
    chunks = block // per
    rows = cx * cy
    me = lax.axis_index("grp")

    moves = [(corner, at_corner), (fraction, at_fraction), (cons, at_cons)]
    ins = [pltpu.make_async_copy(a, b, arrive.at[n]) for n, (a, b) in enumerate(moves)]
    for copy in ins:
        copy.start()

    for q in range(nq):
        at = place(ng, nq // ngy, ngy, me, q)
        out[pl.ds(at, 1)] = jnp.zeros((1,) + out.shape[1:], jnp.float32)

    def weight(count, at, upper):
        place = lax.broadcasted_iota(jnp.int32, (count, lanes), 0)
        return jnp.where(place == at, 1.0 - upper, jnp.where(place == at + 1, upper, 0.0))

    def weigh(n):
        here = pl.ds(n * block, block)
        grids = [(me + away) % ng for away in range(1, ng)]
        cell = packed([at_corner[h, here] for h in grids], slots)
        at_x, at_y, at_z = over(cell, nz * cy), rest_of(over(cell, nz), cy), rest_of(cell, nz)
        fx, fy, fz = (packed([at_fraction[d, h, here] for h in grids], slots) for d in range(3))
        for away in range(1, ng):
            for c in range(chunks):
                row = slice((away - 1) * chunks + c, (away - 1) * chunks + c + 1)
                cols = slice(c * lanes, (c + 1) * lanes)
                wx = weight(cx, at_x[row], fx[row])
                wy = weight(cy, at_y[row], fy[row])
                for x in range(cx):
                    wxys[away - 1, x * cy : (x + 1) * cy, cols] = wx[x : x + 1] * wy
                high, low = split(weight(nz, at_z[row], fz[row]))
                wzs[away - 1, :nz, cols] = high
                wzs[away - 1, nz : 2 * nz, cols] = high
                wzs[away - 1, 2 * nz :, cols] = low

    def blend(n):
        for away in range(1, ng):
            along = jnp.dot(uhl[...], wzs[away - 1], preferred_element_type=jnp.float32)
            along = along.reshape(nv, rows, chunks * lanes)
            values = jnp.sum(along * wxys[away - 1][None], axis=1)
            for c in range(chunks):
                value = values[:, c * lanes : (c + 1) * lanes]
                for turn in range(per):
                    moved[away - 1, turn, n * chunks + c] = (
                        pltpu.roll(value, turn * slots, 1) if turn else value
                    )
            if nq == block:
                assemble(away)

    lane = lax.broadcasted_iota(jnp.int32, (nv, lanes), 1) // slots

    def assemble(away):
        for q in range(nq):
            i, j = q // ngy, q % ngy
            owners = [q] + [a * ngy + b for a, b in (of(i, j) for _, _, of in kinds)]
            for t in range(0, len(owners), per):
                tile = None
                for k, owner in enumerate(owners[t : t + per]):
                    chunk = owner // block * chunks + owner % chunks
                    piece = moved[away - 1, (k - owner % block // chunks) % per, chunk]
                    tile = piece if tile is None else jnp.where(lane == k, piece, tile)
                cols = slice(t // per * lanes, (t // per + 1) * lanes)
                at = place(ng, nq // ngy, ngy, (me + away) % ng, q)
                out[pl.ds(at, 1), :, cols] = tile[None]

    for copy in ins[:2]:
        copy.wait()
    if nq == block:
        weigh(0)
    ins[2].wait()
    high, low = split(at_cons[...].reshape(nv * rows, nz))
    uhl[:, :nz] = high
    uhl[:, nz : 2 * nz] = low
    uhl[:, 2 * nz :] = high
    if nq == block:
        blend(0)
    else:

        def both(n):
            weigh(n)
            blend(n)

        each(nq // block, both)
        for away in range(1, ng):
            assemble(away)


def edge_kernel(kinds, cons, vel, target, sent, aims, *pays):
    del sent
    nv, cx, cy, nz = cons.shape
    ng, nq, slots = target.shape
    me = lax.axis_index("grp")
    for n in range(nq // block):
        here = slice(n * block, (n + 1) * block)
        tiles = [target[(me + away) % ng, here] - cx * cy * nz for away in range(1, ng)]
        aims[here] = packed(tiles, slots).astype(jnp.float32)
    for (axis, phase, _), pay in zip(kinds, pays):
        above = partner_above(axis, phase)
        along = cy if axis == "gx" else cx
        for count, source, start in ((nv, cons, 0), (3, vel, nv * along)):
            if axis == "gx":
                layer = source[:, pl.ds(jnp.where(above, cx - 1, 0), 1)]
            else:
                layer = source[:, :, pl.ds(jnp.where(above, cy - 1, 0), 1)]
            pay[start : start + count * along] = layer.reshape(count * along, nz)
        pay[(nv + 3) * along :] = aims[...]


top = 8


def window(ext, v, cx, cy, move_x=0, move_y=0):
    return ext[v, 1 + move_x : 1 + move_x + cx, top + move_y : top + move_y + cy]


def along_z(value, by):
    nz = value.shape[-1]
    at = lax.broadcasted_iota(jnp.int32, (1,) + value.shape[1:], 2)
    edge = 0 if by < 0 else nz - 1
    return jnp.where(at == edge, 0.0, pltpu.roll(value, (-by) % nz, 2))


def shifted(ext, v, cx, cy, d, by):
    if d == 2 and by:
        return along_z(window(ext, v, cx, cy), by)
    return window(ext, v, cx, cy, by if d == 0 else 0, by if d == 1 else 0)


def face(low, high):
    wave_low = jnp.minimum(jnp.minimum(low, high) - signal_speed, 0.0)
    wave_high = jnp.maximum(jnp.maximum(low, high) + signal_speed, 0.0)
    scale = courant_number / (wave_high - wave_low)
    return (
        scale * wave_high * (low - wave_low),
        scale * wave_low * (wave_high - high),
    )


def prepare_kernel(slots, ng, cons, vel, aims, coefs, base, picks, marks):
    nv, cx, cy, nz = cons.shape
    lanes = nz
    per = lanes // slots
    chunks = block // per
    nq = aims.shape[0]
    spread = 4 if cx % 4 == 0 else 1
    count = cx // spread * cy
    used = (ng - 1) * chunks

    def pick(n):
        cell = aims[pl.ds(n * block, block)].astype(jnp.int32) + cx * cy * nz
        x, y, z = over(cell, nz * cy), rest_of(over(cell, nz), cy), rest_of(cell, nz)
        at_row = over(x, spread) * cy + y
        at_column = (rest_of(x, spread) * nz + z).T
        up = lax.broadcasted_iota(jnp.int32, (count, lanes), 0)
        along = lax.broadcasted_iota(jnp.int32, (lanes, spread * nz), 1)
        total = None
        for at in range(0, used, chunks):
            hits = []
            for c in range(chunks):
                hits.append(jnp.where(up == at_row[at + c : at + c + 1], 1.0, 0.0))
                to = pl.ds(pl.multiple_of((n * used + at + c) * lanes, lanes), lanes)
                chosen = at_column[:, at + c : at + c + 1] == along
                picks[to] = jnp.where(chosen, 1.0, 0.0).astype(jnp.bfloat16)
            to = pl.ds(pl.multiple_of((n * used + at) * lanes, lanes), chunks * lanes)
            term = jnp.dot(
                jnp.concatenate(hits, axis=1).astype(jnp.bfloat16),
                picks[to],
                preferred_element_type=jnp.float32,
            )
            total = term if total is None else total + term
        if nq == block:
            marks[...] = total
        else:
            marks[...] += total

    if nq != block:
        marks[...] = jnp.zeros_like(marks)
    each(nq // block, pick)
    for x in range(cx):
        rows = slice(x // spread * cy, (x // spread + 1) * cy)
        mark = marks[rows, x % spread * nz : (x % spread + 1) * nz]
        base[:, x] = jnp.where(mark[None] > 0.5, 0.0, cons[:, x])

    centre = jnp.ones((cx, cy, nz), jnp.float32)
    none = jnp.zeros((1, cy, nz), jnp.float32)
    low, high = face(vel[0, : cx - 1], vel[0, 1:])
    coefs[0] = jnp.concatenate([none, low], axis=0)
    coefs[1] = -jnp.concatenate([high, none], axis=0)
    centre += jnp.concatenate([none, high], axis=0) - jnp.concatenate([low, none], axis=0)

    at_y = lax.broadcasted_iota(jnp.int32, (1, cy, nz), 1)
    speed = vel[1]
    low, high = face(speed, pltpu.roll(speed, cy - 1, 1))
    low = jnp.where(at_y == cy - 1, 0.0, low)
    high = jnp.where(at_y == cy - 1, 0.0, high)
    coefs[2] = pltpu.roll(low, 1, 1)
    coefs[3] = -high
    centre += pltpu.roll(high, 1, 1) - low

    speed = vel[2]
    up_low, up_high = face(speed, along_z(speed, 1))
    down_low, down_high = face(along_z(speed, -1), speed)
    coefs[4] = down_low
    coefs[5] = -up_high
    coefs[6] = centre + down_high - up_low


def step_kernel(kinds, slots, ng, ngy, vel, aims, given, base, picks, received, *rest):
    halos = rest[: len(kinds)]
    out, coefs, ext, field, acc, result, sems = rest[len(kinds) :]
    nv, cx, cy, nz = base.shape
    lanes = nz
    nq = received.shape[0] // ng
    per = lanes // slots
    chunks = block // per
    used = (ng - 1) * chunks
    spread = 4 if cx % 4 == 0 else 1
    me = lax.axis_index("grp")
    lane = lax.broadcasted_iota(jnp.int32, (nv, lanes), 1) // slots
    above = [partner_above(axis, phase) for axis, phase, _ in kinds]

    parts = [(cx // spread * cy, spread)]
    parts += [(cy if axis == "gx" else cx, 1) for axis, _, _ in kinds]
    starts = [0]
    for count, groups in parts:
        starts.append(starts[-1] + (2 * nv + 1) * count * groups)

    def fill(n):
        for part, (count, groups) in enumerate(parts):
            if part == 0:
                cell = aims[pl.ds(n * block, block)]
            else:
                cell = halos[part - 1][pl.ds((nv + 3) * count + n * block, block)]
            cell = cell.astype(jnp.int32) + cx * cy * nz
            x, y, z = over(cell, nz * cy), rest_of(over(cell, nz), cy), rest_of(cell, nz)
            if part == 0:
                at_row = over(x, spread) * cy + y
            elif kinds[part - 1][0] == "gx":
                at_row = jnp.where(x == jnp.where(above[part - 1], 0, cx - 1), y, -1)
            else:
                at_row = jnp.where(y == jnp.where(above[part - 1], 0, cy - 1), x, -1)
            at_column = z.T
            up = lax.broadcasted_iota(jnp.int32, (count, lanes), 0)
            along = lax.broadcasted_iota(jnp.int32, (lanes, nz), 1)
            here = slice(part // per * lanes, (part // per + 1) * lanes)
            total = None
            for away in range(1, ng):
                g = (me + away) % ng
                lefts, chosen = [], []
                for c in range(chunks):
                    at = (away - 1) * chunks + c
                    value = None
                    for p in range(per):
                        source = n * block + p * chunks + c
                        piece = received[place(ng, nq // ngy, ngy, g, source), :, here]
                        turn = (p - part) % per
                        if turn:
                            piece = pltpu.roll(piece, turn * slots, 1)
                        value = piece if value is None else jnp.where(lane == p, piece, value)
                    high = value.astype(jnp.bfloat16).astype(jnp.float32)
                    low = value - high
                    hit = up == at_row[at : at + 1]
                    pieces = [jnp.where(hit, high[v : v + 1], 0.0) for v in range(nv)]
                    pieces += [jnp.where(hit, low[v : v + 1], 0.0) for v in range(nv)]
                    if part:
                        pieces += [jnp.where(hit, 1.0, 0.0)]
                        pick = jnp.where(at_column[:, at : at + 1] == along, 1.0, 0.0)
                        chosen.append(pick.astype(jnp.bfloat16))
                    lefts.append(jnp.concatenate(pieces, axis=0).astype(jnp.bfloat16))
                if part:
                    chosen = jnp.concatenate(chosen, axis=0)
                else:
                    start = (n * used + (away - 1) * chunks) * lanes
                    chosen = picks[pl.ds(pl.multiple_of(start, lanes), chunks * lanes)]
                term = jnp.dot(
                    jnp.concatenate(lefts, axis=1), chosen, preferred_element_type=jnp.float32
                )
                total = term if total is None else total + term
            rows = total.shape[0]
            for s in range(groups):
                start = starts[part] + s * (2 * nv + 1) * count
                value = total[:, s * nz : (s + 1) * nz]
                if nq == block:
                    acc[start : start + rows] = value
                else:
                    acc[start : start + rows] += value

    if nq != block:
        acc[...] = jnp.zeros_like(acc)
    each(nq // block, fill)

    def brought(part, s):
        count = parts[part][0]
        start = starts[part] + s * (2 * nv + 1) * count
        new = acc[start : start + nv * count] + acc[start + nv * count : start + 2 * nv * count]
        return new.reshape(nv, count, nz)

    def crossed(n, speeds, fields):
        a, b = (n + 1) % 3, (n + 2) % 3
        return speeds[b] * fields[a] - speeds[a] * fields[b]

    inside = slice(top, top + cy)
    for s in range(spread):
        new = brought(0, s)
        for n, x in enumerate(range(s, cx, spread)):
            state = base[:, x] + new[:, n * cy : (n + 1) * cy]
            ext[:fluid_count, 1 + x, inside] = state[:fluid_count]
            field[:, x] = state[fluid_count:]
            for d in range(3):
                ext[fluid_count + d, 1 + x, inside] = crossed(d, vel[:, x], state[fluid_count:])

    sides = {("gx", True): 0.0, ("gx", False): 0.0, ("gy", True): 0.0, ("gy", False): 0.0}
    for n, (axis, _, _) in enumerate(kinds):
        count = parts[n + 1][0]
        d = 0 if axis == "gx" else 1
        halo = halos[n][: (nv + 3) * count].reshape(nv + 3, count, nz)
        mark = acc[starts[n + 1] + 2 * nv * count : starts[n + 1] + (2 * nv + 1) * count]
        state = jnp.where(mark[None] > 0.5, brought(n + 1, 0), halo[:nv])
        electric = [crossed(m, halo[nv:], state[fluid_count:])[None] for m in (1 - d, 2)]
        halo = jnp.concatenate([state[:fluid_count], halo[nv + d : nv + d + 1]] + electric, axis=0)
        sides[axis, True] += jnp.where(above[n], halo, 0.0)
        sides[axis, False] += jnp.where(above[n], 0.0, halo)

    coefs[...] = given[...]
    for (axis, high), halo in sides.items():
        d = 0 if axis == "gx" else 1
        halo = jnp.broadcast_to(halo, (fluid_count + 3, cx if d else cy, nz))
        if d == 0:
            at = (cx + 1 if high else 0, inside)
            edge = (cx - 1 if high else 0,)
        else:
            at = (slice(1, cx + 1), top + cy if high else top - 1)
            edge = (slice(None), cy - 1 if high else 0)
        ext[(slice(0, fluid_count),) + at] = halo[:fluid_count]
        ext[(fluid_count + 1 - d,) + at] = halo[fluid_count + 1]
        ext[(fluid_count + 2,) + at] = halo[fluid_count + 2]
        speed = vel[(d,) + edge]
        if high:
            of_low, of_high = face(speed, halo[fluid_count])
            coefs[(2 * d + 1,) + edge] = -of_high
            coefs[(6,) + edge] -= of_low
        else:
            of_low, of_high = face(halo[fluid_count], speed)
            coefs[(2 * d,) + edge] = of_low
            coefs[(6,) + edge] += of_high

    copies = []

    def finish(v, value):
        result[v] = value
        copies.append(pltpu.make_async_copy(result.at[v], out.at[v], sems.at[v]))
        copies[-1].start()

    def central(n, d):
        v = fluid_count + n
        return shifted(ext, v, cx, cy, d, 1) - shifted(ext, v, cx, cy, d, -1)

    for n in range(3):
        a, b = (n + 1) % 3, (n + 2) % 3
        curl = central(b, a) - central(a, b)
        finish(fluid_count + n, field[n] - (0.5 * courant_number) * curl)
    for v in range(fluid_count):
        total = coefs[6] * window(ext, v, cx, cy)
        for d in range(3):
            total = total + coefs[2 * d] * shifted(ext, v, cx, cy, d, -1)
            total = total + coefs[2 * d + 1] * shifted(ext, v, cx, cy, d, 1)
        finish(v, total)
    for copy in copies:
        copy.wait()


def per_device(ngx, ngy, conserved, velocity, donor_corner, donor_fraction, target_cell):
    kinds = exchanges(ngx, ngy)
    cons = conserved[:, 0]
    vel = velocity[:, 0]
    corner = donor_corner[0, 0, 0]
    fraction = donor_fraction[:, 0, 0, 0]
    target = target_cell[0, 0, 0]
    nv, cx, cy, nz = cons.shape
    ng, nq, slots = corner.shape
    rows = cx * cy
    per = nz // slots
    tiles = -(-(1 + len(kinds)) // per)
    f32 = jnp.float32

    def shape(*dims):
        return jax.ShapeDtypeStruct(dims, f32)

    params = pltpu.CompilerParams(vmem_limit_bytes=(12 + nq // 2) << 20)
    alongs = [cy if axis == "gx" else cx for axis, _, _ in kinds]
    pay_shapes = [((nv + 3) * along + nq, nz) for along in alongs]
    blended = pl.pallas_call(
        functools.partial(blend_kernel, ngy, kinds),
        out_shape=pltpu.VMEM((ng * nq, nv, tiles * nz), f32),
        in_specs=[pl.BlockSpec(memory_space=pl.ANY)] * 3,
        scratch_shapes=[
            pltpu.VMEM(cons.shape, f32),
            pltpu.VMEM(corner.shape, jnp.int32),
            pltpu.VMEM(fraction.shape, f32),
            pltpu.VMEM((nv * rows, 3 * nz), jnp.bfloat16),
            pltpu.VMEM((ng - 1, 3 * nz, block * slots), jnp.bfloat16),
            pltpu.VMEM((ng - 1, rows, block * slots), f32),
            pltpu.VMEM((ng - 1, per, nq // per, nv, nz), f32),
            pltpu.SemaphoreType.DMA((3,)),
        ],
        compiler_params=params,
        name="blend",
    )(*(pltpu.with_memory_space_constraint(value, pltpu.HBM) for value in (cons, corner, fraction)))

    aims, *pays = pl.pallas_call(
        functools.partial(edge_kernel, kinds),
        out_shape=[pltpu.VMEM((nq, nz), f32)] + [pltpu.VMEM(dims, f32) for dims in pay_shapes],
        in_specs=[pl.BlockSpec(memory_space=pltpu.VMEM)] * 3 + [pl.BlockSpec(memory_space=pl.ANY)],
        compiler_params=params,
        name="edge",
    )(cons, vel, target, blended)

    received = lax.all_to_all(
        blended, ("gy", "grp", "gx"), split_axis=0, concat_axis=0, tiled=True
    )
    halos = []
    for (axis, phase, _), pay in zip(kinds, pays):
        count = ngx if axis == "gx" else ngy
        pairs = []
        for low in range(phase, count - 1, 2):
            pairs += [(low, low + 1), (low + 1, low)]
        halos.append(lax.ppermute(pay, axis, pairs))

    spread = 4 if cx % 4 == 0 else 1
    coefs, base, picks = pl.pallas_call(
        functools.partial(prepare_kernel, slots, ng),
        out_shape=[
            pltpu.VMEM((7, cx, cy, nz), f32),
            pltpu.VMEM((nv, cx, cy, nz), f32),
            pltpu.VMEM(((ng - 1) * nq * slots, spread * nz), jnp.bfloat16),
        ],
        scratch_shapes=[pltpu.VMEM((rows // spread, spread * nz), f32)],
        compiler_params=params,
        name="prepare",
    )(cons, vel, aims)
    coefs, base, picks = (
        pltpu.with_memory_space_constraint(value, pltpu.VMEM) for value in (coefs, base, picks)
    )

    result = pl.pallas_call(
        functools.partial(step_kernel, kinds, slots, ng, ngy),
        out_shape=shape(nv, cx, cy, nz),
        out_specs=pl.BlockSpec(memory_space=pl.ANY),
        scratch_shapes=[
            pltpu.VMEM((7, cx, cy, nz), f32),
            pltpu.VMEM((fluid_count + 3, cx + 2, cy + 2 * top, nz), f32),
            pltpu.VMEM((nv - fluid_count, cx, cy, nz), f32),
            pltpu.VMEM(((2 * nv + 1) * (rows + sum(alongs)), nz), f32),
            pltpu.VMEM((nv, cx, cy, nz), f32),
            pltpu.SemaphoreType.DMA((nv,)),
        ],
        compiler_params=params,
        name="step",
    )(vel, aims, coefs, base, picks, received, *halos)
    return result[:, None]


def solution(mesh):
    return jax.shard_map(
        functools.partial(per_device, mesh.shape["gx"], mesh.shape["gy"]),
        mesh=mesh,
        in_specs=(
            P(None, "grp", "gx", "gy", None),
            P(None, "grp", "gx", "gy", None),
            P("grp", "gx", "gy", None, None, None),
            P(None, "grp", "gx", "gy", None, None, None),
            P("grp", "gx", "gy", None, None, None),
        ),
        out_specs=P(None, "grp", "gx", "gy", None),
        check_vma=False,
    )
```

```python
import functools

import jax
import jax.numpy as jnp
from jax import lax
from jax.experimental import pallas as pl
from jax.experimental.pallas import tpu as pltpu
from jax.sharding import PartitionSpec as P

signal_speed = 0.5
courant_number = 0.3
fluid_count = 5
block = 8


def exchanges(ngx, ngy):
    def partner(count, phase, n):
        other = n + 1 if (n + phase) % 2 == 0 else n - 1
        return other if 0 <= other < count else n

    kinds = []
    for phase in range(min(ngx - 1, 2)):
        kinds.append(("gx", phase, lambda i, j, phase=phase: (partner(ngx, phase, i), j)))
    for phase in range(min(ngy - 1, 2)):
        kinds.append(("gy", phase, lambda i, j, phase=phase: (i, partner(ngy, phase, j))))
    return kinds


def partner_above(axis, phase):
    return (lax.axis_index(axis) + phase) % 2 == 0


def split(value):
    high = value.astype(jnp.bfloat16)
    low = (value - high.astype(jnp.float32)).astype(jnp.bfloat16)
    return high, low


def over(value, n):
    return value >> (n.bit_length() - 1) if n & (n - 1) == 0 else value // n


def rest_of(value, n):
    return value & (n - 1) if n & (n - 1) == 0 else value % n


def each(count, body):
    if count == 1:
        body(0)
    else:
        lax.fori_loop(0, count, lambda n, c: (body(n), c)[1], 0)


def block_transpose(value, slots):
    rows, lanes = value.shape
    count = lanes // slots
    each_rows = rows // count
    at_row = lax.broadcasted_iota(jnp.int32, value.shape, 0) // each_rows
    at_lane = lax.broadcasted_iota(jnp.int32, value.shape, 1) // slots
    result = value
    for d in range(1, count):
        turned = pltpu.roll(value, d * each_rows, 0)
        turned = pltpu.roll(turned, lanes - d * slots, 1)
        result = jnp.where((at_row - at_lane) % count == d, turned, result)
    return result


def place(ng, ngx, ngy, grid, q):
    return (q % ngy * ng + grid) * ngx + q // ngy


def packed(tiles, slots):
    empty = jnp.zeros(tiles[0].shape, tiles[0].dtype)
    return block_transpose(jnp.concatenate(tiles + [empty], axis=1), slots)


def blend_kernel(ngy, kinds, cons, corner, fraction, out, *scratch):
    at_cons, at_corner, at_fraction, uhl, wzs, wxys, moved, arrive = scratch
    nv, cx, cy, nz = cons.shape
    ng, nq, slots = corner.shape
    lanes = nz
    per = lanes // slots
    chunks = block // per
    rows = cx * cy
    me = lax.axis_index("grp")

    moves = [(corner, at_corner), (fraction, at_fraction), (cons, at_cons)]
    ins = [pltpu.make_async_copy(a, b, arrive.at[n]) for n, (a, b) in enumerate(moves)]
    for copy in ins:
        copy.start()

    for q in range(nq):
        at = place(ng, nq // ngy, ngy, me, q)
        out[pl.ds(at, 1)] = jnp.zeros((1,) + out.shape[1:], jnp.float32)

    def weight(count, at, upper):
        place = lax.broadcasted_iota(jnp.int32, (count, lanes), 0)
        return jnp.where(place == at, 1.0 - upper, jnp.where(place == at + 1, upper, 0.0))

    def weigh(n):
        here = pl.ds(n * block, block)
        grids = [(me + away) % ng for away in range(1, ng)]
        cell = packed([at_corner[h, here] for h in grids], slots)
        at_x, at_y, at_z = over(cell, nz * cy), rest_of(over(cell, nz), cy), rest_of(cell, nz)
        fx, fy, fz = (packed([at_fraction[d, h, here] for h in grids], slots) for d in range(3))
        for away in range(1, ng):
            for c in range(chunks):
                row = slice((away - 1) * chunks + c, (away - 1) * chunks + c + 1)
                cols = slice(c * lanes, (c + 1) * lanes)
                wx = weight(cx, at_x[row], fx[row])
                wy = weight(cy, at_y[row], fy[row])
                for x in range(cx):
                    wxys[away - 1, x * cy : (x + 1) * cy, cols] = wx[x : x + 1] * wy
                high, low = split(weight(nz, at_z[row], fz[row]))
                wzs[away - 1, :nz, cols] = high
                wzs[away - 1, nz : 2 * nz, cols] = high
                wzs[away - 1, 2 * nz :, cols] = low

    def blend(n):
        for away in range(1, ng):
            along = jnp.dot(uhl[...], wzs[away - 1], preferred_element_type=jnp.float32)
            along = along.reshape(nv, rows, chunks * lanes)
            values = jnp.sum(along * wxys[away - 1][None], axis=1)
            for c in range(chunks):
                value = values[:, c * lanes : (c + 1) * lanes]
                for turn in range(per):
                    moved[away - 1, turn, n * chunks + c] = (
                        pltpu.roll(value, turn * slots, 1) if turn else value
                    )
            if nq == block:
                assemble(away)

    lane = lax.broadcasted_iota(jnp.int32, (nv, lanes), 1) // slots

    def assemble(away):
        for q in range(nq):
            i, j = q // ngy, q % ngy
            owners = [q] + [a * ngy + b for a, b in (of(i, j) for _, _, of in kinds)]
            for t in range(0, len(owners), per):
                tile = None
                for k, owner in enumerate(owners[t : t + per]):
                    chunk = owner // block * chunks + owner % chunks
                    piece = moved[away - 1, (k - owner % block // chunks) % per, chunk]
                    tile = piece if tile is None else jnp.where(lane == k, piece, tile)
                cols = slice(t // per * lanes, (t // per + 1) * lanes)
                at = place(ng, nq // ngy, ngy, (me + away) % ng, q)
                out[pl.ds(at, 1), :, cols] = tile[None]

    for copy in ins[:2]:
        copy.wait()
    if nq == block:
        weigh(0)
    ins[2].wait()
    high, low = split(at_cons[...].reshape(nv * rows, nz))
    uhl[:, :nz] = high
    uhl[:, nz : 2 * nz] = low
    uhl[:, 2 * nz :] = high
    if nq == block:
        blend(0)
    else:

        def both(n):
            weigh(n)
            blend(n)

        each(nq // block, both)
        for away in range(1, ng):
            assemble(away)


def edge_kernel(kinds, cons, vel, target, sent, aims, *pays):
    del sent
    nv, cx, cy, nz = cons.shape
    ng, nq, slots = target.shape
    me = lax.axis_index("grp")
    for n in range(nq // block):
        here = slice(n * block, (n + 1) * block)
        tiles = [target[(me + away) % ng, here] - cx * cy * nz for away in range(1, ng)]
        aims[here] = packed(tiles, slots).astype(jnp.float32)
    for (axis, phase, _), pay in zip(kinds, pays):
        above = partner_above(axis, phase)
        along = cy if axis == "gx" else cx
        for count, source, start in ((nv, cons, 0), (3, vel, nv * along)):
            if axis == "gx":
                layer = source[:, pl.ds(jnp.where(above, cx - 1, 0), 1)]
            else:
                layer = source[:, :, pl.ds(jnp.where(above, cy - 1, 0), 1)]
            pay[start : start + count * along] = layer.reshape(count * along, nz)
        pay[(nv + 3) * along :] = aims[...]


top = 8


def window(ext, v, cx, cy, move_x=0, move_y=0):
    return ext[v, 1 + move_x : 1 + move_x + cx, top + move_y : top + move_y + cy]


def along_z(value, by):
    nz = value.shape[-1]
    at = lax.broadcasted_iota(jnp.int32, (1,) + value.shape[1:], 2)
    edge = 0 if by < 0 else nz - 1
    return jnp.where(at == edge, 0.0, pltpu.roll(value, (-by) % nz, 2))


def shifted(ext, v, cx, cy, d, by):
    if d == 2 and by:
        return along_z(window(ext, v, cx, cy), by)
    return window(ext, v, cx, cy, by if d == 0 else 0, by if d == 1 else 0)


def face(low, high):
    wave_low = jnp.minimum(jnp.minimum(low, high) - signal_speed, 0.0)
    wave_high = jnp.maximum(jnp.maximum(low, high) + signal_speed, 0.0)
    scale = courant_number / (wave_high - wave_low)
    return (
        scale * wave_high * (low - wave_low),
        scale * wave_low * (wave_high - high),
    )


def mark(n, at_row, at_column, count, used, chunks, picks, marks):
    lanes = at_row.shape[1]
    up = lax.broadcasted_iota(jnp.int32, (count, lanes), 0)
    along = lax.broadcasted_iota(jnp.int32, (lanes, picks.shape[1]), 1)
    for at in range(0, used, chunks):
        hits = []
        for c in range(chunks):
            hits.append(jnp.where(up == at_row[at + c : at + c + 1], 1.0, 0.0))
            to = pl.ds(pl.multiple_of((n * used + at + c) * lanes, lanes), lanes)
            chosen = at_column[:, at + c : at + c + 1] == along
            picks[to] = jnp.where(chosen, 1.0, 0.0).astype(jnp.bfloat16)
        to = pl.ds(pl.multiple_of((n * used + at) * lanes, lanes), chunks * lanes)
        marks[...] += jnp.dot(
            jnp.concatenate(hits, axis=1).astype(jnp.bfloat16),
            picks[to],
            preferred_element_type=jnp.float32,
        )


def prepare_kernel(slots, ng, cons, vel, aims, coefs, base, picks, marks):
    nv, cx, cy, nz = cons.shape
    per = nz // slots
    chunks = block // per
    spread = 4 if cx % 4 == 0 else 1
    count = cx // spread * cy

    def pick(n):
        cell = aims[pl.ds(n * block, block)].astype(jnp.int32) + cx * cy * nz
        x, y, z = over(cell, nz * cy), rest_of(over(cell, nz), cy), rest_of(cell, nz)
        at_row = over(x, spread) * cy + y
        at_column = (rest_of(x, spread) * nz + z).T
        mark(n, at_row, at_column, count, (ng - 1) * chunks, chunks, picks, marks)

    marks[...] = jnp.zeros_like(marks)
    each(aims.shape[0] // block, pick)
    for x in range(cx):
        rows = slice(x // spread * cy, (x // spread + 1) * cy)
        seen = marks[rows, x % spread * nz : (x % spread + 1) * nz]
        base[:, x] = jnp.where(seen[None] > 0.5, 0.0, cons[:, x])

    centre = jnp.ones((cx, cy, nz), jnp.float32)
    none = jnp.zeros((1, cy, nz), jnp.float32)
    low, high = face(vel[0, : cx - 1], vel[0, 1:])
    coefs[0] = jnp.concatenate([none, low], axis=0)
    coefs[1] = -jnp.concatenate([high, none], axis=0)
    centre += jnp.concatenate([none, high], axis=0) - jnp.concatenate([low, none], axis=0)

    at_y = lax.broadcasted_iota(jnp.int32, (1, cy, nz), 1)
    speed = vel[1]
    low, high = face(speed, pltpu.roll(speed, cy - 1, 1))
    low = jnp.where(at_y == cy - 1, 0.0, low)
    high = jnp.where(at_y == cy - 1, 0.0, high)
    coefs[2] = pltpu.roll(low, 1, 1)
    coefs[3] = -high
    centre += pltpu.roll(high, 1, 1) - low

    speed = vel[2]
    up_low, up_high = face(speed, along_z(speed, 1))
    down_low, down_high = face(along_z(speed, -1), speed)
    coefs[4] = down_low
    coefs[5] = -up_high
    coefs[6] = centre + down_high - up_low


def border_kernel(kinds, slots, ng, vel, given, *rest):
    halos = rest[: len(kinds)]
    coefs, rows = rest[len(kinds) : len(kinds) + 2]
    cleared = rest[len(kinds) + 2 : 2 * len(kinds) + 2]
    picks = rest[2 * len(kinds) + 2 : 3 * len(kinds) + 2]
    marks = rest[3 * len(kinds) + 2 :]
    cx, cy, nz = vel.shape[1:]
    nq = rows.shape[1]
    chunks = block // (nz // slots)
    used = (ng - 1) * chunks

    sides = {("gx", True): 0.0, ("gx", False): 0.0, ("gy", True): 0.0, ("gy", False): 0.0}
    for k, (axis, phase, _) in enumerate(kinds):
        above = partner_above(axis, phase)
        nv, count = cleared[k].shape[:2]

        def pick(n):
            cell = halos[k][pl.ds((nv + 3) * count + n * block, block)].astype(jnp.int32)
            cell = cell + cx * cy * nz
            x, y, z = over(cell, nz * cy), rest_of(over(cell, nz), cy), rest_of(cell, nz)
            if axis == "gx":
                at_row = jnp.where(x == jnp.where(above, 0, cx - 1), y, -1)
            else:
                at_row = jnp.where(y == jnp.where(above, 0, cy - 1), x, -1)
            rows[k, pl.ds(n * block, block)] = at_row
            mark(n, at_row, z.T, count, used, chunks, picks[k], marks[k])

        marks[k][...] = jnp.zeros_like(marks[k])
        each(nq // block, pick)
        before = halos[k][: nv * count].reshape(nv, count, nz)
        cleared[k][...] = jnp.where(marks[k][...][None] > 0.5, 0.0, before)
        d = 0 if axis == "gx" else 1
        speed = halos[k][(nv + d) * count : (nv + d + 1) * count]
        sides[axis, True] += jnp.where(above, speed, 0.0)
        sides[axis, False] += jnp.where(above, 0.0, speed)

    coefs[...] = given[...]
    for (axis, high), speed in sides.items():
        if axis == "gx":
            d, edge = 0, (cx - 1 if high else 0,)
        else:
            d, edge = 1, (slice(None), cy - 1 if high else 0)
        mine = vel[(d,) + edge]
        speed = jnp.broadcast_to(speed, mine.shape)
        if high:
            of_low, of_high = face(mine, speed)
            coefs[(2 * d + 1,) + edge] = -of_high
            coefs[(6,) + edge] -= of_low
        else:
            of_low, of_high = face(speed, mine)
            coefs[(2 * d,) + edge] = of_low
            coefs[(6,) + edge] += of_high


def step_kernel(kinds, slots, ng, ngy, vel, aims, base, received, coefs, rows_there, *rest):
    halos, cleared = rest[: len(kinds)], rest[len(kinds) : 2 * len(kinds)]
    picks = rest[2 * len(kinds) : 3 * len(kinds) + 1]
    out, ext, field, acc, result, sems = rest[3 * len(kinds) + 1 :]
    nv, cx, cy, nz = base.shape
    lanes = nz
    nq = received.shape[0] // ng
    per = lanes // slots
    chunks = block // per
    used = (ng - 1) * chunks
    spread = 4 if cx % 4 == 0 else 1
    me = lax.axis_index("grp")
    lane = lax.broadcasted_iota(jnp.int32, (nv, lanes), 1) // slots
    above = [partner_above(axis, phase) for axis, phase, _ in kinds]

    parts = [(cx // spread * cy, spread)]
    parts += [(cy if axis == "gx" else cx, 1) for axis, _, _ in kinds]
    starts = [0]
    for count, groups in parts:
        starts.append(starts[-1] + 2 * nv * count * groups)

    def fill(n):
        for part, (count, groups) in enumerate(parts):
            if part == 0:
                cell = aims[pl.ds(n * block, block)].astype(jnp.int32) + cx * cy * nz
                x, y = over(cell, nz * cy), rest_of(over(cell, nz), cy)
                at_row = over(x, spread) * cy + y
            else:
                at_row = rows_there[part - 1, pl.ds(n * block, block)]
            up = lax.broadcasted_iota(jnp.int32, (count, lanes), 0)
            here = slice(part // per * lanes, (part // per + 1) * lanes)
            total = None
            for away in range(1, ng):
                g = (me + away) % ng
                lefts = []
                for c in range(chunks):
                    at = (away - 1) * chunks + c
                    value = None
                    for p in range(per):
                        source = n * block + p * chunks + c
                        piece = received[place(ng, nq // ngy, ngy, g, source), :, here]
                        turn = (p - part) % per
                        if turn:
                            piece = pltpu.roll(piece, turn * slots, 1)
                        value = piece if value is None else jnp.where(lane == p, piece, value)
                    high = value.astype(jnp.bfloat16).astype(jnp.float32)
                    low = value - high
                    hit = up == at_row[at : at + 1]
                    pieces = [jnp.where(hit, high[v : v + 1], 0.0) for v in range(nv)]
                    pieces += [jnp.where(hit, low[v : v + 1], 0.0) for v in range(nv)]
                    lefts.append(jnp.concatenate(pieces, axis=0).astype(jnp.bfloat16))
                start = (n * used + (away - 1) * chunks) * lanes
                chosen = picks[part][pl.ds(pl.multiple_of(start, lanes), chunks * lanes)]
                term = jnp.dot(
                    jnp.concatenate(lefts, axis=1), chosen, preferred_element_type=jnp.float32
                )
                total = term if total is None else total + term
            rows = total.shape[0]
            for s in range(groups):
                start = starts[part] + s * 2 * nv * count
                value = total[:, s * nz : (s + 1) * nz]
                if nq == block:
                    acc[start : start + rows] = value
                else:
                    acc[start : start + rows] += value

    if nq != block:
        acc[...] = jnp.zeros_like(acc)
    each(nq // block, fill)

    def brought(part, s):
        count = parts[part][0]
        start = starts[part] + s * 2 * nv * count
        new = acc[start : start + nv * count] + acc[start + nv * count : start + 2 * nv * count]
        return new.reshape(nv, count, nz)

    def crossed(n, speeds, fields):
        a, b = (n + 1) % 3, (n + 2) % 3
        return speeds[b] * fields[a] - speeds[a] * fields[b]

    inside = slice(top, top + cy)
    for s in range(spread):
        new = brought(0, s)
        for n, x in enumerate(range(s, cx, spread)):
            state = base[:, x] + new[:, n * cy : (n + 1) * cy]
            ext[:fluid_count, 1 + x, inside] = state[:fluid_count]
            field[:, x] = state[fluid_count:]
            for d in range(3):
                ext[fluid_count + d, 1 + x, inside] = crossed(d, vel[:, x], state[fluid_count:])

    sides = {("gx", True): 0.0, ("gx", False): 0.0, ("gy", True): 0.0, ("gy", False): 0.0}
    for n, (axis, _, _) in enumerate(kinds):
        count = parts[n + 1][0]
        d = 0 if axis == "gx" else 1
        halo = halos[n][: (nv + 3) * count].reshape(nv + 3, count, nz)
        state = cleared[n][...] + brought(n + 1, 0)
        electric = [crossed(m, halo[nv:], state[fluid_count:])[None] for m in (1 - d, 2)]
        halo = jnp.concatenate([state[:fluid_count]] + electric, axis=0)
        sides[axis, True] += jnp.where(above[n], halo, 0.0)
        sides[axis, False] += jnp.where(above[n], 0.0, halo)

    for (axis, high), halo in sides.items():
        d = 0 if axis == "gx" else 1
        halo = jnp.broadcast_to(halo, (fluid_count + 2, cx if d else cy, nz))
        if d == 0:
            at = (cx + 1 if high else 0, inside)
        else:
            at = (slice(1, cx + 1), top + cy if high else top - 1)
        ext[(slice(0, fluid_count),) + at] = halo[:fluid_count]
        ext[(fluid_count + 1 - d,) + at] = halo[fluid_count]
        ext[(fluid_count + 2,) + at] = halo[fluid_count + 1]

    copies = []

    def finish(v, value):
        result[v] = value
        copies.append(pltpu.make_async_copy(result.at[v], out.at[v], sems.at[v]))
        copies[-1].start()

    def central(n, d):
        v = fluid_count + n
        return shifted(ext, v, cx, cy, d, 1) - shifted(ext, v, cx, cy, d, -1)

    for n in range(3):
        a, b = (n + 1) % 3, (n + 2) % 3
        curl = central(b, a) - central(a, b)
        finish(fluid_count + n, field[n] - (0.5 * courant_number) * curl)
    for v in range(fluid_count):
        total = coefs[6] * window(ext, v, cx, cy)
        for d in range(3):
            total = total + coefs[2 * d] * shifted(ext, v, cx, cy, d, -1)
            total = total + coefs[2 * d + 1] * shifted(ext, v, cx, cy, d, 1)
        finish(v, total)
    for copy in copies:
        copy.wait()


def per_device(ngx, ngy, conserved, velocity, donor_corner, donor_fraction, target_cell):
    kinds = exchanges(ngx, ngy)
    cons = conserved[:, 0]
    vel = velocity[:, 0]
    corner = donor_corner[0, 0, 0]
    fraction = donor_fraction[:, 0, 0, 0]
    target = target_cell[0, 0, 0]
    nv, cx, cy, nz = cons.shape
    ng, nq, slots = corner.shape
    rows = cx * cy
    per = nz // slots
    tiles = -(-(1 + len(kinds)) // per)
    f32 = jnp.float32

    def shape(*dims):
        return jax.ShapeDtypeStruct(dims, f32)

    params = pltpu.CompilerParams(vmem_limit_bytes=(12 + nq // 2) << 20)
    alongs = [cy if axis == "gx" else cx for axis, _, _ in kinds]
    pay_shapes = [((nv + 3) * along + nq, nz) for along in alongs]
    blended = pl.pallas_call(
        functools.partial(blend_kernel, ngy, kinds),
        out_shape=pltpu.VMEM((ng * nq, nv, tiles * nz), f32),
        in_specs=[pl.BlockSpec(memory_space=pl.ANY)] * 3,
        scratch_shapes=[
            pltpu.VMEM(cons.shape, f32),
            pltpu.VMEM(corner.shape, jnp.int32),
            pltpu.VMEM(fraction.shape, f32),
            pltpu.VMEM((nv * rows, 3 * nz), jnp.bfloat16),
            pltpu.VMEM((ng - 1, 3 * nz, block * slots), jnp.bfloat16),
            pltpu.VMEM((ng - 1, rows, block * slots), f32),
            pltpu.VMEM((ng - 1, per, nq // per, nv, nz), f32),
            pltpu.SemaphoreType.DMA((3,)),
        ],
        compiler_params=params,
        name="blend",
    )(*(pltpu.with_memory_space_constraint(value, pltpu.HBM) for value in (cons, corner, fraction)))

    aims, *pays = pl.pallas_call(
        functools.partial(edge_kernel, kinds),
        out_shape=[pltpu.VMEM((nq, nz), f32)] + [pltpu.VMEM(dims, f32) for dims in pay_shapes],
        in_specs=[pl.BlockSpec(memory_space=pltpu.VMEM)] * 3 + [pl.BlockSpec(memory_space=pl.ANY)],
        compiler_params=params,
        name="edge",
    )(cons, vel, target, blended)

    received = lax.all_to_all(
        blended, ("gy", "grp", "gx"), split_axis=0, concat_axis=0, tiled=True
    )
    halos = []
    for (axis, phase, _), pay in zip(kinds, pays):
        count = ngx if axis == "gx" else ngy
        pairs = []
        for low in range(phase, count - 1, 2):
            pairs += [(low, low + 1), (low + 1, low)]
        halos.append(lax.ppermute(pay, axis, pairs))

    spread = 4 if cx % 4 == 0 else 1
    coefs, base, picks = pl.pallas_call(
        functools.partial(prepare_kernel, slots, ng),
        out_shape=[
            pltpu.VMEM((7, cx, cy, nz), f32),
            pltpu.VMEM((nv, cx, cy, nz), f32),
            pltpu.VMEM(((ng - 1) * nq * slots, spread * nz), jnp.bfloat16),
        ],
        scratch_shapes=[pltpu.VMEM((rows // spread, spread * nz), f32)],
        compiler_params=params,
        name="prepare",
    )(cons, vel, aims)
    def kept(values):
        return [pltpu.with_memory_space_constraint(value, pltpu.VMEM) for value in values]

    coefs, base, picks = kept((coefs, base, picks))
    border = pl.pallas_call(
        functools.partial(border_kernel, kinds, slots, ng),
        out_shape=[
            pltpu.VMEM((7, cx, cy, nz), f32),
            pltpu.VMEM((len(kinds), nq, nz), jnp.int32),
        ]
        + [pltpu.VMEM((nv, along, nz), f32) for along in alongs]
        + [pltpu.VMEM(((ng - 1) * nq * slots, nz), jnp.bfloat16) for _ in kinds],
        scratch_shapes=[pltpu.VMEM((along, nz), f32) for along in alongs],
        compiler_params=params,
        name="border",
    )(vel, coefs, *halos)
    coefs, rows_there, *border = kept(border)
    cleared, picks_there = border[: len(kinds)], border[len(kinds) :]

    result = pl.pallas_call(
        functools.partial(step_kernel, kinds, slots, ng, ngy),
        out_shape=shape(nv, cx, cy, nz),
        out_specs=pl.BlockSpec(memory_space=pl.ANY),
        scratch_shapes=[
            pltpu.VMEM((fluid_count + 3, cx + 2, cy + 2 * top, nz), f32),
            pltpu.VMEM((nv - fluid_count, cx, cy, nz), f32),
            pltpu.VMEM((2 * nv * (rows + sum(alongs)), nz), f32),
            pltpu.VMEM((nv, cx, cy, nz), f32),
            pltpu.SemaphoreType.DMA((nv,)),
        ],
        compiler_params=params,
        name="step",
    )(vel, aims, base, received, coefs, rows_there, *halos, *cleared, picks, *picks_there)
    return result[:, None]


def solution(mesh):
    return jax.shard_map(
        functools.partial(per_device, mesh.shape["gx"], mesh.shape["gy"]),
        mesh=mesh,
        in_specs=(
            P(None, "grp", "gx", "gy", None),
            P(None, "grp", "gx", "gy", None),
            P("grp", "gx", "gy", None, None, None),
            P(None, "grp", "gx", "gy", None, None, None),
            P("grp", "gx", "gy", None, None, None),
        ),
        out_specs=P(None, "grp", "gx", "gy", None),
        check_vma=False,
    )
```

```python
import functools

import jax
import jax.numpy as jnp
from jax import lax
from jax.experimental import pallas as pl
from jax.experimental.pallas import tpu as pltpu
from jax.sharding import PartitionSpec as P

signal_speed = 0.5
courant_number = 0.3
fluid_count = 5
block = 8


def exchanges(ngx, ngy):
    def partner(count, phase, n):
        other = n + 1 if (n + phase) % 2 == 0 else n - 1
        return other if 0 <= other < count else n

    kinds = []
    for phase in range(min(ngx - 1, 2)):
        kinds.append(("gx", phase, lambda i, j, phase=phase: (partner(ngx, phase, i), j)))
    for phase in range(min(ngy - 1, 2)):
        kinds.append(("gy", phase, lambda i, j, phase=phase: (i, partner(ngy, phase, j))))
    return kinds


def partner_above(axis, phase):
    return (lax.axis_index(axis) + phase) % 2 == 0


def split(value):
    high = value.astype(jnp.bfloat16)
    low = (value - high.astype(jnp.float32)).astype(jnp.bfloat16)
    return high, low


def spread_of(cx):
    return next(n for n in (8, 4, 2, 1) if cx % n == 0)


def over(value, n):
    return value >> (n.bit_length() - 1) if n & (n - 1) == 0 else value // n


def rest_of(value, n):
    return value & (n - 1) if n & (n - 1) == 0 else value % n


def each(count, body):
    if count == 1:
        body(0)
    else:
        lax.fori_loop(0, count, lambda n, c: (body(n), c)[1], 0)


def block_transpose(value, slots):
    rows, lanes = value.shape
    count = lanes // slots
    each_rows = rows // count
    at_row = lax.broadcasted_iota(jnp.int32, value.shape, 0) // each_rows
    at_lane = lax.broadcasted_iota(jnp.int32, value.shape, 1) // slots
    result = value
    for d in range(1, count):
        turned = pltpu.roll(value, d * each_rows, 0)
        turned = pltpu.roll(turned, lanes - d * slots, 1)
        result = jnp.where((at_row - at_lane) % count == d, turned, result)
    return result


def place(ng, ngx, ngy, grid, q):
    return (q % ngy * ng + grid) * ngx + q // ngy


def packed(tiles, slots):
    empty = jnp.zeros(tiles[0].shape, tiles[0].dtype)
    return block_transpose(jnp.concatenate(tiles + [empty], axis=1), slots)


def blend_kernel(ngy, kinds, cons, corner, fraction, out, *scratch):
    at_cons, at_corner, at_fraction, uhl, wzs, wxys, moved, arrive = scratch
    nv, cx, cy, nz = cons.shape
    ng, nq, slots = corner.shape
    lanes = nz
    per = lanes // slots
    chunks = block // per
    rows = cx * cy
    me = lax.axis_index("grp")

    moves = [(corner, at_corner), (fraction, at_fraction), (cons, at_cons)]
    ins = [pltpu.make_async_copy(a, b, arrive.at[n]) for n, (a, b) in enumerate(moves)]
    for copy in ins:
        copy.start()

    for q in range(nq):
        at = place(ng, nq // ngy, ngy, me, q)
        out[pl.ds(at, 1)] = jnp.zeros((1,) + out.shape[1:], jnp.float32)

    def weight(count, at, upper):
        place = lax.broadcasted_iota(jnp.int32, (count, lanes), 0)
        return jnp.where(place == at, 1.0 - upper, jnp.where(place == at + 1, upper, 0.0))

    def weigh(n):
        here = pl.ds(n * block, block)
        grids = [(me + away) % ng for away in range(1, ng)]
        cell = packed([at_corner[h, here] for h in grids], slots)
        at_x, at_y, at_z = over(cell, nz * cy), rest_of(over(cell, nz), cy), rest_of(cell, nz)
        fx, fy, fz = (packed([at_fraction[d, h, here] for h in grids], slots) for d in range(3))
        for away in range(1, ng):
            for c in range(chunks):
                row = slice((away - 1) * chunks + c, (away - 1) * chunks + c + 1)
                cols = slice(c * lanes, (c + 1) * lanes)
                wx = weight(cx, at_x[row], fx[row])
                wy = weight(cy, at_y[row], fy[row])
                for x in range(cx):
                    wxys[away - 1, x * cy : (x + 1) * cy, cols] = wx[x : x + 1] * wy
                high, low = split(weight(nz, at_z[row], fz[row]))
                wzs[away - 1, :nz, cols] = high
                wzs[away - 1, nz : 2 * nz, cols] = high
                wzs[away - 1, 2 * nz :, cols] = low

    def blend(n):
        for away in range(1, ng):
            along = jnp.dot(uhl[...], wzs[away - 1], preferred_element_type=jnp.float32)
            along = along.reshape(nv, rows, chunks * lanes)
            values = jnp.sum(along * wxys[away - 1][None], axis=1)
            for c in range(chunks):
                value = values[:, c * lanes : (c + 1) * lanes]
                for turn in range(per):
                    moved[away - 1, turn, n * chunks + c] = (
                        pltpu.roll(value, turn * slots, 1) if turn else value
                    )
            if nq == block:
                assemble(away)

    lane = lax.broadcasted_iota(jnp.int32, (nv, lanes), 1) // slots

    def assemble(away):
        for q in range(nq):
            i, j = q // ngy, q % ngy
            owners = [q] + [a * ngy + b for a, b in (of(i, j) for _, _, of in kinds)]
            for t in range(0, len(owners), per):
                tile = None
                for k, owner in enumerate(owners[t : t + per]):
                    chunk = owner // block * chunks + owner % chunks
                    piece = moved[away - 1, (k - owner % block // chunks) % per, chunk]
                    tile = piece if tile is None else jnp.where(lane == k, piece, tile)
                cols = slice(t // per * lanes, (t // per + 1) * lanes)
                at = place(ng, nq // ngy, ngy, (me + away) % ng, q)
                out[pl.ds(at, 1), :, cols] = tile[None]

    for copy in ins[:2]:
        copy.wait()
    if nq == block:
        weigh(0)
    ins[2].wait()
    high, low = split(at_cons[...].reshape(nv * rows, nz))
    uhl[:, :nz] = high
    uhl[:, nz : 2 * nz] = low
    uhl[:, 2 * nz :] = high
    if nq == block:
        blend(0)
    else:

        def both(n):
            weigh(n)
            blend(n)

        each(nq // block, both)
        for away in range(1, ng):
            assemble(away)


def edge_kernel(kinds, cons, vel, target, sent, aims, *pays):
    del sent
    nv, cx, cy, nz = cons.shape
    ng, nq, slots = target.shape
    me = lax.axis_index("grp")
    for n in range(nq // block):
        here = slice(n * block, (n + 1) * block)
        tiles = [target[(me + away) % ng, here] - cx * cy * nz for away in range(1, ng)]
        aims[here] = packed(tiles, slots).astype(jnp.float32)
    for (axis, phase, _), pay in zip(kinds, pays):
        above = partner_above(axis, phase)
        along = cy if axis == "gx" else cx
        for count, source, start in ((nv, cons, 0), (3, vel, nv * along)):
            if axis == "gx":
                layer = source[:, pl.ds(jnp.where(above, cx - 1, 0), 1)]
            else:
                layer = source[:, :, pl.ds(jnp.where(above, cy - 1, 0), 1)]
            pay[start : start + count * along] = layer.reshape(count * along, nz)
        pay[(nv + 3) * along :] = aims[...]


top = 8


def window(ext, v, cx, cy, move_x=0, move_y=0):
    return ext[v, 1 + move_x : 1 + move_x + cx, top + move_y : top + move_y + cy]


def along_z(value, by):
    nz = value.shape[-1]
    at = lax.broadcasted_iota(jnp.int32, (1,) + value.shape[1:], 2)
    edge = 0 if by < 0 else nz - 1
    return jnp.where(at == edge, 0.0, pltpu.roll(value, (-by) % nz, 2))


def shifted(ext, v, cx, cy, d, by):
    if d == 2 and by:
        return along_z(window(ext, v, cx, cy), by)
    return window(ext, v, cx, cy, by if d == 0 else 0, by if d == 1 else 0)


def face(low, high):
    wave_low = jnp.minimum(jnp.minimum(low, high) - signal_speed, 0.0)
    wave_high = jnp.maximum(jnp.maximum(low, high) + signal_speed, 0.0)
    scale = courant_number / (wave_high - wave_low)
    return (
        scale * wave_high * (low - wave_low),
        scale * wave_low * (wave_high - high),
    )


def mark(n, at_row, at_column, count, used, chunks, picks, marks):
    lanes = at_row.shape[1]
    up = lax.broadcasted_iota(jnp.int32, (count, lanes), 0)
    along = lax.broadcasted_iota(jnp.int32, (lanes, picks.shape[1]), 1)
    for at in range(0, used, chunks):
        hits = []
        for c in range(chunks):
            hits.append(jnp.where(up == at_row[at + c : at + c + 1], 1.0, 0.0))
            to = pl.ds(pl.multiple_of((n * used + at + c) * lanes, lanes), lanes)
            chosen = at_column[:, at + c : at + c + 1] == along
            picks[to] = jnp.where(chosen, 1.0, 0.0).astype(jnp.bfloat16)
        to = pl.ds(pl.multiple_of((n * used + at) * lanes, lanes), chunks * lanes)
        marks[...] += jnp.dot(
            jnp.concatenate(hits, axis=1).astype(jnp.bfloat16),
            picks[to],
            preferred_element_type=jnp.float32,
        )


def prepare_kernel(slots, ng, cons, vel, aims, coefs, base, picks, marks):
    nv, cx, cy, nz = cons.shape
    per = nz // slots
    chunks = block // per
    spread = spread_of(cx)
    count = cx // spread * cy

    def pick(n):
        cell = aims[pl.ds(n * block, block)].astype(jnp.int32) + cx * cy * nz
        x, y, z = over(cell, nz * cy), rest_of(over(cell, nz), cy), rest_of(cell, nz)
        at_row = over(x, spread) * cy + y
        at_column = (rest_of(x, spread) * nz + z).T
        mark(n, at_row, at_column, count, (ng - 1) * chunks, chunks, picks, marks)

    marks[...] = jnp.zeros_like(marks)
    each(aims.shape[0] // block, pick)
    for x in range(cx):
        rows = slice(x // spread * cy, (x // spread + 1) * cy)
        seen = marks[rows, x % spread * nz : (x % spread + 1) * nz]
        base[:, x] = jnp.where(seen[None] > 0.5, 0.0, cons[:, x])

    centre = jnp.ones((cx, cy, nz), jnp.float32)
    none = jnp.zeros((1, cy, nz), jnp.float32)
    low, high = face(vel[0, : cx - 1], vel[0, 1:])
    coefs[0] = jnp.concatenate([none, low], axis=0)
    coefs[1] = -jnp.concatenate([high, none], axis=0)
    centre += jnp.concatenate([none, high], axis=0) - jnp.concatenate([low, none], axis=0)

    at_y = lax.broadcasted_iota(jnp.int32, (1, cy, nz), 1)
    speed = vel[1]
    low, high = face(speed, pltpu.roll(speed, cy - 1, 1))
    low = jnp.where(at_y == cy - 1, 0.0, low)
    high = jnp.where(at_y == cy - 1, 0.0, high)
    coefs[2] = pltpu.roll(low, 1, 1)
    coefs[3] = -high
    centre += pltpu.roll(high, 1, 1) - low

    speed = vel[2]
    up_low, up_high = face(speed, along_z(speed, 1))
    down_low, down_high = face(along_z(speed, -1), speed)
    coefs[4] = down_low
    coefs[5] = -up_high
    coefs[6] = centre + down_high - up_low


def border_kernel(kinds, slots, ng, vel, given, *rest):
    halos = rest[: len(kinds)]
    coefs, rows = rest[len(kinds) : len(kinds) + 2]
    cleared = rest[len(kinds) + 2 : 2 * len(kinds) + 2]
    picks = rest[2 * len(kinds) + 2 : 3 * len(kinds) + 2]
    marks = rest[3 * len(kinds) + 2 :]
    cx, cy, nz = vel.shape[1:]
    nq = rows.shape[1]
    chunks = block // (nz // slots)
    used = (ng - 1) * chunks

    sides = {("gx", True): 0.0, ("gx", False): 0.0, ("gy", True): 0.0, ("gy", False): 0.0}
    for k, (axis, phase, _) in enumerate(kinds):
        above = partner_above(axis, phase)
        nv, count = cleared[k].shape[:2]

        def pick(n):
            cell = halos[k][pl.ds((nv + 3) * count + n * block, block)].astype(jnp.int32)
            cell = cell + cx * cy * nz
            x, y, z = over(cell, nz * cy), rest_of(over(cell, nz), cy), rest_of(cell, nz)
            if axis == "gx":
                at_row = jnp.where(x == jnp.where(above, 0, cx - 1), y, -1)
            else:
                at_row = jnp.where(y == jnp.where(above, 0, cy - 1), x, -1)
            rows[k, pl.ds(n * block, block)] = at_row
            mark(n, at_row, z.T, count, used, chunks, picks[k], marks[k])

        marks[k][...] = jnp.zeros_like(marks[k])
        each(nq // block, pick)
        before = halos[k][: nv * count].reshape(nv, count, nz)
        cleared[k][...] = jnp.where(marks[k][...][None] > 0.5, 0.0, before)
        d = 0 if axis == "gx" else 1
        speed = halos[k][(nv + d) * count : (nv + d + 1) * count]
        sides[axis, True] += jnp.where(above, speed, 0.0)
        sides[axis, False] += jnp.where(above, 0.0, speed)

    coefs[...] = given[...]
    for (axis, high), speed in sides.items():
        if axis == "gx":
            d, edge = 0, (cx - 1 if high else 0,)
        else:
            d, edge = 1, (slice(None), cy - 1 if high else 0)
        mine = vel[(d,) + edge]
        speed = jnp.broadcast_to(speed, mine.shape)
        if high:
            of_low, of_high = face(mine, speed)
            coefs[(2 * d + 1,) + edge] = -of_high
            coefs[(6,) + edge] -= of_low
        else:
            of_low, of_high = face(speed, mine)
            coefs[(2 * d,) + edge] = of_low
            coefs[(6,) + edge] += of_high


def step_kernel(kinds, slots, ng, ngy, vel, aims, base, received, coefs, rows_there, *rest):
    halos, cleared = rest[: len(kinds)], rest[len(kinds) : 2 * len(kinds)]
    picks = rest[2 * len(kinds) : 3 * len(kinds) + 1]
    out, ext, field, acc, result, sems = rest[3 * len(kinds) + 1 :]
    nv, cx, cy, nz = base.shape
    lanes = nz
    nq = received.shape[0] // ng
    per = lanes // slots
    chunks = block // per
    used = (ng - 1) * chunks
    spread = spread_of(cx)
    me = lax.axis_index("grp")
    lane = lax.broadcasted_iota(jnp.int32, (nv, lanes), 1) // slots
    above = [partner_above(axis, phase) for axis, phase, _ in kinds]

    parts = [(cx // spread * cy, spread)]
    parts += [(cy if axis == "gx" else cx, 1) for axis, _, _ in kinds]
    starts = [0]
    for count, groups in parts:
        starts.append(starts[-1] + 2 * nv * count * groups)

    def fill(n):
        for part, (count, groups) in enumerate(parts):
            if part == 0:
                cell = aims[pl.ds(n * block, block)].astype(jnp.int32) + cx * cy * nz
                x, y = over(cell, nz * cy), rest_of(over(cell, nz), cy)
                at_row = over(x, spread) * cy + y
            else:
                at_row = rows_there[part - 1, pl.ds(n * block, block)]
            up = lax.broadcasted_iota(jnp.int32, (count, lanes), 0)
            here = slice(part // per * lanes, (part // per + 1) * lanes)
            lefts = []
            for away in range(1, ng):
                g = (me + away) % ng
                for c in range(chunks):
                    at = (away - 1) * chunks + c
                    value = None
                    for p in range(per):
                        source = n * block + p * chunks + c
                        piece = received[place(ng, nq // ngy, ngy, g, source), :, here]
                        turn = (p - part) % per
                        if turn:
                            piece = pltpu.roll(piece, turn * slots, 1)
                        value = piece if value is None else jnp.where(lane == p, piece, value)
                    high = value.astype(jnp.bfloat16).astype(jnp.float32)
                    low = value - high
                    hit = up == at_row[at : at + 1]
                    pieces = [jnp.where(hit, high[v : v + 1], 0.0) for v in range(nv)]
                    pieces += [jnp.where(hit, low[v : v + 1], 0.0) for v in range(nv)]
                    lefts.append(jnp.concatenate(pieces, axis=0).astype(jnp.bfloat16))
            chosen = picks[part][pl.ds(pl.multiple_of(n * used * lanes, lanes), used * lanes)]
            total = jnp.dot(
                jnp.concatenate(lefts, axis=1), chosen, preferred_element_type=jnp.float32
            )
            rows = total.shape[0]
            for s in range(groups):
                start = starts[part] + s * 2 * nv * count
                value = total[:, s * nz : (s + 1) * nz]
                if nq == block:
                    acc[start : start + rows] = value
                else:
                    acc[start : start + rows] += value

    if nq != block:
        acc[...] = jnp.zeros_like(acc)
    each(nq // block, fill)

    def brought(part, s):
        count = parts[part][0]
        start = starts[part] + s * 2 * nv * count
        new = acc[start : start + nv * count] + acc[start + nv * count : start + 2 * nv * count]
        return new.reshape(nv, count, nz)

    def crossed(n, speeds, fields):
        a, b = (n + 1) % 3, (n + 2) % 3
        return speeds[b] * fields[a] - speeds[a] * fields[b]

    inside = slice(top, top + cy)
    for s in range(spread):
        new = brought(0, s)
        for n, x in enumerate(range(s, cx, spread)):
            state = base[:, x] + new[:, n * cy : (n + 1) * cy]
            ext[:fluid_count, 1 + x, inside] = state[:fluid_count]
            field[:, x] = state[fluid_count:]
            for d in range(3):
                ext[fluid_count + d, 1 + x, inside] = crossed(d, vel[:, x], state[fluid_count:])

    sides = {("gx", True): 0.0, ("gx", False): 0.0, ("gy", True): 0.0, ("gy", False): 0.0}
    for n, (axis, _, _) in enumerate(kinds):
        count = parts[n + 1][0]
        d = 0 if axis == "gx" else 1
        halo = halos[n][: (nv + 3) * count].reshape(nv + 3, count, nz)
        state = cleared[n][...] + brought(n + 1, 0)
        electric = [crossed(m, halo[nv:], state[fluid_count:])[None] for m in (1 - d, 2)]
        halo = jnp.concatenate([state[:fluid_count]] + electric, axis=0)
        sides[axis, True] += jnp.where(above[n], halo, 0.0)
        sides[axis, False] += jnp.where(above[n], 0.0, halo)

    for (axis, high), halo in sides.items():
        d = 0 if axis == "gx" else 1
        halo = jnp.broadcast_to(halo, (fluid_count + 2, cx if d else cy, nz))
        if d == 0:
            at = (cx + 1 if high else 0, inside)
        else:
            at = (slice(1, cx + 1), top + cy if high else top - 1)
        ext[(slice(0, fluid_count),) + at] = halo[:fluid_count]
        ext[(fluid_count + 1 - d,) + at] = halo[fluid_count]
        ext[(fluid_count + 2,) + at] = halo[fluid_count + 1]

    copies = []

    def finish(v, value):
        result[v] = value
        copies.append(pltpu.make_async_copy(result.at[v], out.at[v], sems.at[v]))
        copies[-1].start()

    def central(n, d):
        v = fluid_count + n
        return shifted(ext, v, cx, cy, d, 1) - shifted(ext, v, cx, cy, d, -1)

    for n in range(3):
        a, b = (n + 1) % 3, (n + 2) % 3
        curl = central(b, a) - central(a, b)
        finish(fluid_count + n, field[n] - (0.5 * courant_number) * curl)
    for v in range(fluid_count):
        total = coefs[6] * window(ext, v, cx, cy)
        for d in range(3):
            total = total + coefs[2 * d] * shifted(ext, v, cx, cy, d, -1)
            total = total + coefs[2 * d + 1] * shifted(ext, v, cx, cy, d, 1)
        finish(v, total)
    for copy in copies:
        copy.wait()


def per_device(ngx, ngy, conserved, velocity, donor_corner, donor_fraction, target_cell):
    kinds = exchanges(ngx, ngy)
    cons = conserved[:, 0]
    vel = velocity[:, 0]
    corner = donor_corner[0, 0, 0]
    fraction = donor_fraction[:, 0, 0, 0]
    target = target_cell[0, 0, 0]
    nv, cx, cy, nz = cons.shape
    ng, nq, slots = corner.shape
    rows = cx * cy
    per = nz // slots
    tiles = -(-(1 + len(kinds)) // per)
    f32 = jnp.float32

    def shape(*dims):
        return jax.ShapeDtypeStruct(dims, f32)

    params = pltpu.CompilerParams(vmem_limit_bytes=(12 + nq // 2) << 20)
    alongs = [cy if axis == "gx" else cx for axis, _, _ in kinds]
    pay_shapes = [((nv + 3) * along + nq, nz) for along in alongs]
    blended = pl.pallas_call(
        functools.partial(blend_kernel, ngy, kinds),
        out_shape=pltpu.VMEM((ng * nq, nv, tiles * nz), f32),
        in_specs=[pl.BlockSpec(memory_space=pl.ANY)] * 3,
        scratch_shapes=[
            pltpu.VMEM(cons.shape, f32),
            pltpu.VMEM(corner.shape, jnp.int32),
            pltpu.VMEM(fraction.shape, f32),
            pltpu.VMEM((nv * rows, 3 * nz), jnp.bfloat16),
            pltpu.VMEM((ng - 1, 3 * nz, block * slots), jnp.bfloat16),
            pltpu.VMEM((ng - 1, rows, block * slots), f32),
            pltpu.VMEM((ng - 1, per, nq // per, nv, nz), f32),
            pltpu.SemaphoreType.DMA((3,)),
        ],
        compiler_params=params,
        name="blend",
    )(*(pltpu.with_memory_space_constraint(value, pltpu.HBM) for value in (cons, corner, fraction)))

    aims, *pays = pl.pallas_call(
        functools.partial(edge_kernel, kinds),
        out_shape=[pltpu.VMEM((nq, nz), f32)] + [pltpu.VMEM(dims, f32) for dims in pay_shapes],
        in_specs=[pl.BlockSpec(memory_space=pltpu.VMEM)] * 3 + [pl.BlockSpec(memory_space=pl.ANY)],
        compiler_params=params,
        name="edge",
    )(cons, vel, target, blended)

    received = lax.all_to_all(
        blended, ("gy", "grp", "gx"), split_axis=0, concat_axis=0, tiled=True
    )
    halos = []
    for (axis, phase, _), pay in zip(kinds, pays):
        count = ngx if axis == "gx" else ngy
        pairs = []
        for low in range(phase, count - 1, 2):
            pairs += [(low, low + 1), (low + 1, low)]
        halos.append(lax.ppermute(pay, axis, pairs))

    spread = spread_of(cx)
    coefs, base, picks = pl.pallas_call(
        functools.partial(prepare_kernel, slots, ng),
        out_shape=[
            pltpu.VMEM((7, cx, cy, nz), f32),
            pltpu.VMEM((nv, cx, cy, nz), f32),
            pltpu.VMEM(((ng - 1) * nq * slots, spread * nz), jnp.bfloat16),
        ],
        scratch_shapes=[pltpu.VMEM((rows // spread, spread * nz), f32)],
        compiler_params=params,
        name="prepare",
    )(cons, vel, aims)
    def kept(values):
        return [pltpu.with_memory_space_constraint(value, pltpu.VMEM) for value in values]

    coefs, base, picks = kept((coefs, base, picks))
    border = pl.pallas_call(
        functools.partial(border_kernel, kinds, slots, ng),
        out_shape=[
            pltpu.VMEM((7, cx, cy, nz), f32),
            pltpu.VMEM((len(kinds), nq, nz), jnp.int32),
        ]
        + [pltpu.VMEM((nv, along, nz), f32) for along in alongs]
        + [pltpu.VMEM(((ng - 1) * nq * slots, nz), jnp.bfloat16) for _ in kinds],
        scratch_shapes=[pltpu.VMEM((along, nz), f32) for along in alongs],
        compiler_params=params,
        name="border",
    )(vel, coefs, *halos)
    coefs, rows_there, *border = kept(border)
    cleared, picks_there = border[: len(kinds)], border[len(kinds) :]

    result = pl.pallas_call(
        functools.partial(step_kernel, kinds, slots, ng, ngy),
        out_shape=shape(nv, cx, cy, nz),
        out_specs=pl.BlockSpec(memory_space=pl.ANY),
        scratch_shapes=[
            pltpu.VMEM((fluid_count + 3, cx + 2, cy + 2 * top, nz), f32),
            pltpu.VMEM((nv - fluid_count, cx, cy, nz), f32),
            pltpu.VMEM((2 * nv * (rows + sum(alongs)), nz), f32),
            pltpu.VMEM((nv, cx, cy, nz), f32),
            pltpu.SemaphoreType.DMA((nv,)),
        ],
        compiler_params=params,
        name="step",
    )(vel, aims, base, received, coefs, rows_there, *halos, *cleared, picks, *picks_there)
    return result[:, None]


def solution(mesh):
    return jax.shard_map(
        functools.partial(per_device, mesh.shape["gx"], mesh.shape["gy"]),
        mesh=mesh,
        in_specs=(
            P(None, "grp", "gx", "gy", None),
            P(None, "grp", "gx", "gy", None),
            P("grp", "gx", "gy", None, None, None),
            P(None, "grp", "gx", "gy", None, None, None),
            P("grp", "gx", "gy", None, None, None),
        ),
        out_specs=P(None, "grp", "gx", "gy", None),
        check_vma=False,
    )
```

```python
import functools

import jax
import jax.numpy as jnp
from jax import lax
from jax.experimental import pallas as pl
from jax.experimental.pallas import tpu as pltpu
from jax.sharding import PartitionSpec as P

signal_speed = 0.5
courant_number = 0.3
fluid_count = 5
block = 8


def exchanges(ngx, ngy):
    def partner(count, phase, n):
        other = n + 1 if (n + phase) % 2 == 0 else n - 1
        return other if 0 <= other < count else n

    kinds = []
    for phase in range(min(ngx - 1, 2)):
        kinds.append(("gx", phase, lambda i, j, phase=phase: (partner(ngx, phase, i), j)))
    for phase in range(min(ngy - 1, 2)):
        kinds.append(("gy", phase, lambda i, j, phase=phase: (i, partner(ngy, phase, j))))
    return kinds


def partner_above(axis, phase):
    return (lax.axis_index(axis) + phase) % 2 == 0


def split(value):
    high = value.astype(jnp.bfloat16)
    low = (value - high.astype(jnp.float32)).astype(jnp.bfloat16)
    return high, low


def spread_of(cx):
    return next(n for n in (4, 2, 1) if cx % n == 0)


def over(value, n):
    return value >> (n.bit_length() - 1) if n & (n - 1) == 0 else value // n


def rest_of(value, n):
    return value & (n - 1) if n & (n - 1) == 0 else value % n


def each(count, body):
    if count == 1:
        body(0)
    else:
        lax.fori_loop(0, count, lambda n, c: (body(n), c)[1], 0)


def block_transpose(value, slots):
    rows, lanes = value.shape
    count = lanes // slots
    each_rows = rows // count
    at_row = lax.broadcasted_iota(jnp.int32, value.shape, 0) // each_rows
    at_lane = lax.broadcasted_iota(jnp.int32, value.shape, 1) // slots
    result = value
    for d in range(1, count):
        turned = pltpu.roll(value, d * each_rows, 0)
        turned = pltpu.roll(turned, lanes - d * slots, 1)
        result = jnp.where((at_row - at_lane) % count == d, turned, result)
    return result


def place(ng, ngx, ngy, grid, q):
    return ng * ngx * ngy - 1 - ((q % ngy * ng + grid) * ngx + q // ngy)


def packed(tiles, slots):
    empty = jnp.zeros(tiles[0].shape, tiles[0].dtype)
    return block_transpose(jnp.concatenate(tiles + [empty], axis=1), slots)


def blend_kernel(ngy, kinds, cons, corner, fraction, out, *scratch):
    at_cons, at_corner, at_fraction, uhl, wzs, wxys, moved, arrive = scratch
    nv, cx, cy, nz = cons.shape
    ng, nq, slots = corner.shape
    lanes = nz
    per = lanes // slots
    chunks = block // per
    rows = cx * cy
    me = lax.axis_index("grp")

    moves = [(corner, at_corner), (fraction, at_fraction), (cons, at_cons)]
    ins = [pltpu.make_async_copy(a, b, arrive.at[n]) for n, (a, b) in enumerate(moves)]
    for copy in ins:
        copy.start()

    for q in range(nq):
        at = place(ng, nq // ngy, ngy, me, q)
        out[pl.ds(at, 1)] = jnp.zeros((1,) + out.shape[1:], jnp.float32)

    def weight(count, at, upper):
        place = lax.broadcasted_iota(jnp.int32, (count, lanes), 0)
        return jnp.where(place == at, 1.0 - upper, jnp.where(place == at + 1, upper, 0.0))

    def weigh(n):
        here = pl.ds(n * block, block)
        grids = [(me + away) % ng for away in range(1, ng)]
        cell = packed([at_corner[h, here] for h in grids], slots)
        at_x, at_y, at_z = over(cell, nz * cy), rest_of(over(cell, nz), cy), rest_of(cell, nz)
        fx, fy, fz = (packed([at_fraction[d, h, here] for h in grids], slots) for d in range(3))
        for away in range(1, ng):
            for c in range(chunks):
                row = slice((away - 1) * chunks + c, (away - 1) * chunks + c + 1)
                cols = slice(c * lanes, (c + 1) * lanes)
                wx = weight(cx, at_x[row], fx[row])
                wy = weight(cy, at_y[row], fy[row])
                for x in range(cx):
                    wxys[away - 1, x * cy : (x + 1) * cy, cols] = wx[x : x + 1] * wy
                high, low = split(weight(nz, at_z[row], fz[row]))
                wzs[away - 1, :nz, cols] = high
                wzs[away - 1, nz : 2 * nz, cols] = high
                wzs[away - 1, 2 * nz :, cols] = low

    def blend(n):
        for away in range(1, ng):
            along = jnp.dot(uhl[...], wzs[away - 1], preferred_element_type=jnp.float32)
            along = along.reshape(nv, rows, chunks * lanes)
            values = jnp.sum(along * wxys[away - 1][None], axis=1)
            for c in range(chunks):
                value = values[:, c * lanes : (c + 1) * lanes]
                for turn in range(per):
                    moved[away - 1, turn, n * chunks + c] = (
                        pltpu.roll(value, turn * slots, 1) if turn else value
                    )
            if nq == block:
                assemble(away)

    lane = lax.broadcasted_iota(jnp.int32, (nv, lanes), 1) // slots

    def assemble(away):
        for q in range(nq):
            i, j = q // ngy, q % ngy
            owners = [q] + [a * ngy + b for a, b in (of(i, j) for _, _, of in kinds)]
            for t in range(0, len(owners), per):
                tile = None
                for k, owner in enumerate(owners[t : t + per]):
                    chunk = owner // block * chunks + owner % chunks
                    piece = moved[away - 1, (k - owner % block // chunks) % per, chunk]
                    tile = piece if tile is None else jnp.where(lane == k, piece, tile)
                cols = slice(t // per * lanes, (t // per + 1) * lanes)
                at = place(ng, nq // ngy, ngy, (me + away) % ng, q)
                out[pl.ds(at, 1), :, cols] = tile[None]

    for copy in ins[:2]:
        copy.wait()
    if nq == block:
        weigh(0)
    ins[2].wait()
    high, low = split(at_cons[...].reshape(nv * rows, nz))
    uhl[:, :nz] = high
    uhl[:, nz : 2 * nz] = low
    uhl[:, 2 * nz :] = high
    if nq == block:
        blend(0)
    else:

        def both(n):
            weigh(n)
            blend(n)

        each(nq // block, both)
        for away in range(1, ng):
            assemble(away)


def edge_kernel(kinds, cons, vel, target, sent, aims, *pays):
    del sent
    nv, cx, cy, nz = cons.shape
    ng, nq, slots = target.shape
    me = lax.axis_index("grp")
    for n in range(nq // block):
        here = slice(n * block, (n + 1) * block)
        tiles = [target[(me + away) % ng, here] - cx * cy * nz for away in range(1, ng)]
        aims[here] = packed(tiles, slots).astype(jnp.float32)
    for (axis, phase, _), pay in zip(kinds, pays):
        above = partner_above(axis, phase)
        along = cy if axis == "gx" else cx
        for count, source, start in ((nv, cons, 0), (3, vel, nv * along)):
            if axis == "gx":
                layer = source[:, pl.ds(jnp.where(above, cx - 1, 0), 1)]
            else:
                layer = source[:, :, pl.ds(jnp.where(above, cy - 1, 0), 1)]
            pay[start : start + count * along] = layer.reshape(count * along, nz)
        pay[(nv + 3) * along :] = aims[...]


top = 8


def window(ext, v, cx, cy, move_x=0, move_y=0):
    return ext[v, 1 + move_x : 1 + move_x + cx, top + move_y : top + move_y + cy]


def along_z(value, by):
    nz = value.shape[-1]
    at = lax.broadcasted_iota(jnp.int32, (1,) + value.shape[1:], 2)
    edge = 0 if by < 0 else nz - 1
    return jnp.where(at == edge, 0.0, pltpu.roll(value, (-by) % nz, 2))


def shifted(ext, v, cx, cy, d, by):
    if d == 2 and by:
        return along_z(window(ext, v, cx, cy), by)
    return window(ext, v, cx, cy, by if d == 0 else 0, by if d == 1 else 0)


def face(low, high):
    wave_low = jnp.minimum(jnp.minimum(low, high) - signal_speed, 0.0)
    wave_high = jnp.maximum(jnp.maximum(low, high) + signal_speed, 0.0)
    scale = courant_number / (wave_high - wave_low)
    return (
        scale * wave_high * (low - wave_low),
        scale * wave_low * (wave_high - high),
    )


def mark(n, at_row, at_column, count, used, chunks, picks, marks):
    lanes = at_row.shape[1]
    up = lax.broadcasted_iota(jnp.int32, (count, lanes), 0)
    along = lax.broadcasted_iota(jnp.int32, (lanes, picks.shape[1]), 1)
    for at in range(0, used, chunks):
        hits = []
        for c in range(chunks):
            hits.append(jnp.where(up == at_row[at + c : at + c + 1], 1.0, 0.0))
            to = pl.ds(pl.multiple_of((n * used + at + c) * lanes, lanes), lanes)
            chosen = at_column[:, at + c : at + c + 1] == along
            picks[to] = jnp.where(chosen, 1.0, 0.0).astype(jnp.bfloat16)
        to = pl.ds(pl.multiple_of((n * used + at) * lanes, lanes), chunks * lanes)
        marks[...] += jnp.dot(
            jnp.concatenate(hits, axis=1).astype(jnp.bfloat16),
            picks[to],
            preferred_element_type=jnp.float32,
        )


def prepare_kernel(slots, ng, cons, vel, aims, coefs, base, picks, marks):
    nv, cx, cy, nz = cons.shape
    per = nz // slots
    chunks = block // per
    spread = spread_of(cx)
    count = cx // spread * cy

    def pick(n):
        cell = aims[pl.ds(n * block, block)].astype(jnp.int32) + cx * cy * nz
        x, y, z = over(cell, nz * cy), rest_of(over(cell, nz), cy), rest_of(cell, nz)
        at_row = over(x, spread) * cy + y
        at_column = (rest_of(x, spread) * nz + z).T
        mark(n, at_row, at_column, count, (ng - 1) * chunks, chunks, picks, marks)

    marks[...] = jnp.zeros_like(marks)
    each(aims.shape[0] // block, pick)
    for x in range(cx):
        rows = slice(x // spread * cy, (x // spread + 1) * cy)
        seen = marks[rows, x % spread * nz : (x % spread + 1) * nz]
        base[:, x] = jnp.where(seen[None] > 0.5, 0.0, cons[:, x])

    centre = jnp.ones((cx, cy, nz), jnp.float32)
    none = jnp.zeros((1, cy, nz), jnp.float32)
    low, high = face(vel[0, : cx - 1], vel[0, 1:])
    coefs[0] = jnp.concatenate([none, low], axis=0)
    coefs[1] = -jnp.concatenate([high, none], axis=0)
    centre += jnp.concatenate([none, high], axis=0) - jnp.concatenate([low, none], axis=0)

    at_y = lax.broadcasted_iota(jnp.int32, (1, cy, nz), 1)
    speed = vel[1]
    low, high = face(speed, pltpu.roll(speed, cy - 1, 1))
    low = jnp.where(at_y == cy - 1, 0.0, low)
    high = jnp.where(at_y == cy - 1, 0.0, high)
    coefs[2] = pltpu.roll(low, 1, 1)
    coefs[3] = -high
    centre += pltpu.roll(high, 1, 1) - low

    speed = vel[2]
    up_low, up_high = face(speed, along_z(speed, 1))
    down_low, down_high = face(along_z(speed, -1), speed)
    coefs[4] = down_low
    coefs[5] = -up_high
    coefs[6] = centre + down_high - up_low


def border_kernel(kinds, slots, ng, vel, given, *rest):
    halos = rest[: len(kinds)]
    coefs, rows = rest[len(kinds) : len(kinds) + 2]
    cleared = rest[len(kinds) + 2 : 2 * len(kinds) + 2]
    picks = rest[2 * len(kinds) + 2 : 3 * len(kinds) + 2]
    marks = rest[3 * len(kinds) + 2 :]
    cx, cy, nz = vel.shape[1:]
    nq = rows.shape[1]
    chunks = block // (nz // slots)
    used = (ng - 1) * chunks

    sides = {("gx", True): 0.0, ("gx", False): 0.0, ("gy", True): 0.0, ("gy", False): 0.0}
    for k, (axis, phase, _) in enumerate(kinds):
        above = partner_above(axis, phase)
        nv, count = cleared[k].shape[:2]

        def pick(n):
            cell = halos[k][pl.ds((nv + 3) * count + n * block, block)].astype(jnp.int32)
            cell = cell + cx * cy * nz
            x, y, z = over(cell, nz * cy), rest_of(over(cell, nz), cy), rest_of(cell, nz)
            if axis == "gx":
                at_row = jnp.where(x == jnp.where(above, 0, cx - 1), y, -1)
            else:
                at_row = jnp.where(y == jnp.where(above, 0, cy - 1), x, -1)
            rows[k, pl.ds(n * block, block)] = at_row
            mark(n, at_row, z.T, count, used, chunks, picks[k], marks[k])

        marks[k][...] = jnp.zeros_like(marks[k])
        each(nq // block, pick)
        before = halos[k][: nv * count].reshape(nv, count, nz)
        cleared[k][...] = jnp.where(marks[k][...][None] > 0.5, 0.0, before)
        d = 0 if axis == "gx" else 1
        speed = halos[k][(nv + d) * count : (nv + d + 1) * count]
        sides[axis, True] += jnp.where(above, speed, 0.0)
        sides[axis, False] += jnp.where(above, 0.0, speed)

    coefs[...] = given[...]
    for (axis, high), speed in sides.items():
        if axis == "gx":
            d, edge = 0, (cx - 1 if high else 0,)
        else:
            d, edge = 1, (slice(None), cy - 1 if high else 0)
        mine = vel[(d,) + edge]
        speed = jnp.broadcast_to(speed, mine.shape)
        if high:
            of_low, of_high = face(mine, speed)
            coefs[(2 * d + 1,) + edge] = -of_high
            coefs[(6,) + edge] -= of_low
        else:
            of_low, of_high = face(speed, mine)
            coefs[(2 * d,) + edge] = of_low
            coefs[(6,) + edge] += of_high


def step_kernel(kinds, slots, ng, ngy, vel, aims, base, received, coefs, rows_there, *rest):
    halos, cleared = rest[: len(kinds)], rest[len(kinds) : 2 * len(kinds)]
    picks = rest[2 * len(kinds) : 3 * len(kinds) + 1]
    out, ext, field, acc, result, sems = rest[3 * len(kinds) + 1 :]
    nv, cx, cy, nz = base.shape
    lanes = nz
    nq = received.shape[0] // ng
    per = lanes // slots
    chunks = block // per
    used = (ng - 1) * chunks
    spread = spread_of(cx)
    me = lax.axis_index("grp")
    lane = lax.broadcasted_iota(jnp.int32, (nv, lanes), 1) // slots
    above = [partner_above(axis, phase) for axis, phase, _ in kinds]

    parts = [(cx // spread * cy, spread)]
    parts += [(cy if axis == "gx" else cx, 1) for axis, _, _ in kinds]
    starts = [0]
    for count, groups in parts:
        starts.append(starts[-1] + 2 * nv * count * groups)

    def fill(n):
        for part, (count, groups) in enumerate(parts):
            if part == 0:
                cell = aims[pl.ds(n * block, block)].astype(jnp.int32) + cx * cy * nz
                x, y = over(cell, nz * cy), rest_of(over(cell, nz), cy)
                at_row = over(x, spread) * cy + y
            else:
                at_row = rows_there[part - 1, pl.ds(n * block, block)]
            up = lax.broadcasted_iota(jnp.int32, (count, lanes), 0)
            here = slice(part // per * lanes, (part // per + 1) * lanes)
            lefts = []
            for away in range(1, ng):
                g = (me + away) % ng
                for c in range(chunks):
                    at = (away - 1) * chunks + c
                    value = None
                    for p in range(per):
                        source = n * block + p * chunks + c
                        piece = received[place(ng, nq // ngy, ngy, g, source), :, here]
                        turn = (p - part) % per
                        if turn:
                            piece = pltpu.roll(piece, turn * slots, 1)
                        value = piece if value is None else jnp.where(lane == p, piece, value)
                    high = value.astype(jnp.bfloat16).astype(jnp.float32)
                    low = value - high
                    hit = up == at_row[at : at + 1]
                    pieces = [jnp.where(hit, high[v : v + 1], 0.0) for v in range(nv)]
                    pieces += [jnp.where(hit, low[v : v + 1], 0.0) for v in range(nv)]
                    lefts.append(jnp.concatenate(pieces, axis=0).astype(jnp.bfloat16))
            chosen = picks[part][pl.ds(pl.multiple_of(n * used * lanes, lanes), used * lanes)]
            total = jnp.dot(
                jnp.concatenate(lefts, axis=1), chosen, preferred_element_type=jnp.float32
            )
            rows = total.shape[0]
            for s in range(groups):
                start = starts[part] + s * 2 * nv * count
                value = total[:, s * nz : (s + 1) * nz]
                if nq == block:
                    acc[start : start + rows] = value
                else:
                    acc[start : start + rows] += value

    if nq != block:
        acc[...] = jnp.zeros_like(acc)
    each(nq // block, fill)

    def brought(part, s):
        count = parts[part][0]
        start = starts[part] + s * 2 * nv * count
        new = acc[start : start + nv * count] + acc[start + nv * count : start + 2 * nv * count]
        return new.reshape(nv, count, nz)

    def crossed(n, speeds, fields):
        a, b = (n + 1) % 3, (n + 2) % 3
        return speeds[b] * fields[a] - speeds[a] * fields[b]

    inside = slice(top, top + cy)
    for s in range(spread):
        new = brought(0, s)
        for n, x in enumerate(range(s, cx, spread)):
            state = base[:, x] + new[:, n * cy : (n + 1) * cy]
            ext[:fluid_count, 1 + x, inside] = state[:fluid_count]
            field[:, x] = state[fluid_count:]
            for d in range(3):
                ext[fluid_count + d, 1 + x, inside] = crossed(d, vel[:, x], state[fluid_count:])

    sides = {("gx", True): 0.0, ("gx", False): 0.0, ("gy", True): 0.0, ("gy", False): 0.0}
    for n, (axis, _, _) in enumerate(kinds):
        count = parts[n + 1][0]
        d = 0 if axis == "gx" else 1
        halo = halos[n][: (nv + 3) * count].reshape(nv + 3, count, nz)
        state = cleared[n][...] + brought(n + 1, 0)
        electric = [crossed(m, halo[nv:], state[fluid_count:])[None] for m in (1 - d, 2)]
        halo = jnp.concatenate([state[:fluid_count]] + electric, axis=0)
        sides[axis, True] += jnp.where(above[n], halo, 0.0)
        sides[axis, False] += jnp.where(above[n], 0.0, halo)

    for (axis, high), halo in sides.items():
        d = 0 if axis == "gx" else 1
        halo = jnp.broadcast_to(halo, (fluid_count + 2, cx if d else cy, nz))
        if d == 0:
            at = (cx + 1 if high else 0, inside)
        else:
            at = (slice(1, cx + 1), top + cy if high else top - 1)
        ext[(slice(0, fluid_count),) + at] = halo[:fluid_count]
        ext[(fluid_count + 1 - d,) + at] = halo[fluid_count]
        ext[(fluid_count + 2,) + at] = halo[fluid_count + 1]

    copies = []

    def finish(v, value):
        result[v] = value
        copies.append(pltpu.make_async_copy(result.at[v], out.at[v], sems.at[v]))
        copies[-1].start()

    def central(n, d):
        v = fluid_count + n
        return shifted(ext, v, cx, cy, d, 1) - shifted(ext, v, cx, cy, d, -1)

    for n in range(3):
        a, b = (n + 1) % 3, (n + 2) % 3
        curl = central(b, a) - central(a, b)
        finish(fluid_count + n, field[n] - (0.5 * courant_number) * curl)
    for v in range(fluid_count):
        total = coefs[6] * window(ext, v, cx, cy)
        for d in range(3):
            total = total + coefs[2 * d] * shifted(ext, v, cx, cy, d, -1)
            total = total + coefs[2 * d + 1] * shifted(ext, v, cx, cy, d, 1)
        finish(v, total)
    for copy in copies:
        copy.wait()


def per_device(ngx, ngy, conserved, velocity, donor_corner, donor_fraction, target_cell):
    kinds = exchanges(ngx, ngy)
    cons = conserved[:, 0]
    vel = velocity[:, 0]
    corner = donor_corner[0, 0, 0]
    fraction = donor_fraction[:, 0, 0, 0]
    target = target_cell[0, 0, 0]
    nv, cx, cy, nz = cons.shape
    ng, nq, slots = corner.shape
    rows = cx * cy
    per = nz // slots
    tiles = -(-(1 + len(kinds)) // per)
    f32 = jnp.float32

    def shape(*dims):
        return jax.ShapeDtypeStruct(dims, f32)

    params = pltpu.CompilerParams(vmem_limit_bytes=(12 + nq // 2) << 20)
    alongs = [cy if axis == "gx" else cx for axis, _, _ in kinds]
    pay_shapes = [((nv + 3) * along + nq, nz) for along in alongs]
    blended = pl.pallas_call(
        functools.partial(blend_kernel, ngy, kinds),
        out_shape=pltpu.VMEM((ng * nq, nv, tiles * nz), f32),
        in_specs=[pl.BlockSpec(memory_space=pl.ANY)] * 3,
        scratch_shapes=[
            pltpu.VMEM(cons.shape, f32),
            pltpu.VMEM(corner.shape, jnp.int32),
            pltpu.VMEM(fraction.shape, f32),
            pltpu.VMEM((nv * rows, 3 * nz), jnp.bfloat16),
            pltpu.VMEM((ng - 1, 3 * nz, block * slots), jnp.bfloat16),
            pltpu.VMEM((ng - 1, rows, block * slots), f32),
            pltpu.VMEM((ng - 1, per, nq // per, nv, nz), f32),
            pltpu.SemaphoreType.DMA((3,)),
        ],
        compiler_params=params,
        name="blend",
    )(*(pltpu.with_memory_space_constraint(value, pltpu.HBM) for value in (cons, corner, fraction)))

    aims, *pays = pl.pallas_call(
        functools.partial(edge_kernel, kinds),
        out_shape=[pltpu.VMEM((nq, nz), f32)] + [pltpu.VMEM(dims, f32) for dims in pay_shapes],
        in_specs=[pl.BlockSpec(memory_space=pltpu.VMEM)] * 3 + [pl.BlockSpec(memory_space=pl.ANY)],
        compiler_params=params,
        name="edge",
    )(cons, vel, target, blended)

    received = lax.all_to_all(
        blended,
        ("gy", "grp", "gx"),
        split_axis=0,
        concat_axis=0,
        tiled=True,
        axis_index_groups=[list(reversed(range(ng * nq)))],
    )
    halos = []
    for (axis, phase, _), pay in zip(kinds, pays):
        count = ngx if axis == "gx" else ngy
        pairs = []
        for low in range(phase, count - 1, 2):
            pairs += [(low, low + 1), (low + 1, low)]
        halos.append(lax.ppermute(pay, axis, pairs))

    spread = spread_of(cx)
    coefs, base, picks = pl.pallas_call(
        functools.partial(prepare_kernel, slots, ng),
        out_shape=[
            pltpu.VMEM((7, cx, cy, nz), f32),
            pltpu.VMEM((nv, cx, cy, nz), f32),
            pltpu.VMEM(((ng - 1) * nq * slots, spread * nz), jnp.bfloat16),
        ],
        scratch_shapes=[pltpu.VMEM((rows // spread, spread * nz), f32)],
        compiler_params=params,
        name="prepare",
    )(cons, vel, aims)
    def kept(values):
        return [pltpu.with_memory_space_constraint(value, pltpu.VMEM) for value in values]

    coefs, base, picks = kept((coefs, base, picks))
    border = pl.pallas_call(
        functools.partial(border_kernel, kinds, slots, ng),
        out_shape=[
            pltpu.VMEM((7, cx, cy, nz), f32),
            pltpu.VMEM((len(kinds), nq, nz), jnp.int32),
        ]
        + [pltpu.VMEM((nv, along, nz), f32) for along in alongs]
        + [pltpu.VMEM(((ng - 1) * nq * slots, nz), jnp.bfloat16) for _ in kinds],
        scratch_shapes=[pltpu.VMEM((along, nz), f32) for along in alongs],
        compiler_params=params,
        name="border",
    )(vel, coefs, *halos)
    coefs, rows_there, *border = kept(border)
    cleared, picks_there = border[: len(kinds)], border[len(kinds) :]

    result = pl.pallas_call(
        functools.partial(step_kernel, kinds, slots, ng, ngy),
        out_shape=shape(nv, cx, cy, nz),
        out_specs=pl.BlockSpec(memory_space=pl.ANY),
        scratch_shapes=[
            pltpu.VMEM((fluid_count + 3, cx + 2, cy + 2 * top, nz), f32),
            pltpu.VMEM((nv - fluid_count, cx, cy, nz), f32),
            pltpu.VMEM((2 * nv * (rows + sum(alongs)), nz), f32),
            pltpu.VMEM((nv, cx, cy, nz), f32),
            pltpu.SemaphoreType.DMA((nv,)),
        ],
        compiler_params=params,
        name="step",
    )(vel, aims, base, received, coefs, rows_there, *halos, *cleared, picks, *picks_there)
    return result[:, None]


def solution(mesh):
    return jax.shard_map(
        functools.partial(per_device, mesh.shape["gx"], mesh.shape["gy"]),
        mesh=mesh,
        in_specs=(
            P(None, "grp", "gx", "gy", None),
            P(None, "grp", "gx", "gy", None),
            P("grp", "gx", "gy", None, None, None),
            P(None, "grp", "gx", "gy", None, None, None),
            P("grp", "gx", "gy", None, None, None),
        ),
        out_specs=P(None, "grp", "gx", "gy", None),
        check_vma=False,
    )
```

```python
import functools

import jax
import jax.numpy as jnp
from jax import lax
from jax.experimental import pallas as pl
from jax.experimental.pallas import tpu as pltpu
from jax.sharding import PartitionSpec as P

signal_speed = 0.5
courant_number = 0.3
fluid_count = 5
block = 8


def exchanges(ngx, ngy):
    def partner(count, phase, n):
        other = n + 1 if (n + phase) % 2 == 0 else n - 1
        return other if 0 <= other < count else n

    kinds = []
    for phase in range(min(ngx - 1, 2)):
        kinds.append(("gx", phase, lambda i, j, phase=phase: (partner(ngx, phase, i), j)))
    for phase in range(min(ngy - 1, 2)):
        kinds.append(("gy", phase, lambda i, j, phase=phase: (i, partner(ngy, phase, j))))
    return kinds


def partner_above(axis, phase):
    return (lax.axis_index(axis) + phase) % 2 == 0


def split(value):
    high = value.astype(jnp.bfloat16)
    low = (value - high.astype(jnp.float32)).astype(jnp.bfloat16)
    return high, low


def spread_of(cx):
    return next(n for n in (4, 2, 1) if cx % n == 0)


def over(value, n):
    return value >> (n.bit_length() - 1) if n & (n - 1) == 0 else value // n


def rest_of(value, n):
    return value & (n - 1) if n & (n - 1) == 0 else value % n


def each(count, body):
    if count == 1:
        body(0)
    else:
        lax.fori_loop(0, count, lambda n, c: (body(n), c)[1], 0)


def block_transpose(value, slots):
    rows, lanes = value.shape
    count = lanes // slots
    each_rows = rows // count
    at_row = lax.broadcasted_iota(jnp.int32, value.shape, 0) // each_rows
    at_lane = lax.broadcasted_iota(jnp.int32, value.shape, 1) // slots
    result = value
    for d in range(1, count):
        turned = pltpu.roll(value, d * each_rows, 0)
        turned = pltpu.roll(turned, lanes - d * slots, 1)
        result = jnp.where((at_row - at_lane) % count == d, turned, result)
    return result


def place(ng, ngx, ngy, grid, q):
    return ng * ngx * ngy - 1 - (grid * ngx * ngy + q)


def packed(tiles, slots):
    empty = jnp.zeros(tiles[0].shape, tiles[0].dtype)
    return block_transpose(jnp.concatenate(tiles + [empty], axis=1), slots)


def blend_kernel(ngy, kinds, cons, corner, fraction, out, *scratch):
    at_cons, at_corner, at_fraction, uhl, wzs, wxys, moved, arrive = scratch
    nv, cx, cy, nz = cons.shape
    ng, nq, slots = corner.shape
    lanes = nz
    per = lanes // slots
    chunks = block // per
    rows = cx * cy
    me = lax.axis_index("grp")

    moves = [(corner, at_corner), (fraction, at_fraction), (cons, at_cons)]
    ins = [pltpu.make_async_copy(a, b, arrive.at[n]) for n, (a, b) in enumerate(moves)]
    for copy in ins:
        copy.start()

    for q in range(nq):
        at = place(ng, nq // ngy, ngy, me, q)
        out[pl.ds(at, 1)] = jnp.zeros((1,) + out.shape[1:], jnp.float32)

    def weight(count, at, upper):
        place = lax.broadcasted_iota(jnp.int32, (count, lanes), 0)
        return jnp.where(place == at, 1.0 - upper, jnp.where(place == at + 1, upper, 0.0))

    def weigh(n):
        here = pl.ds(n * block, block)
        grids = [(me + away) % ng for away in range(1, ng)]
        cell = packed([at_corner[h, here] for h in grids], slots)
        at_x, at_y, at_z = over(cell, nz * cy), rest_of(over(cell, nz), cy), rest_of(cell, nz)
        fx, fy, fz = (packed([at_fraction[d, h, here] for h in grids], slots) for d in range(3))
        for away in range(1, ng):
            for c in range(chunks):
                row = slice((away - 1) * chunks + c, (away - 1) * chunks + c + 1)
                cols = slice(c * lanes, (c + 1) * lanes)
                wx = weight(cx, at_x[row], fx[row])
                wy = weight(cy, at_y[row], fy[row])
                for x in range(cx):
                    wxys[away - 1, x * cy : (x + 1) * cy, cols] = wx[x : x + 1] * wy
                high, low = split(weight(nz, at_z[row], fz[row]))
                wzs[away - 1, :nz, cols] = high
                wzs[away - 1, nz : 2 * nz, cols] = high
                wzs[away - 1, 2 * nz :, cols] = low

    def blend(n):
        for away in range(1, ng):
            along = jnp.dot(uhl[...], wzs[away - 1], preferred_element_type=jnp.float32)
            along = along.reshape(nv, rows, chunks * lanes)
            values = jnp.sum(along * wxys[away - 1][None], axis=1)
            for c in range(chunks):
                value = values[:, c * lanes : (c + 1) * lanes]
                for turn in range(per):
                    moved[away - 1, turn, n * chunks + c] = (
                        pltpu.roll(value, turn * slots, 1) if turn else value
                    )
            if nq == block:
                assemble(away)

    lane = lax.broadcasted_iota(jnp.int32, (nv, lanes), 1) // slots

    def assemble(away):
        for q in range(nq):
            i, j = q // ngy, q % ngy
            owners = [q] + [a * ngy + b for a, b in (of(i, j) for _, _, of in kinds)]
            for t in range(0, len(owners), per):
                tile = None
                for k, owner in enumerate(owners[t : t + per]):
                    chunk = owner // block * chunks + owner % chunks
                    piece = moved[away - 1, (k - owner % block // chunks) % per, chunk]
                    tile = piece if tile is None else jnp.where(lane == k, piece, tile)
                cols = slice(t // per * lanes, (t // per + 1) * lanes)
                at = place(ng, nq // ngy, ngy, (me + away) % ng, q)
                out[pl.ds(at, 1), :, cols] = tile[None]

    for copy in ins[:2]:
        copy.wait()
    if nq == block:
        weigh(0)
    ins[2].wait()
    high, low = split(at_cons[...].reshape(nv * rows, nz))
    uhl[:, :nz] = high
    uhl[:, nz : 2 * nz] = low
    uhl[:, 2 * nz :] = high
    if nq == block:
        blend(0)
    else:

        def both(n):
            weigh(n)
            blend(n)

        each(nq // block, both)
        for away in range(1, ng):
            assemble(away)


def edge_kernel(kinds, cons, vel, target, sent, aims, *pays):
    del sent
    nv, cx, cy, nz = cons.shape
    ng, nq, slots = target.shape
    me = lax.axis_index("grp")
    for n in range(nq // block):
        here = slice(n * block, (n + 1) * block)
        tiles = [target[(me + away) % ng, here] - cx * cy * nz for away in range(1, ng)]
        aims[here] = packed(tiles, slots).astype(jnp.float32)
    for (axis, phase, _), pay in zip(kinds, pays):
        above = partner_above(axis, phase)
        along = cy if axis == "gx" else cx
        for count, source, start in ((nv, cons, 0), (3, vel, nv * along)):
            if axis == "gx":
                layer = source[:, pl.ds(jnp.where(above, cx - 1, 0), 1)]
            else:
                layer = source[:, :, pl.ds(jnp.where(above, cy - 1, 0), 1)]
            pay[start : start + count * along] = layer.reshape(count * along, nz)
        pay[(nv + 3) * along :] = aims[...]


top = 8


def window(ext, v, cx, cy, move_x=0, move_y=0):
    return ext[v, 1 + move_x : 1 + move_x + cx, top + move_y : top + move_y + cy]


def along_z(value, by):
    nz = value.shape[-1]
    at = lax.broadcasted_iota(jnp.int32, (1,) + value.shape[1:], 2)
    edge = 0 if by < 0 else nz - 1
    return jnp.where(at == edge, 0.0, pltpu.roll(value, (-by) % nz, 2))


def shifted(ext, v, cx, cy, d, by):
    if d == 2 and by:
        return along_z(window(ext, v, cx, cy), by)
    return window(ext, v, cx, cy, by if d == 0 else 0, by if d == 1 else 0)


def face(low, high):
    wave_low = jnp.minimum(jnp.minimum(low, high) - signal_speed, 0.0)
    wave_high = jnp.maximum(jnp.maximum(low, high) + signal_speed, 0.0)
    scale = courant_number / (wave_high - wave_low)
    return (
        scale * wave_high * (low - wave_low),
        scale * wave_low * (wave_high - high),
    )


def mark(n, at_row, at_column, count, used, chunks, picks, marks):
    lanes = at_row.shape[1]
    up = lax.broadcasted_iota(jnp.int32, (count, lanes), 0)
    along = lax.broadcasted_iota(jnp.int32, (lanes, picks.shape[1]), 1)
    for at in range(0, used, chunks):
        hits = []
        for c in range(chunks):
            hits.append(jnp.where(up == at_row[at + c : at + c + 1], 1.0, 0.0))
            to = pl.ds(pl.multiple_of((n * used + at + c) * lanes, lanes), lanes)
            chosen = at_column[:, at + c : at + c + 1] == along
            picks[to] = jnp.where(chosen, 1.0, 0.0).astype(jnp.bfloat16)
        to = pl.ds(pl.multiple_of((n * used + at) * lanes, lanes), chunks * lanes)
        marks[...] += jnp.dot(
            jnp.concatenate(hits, axis=1).astype(jnp.bfloat16),
            picks[to],
            preferred_element_type=jnp.float32,
        )


def prepare_kernel(slots, ng, cons, vel, aims, coefs, base, picks, marks):
    nv, cx, cy, nz = cons.shape
    per = nz // slots
    chunks = block // per
    spread = spread_of(cx)
    count = cx // spread * cy

    def pick(n):
        cell = aims[pl.ds(n * block, block)].astype(jnp.int32) + cx * cy * nz
        x, y, z = over(cell, nz * cy), rest_of(over(cell, nz), cy), rest_of(cell, nz)
        at_row = over(x, spread) * cy + y
        at_column = (rest_of(x, spread) * nz + z).T
        mark(n, at_row, at_column, count, (ng - 1) * chunks, chunks, picks, marks)

    marks[...] = jnp.zeros_like(marks)
    each(aims.shape[0] // block, pick)
    for x in range(cx):
        rows = slice(x // spread * cy, (x // spread + 1) * cy)
        seen = marks[rows, x % spread * nz : (x % spread + 1) * nz]
        base[:, x] = jnp.where(seen[None] > 0.5, 0.0, cons[:, x])

    centre = jnp.ones((cx, cy, nz), jnp.float32)
    none = jnp.zeros((1, cy, nz), jnp.float32)
    low, high = face(vel[0, : cx - 1], vel[0, 1:])
    coefs[0] = jnp.concatenate([none, low], axis=0)
    coefs[1] = -jnp.concatenate([high, none], axis=0)
    centre += jnp.concatenate([none, high], axis=0) - jnp.concatenate([low, none], axis=0)

    at_y = lax.broadcasted_iota(jnp.int32, (1, cy, nz), 1)
    speed = vel[1]
    low, high = face(speed, pltpu.roll(speed, cy - 1, 1))
    low = jnp.where(at_y == cy - 1, 0.0, low)
    high = jnp.where(at_y == cy - 1, 0.0, high)
    coefs[2] = pltpu.roll(low, 1, 1)
    coefs[3] = -high
    centre += pltpu.roll(high, 1, 1) - low

    speed = vel[2]
    up_low, up_high = face(speed, along_z(speed, 1))
    down_low, down_high = face(along_z(speed, -1), speed)
    coefs[4] = down_low
    coefs[5] = -up_high
    coefs[6] = centre + down_high - up_low


def border_kernel(kinds, slots, ng, vel, given, *rest):
    halos = rest[: len(kinds)]
    coefs, rows = rest[len(kinds) : len(kinds) + 2]
    cleared = rest[len(kinds) + 2 : 2 * len(kinds) + 2]
    picks = rest[2 * len(kinds) + 2 : 3 * len(kinds) + 2]
    marks = rest[3 * len(kinds) + 2 :]
    cx, cy, nz = vel.shape[1:]
    nq = rows.shape[1]
    chunks = block // (nz // slots)
    used = (ng - 1) * chunks

    sides = {("gx", True): 0.0, ("gx", False): 0.0, ("gy", True): 0.0, ("gy", False): 0.0}
    for k, (axis, phase, _) in enumerate(kinds):
        above = partner_above(axis, phase)
        nv, count = cleared[k].shape[:2]

        def pick(n):
            cell = halos[k][pl.ds((nv + 3) * count + n * block, block)].astype(jnp.int32)
            cell = cell + cx * cy * nz
            x, y, z = over(cell, nz * cy), rest_of(over(cell, nz), cy), rest_of(cell, nz)
            if axis == "gx":
                at_row = jnp.where(x == jnp.where(above, 0, cx - 1), y, -1)
            else:
                at_row = jnp.where(y == jnp.where(above, 0, cy - 1), x, -1)
            rows[k, pl.ds(n * block, block)] = at_row
            mark(n, at_row, z.T, count, used, chunks, picks[k], marks[k])

        marks[k][...] = jnp.zeros_like(marks[k])
        each(nq // block, pick)
        before = halos[k][: nv * count].reshape(nv, count, nz)
        cleared[k][...] = jnp.where(marks[k][...][None] > 0.5, 0.0, before)
        d = 0 if axis == "gx" else 1
        speed = halos[k][(nv + d) * count : (nv + d + 1) * count]
        sides[axis, True] += jnp.where(above, speed, 0.0)
        sides[axis, False] += jnp.where(above, 0.0, speed)

    coefs[...] = given[...]
    for (axis, high), speed in sides.items():
        if axis == "gx":
            d, edge = 0, (cx - 1 if high else 0,)
        else:
            d, edge = 1, (slice(None), cy - 1 if high else 0)
        mine = vel[(d,) + edge]
        speed = jnp.broadcast_to(speed, mine.shape)
        if high:
            of_low, of_high = face(mine, speed)
            coefs[(2 * d + 1,) + edge] = -of_high
            coefs[(6,) + edge] -= of_low
        else:
            of_low, of_high = face(speed, mine)
            coefs[(2 * d,) + edge] = of_low
            coefs[(6,) + edge] += of_high


def step_kernel(kinds, slots, ng, ngy, vel, aims, base, received, coefs, rows_there, *rest):
    halos, cleared = rest[: len(kinds)], rest[len(kinds) : 2 * len(kinds)]
    picks = rest[2 * len(kinds) : 3 * len(kinds) + 1]
    out, ext, field, acc, result, sems = rest[3 * len(kinds) + 1 :]
    nv, cx, cy, nz = base.shape
    lanes = nz
    nq = received.shape[0] // ng
    per = lanes // slots
    chunks = block // per
    used = (ng - 1) * chunks
    spread = spread_of(cx)
    me = lax.axis_index("grp")
    lane = lax.broadcasted_iota(jnp.int32, (nv, lanes), 1) // slots
    above = [partner_above(axis, phase) for axis, phase, _ in kinds]

    parts = [(cx // spread * cy, spread)]
    parts += [(cy if axis == "gx" else cx, 1) for axis, _, _ in kinds]
    starts = [0]
    for count, groups in parts:
        starts.append(starts[-1] + 2 * nv * count * groups)

    def fill(n):
        for part, (count, groups) in enumerate(parts):
            if part == 0:
                cell = aims[pl.ds(n * block, block)].astype(jnp.int32) + cx * cy * nz
                x, y = over(cell, nz * cy), rest_of(over(cell, nz), cy)
                at_row = over(x, spread) * cy + y
            else:
                at_row = rows_there[part - 1, pl.ds(n * block, block)]
            up = lax.broadcasted_iota(jnp.int32, (count, lanes), 0)
            here = slice(part // per * lanes, (part // per + 1) * lanes)
            lefts = []
            for away in range(1, ng):
                g = (me + away) % ng
                for c in range(chunks):
                    at = (away - 1) * chunks + c
                    value = None
                    for p in range(per):
                        source = n * block + p * chunks + c
                        piece = received[place(ng, nq // ngy, ngy, g, source), :, here]
                        turn = (p - part) % per
                        if turn:
                            piece = pltpu.roll(piece, turn * slots, 1)
                        value = piece if value is None else jnp.where(lane == p, piece, value)
                    high = value.astype(jnp.bfloat16).astype(jnp.float32)
                    low = value - high
                    hit = up == at_row[at : at + 1]
                    pieces = [jnp.where(hit, high[v : v + 1], 0.0) for v in range(nv)]
                    pieces += [jnp.where(hit, low[v : v + 1], 0.0) for v in range(nv)]
                    lefts.append(jnp.concatenate(pieces, axis=0).astype(jnp.bfloat16))
            chosen = picks[part][pl.ds(pl.multiple_of(n * used * lanes, lanes), used * lanes)]
            total = jnp.dot(
                jnp.concatenate(lefts, axis=1), chosen, preferred_element_type=jnp.float32
            )
            if nq == block:
                totals[part] = total
            else:
                rows = total.shape[0]
                for s in range(groups):
                    start = starts[part] + s * rows
                    acc[start : start + rows] += total[:, s * nz : (s + 1) * nz]

    totals = {}
    if nq != block:
        acc[...] = jnp.zeros_like(acc)
    each(nq // block, fill)

    def brought(part, s):
        count = parts[part][0]
        if nq == block:
            new = totals[part][:, s * nz : (s + 1) * nz]
        else:
            start = starts[part] + s * 2 * nv * count
            new = acc[start : start + 2 * nv * count]
        return (new[: nv * count] + new[nv * count :]).reshape(nv, count, nz)

    def crossed(n, speeds, fields):
        a, b = (n + 1) % 3, (n + 2) % 3
        return speeds[b] * fields[a] - speeds[a] * fields[b]

    inside = slice(top, top + cy)
    for s in range(spread):
        new = brought(0, s)
        for n, x in enumerate(range(s, cx, spread)):
            state = base[:, x] + new[:, n * cy : (n + 1) * cy]
            ext[:fluid_count, 1 + x, inside] = state[:fluid_count]
            field[:, x] = state[fluid_count:]
            for d in range(3):
                ext[fluid_count + d, 1 + x, inside] = crossed(d, vel[:, x], state[fluid_count:])

    sides = {("gx", True): 0.0, ("gx", False): 0.0, ("gy", True): 0.0, ("gy", False): 0.0}
    for n, (axis, _, _) in enumerate(kinds):
        count = parts[n + 1][0]
        d = 0 if axis == "gx" else 1
        halo = halos[n][: (nv + 3) * count].reshape(nv + 3, count, nz)
        state = cleared[n][...] + brought(n + 1, 0)
        electric = [crossed(m, halo[nv:], state[fluid_count:])[None] for m in (1 - d, 2)]
        halo = jnp.concatenate([state[:fluid_count]] + electric, axis=0)
        sides[axis, True] += jnp.where(above[n], halo, 0.0)
        sides[axis, False] += jnp.where(above[n], 0.0, halo)

    for (axis, high), halo in sides.items():
        d = 0 if axis == "gx" else 1
        halo = jnp.broadcast_to(halo, (fluid_count + 2, cx if d else cy, nz))
        if d == 0:
            at = (cx + 1 if high else 0, inside)
        else:
            at = (slice(1, cx + 1), top + cy if high else top - 1)
        ext[(slice(0, fluid_count),) + at] = halo[:fluid_count]
        ext[(fluid_count + 1 - d,) + at] = halo[fluid_count]
        ext[(fluid_count + 2,) + at] = halo[fluid_count + 1]

    copies = []

    def finish(v, value):
        result[v] = value
        copies.append(pltpu.make_async_copy(result.at[v], out.at[v], sems.at[v]))
        copies[-1].start()

    def central(n, d):
        v = fluid_count + n
        return shifted(ext, v, cx, cy, d, 1) - shifted(ext, v, cx, cy, d, -1)

    for n in range(3):
        a, b = (n + 1) % 3, (n + 2) % 3
        curl = central(b, a) - central(a, b)
        finish(fluid_count + n, field[n] - (0.5 * courant_number) * curl)
    for v in range(fluid_count):
        total = coefs[6] * window(ext, v, cx, cy)
        for d in range(3):
            total = total + coefs[2 * d] * shifted(ext, v, cx, cy, d, -1)
            total = total + coefs[2 * d + 1] * shifted(ext, v, cx, cy, d, 1)
        finish(v, total)
    for copy in copies:
        copy.wait()


def per_device(ngx, ngy, conserved, velocity, donor_corner, donor_fraction, target_cell):
    kinds = exchanges(ngx, ngy)
    cons = conserved[:, 0]
    vel = velocity[:, 0]
    corner = donor_corner[0, 0, 0]
    fraction = donor_fraction[:, 0, 0, 0]
    target = target_cell[0, 0, 0]
    nv, cx, cy, nz = cons.shape
    ng, nq, slots = corner.shape
    rows = cx * cy
    per = nz // slots
    tiles = -(-(1 + len(kinds)) // per)
    f32 = jnp.float32

    def shape(*dims):
        return jax.ShapeDtypeStruct(dims, f32)

    params = pltpu.CompilerParams(vmem_limit_bytes=(12 + nq // 2) << 20)
    alongs = [cy if axis == "gx" else cx for axis, _, _ in kinds]
    pay_shapes = [((nv + 3) * along + nq, nz) for along in alongs]
    blended = pl.pallas_call(
        functools.partial(blend_kernel, ngy, kinds),
        out_shape=pltpu.VMEM((ng * nq, nv, tiles * nz), f32),
        in_specs=[pl.BlockSpec(memory_space=pl.ANY)] * 3,
        scratch_shapes=[
            pltpu.VMEM(cons.shape, f32),
            pltpu.VMEM(corner.shape, jnp.int32),
            pltpu.VMEM(fraction.shape, f32),
            pltpu.VMEM((nv * rows, 3 * nz), jnp.bfloat16),
            pltpu.VMEM((ng - 1, 3 * nz, block * slots), jnp.bfloat16),
            pltpu.VMEM((ng - 1, rows, block * slots), f32),
            pltpu.VMEM((ng - 1, per, nq // per, nv, nz), f32),
            pltpu.SemaphoreType.DMA((3,)),
        ],
        compiler_params=params,
        name="blend",
    )(*(pltpu.with_memory_space_constraint(value, pltpu.HBM) for value in (cons, corner, fraction)))

    aims, *pays = pl.pallas_call(
        functools.partial(edge_kernel, kinds),
        out_shape=[pltpu.VMEM((nq, nz), f32)] + [pltpu.VMEM(dims, f32) for dims in pay_shapes],
        in_specs=[pl.BlockSpec(memory_space=pltpu.VMEM)] * 3 + [pl.BlockSpec(memory_space=pl.ANY)],
        compiler_params=params,
        name="edge",
    )(cons, vel, target, blended)

    received = lax.all_to_all(
        blended,
        ("grp", "gx", "gy"),
        split_axis=0,
        concat_axis=0,
        tiled=True,
        axis_index_groups=[list(reversed(range(ng * nq)))],
    )
    halos = []
    for (axis, phase, _), pay in zip(kinds, pays):
        count = ngx if axis == "gx" else ngy
        pairs = []
        for low in range(phase, count - 1, 2):
            pairs += [(low, low + 1), (low + 1, low)]
        halos.append(lax.ppermute(pay, axis, pairs))

    spread = spread_of(cx)
    coefs, base, picks = pl.pallas_call(
        functools.partial(prepare_kernel, slots, ng),
        out_shape=[
            pltpu.VMEM((7, cx, cy, nz), f32),
            pltpu.VMEM((nv, cx, cy, nz), f32),
            pltpu.VMEM(((ng - 1) * nq * slots, spread * nz), jnp.bfloat16),
        ],
        scratch_shapes=[pltpu.VMEM((rows // spread, spread * nz), f32)],
        compiler_params=params,
        name="prepare",
    )(cons, vel, aims)
    def kept(values):
        return [pltpu.with_memory_space_constraint(value, pltpu.VMEM) for value in values]

    coefs, base, picks = kept((coefs, base, picks))
    border = pl.pallas_call(
        functools.partial(border_kernel, kinds, slots, ng),
        out_shape=[
            pltpu.VMEM((7, cx, cy, nz), f32),
            pltpu.VMEM((len(kinds), nq, nz), jnp.int32),
        ]
        + [pltpu.VMEM((nv, along, nz), f32) for along in alongs]
        + [pltpu.VMEM(((ng - 1) * nq * slots, nz), jnp.bfloat16) for _ in kinds],
        scratch_shapes=[pltpu.VMEM((along, nz), f32) for along in alongs],
        compiler_params=params,
        name="border",
    )(vel, coefs, *halos)
    coefs, rows_there, *border = kept(border)
    cleared, picks_there = border[: len(kinds)], border[len(kinds) :]

    result = pl.pallas_call(
        functools.partial(step_kernel, kinds, slots, ng, ngy),
        out_shape=shape(nv, cx, cy, nz),
        out_specs=pl.BlockSpec(memory_space=pl.ANY),
        scratch_shapes=[
            pltpu.VMEM((fluid_count + 3, cx + 2, cy + 2 * top, nz), f32),
            pltpu.VMEM((nv - fluid_count, cx, cy, nz), f32),
            pltpu.VMEM((2 * nv * (rows + sum(alongs)), nz), f32),
            pltpu.VMEM((nv, cx, cy, nz), f32),
            pltpu.SemaphoreType.DMA((nv,)),
        ],
        compiler_params=params,
        name="step",
    )(vel, aims, base, received, coefs, rows_there, *halos, *cleared, picks, *picks_there)
    return result[:, None]


def solution(mesh):
    return jax.shard_map(
        functools.partial(per_device, mesh.shape["gx"], mesh.shape["gy"]),
        mesh=mesh,
        in_specs=(
            P(None, "grp", "gx", "gy", None),
            P(None, "grp", "gx", "gy", None),
            P("grp", "gx", "gy", None, None, None),
            P(None, "grp", "gx", "gy", None, None, None),
            P("grp", "gx", "gy", None, None, None),
        ),
        out_specs=P(None, "grp", "gx", "gy", None),
        check_vma=False,
    )
```

```python
import functools

import jax
import jax.numpy as jnp
from jax import lax
from jax.experimental import pallas as pl
from jax.experimental.pallas import tpu as pltpu
from jax.sharding import PartitionSpec as P

signal_speed = 0.5
courant_number = 0.3
fluid_count = 5
block = 8


def exchanges(ngx, ngy):
    def partner(count, phase, n):
        other = n + 1 if (n + phase) % 2 == 0 else n - 1
        return other if 0 <= other < count else n

    kinds = []
    for phase in range(min(ngx - 1, 2)):
        kinds.append(("gx", phase, lambda i, j, phase=phase: (partner(ngx, phase, i), j)))
    for phase in range(min(ngy - 1, 2)):
        kinds.append(("gy", phase, lambda i, j, phase=phase: (i, partner(ngy, phase, j))))
    return kinds


def partner_above(axis, phase):
    return (lax.axis_index(axis) + phase) % 2 == 0


def split(value):
    high = value.astype(jnp.bfloat16)
    low = (value - high.astype(jnp.float32)).astype(jnp.bfloat16)
    return high, low


def spread_of(cx):
    return next(n for n in (4, 2, 1) if cx % n == 0)


def over(value, n):
    return value >> (n.bit_length() - 1) if n & (n - 1) == 0 else value // n


def rest_of(value, n):
    return value & (n - 1) if n & (n - 1) == 0 else value % n


def each(count, body):
    if count == 1:
        body(0)
    else:
        lax.fori_loop(0, count, lambda n, c: (body(n), c)[1], 0)


def block_transpose(value, slots):
    rows, lanes = value.shape
    count = lanes // slots
    each_rows = rows // count
    at_row = lax.broadcasted_iota(jnp.int32, value.shape, 0) // each_rows
    at_lane = lax.broadcasted_iota(jnp.int32, value.shape, 1) // slots
    result = value
    for d in range(1, count):
        turned = pltpu.roll(value, d * each_rows, 0)
        turned = pltpu.roll(turned, lanes - d * slots, 1)
        result = jnp.where((at_row - at_lane) % count == d, turned, result)
    return result


def place(ng, ngx, ngy, grid, q):
    return ng * ngx * ngy - 1 - (grid * ngx * ngy + q)


def packed(tiles, slots):
    empty = jnp.zeros(tiles[0].shape, tiles[0].dtype)
    return block_transpose(jnp.concatenate(tiles + [empty], axis=1), slots)


def blend_kernel(ngy, kinds, cons, corner, fraction, out, *scratch):
    at_cons, at_corner, at_fraction, uhl, wzs, wxys, moved, arrive = scratch
    nv, cx, cy, nz = cons.shape
    ng, nq, slots = corner.shape
    lanes = nz
    per = lanes // slots
    rows = cx * cy

    moves = [(corner, at_corner), (fraction, at_fraction), (cons, at_cons)]
    ins = [pltpu.make_async_copy(a, b, arrive.at[n]) for n, (a, b) in enumerate(moves)]
    for copy in ins:
        copy.start()

    def weight(count, at, upper):
        place = lax.broadcasted_iota(jnp.int32, (count, lanes), 0)
        return jnp.where(place == at, 1.0 - upper, jnp.where(place == at + 1, upper, 0.0))

    def lay(refs):
        return jnp.concatenate(refs, axis=1)

    def weigh(n):
        here = pl.ds(n * block, block)
        cell = lay([at_corner[h, here] for h in range(ng)])
        at_x, at_y, at_z = over(cell, nz * cy), rest_of(over(cell, nz), cy), rest_of(cell, nz)
        fx, fy, fz = (lay([at_fraction[d, h, here] for h in range(ng)]) for d in range(3))
        for q in range(block):
            row = slice(q, q + 1)
            cols = slice(q * lanes, (q + 1) * lanes)
            wx = weight(cx, at_x[row], fx[row])
            wy = weight(cy, at_y[row], fy[row])
            for x in range(cx):
                wxys[x * cy : (x + 1) * cy, cols] = wx[x : x + 1] * wy
            high, low = split(weight(nz, at_z[row], fz[row]))
            wzs[:nz, cols] = high
            wzs[nz : 2 * nz, cols] = high
            wzs[2 * nz :, cols] = low

    def blend(n):
        for q in range(0, block, 2):
            cols = slice(q * lanes, (q + 2) * lanes)
            both = jnp.dot(uhl[...], wzs[: 2 * nz, cols], preferred_element_type=jnp.float32)
            small = jnp.dot(uhl[:, :nz], wzs[2 * nz :, cols], preferred_element_type=jnp.float32)
            along = (both + small).reshape(nv, rows, 2 * lanes)
            values = jnp.sum(along * wxys[:, cols][None], axis=1)
            for half in range(2):
                value = values[:, half * lanes : (half + 1) * lanes]
                for turn in range(per):
                    moved[turn, n * block + q + half] = (
                        pltpu.roll(value, turn * slots, 1) if turn else value
                    )

    lane = lax.broadcasted_iota(jnp.int32, (nv, lanes), 1) // slots

    def assemble():
        for h in range(ng):
            for q in range(nq):
                i, j = q // ngy, q % ngy
                owners = [q] + [a * ngy + b for a, b in (of(i, j) for _, _, of in kinds)]
                for t in range(0, len(owners), per):
                    tile = None
                    for k, owner in enumerate(owners[t : t + per]):
                        piece = moved[(k - h) % per, owner]
                        tile = piece if tile is None else jnp.where(lane == k, piece, tile)
                    cols = slice(t // per * lanes, (t // per + 1) * lanes)
                    out[place(ng, nq // ngy, ngy, h, q), :, cols] = tile

    for copy in ins[:2]:
        copy.wait()
    if nq == block:
        weigh(0)
    ins[2].wait()
    high, low = split(at_cons[...].reshape(nv * rows, nz))
    uhl[:, :nz] = high
    uhl[:, nz:] = low
    if nq == block:
        blend(0)
    else:

        def both(n):
            weigh(n)
            blend(n)

        each(nq // block, both)
    assemble()


def edge_kernel(kinds, cons, vel, target, sent, aims, *pays):
    del sent
    nv, cx, cy, nz = cons.shape
    ng, nq, slots = target.shape
    me = lax.axis_index("grp")
    for n in range(nq // block):
        here = slice(n * block, (n + 1) * block)
        tiles = [target[(me + away) % ng, here] - cx * cy * nz for away in range(1, ng)]
        aims[here] = packed(tiles, slots).astype(jnp.float32)
    for (axis, phase, _), pay in zip(kinds, pays):
        above = partner_above(axis, phase)
        along = cy if axis == "gx" else cx
        for count, source, start in ((nv, cons, 0), (3, vel, nv * along)):
            if axis == "gx":
                layer = source[:, pl.ds(jnp.where(above, cx - 1, 0), 1)]
            else:
                layer = source[:, :, pl.ds(jnp.where(above, cy - 1, 0), 1)]
            pay[start : start + count * along] = layer.reshape(count * along, nz)
        pay[(nv + 3) * along :] = aims[...]


top = 8


def window(ext, v, cx, cy, move_x=0, move_y=0):
    return ext[v, 1 + move_x : 1 + move_x + cx, top + move_y : top + move_y + cy]


def along_z(value, by):
    nz = value.shape[-1]
    at = lax.broadcasted_iota(jnp.int32, (1,) + value.shape[1:], 2)
    edge = 0 if by < 0 else nz - 1
    return jnp.where(at == edge, 0.0, pltpu.roll(value, (-by) % nz, 2))


def shifted(ext, v, cx, cy, d, by):
    if d == 2 and by:
        return along_z(window(ext, v, cx, cy), by)
    return window(ext, v, cx, cy, by if d == 0 else 0, by if d == 1 else 0)


def face(low, high):
    wave_low = jnp.minimum(jnp.minimum(low, high) - signal_speed, 0.0)
    wave_high = jnp.maximum(jnp.maximum(low, high) + signal_speed, 0.0)
    scale = courant_number / (wave_high - wave_low)
    return (
        scale * wave_high * (low - wave_low),
        scale * wave_low * (wave_high - high),
    )


def mark(n, at_row, at_column, count, used, chunks, picks, marks):
    lanes = at_row.shape[1]
    up = lax.broadcasted_iota(jnp.int32, (count, lanes), 0)
    along = lax.broadcasted_iota(jnp.int32, (lanes, picks.shape[1]), 1)
    for at in range(0, used, chunks):
        hits = []
        for c in range(chunks):
            hits.append(jnp.where(up == at_row[at + c : at + c + 1], 1.0, 0.0))
            to = pl.ds(pl.multiple_of((n * used + at + c) * lanes, lanes), lanes)
            chosen = at_column[:, at + c : at + c + 1] == along
            picks[to] = jnp.where(chosen, 1.0, 0.0).astype(jnp.bfloat16)
        to = pl.ds(pl.multiple_of((n * used + at) * lanes, lanes), chunks * lanes)
        marks[...] += jnp.dot(
            jnp.concatenate(hits, axis=1).astype(jnp.bfloat16),
            picks[to],
            preferred_element_type=jnp.float32,
        )


def prepare_kernel(slots, ng, cons, vel, aims, coefs, base, picks, marks):
    nv, cx, cy, nz = cons.shape
    per = nz // slots
    chunks = block // per
    spread = spread_of(cx)
    count = cx // spread * cy

    def pick(n):
        cell = aims[pl.ds(n * block, block)].astype(jnp.int32) + cx * cy * nz
        x, y, z = over(cell, nz * cy), rest_of(over(cell, nz), cy), rest_of(cell, nz)
        at_row = over(x, spread) * cy + y
        at_column = (rest_of(x, spread) * nz + z).T
        mark(n, at_row, at_column, count, (ng - 1) * chunks, chunks, picks, marks)

    marks[...] = jnp.zeros_like(marks)
    each(aims.shape[0] // block, pick)
    for x in range(cx):
        rows = slice(x // spread * cy, (x // spread + 1) * cy)
        seen = marks[rows, x % spread * nz : (x % spread + 1) * nz]
        base[:, x] = jnp.where(seen[None] > 0.5, 0.0, cons[:, x])

    centre = jnp.ones((cx, cy, nz), jnp.float32)
    none = jnp.zeros((1, cy, nz), jnp.float32)
    low, high = face(vel[0, : cx - 1], vel[0, 1:])
    coefs[0] = jnp.concatenate([none, low], axis=0)
    coefs[1] = -jnp.concatenate([high, none], axis=0)
    centre += jnp.concatenate([none, high], axis=0) - jnp.concatenate([low, none], axis=0)

    at_y = lax.broadcasted_iota(jnp.int32, (1, cy, nz), 1)
    speed = vel[1]
    low, high = face(speed, pltpu.roll(speed, cy - 1, 1))
    low = jnp.where(at_y == cy - 1, 0.0, low)
    high = jnp.where(at_y == cy - 1, 0.0, high)
    coefs[2] = pltpu.roll(low, 1, 1)
    coefs[3] = -high
    centre += pltpu.roll(high, 1, 1) - low

    speed = vel[2]
    up_low, up_high = face(speed, along_z(speed, 1))
    down_low, down_high = face(along_z(speed, -1), speed)
    coefs[4] = down_low
    coefs[5] = -up_high
    coefs[6] = centre + down_high - up_low


def border_kernel(kinds, slots, ng, vel, given, *rest):
    halos = rest[: len(kinds)]
    coefs, rows = rest[len(kinds) : len(kinds) + 2]
    cleared = rest[len(kinds) + 2 : 2 * len(kinds) + 2]
    picks = rest[2 * len(kinds) + 2 : 3 * len(kinds) + 2]
    marks = rest[3 * len(kinds) + 2 :]
    cx, cy, nz = vel.shape[1:]
    nq = rows.shape[1]
    chunks = block // (nz // slots)
    used = (ng - 1) * chunks

    sides = {("gx", True): 0.0, ("gx", False): 0.0, ("gy", True): 0.0, ("gy", False): 0.0}
    for k, (axis, phase, _) in enumerate(kinds):
        above = partner_above(axis, phase)
        nv, count = cleared[k].shape[:2]

        def pick(n):
            cell = halos[k][pl.ds((nv + 3) * count + n * block, block)].astype(jnp.int32)
            cell = cell + cx * cy * nz
            x, y, z = over(cell, nz * cy), rest_of(over(cell, nz), cy), rest_of(cell, nz)
            if axis == "gx":
                at_row = jnp.where(x == jnp.where(above, 0, cx - 1), y, -1)
            else:
                at_row = jnp.where(y == jnp.where(above, 0, cy - 1), x, -1)
            rows[k, pl.ds(n * block, block)] = at_row
            mark(n, at_row, z.T, count, used, chunks, picks[k], marks[k])

        marks[k][...] = jnp.zeros_like(marks[k])
        each(nq // block, pick)
        before = halos[k][: nv * count].reshape(nv, count, nz)
        cleared[k][...] = jnp.where(marks[k][...][None] > 0.5, 0.0, before)
        d = 0 if axis == "gx" else 1
        speed = halos[k][(nv + d) * count : (nv + d + 1) * count]
        sides[axis, True] += jnp.where(above, speed, 0.0)
        sides[axis, False] += jnp.where(above, 0.0, speed)

    coefs[...] = given[...]
    for (axis, high), speed in sides.items():
        if axis == "gx":
            d, edge = 0, (cx - 1 if high else 0,)
        else:
            d, edge = 1, (slice(None), cy - 1 if high else 0)
        mine = vel[(d,) + edge]
        speed = jnp.broadcast_to(speed, mine.shape)
        if high:
            of_low, of_high = face(mine, speed)
            coefs[(2 * d + 1,) + edge] = -of_high
            coefs[(6,) + edge] -= of_low
        else:
            of_low, of_high = face(speed, mine)
            coefs[(2 * d,) + edge] = of_low
            coefs[(6,) + edge] += of_high


def step_kernel(kinds, slots, ng, ngy, vel, aims, base, received, coefs, rows_there, *rest):
    halos, cleared = rest[: len(kinds)], rest[len(kinds) : 2 * len(kinds)]
    picks = rest[2 * len(kinds) : 3 * len(kinds) + 1]
    out, ext, field, acc, result, sems = rest[3 * len(kinds) + 1 :]
    nv, cx, cy, nz = base.shape
    lanes = nz
    nq = received.shape[0] // ng
    per = lanes // slots
    chunks = block // per
    used = (ng - 1) * chunks
    spread = spread_of(cx)
    me = lax.axis_index("grp")
    lane = lax.broadcasted_iota(jnp.int32, (nv, lanes), 1) // slots
    above = [partner_above(axis, phase) for axis, phase, _ in kinds]

    parts = [(cx // spread * cy, spread)]
    parts += [(cy if axis == "gx" else cx, 1) for axis, _, _ in kinds]
    starts = [0]
    for count, groups in parts:
        starts.append(starts[-1] + 2 * nv * count * groups)

    def fill(n):
        for part, (count, groups) in enumerate(parts):
            if part == 0:
                cell = aims[pl.ds(n * block, block)].astype(jnp.int32) + cx * cy * nz
                x, y = over(cell, nz * cy), rest_of(over(cell, nz), cy)
                at_row = over(x, spread) * cy + y
            else:
                at_row = rows_there[part - 1, pl.ds(n * block, block)]
            up = lax.broadcasted_iota(jnp.int32, (count, lanes), 0)
            here = slice(part // per * lanes, (part // per + 1) * lanes)
            lefts = []
            for away in range(1, ng):
                g = (me + away) % ng
                for c in range(chunks):
                    at = (away - 1) * chunks + c
                    value = None
                    for p in range(per):
                        source = n * block + p * chunks + c
                        piece = received[place(ng, nq // ngy, ngy, g, source), :, here]
                        turn = (p - part) % per
                        if turn:
                            piece = pltpu.roll(piece, turn * slots, 1)
                        value = piece if value is None else jnp.where(lane == p, piece, value)
                    high = value.astype(jnp.bfloat16).astype(jnp.float32)
                    low = value - high
                    hit = up == at_row[at : at + 1]
                    pieces = [jnp.where(hit, high[v : v + 1], 0.0) for v in range(nv)]
                    pieces += [jnp.where(hit, low[v : v + 1], 0.0) for v in range(nv)]
                    lefts.append(jnp.concatenate(pieces, axis=0).astype(jnp.bfloat16))
            chosen = picks[part][pl.ds(pl.multiple_of(n * used * lanes, lanes), used * lanes)]
            total = jnp.dot(
                jnp.concatenate(lefts, axis=1), chosen, preferred_element_type=jnp.float32
            )
            if nq == block:
                totals[part] = total
            else:
                rows = total.shape[0]
                for s in range(groups):
                    start = starts[part] + s * rows
                    acc[start : start + rows] += total[:, s * nz : (s + 1) * nz]

    totals = {}
    if nq != block:
        acc[...] = jnp.zeros_like(acc)
    each(nq // block, fill)

    def brought(part, s):
        count = parts[part][0]
        if nq == block:
            new = totals[part][:, s * nz : (s + 1) * nz]
        else:
            start = starts[part] + s * 2 * nv * count
            new = acc[start : start + 2 * nv * count]
        return (new[: nv * count] + new[nv * count :]).reshape(nv, count, nz)

    def crossed(n, speeds, fields):
        a, b = (n + 1) % 3, (n + 2) % 3
        return speeds[b] * fields[a] - speeds[a] * fields[b]

    inside = slice(top, top + cy)
    for s in range(spread):
        new = brought(0, s)
        for n, x in enumerate(range(s, cx, spread)):
            state = base[:, x] + new[:, n * cy : (n + 1) * cy]
            ext[:fluid_count, 1 + x, inside] = state[:fluid_count]
            field[:, x] = state[fluid_count:]
            for d in range(3):
                ext[fluid_count + d, 1 + x, inside] = crossed(d, vel[:, x], state[fluid_count:])

    sides = {("gx", True): 0.0, ("gx", False): 0.0, ("gy", True): 0.0, ("gy", False): 0.0}
    for n, (axis, _, _) in enumerate(kinds):
        count = parts[n + 1][0]
        d = 0 if axis == "gx" else 1
        halo = halos[n][: (nv + 3) * count].reshape(nv + 3, count, nz)
        state = cleared[n][...] + brought(n + 1, 0)
        electric = [crossed(m, halo[nv:], state[fluid_count:])[None] for m in (1 - d, 2)]
        halo = jnp.concatenate([state[:fluid_count]] + electric, axis=0)
        sides[axis, True] += jnp.where(above[n], halo, 0.0)
        sides[axis, False] += jnp.where(above[n], 0.0, halo)

    for (axis, high), halo in sides.items():
        d = 0 if axis == "gx" else 1
        halo = jnp.broadcast_to(halo, (fluid_count + 2, cx if d else cy, nz))
        if d == 0:
            at = (cx + 1 if high else 0, inside)
        else:
            at = (slice(1, cx + 1), top + cy if high else top - 1)
        ext[(slice(0, fluid_count),) + at] = halo[:fluid_count]
        ext[(fluid_count + 1 - d,) + at] = halo[fluid_count]
        ext[(fluid_count + 2,) + at] = halo[fluid_count + 1]

    copies = []

    def finish(v, value):
        result[v] = value
        copies.append(pltpu.make_async_copy(result.at[v], out.at[v], sems.at[v]))
        copies[-1].start()

    def central(n, d):
        v = fluid_count + n
        return shifted(ext, v, cx, cy, d, 1) - shifted(ext, v, cx, cy, d, -1)

    for n in range(3):
        a, b = (n + 1) % 3, (n + 2) % 3
        curl = central(b, a) - central(a, b)
        finish(fluid_count + n, field[n] - (0.5 * courant_number) * curl)
    for v in range(fluid_count):
        total = coefs[6] * window(ext, v, cx, cy)
        for d in range(3):
            total = total + coefs[2 * d] * shifted(ext, v, cx, cy, d, -1)
            total = total + coefs[2 * d + 1] * shifted(ext, v, cx, cy, d, 1)
        finish(v, total)
    for copy in copies:
        copy.wait()


def per_device(ngx, ngy, conserved, velocity, donor_corner, donor_fraction, target_cell):
    kinds = exchanges(ngx, ngy)
    cons = conserved[:, 0]
    vel = velocity[:, 0]
    corner = donor_corner[0, 0, 0]
    fraction = donor_fraction[:, 0, 0, 0]
    target = target_cell[0, 0, 0]
    nv, cx, cy, nz = cons.shape
    ng, nq, slots = corner.shape
    rows = cx * cy
    per = nz // slots
    tiles = -(-(1 + len(kinds)) // per)
    f32 = jnp.float32

    def shape(*dims):
        return jax.ShapeDtypeStruct(dims, f32)

    params = pltpu.CompilerParams(vmem_limit_bytes=(12 + nq // 2) << 20)
    alongs = [cy if axis == "gx" else cx for axis, _, _ in kinds]
    pay_shapes = [((nv + 3) * along + nq, nz) for along in alongs]
    blended = pl.pallas_call(
        functools.partial(blend_kernel, ngy, kinds),
        out_shape=pltpu.VMEM((ng * nq, nv, tiles * nz), f32),
        in_specs=[pl.BlockSpec(memory_space=pl.ANY)] * 3,
        scratch_shapes=[
            pltpu.VMEM(cons.shape, f32),
            pltpu.VMEM(corner.shape, jnp.int32),
            pltpu.VMEM(fraction.shape, f32),
            pltpu.VMEM((nv * rows, 2 * nz), jnp.bfloat16),
            pltpu.VMEM((3 * nz, block * nz), jnp.bfloat16),
            pltpu.VMEM((rows, block * nz), f32),
            pltpu.VMEM((per, nq, nv, nz), f32),
            pltpu.SemaphoreType.DMA((3,)),
        ],
        compiler_params=params,
        name="blend",
    )(*(pltpu.with_memory_space_constraint(value, pltpu.HBM) for value in (cons, corner, fraction)))

    aims, *pays = pl.pallas_call(
        functools.partial(edge_kernel, kinds),
        out_shape=[pltpu.VMEM((nq, nz), f32)] + [pltpu.VMEM(dims, f32) for dims in pay_shapes],
        in_specs=[pl.BlockSpec(memory_space=pltpu.VMEM)] * 3 + [pl.BlockSpec(memory_space=pl.ANY)],
        compiler_params=params,
        name="edge",
    )(cons, vel, target, blended)

    received = lax.all_to_all(
        blended,
        ("grp", "gx", "gy"),
        split_axis=0,
        concat_axis=0,
        tiled=True,
        axis_index_groups=[list(reversed(range(ng * nq)))],
    )
    halos = []
    for (axis, phase, _), pay in zip(kinds, pays):
        count = ngx if axis == "gx" else ngy
        pairs = []
        for low in range(phase, count - 1, 2):
            pairs += [(low, low + 1), (low + 1, low)]
        halos.append(lax.ppermute(pay, axis, pairs))

    spread = spread_of(cx)
    coefs, base, picks = pl.pallas_call(
        functools.partial(prepare_kernel, slots, ng),
        out_shape=[
            pltpu.VMEM((7, cx, cy, nz), f32),
            pltpu.VMEM((nv, cx, cy, nz), f32),
            pltpu.VMEM(((ng - 1) * nq * slots, spread * nz), jnp.bfloat16),
        ],
        scratch_shapes=[pltpu.VMEM((rows // spread, spread * nz), f32)],
        compiler_params=params,
        name="prepare",
    )(cons, vel, aims)
    def kept(values):
        return [pltpu.with_memory_space_constraint(value, pltpu.VMEM) for value in values]

    coefs, base, picks = kept((coefs, base, picks))
    border = pl.pallas_call(
        functools.partial(border_kernel, kinds, slots, ng),
        out_shape=[
            pltpu.VMEM((7, cx, cy, nz), f32),
            pltpu.VMEM((len(kinds), nq, nz), jnp.int32),
        ]
        + [pltpu.VMEM((nv, along, nz), f32) for along in alongs]
        + [pltpu.VMEM(((ng - 1) * nq * slots, nz), jnp.bfloat16) for _ in kinds],
        scratch_shapes=[pltpu.VMEM((along, nz), f32) for along in alongs],
        compiler_params=params,
        name="border",
    )(vel, coefs, *halos)
    coefs, rows_there, *border = kept(border)
    cleared, picks_there = border[: len(kinds)], border[len(kinds) :]

    result = pl.pallas_call(
        functools.partial(step_kernel, kinds, slots, ng, ngy),
        out_shape=shape(nv, cx, cy, nz),
        out_specs=pl.BlockSpec(memory_space=pl.ANY),
        scratch_shapes=[
            pltpu.VMEM((fluid_count + 3, cx + 2, cy + 2 * top, nz), f32),
            pltpu.VMEM((nv - fluid_count, cx, cy, nz), f32),
            pltpu.VMEM((2 * nv * (rows + sum(alongs)), nz), f32),
            pltpu.VMEM((nv, cx, cy, nz), f32),
            pltpu.SemaphoreType.DMA((nv,)),
        ],
        compiler_params=params,
        name="step",
    )(vel, aims, base, received, coefs, rows_there, *halos, *cleared, picks, *picks_there)
    return result[:, None]


def solution(mesh):
    return jax.shard_map(
        functools.partial(per_device, mesh.shape["gx"], mesh.shape["gy"]),
        mesh=mesh,
        in_specs=(
            P(None, "grp", "gx", "gy", None),
            P(None, "grp", "gx", "gy", None),
            P("grp", "gx", "gy", None, None, None),
            P(None, "grp", "gx", "gy", None, None, None),
            P("grp", "gx", "gy", None, None, None),
        ),
        out_specs=P(None, "grp", "gx", "gy", None),
        check_vma=False,
    )
```

```python
import functools

import jax
import jax.numpy as jnp
from jax import lax
from jax.experimental import pallas as pl
from jax.experimental.pallas import tpu as pltpu
from jax.sharding import PartitionSpec as P

signal_speed = 0.5
courant_number = 0.3
fluid_count = 5
block = 8


def exchanges(ngx, ngy):
    def partner(count, phase, n):
        other = n + 1 if (n + phase) % 2 == 0 else n - 1
        return other if 0 <= other < count else n

    kinds = []
    for phase in range(min(ngx - 1, 2)):
        kinds.append(("gx", phase, lambda i, j, phase=phase: (partner(ngx, phase, i), j)))
    for phase in range(min(ngy - 1, 2)):
        kinds.append(("gy", phase, lambda i, j, phase=phase: (i, partner(ngy, phase, j))))
    return kinds


def partner_above(axis, phase):
    return (lax.axis_index(axis) + phase) % 2 == 0


def split(value):
    high = value.astype(jnp.bfloat16)
    low = (value - high.astype(jnp.float32)).astype(jnp.bfloat16)
    return high, low


def spread_of(cx):
    return next(n for n in (4, 2, 1) if cx % n == 0)


def over(value, n):
    return value >> (n.bit_length() - 1) if n & (n - 1) == 0 else value // n


def rest_of(value, n):
    return value & (n - 1) if n & (n - 1) == 0 else value % n


def each(count, body):
    if count == 1:
        body(0)
    else:
        lax.fori_loop(0, count, lambda n, c: (body(n), c)[1], 0)


def block_transpose(value, slots):
    rows, lanes = value.shape
    count = lanes // slots
    each_rows = rows // count
    at_row = lax.broadcasted_iota(jnp.int32, value.shape, 0) // each_rows
    at_lane = lax.broadcasted_iota(jnp.int32, value.shape, 1) // slots
    result = value
    for d in range(1, count):
        turned = pltpu.roll(value, d * each_rows, 0)
        turned = pltpu.roll(turned, lanes - d * slots, 1)
        result = jnp.where((at_row - at_lane) % count == d, turned, result)
    return result


def place(ng, ngx, ngy, grid, q):
    return ng * ngx * ngy - 1 - ((q % ngy * ng + grid) * ngx + q // ngy)


def packed(tiles, slots):
    empty = jnp.zeros(tiles[0].shape, tiles[0].dtype)
    return block_transpose(jnp.concatenate(tiles + [empty], axis=1), slots)


def blend_kernel(ngy, kinds, cons, corner, fraction, out, *scratch):
    at_cons, at_corner, at_fraction, uhl, wzs, wxys, moved, arrive = scratch
    nv, cx, cy, nz = cons.shape
    ng, nq, slots = corner.shape
    lanes = nz
    per = lanes // slots
    chunks = block // per
    rows = cx * cy
    me = lax.axis_index("grp")

    moves = [(corner, at_corner), (fraction, at_fraction), (cons, at_cons)]
    ins = [pltpu.make_async_copy(a, b, arrive.at[n]) for n, (a, b) in enumerate(moves)]
    for copy in ins:
        copy.start()

    for q in range(nq):
        at = place(ng, nq // ngy, ngy, me, q)
        out[pl.ds(at, 1)] = jnp.zeros((1,) + out.shape[1:], jnp.float32)

    def weight(count, at, upper):
        place = lax.broadcasted_iota(jnp.int32, (count, lanes), 0)
        return jnp.where(place == at, 1.0 - upper, jnp.where(place == at + 1, upper, 0.0))

    def weigh(n):
        here = pl.ds(n * block, block)
        grids = [(me + away) % ng for away in range(1, ng)]
        cell = packed([at_corner[h, here] for h in grids], slots)
        at_x, at_y, at_z = over(cell, nz * cy), rest_of(over(cell, nz), cy), rest_of(cell, nz)
        fx, fy, fz = (packed([at_fraction[d, h, here] for h in grids], slots) for d in range(3))
        for away in range(1, ng):
            for c in range(chunks):
                row = slice((away - 1) * chunks + c, (away - 1) * chunks + c + 1)
                cols = slice(c * lanes, (c + 1) * lanes)
                wx = weight(cx, at_x[row], fx[row])
                wy = weight(cy, at_y[row], fy[row])
                for x in range(cx):
                    wxys[away - 1, x * cy : (x + 1) * cy, cols] = wx[x : x + 1] * wy
                high, low = split(weight(nz, at_z[row], fz[row]))
                wzs[away - 1, :nz, cols] = high
                wzs[away - 1, nz : 2 * nz, cols] = high
                wzs[away - 1, 2 * nz :, cols] = low

    def blend(n):
        for away in range(1, ng):
            along = jnp.dot(uhl[...], wzs[away - 1], preferred_element_type=jnp.float32)
            along = along.reshape(nv, rows, chunks * lanes)
            values = jnp.sum(along * wxys[away - 1][None], axis=1)
            for c in range(chunks):
                value = values[:, c * lanes : (c + 1) * lanes]
                for turn in range(per):
                    moved[away - 1, turn, n * chunks + c] = (
                        pltpu.roll(value, turn * slots, 1) if turn else value
                    )
            if nq == block:
                assemble(away)

    lane = lax.broadcasted_iota(jnp.int32, (nv, lanes), 1) // slots

    def assemble(away):
        for q in range(nq):
            i, j = q // ngy, q % ngy
            owners = [q] + [a * ngy + b for a, b in (of(i, j) for _, _, of in kinds)]
            for t in range(0, len(owners), per):
                tile = None
                for k, owner in enumerate(owners[t : t + per]):
                    chunk = owner // block * chunks + owner % chunks
                    piece = moved[away - 1, (k - owner % block // chunks) % per, chunk]
                    tile = piece if tile is None else jnp.where(lane == k, piece, tile)
                cols = slice(t // per * lanes, (t // per + 1) * lanes)
                at = place(ng, nq // ngy, ngy, (me + away) % ng, q)
                out[pl.ds(at, 1), :, cols] = tile[None]

    for copy in ins[:2]:
        copy.wait()
    if nq == block:
        weigh(0)
    ins[2].wait()
    high, low = split(at_cons[...].reshape(nv * rows, nz))
    uhl[:, :nz] = high
    uhl[:, nz : 2 * nz] = low
    uhl[:, 2 * nz :] = high
    if nq == block:
        blend(0)
    else:

        def both(n):
            weigh(n)
            blend(n)

        each(nq // block, both)
        for away in range(1, ng):
            assemble(away)


def edge_kernel(kinds, cons, vel, target, sent, aims, *pays):
    del sent
    nv, cx, cy, nz = cons.shape
    ng, nq, slots = target.shape
    me = lax.axis_index("grp")
    for n in range(nq // block):
        here = slice(n * block, (n + 1) * block)
        tiles = [target[(me + away) % ng, here] - cx * cy * nz for away in range(1, ng)]
        aims[here] = packed(tiles, slots).astype(jnp.float32)
    for (axis, phase, _), pay in zip(kinds, pays):
        above = partner_above(axis, phase)
        along = cy if axis == "gx" else cx
        for count, source, start in ((nv, cons, 0), (3, vel, nv * along)):
            if axis == "gx":
                layer = source[:, pl.ds(jnp.where(above, cx - 1, 0), 1)]
            else:
                layer = source[:, :, pl.ds(jnp.where(above, cy - 1, 0), 1)]
            pay[start : start + count * along] = layer.reshape(count * along, nz)
        pay[(nv + 3) * along :] = aims[...]


top = 8


def window(ext, v, cx, cy, move_x=0, move_y=0):
    return ext[v, 1 + move_x : 1 + move_x + cx, top + move_y : top + move_y + cy]


def along_z(value, by):
    nz = value.shape[-1]
    at = lax.broadcasted_iota(jnp.int32, (1,) + value.shape[1:], 2)
    edge = 0 if by < 0 else nz - 1
    return jnp.where(at == edge, 0.0, pltpu.roll(value, (-by) % nz, 2))


def shifted(ext, v, cx, cy, d, by):
    if d == 2 and by:
        return along_z(window(ext, v, cx, cy), by)
    return window(ext, v, cx, cy, by if d == 0 else 0, by if d == 1 else 0)


def face(low, high):
    wave_low = jnp.minimum(jnp.minimum(low, high) - signal_speed, 0.0)
    wave_high = jnp.maximum(jnp.maximum(low, high) + signal_speed, 0.0)
    scale = courant_number / (wave_high - wave_low)
    return (
        scale * wave_high * (low - wave_low),
        scale * wave_low * (wave_high - high),
    )


def mark(n, at_row, at_column, count, used, chunks, picks, marks):
    lanes = at_row.shape[1]
    up = lax.broadcasted_iota(jnp.int32, (count, lanes), 0)
    along = lax.broadcasted_iota(jnp.int32, (lanes, picks.shape[1]), 1)
    for at in range(0, used, chunks):
        hits = []
        for c in range(chunks):
            hits.append(jnp.where(up == at_row[at + c : at + c + 1], 1.0, 0.0))
            to = pl.ds(pl.multiple_of((n * used + at + c) * lanes, lanes), lanes)
            chosen = at_column[:, at + c : at + c + 1] == along
            picks[to] = jnp.where(chosen, 1.0, 0.0).astype(jnp.bfloat16)
        to = pl.ds(pl.multiple_of((n * used + at) * lanes, lanes), chunks * lanes)
        marks[...] += jnp.dot(
            jnp.concatenate(hits, axis=1).astype(jnp.bfloat16),
            picks[to],
            preferred_element_type=jnp.float32,
        )


def prepare_kernel(slots, ng, cons, vel, aims, coefs, base, picks, marks):
    nv, cx, cy, nz = cons.shape
    per = nz // slots
    chunks = block // per
    spread = spread_of(cx)
    count = cx // spread * cy

    def pick(n):
        cell = aims[pl.ds(n * block, block)].astype(jnp.int32) + cx * cy * nz
        x, y, z = over(cell, nz * cy), rest_of(over(cell, nz), cy), rest_of(cell, nz)
        at_row = over(x, spread) * cy + y
        at_column = (rest_of(x, spread) * nz + z).T
        mark(n, at_row, at_column, count, (ng - 1) * chunks, chunks, picks, marks)

    marks[...] = jnp.zeros_like(marks)
    each(aims.shape[0] // block, pick)
    for x in range(cx):
        rows = slice(x // spread * cy, (x // spread + 1) * cy)
        seen = marks[rows, x % spread * nz : (x % spread + 1) * nz]
        base[:, x] = jnp.where(seen[None] > 0.5, 0.0, cons[:, x])

    centre = jnp.ones((cx, cy, nz), jnp.float32)
    none = jnp.zeros((1, cy, nz), jnp.float32)
    low, high = face(vel[0, : cx - 1], vel[0, 1:])
    coefs[0] = jnp.concatenate([none, low], axis=0)
    coefs[1] = -jnp.concatenate([high, none], axis=0)
    centre += jnp.concatenate([none, high], axis=0) - jnp.concatenate([low, none], axis=0)

    at_y = lax.broadcasted_iota(jnp.int32, (1, cy, nz), 1)
    speed = vel[1]
    low, high = face(speed, pltpu.roll(speed, cy - 1, 1))
    low = jnp.where(at_y == cy - 1, 0.0, low)
    high = jnp.where(at_y == cy - 1, 0.0, high)
    coefs[2] = pltpu.roll(low, 1, 1)
    coefs[3] = -high
    centre += pltpu.roll(high, 1, 1) - low

    speed = vel[2]
    up_low, up_high = face(speed, along_z(speed, 1))
    down_low, down_high = face(along_z(speed, -1), speed)
    coefs[4] = down_low
    coefs[5] = -up_high
    coefs[6] = centre + down_high - up_low


def border_kernel(kinds, slots, ng, vel, given, *rest):
    halos = rest[: len(kinds)]
    coefs, rows = rest[len(kinds) : len(kinds) + 2]
    cleared = rest[len(kinds) + 2 : 2 * len(kinds) + 2]
    picks = rest[2 * len(kinds) + 2 : 3 * len(kinds) + 2]
    marks = rest[3 * len(kinds) + 2 :]
    cx, cy, nz = vel.shape[1:]
    nq = rows.shape[1]
    chunks = block // (nz // slots)
    used = (ng - 1) * chunks

    sides = {("gx", True): 0.0, ("gx", False): 0.0, ("gy", True): 0.0, ("gy", False): 0.0}
    for k, (axis, phase, _) in enumerate(kinds):
        above = partner_above(axis, phase)
        nv, count = cleared[k].shape[:2]

        def pick(n):
            cell = halos[k][pl.ds((nv + 3) * count + n * block, block)].astype(jnp.int32)
            cell = cell + cx * cy * nz
            x, y, z = over(cell, nz * cy), rest_of(over(cell, nz), cy), rest_of(cell, nz)
            if axis == "gx":
                at_row = jnp.where(x == jnp.where(above, 0, cx - 1), y, -1)
            else:
                at_row = jnp.where(y == jnp.where(above, 0, cy - 1), x, -1)
            rows[k, pl.ds(n * block, block)] = at_row
            mark(n, at_row, z.T, count, used, chunks, picks[k], marks[k])

        marks[k][...] = jnp.zeros_like(marks[k])
        each(nq // block, pick)
        before = halos[k][: nv * count].reshape(nv, count, nz)
        cleared[k][...] = jnp.where(marks[k][...][None] > 0.5, 0.0, before)
        d = 0 if axis == "gx" else 1
        speed = halos[k][(nv + d) * count : (nv + d + 1) * count]
        sides[axis, True] += jnp.where(above, speed, 0.0)
        sides[axis, False] += jnp.where(above, 0.0, speed)

    coefs[...] = given[...]
    for (axis, high), speed in sides.items():
        if axis == "gx":
            d, edge = 0, (cx - 1 if high else 0,)
        else:
            d, edge = 1, (slice(None), cy - 1 if high else 0)
        mine = vel[(d,) + edge]
        speed = jnp.broadcast_to(speed, mine.shape)
        if high:
            of_low, of_high = face(mine, speed)
            coefs[(2 * d + 1,) + edge] = -of_high
            coefs[(6,) + edge] -= of_low
        else:
            of_low, of_high = face(speed, mine)
            coefs[(2 * d,) + edge] = of_low
            coefs[(6,) + edge] += of_high


def step_kernel(kinds, slots, ng, ngy, vel, aims, base, received, coefs, rows_there, *rest):
    halos, cleared = rest[: len(kinds)], rest[len(kinds) : 2 * len(kinds)]
    picks = rest[2 * len(kinds) : 3 * len(kinds) + 1]
    out, ext, field, acc, result, sems = rest[3 * len(kinds) + 1 :]
    nv, cx, cy, nz = base.shape
    lanes = nz
    nq = received.shape[0] // ng
    per = lanes // slots
    chunks = block // per
    used = (ng - 1) * chunks
    spread = spread_of(cx)
    me = lax.axis_index("grp")
    lane = lax.broadcasted_iota(jnp.int32, (nv, lanes), 1) // slots
    above = [partner_above(axis, phase) for axis, phase, _ in kinds]

    parts = [(cx // spread * cy, spread)]
    parts += [(cy if axis == "gx" else cx, 1) for axis, _, _ in kinds]
    starts = [0]
    for count, groups in parts:
        starts.append(starts[-1] + 2 * nv * count * groups)

    def fill(n):
        for part, (count, groups) in enumerate(parts):
            if part == 0:
                cell = aims[pl.ds(n * block, block)].astype(jnp.int32) + cx * cy * nz
                x, y = over(cell, nz * cy), rest_of(over(cell, nz), cy)
                at_row = over(x, spread) * cy + y
            else:
                at_row = rows_there[part - 1, pl.ds(n * block, block)]
            up = lax.broadcasted_iota(jnp.int32, (count, lanes), 0)
            here = slice(part // per * lanes, (part // per + 1) * lanes)
            lefts = []
            for away in range(1, ng):
                g = (me + away) % ng
                for c in range(chunks):
                    at = (away - 1) * chunks + c
                    value = None
                    for p in range(per):
                        source = n * block + p * chunks + c
                        piece = received[place(ng, nq // ngy, ngy, g, source), :, here]
                        turn = (p - part) % per
                        if turn:
                            piece = pltpu.roll(piece, turn * slots, 1)
                        value = piece if value is None else jnp.where(lane == p, piece, value)
                    high = value.astype(jnp.bfloat16).astype(jnp.float32)
                    low = value - high
                    hit = up == at_row[at : at + 1]
                    pieces = [jnp.where(hit, high[v : v + 1], 0.0) for v in range(nv)]
                    pieces += [jnp.where(hit, low[v : v + 1], 0.0) for v in range(nv)]
                    lefts.append(jnp.concatenate(pieces, axis=0).astype(jnp.bfloat16))
            chosen = picks[part][pl.ds(pl.multiple_of(n * used * lanes, lanes), used * lanes)]
            total = jnp.dot(
                jnp.concatenate(lefts, axis=1), chosen, preferred_element_type=jnp.float32
            )
            if nq == block:
                totals[part] = total
            else:
                rows = total.shape[0]
                for s in range(groups):
                    start = starts[part] + s * rows
                    acc[start : start + rows] += total[:, s * nz : (s + 1) * nz]

    totals = {}
    if nq != block:
        acc[...] = jnp.zeros_like(acc)
    each(nq // block, fill)

    def brought(part, s):
        count = parts[part][0]
        if nq == block:
            new = totals[part][:, s * nz : (s + 1) * nz]
        else:
            start = starts[part] + s * 2 * nv * count
            new = acc[start : start + 2 * nv * count]
        return (new[: nv * count] + new[nv * count :]).reshape(nv, count, nz)

    def crossed(n, speeds, fields):
        a, b = (n + 1) % 3, (n + 2) % 3
        return speeds[b] * fields[a] - speeds[a] * fields[b]

    inside = slice(top, top + cy)
    for s in range(spread):
        new = brought(0, s)
        for n, x in enumerate(range(s, cx, spread)):
            state = base[:, x] + new[:, n * cy : (n + 1) * cy]
            ext[:fluid_count, 1 + x, inside] = state[:fluid_count]
            field[:, x] = state[fluid_count:]
            for d in range(3):
                ext[fluid_count + d, 1 + x, inside] = crossed(d, vel[:, x], state[fluid_count:])

    sides = {("gx", True): 0.0, ("gx", False): 0.0, ("gy", True): 0.0, ("gy", False): 0.0}
    for n, (axis, _, _) in enumerate(kinds):
        count = parts[n + 1][0]
        d = 0 if axis == "gx" else 1
        halo = halos[n][: (nv + 3) * count].reshape(nv + 3, count, nz)
        state = cleared[n][...] + brought(n + 1, 0)
        electric = [crossed(m, halo[nv:], state[fluid_count:])[None] for m in (1 - d, 2)]
        halo = jnp.concatenate([state[:fluid_count]] + electric, axis=0)
        sides[axis, True] += jnp.where(above[n], halo, 0.0)
        sides[axis, False] += jnp.where(above[n], 0.0, halo)

    for (axis, high), halo in sides.items():
        d = 0 if axis == "gx" else 1
        halo = jnp.broadcast_to(halo, (fluid_count + 2, cx if d else cy, nz))
        if d == 0:
            at = (cx + 1 if high else 0, inside)
        else:
            at = (slice(1, cx + 1), top + cy if high else top - 1)
        ext[(slice(0, fluid_count),) + at] = halo[:fluid_count]
        ext[(fluid_count + 1 - d,) + at] = halo[fluid_count]
        ext[(fluid_count + 2,) + at] = halo[fluid_count + 1]

    copies = []

    def finish(v, value):
        result[v] = value
        copies.append(pltpu.make_async_copy(result.at[v], out.at[v], sems.at[v]))
        copies[-1].start()

    def central(n, d):
        v = fluid_count + n
        return shifted(ext, v, cx, cy, d, 1) - shifted(ext, v, cx, cy, d, -1)

    for n in range(3):
        a, b = (n + 1) % 3, (n + 2) % 3
        curl = central(b, a) - central(a, b)
        finish(fluid_count + n, field[n] - (0.5 * courant_number) * curl)
    for v in range(fluid_count):
        total = coefs[6] * window(ext, v, cx, cy)
        for d in range(3):
            total = total + coefs[2 * d] * shifted(ext, v, cx, cy, d, -1)
            total = total + coefs[2 * d + 1] * shifted(ext, v, cx, cy, d, 1)
        finish(v, total)
    for copy in copies:
        copy.wait()


def per_device(ngx, ngy, conserved, velocity, donor_corner, donor_fraction, target_cell):
    kinds = exchanges(ngx, ngy)
    cons = conserved[:, 0]
    vel = velocity[:, 0]
    corner = donor_corner[0, 0, 0]
    fraction = donor_fraction[:, 0, 0, 0]
    target = target_cell[0, 0, 0]
    nv, cx, cy, nz = cons.shape
    ng, nq, slots = corner.shape
    rows = cx * cy
    per = nz // slots
    tiles = -(-(1 + len(kinds)) // per)
    f32 = jnp.float32

    def shape(*dims):
        return jax.ShapeDtypeStruct(dims, f32)

    params = pltpu.CompilerParams(vmem_limit_bytes=(12 + nq // 2) << 20)
    alongs = [cy if axis == "gx" else cx for axis, _, _ in kinds]
    pay_shapes = [((nv + 3) * along + nq, nz) for along in alongs]
    blended = pl.pallas_call(
        functools.partial(blend_kernel, ngy, kinds),
        out_shape=pltpu.VMEM((ng * nq, nv, tiles * nz), f32),
        in_specs=[pl.BlockSpec(memory_space=pl.ANY)] * 3,
        scratch_shapes=[
            pltpu.VMEM(cons.shape, f32),
            pltpu.VMEM(corner.shape, jnp.int32),
            pltpu.VMEM(fraction.shape, f32),
            pltpu.VMEM((nv * rows, 3 * nz), jnp.bfloat16),
            pltpu.VMEM((ng - 1, 3 * nz, block * slots), jnp.bfloat16),
            pltpu.VMEM((ng - 1, rows, block * slots), f32),
            pltpu.VMEM((ng - 1, per, nq // per, nv, nz), f32),
            pltpu.SemaphoreType.DMA((3,)),
        ],
        compiler_params=params,
        name="blend",
    )(*(pltpu.with_memory_space_constraint(value, pltpu.HBM) for value in (cons, corner, fraction)))

    aims, *pays = pl.pallas_call(
        functools.partial(edge_kernel, kinds),
        out_shape=[pltpu.VMEM((nq, nz), f32)] + [pltpu.VMEM(dims, f32) for dims in pay_shapes],
        in_specs=[pl.BlockSpec(memory_space=pltpu.VMEM)] * 3 + [pl.BlockSpec(memory_space=pl.ANY)],
        compiler_params=params,
        name="edge",
    )(cons, vel, target, blended)

    received = lax.all_to_all(
        blended,
        ("gy", "grp", "gx"),
        split_axis=0,
        concat_axis=0,
        tiled=True,
        axis_index_groups=[list(reversed(range(ng * nq)))],
    )
    halos = []
    for (axis, phase, _), pay in zip(kinds, pays):
        count = ngx if axis == "gx" else ngy
        pairs = []
        for low in range(phase, count - 1, 2):
            pairs += [(low, low + 1), (low + 1, low)]
        halos.append(lax.ppermute(pay, axis, pairs))

    spread = spread_of(cx)
    coefs, base, picks = pl.pallas_call(
        functools.partial(prepare_kernel, slots, ng),
        out_shape=[
            pltpu.VMEM((7, cx, cy, nz), f32),
            pltpu.VMEM((nv, cx, cy, nz), f32),
            pltpu.VMEM(((ng - 1) * nq * slots, spread * nz), jnp.bfloat16),
        ],
        scratch_shapes=[pltpu.VMEM((rows // spread, spread * nz), f32)],
        compiler_params=params,
        name="prepare",
    )(cons, vel, aims)
    def kept(values):
        return [pltpu.with_memory_space_constraint(value, pltpu.VMEM) for value in values]

    coefs, base, picks = kept((coefs, base, picks))
    border = pl.pallas_call(
        functools.partial(border_kernel, kinds, slots, ng),
        out_shape=[
            pltpu.VMEM((7, cx, cy, nz), f32),
            pltpu.VMEM((len(kinds), nq, nz), jnp.int32),
        ]
        + [pltpu.VMEM((nv, along, nz), f32) for along in alongs]
        + [pltpu.VMEM(((ng - 1) * nq * slots, nz), jnp.bfloat16) for _ in kinds],
        scratch_shapes=[pltpu.VMEM((along, nz), f32) for along in alongs],
        compiler_params=params,
        name="border",
    )(vel, coefs, *halos)
    coefs, rows_there, *border = kept(border)
    cleared, picks_there = border[: len(kinds)], border[len(kinds) :]

    result = pl.pallas_call(
        functools.partial(step_kernel, kinds, slots, ng, ngy),
        out_shape=shape(nv, cx, cy, nz),
        out_specs=pl.BlockSpec(memory_space=pl.ANY),
        scratch_shapes=[
            pltpu.VMEM((fluid_count + 3, cx + 2, cy + 2 * top, nz), f32),
            pltpu.VMEM((nv - fluid_count, cx, cy, nz), f32),
            pltpu.VMEM((2 * nv * (rows + sum(alongs)), nz), f32),
            pltpu.VMEM((nv, cx, cy, nz), f32),
            pltpu.SemaphoreType.DMA((nv,)),
        ],
        compiler_params=params,
        name="step",
    )(vel, aims, base, received, coefs, rows_there, *halos, *cleared, picks, *picks_there)
    return result[:, None]


def solution(mesh):
    return jax.shard_map(
        functools.partial(per_device, mesh.shape["gx"], mesh.shape["gy"]),
        mesh=mesh,
        in_specs=(
            P(None, "grp", "gx", "gy", None),
            P(None, "grp", "gx", "gy", None),
            P("grp", "gx", "gy", None, None, None),
            P(None, "grp", "gx", "gy", None, None, None),
            P("grp", "gx", "gy", None, None, None),
        ),
        out_specs=P(None, "grp", "gx", "gy", None),
        check_vma=False,
    )
```

```python
import functools

import jax
import jax.numpy as jnp
from jax import lax
from jax.experimental import pallas as pl
from jax.experimental.pallas import tpu as pltpu
from jax.sharding import PartitionSpec as P

signal_speed = 0.5
courant_number = 0.3
fluid_count = 5
block = 8


def exchanges(ngx, ngy):
    def partner(count, phase, n):
        other = n + 1 if (n + phase) % 2 == 0 else n - 1
        return other if 0 <= other < count else n

    kinds = []
    for phase in range(min(ngx - 1, 2)):
        kinds.append(("gx", phase, lambda i, j, phase=phase: (partner(ngx, phase, i), j)))
    for phase in range(min(ngy - 1, 2)):
        kinds.append(("gy", phase, lambda i, j, phase=phase: (i, partner(ngy, phase, j))))
    return kinds


def partner_above(axis, phase):
    return (lax.axis_index(axis) + phase) % 2 == 0


def split(value):
    high = value.astype(jnp.bfloat16)
    low = (value - high.astype(jnp.float32)).astype(jnp.bfloat16)
    return high, low


def spread_of(cx):
    return next(n for n in (4, 2, 1) if cx % n == 0)


def over(value, n):
    return value >> (n.bit_length() - 1) if n & (n - 1) == 0 else value // n


def rest_of(value, n):
    return value & (n - 1) if n & (n - 1) == 0 else value % n


def each(count, body):
    if count == 1:
        body(0)
    else:
        lax.fori_loop(0, count, lambda n, c: (body(n), c)[1], 0)


def block_transpose(value, slots):
    rows, lanes = value.shape
    count = lanes // slots
    each_rows = rows // count
    at_row = lax.broadcasted_iota(jnp.int32, value.shape, 0) // each_rows
    at_lane = lax.broadcasted_iota(jnp.int32, value.shape, 1) // slots
    result = value
    for d in range(1, count):
        turned = pltpu.roll(value, d * each_rows, 0)
        turned = pltpu.roll(turned, lanes - d * slots, 1)
        result = jnp.where((at_row - at_lane) % count == d, turned, result)
    return result


def place(ng, ngx, ngy, grid, q):
    return ng * ngx * ngy - 1 - (grid * ngx * ngy + q)


def packed(tiles, slots):
    empty = jnp.zeros(tiles[0].shape, tiles[0].dtype)
    return block_transpose(jnp.concatenate(tiles + [empty], axis=1), slots)


def blend_kernel(ngy, kinds, cons, corner, fraction, out, *scratch):
    at_cons, at_corner, at_fraction, uhl, wzs, wxys, moved, arrive = scratch
    nv, cx, cy, nz = cons.shape
    ng, nq, slots = corner.shape
    lanes = nz
    per = lanes // slots
    chunks = block // per
    rows = cx * cy
    me = lax.axis_index("grp")

    moves = [(corner, at_corner), (fraction, at_fraction), (cons, at_cons)]
    ins = [pltpu.make_async_copy(a, b, arrive.at[n]) for n, (a, b) in enumerate(moves)]
    for copy in reversed(ins):
        copy.start()

    for q in range(nq):
        at = place(ng, nq // ngy, ngy, me, q)
        out[pl.ds(at, 1)] = jnp.zeros((1,) + out.shape[1:], jnp.float32)

    def weight(count, at, upper):
        place = lax.broadcasted_iota(jnp.int32, (count, lanes), 0)
        return jnp.where(place == at, 1.0 - upper, jnp.where(place == at + 1, upper, 0.0))

    def weigh(n):
        here = pl.ds(n * block, block)
        grids = [(me + away) % ng for away in range(1, ng)]
        cell = packed([at_corner[h, here] for h in grids], slots)
        at_x, at_y, at_z = over(cell, nz * cy), rest_of(over(cell, nz), cy), rest_of(cell, nz)
        fx, fy, fz = (packed([at_fraction[d, h, here] for h in grids], slots) for d in range(3))
        for away in range(1, ng):
            for c in range(chunks):
                row = slice((away - 1) * chunks + c, (away - 1) * chunks + c + 1)
                cols = slice(c * lanes, (c + 1) * lanes)
                wx = weight(cx, at_x[row], fx[row])
                wy = weight(cy, at_y[row], fy[row])
                for x in range(cx):
                    wxys[away - 1, x * cy : (x + 1) * cy, cols] = wx[x : x + 1] * wy
                high, low = split(weight(nz, at_z[row], fz[row]))
                wzs[away - 1, :nz, cols] = high
                wzs[away - 1, nz : 2 * nz, cols] = high
                wzs[away - 1, 2 * nz :, cols] = low

    pieces = {}

    def blend(n):
        for away in range(1, ng):
            along = jnp.dot(uhl[...], wzs[away - 1], preferred_element_type=jnp.float32)
            along = along.reshape(nv, rows, chunks * lanes)
            values = jnp.sum(along * wxys[away - 1][None], axis=1)
            for c in range(chunks):
                value = values[:, c * lanes : (c + 1) * lanes]
                for turn in range(per):
                    turned = pltpu.roll(value, turn * slots, 1) if turn else value
                    if nq == block:
                        pieces[away - 1, turn, c] = turned
                    else:
                        moved[away - 1, turn, n * chunks + c] = turned
            if nq == block:
                assemble(away)

    lane = lax.broadcasted_iota(jnp.int32, (nv, lanes), 1) // slots

    def assemble(away):
        for q in range(nq):
            i, j = q // ngy, q % ngy
            owners = [q] + [a * ngy + b for a, b in (of(i, j) for _, _, of in kinds)]
            for t in range(0, len(owners), per):
                tile = None
                for k, owner in enumerate(owners[t : t + per]):
                    chunk = owner // block * chunks + owner % chunks
                    at = (away - 1, (k - owner % block // chunks) % per, chunk)
                    piece = pieces[at] if nq == block else moved[at]
                    tile = piece if tile is None else jnp.where(lane == k, piece, tile)
                cols = slice(t // per * lanes, (t // per + 1) * lanes)
                at = place(ng, nq // ngy, ngy, (me + away) % ng, q)
                out[pl.ds(at, 1), :, cols] = tile[None]

    for copy in ins[:2]:
        copy.wait()
    if nq == block:
        weigh(0)
    ins[2].wait()
    high, low = split(at_cons[...].reshape(nv * rows, nz))
    uhl[:, :nz] = high
    uhl[:, nz : 2 * nz] = low
    uhl[:, 2 * nz :] = high
    if nq == block:
        blend(0)
    else:

        def both(n):
            weigh(n)
            blend(n)

        each(nq // block, both)
        for away in range(1, ng):
            assemble(away)


def edge_kernel(kinds, cons, vel, target, sent, aims, *pays):
    del sent
    nv, cx, cy, nz = cons.shape
    ng, nq, slots = target.shape
    me = lax.axis_index("grp")
    for n in range(nq // block):
        here = slice(n * block, (n + 1) * block)
        tiles = [target[(me + away) % ng, here] - cx * cy * nz for away in range(1, ng)]
        aims[here] = packed(tiles, slots).astype(jnp.float32)
    for (axis, phase, _), pay in zip(kinds, pays):
        above = partner_above(axis, phase)
        along = cy if axis == "gx" else cx
        for count, source, start in ((nv, cons, 0), (3, vel, nv * along)):
            if axis == "gx":
                layer = source[:, pl.ds(jnp.where(above, cx - 1, 0), 1)]
            else:
                layer = source[:, :, pl.ds(jnp.where(above, cy - 1, 0), 1)]
            pay[start : start + count * along] = layer.reshape(count * along, nz)
        pay[(nv + 3) * along :] = aims[...]


top = 8


def window(ext, v, cx, cy, move_x=0, move_y=0):
    return ext[v, 1 + move_x : 1 + move_x + cx, top + move_y : top + move_y + cy]


def along_z(value, by):
    nz = value.shape[-1]
    at = lax.broadcasted_iota(jnp.int32, (1,) + value.shape[1:], 2)
    edge = 0 if by < 0 else nz - 1
    return jnp.where(at == edge, 0.0, pltpu.roll(value, (-by) % nz, 2))


def shifted(ext, v, cx, cy, d, by):
    if d == 2 and by:
        return along_z(window(ext, v, cx, cy), by)
    return window(ext, v, cx, cy, by if d == 0 else 0, by if d == 1 else 0)


def face(low, high):
    wave_low = jnp.minimum(jnp.minimum(low, high) - signal_speed, 0.0)
    wave_high = jnp.maximum(jnp.maximum(low, high) + signal_speed, 0.0)
    scale = courant_number / (wave_high - wave_low)
    return (
        scale * wave_high * (low - wave_low),
        scale * wave_low * (wave_high - high),
    )


def mark(n, at_row, at_column, count, used, chunks, picks, marks):
    lanes = at_row.shape[1]
    up = lax.broadcasted_iota(jnp.int32, (count, lanes), 0)
    along = lax.broadcasted_iota(jnp.int32, (lanes, picks.shape[1]), 1)
    for at in range(0, used, chunks):
        hits = []
        for c in range(chunks):
            hits.append(jnp.where(up == at_row[at + c : at + c + 1], 1.0, 0.0))
            to = pl.ds(pl.multiple_of((n * used + at + c) * lanes, lanes), lanes)
            chosen = at_column[:, at + c : at + c + 1] == along
            picks[to] = jnp.where(chosen, 1.0, 0.0).astype(jnp.bfloat16)
        to = pl.ds(pl.multiple_of((n * used + at) * lanes, lanes), chunks * lanes)
        marks[...] += jnp.dot(
            jnp.concatenate(hits, axis=1).astype(jnp.bfloat16),
            picks[to],
            preferred_element_type=jnp.float32,
        )


def prepare_kernel(slots, ng, cons, vel, aims, coefs, base, picks, marks):
    nv, cx, cy, nz = cons.shape
    per = nz // slots
    chunks = block // per
    spread = spread_of(cx)
    count = cx // spread * cy

    def pick(n):
        cell = aims[pl.ds(n * block, block)].astype(jnp.int32) + cx * cy * nz
        x, y, z = over(cell, nz * cy), rest_of(over(cell, nz), cy), rest_of(cell, nz)
        at_row = over(x, spread) * cy + y
        at_column = (rest_of(x, spread) * nz + z).T
        mark(n, at_row, at_column, count, (ng - 1) * chunks, chunks, picks, marks)

    marks[...] = jnp.zeros_like(marks)
    each(aims.shape[0] // block, pick)
    for x in range(cx):
        rows = slice(x // spread * cy, (x // spread + 1) * cy)
        seen = marks[rows, x % spread * nz : (x % spread + 1) * nz]
        base[:, x] = jnp.where(seen[None] > 0.5, 0.0, cons[:, x])

    centre = jnp.ones((cx, cy, nz), jnp.float32)
    none = jnp.zeros((1, cy, nz), jnp.float32)
    low, high = face(vel[0, : cx - 1], vel[0, 1:])
    coefs[0] = jnp.concatenate([none, low], axis=0)
    coefs[1] = -jnp.concatenate([high, none], axis=0)
    centre += jnp.concatenate([none, high], axis=0) - jnp.concatenate([low, none], axis=0)

    at_y = lax.broadcasted_iota(jnp.int32, (1, cy, nz), 1)
    speed = vel[1]
    low, high = face(speed, pltpu.roll(speed, cy - 1, 1))
    low = jnp.where(at_y == cy - 1, 0.0, low)
    high = jnp.where(at_y == cy - 1, 0.0, high)
    coefs[2] = pltpu.roll(low, 1, 1)
    coefs[3] = -high
    centre += pltpu.roll(high, 1, 1) - low

    speed = vel[2]
    up_low, up_high = face(speed, along_z(speed, 1))
    down_low, down_high = face(along_z(speed, -1), speed)
    coefs[4] = down_low
    coefs[5] = -up_high
    coefs[6] = centre + down_high - up_low


def border_kernel(kinds, slots, ng, vel, given, *rest):
    halos = rest[: len(kinds)]
    coefs, rows = rest[len(kinds) : len(kinds) + 2]
    cleared = rest[len(kinds) + 2 : 2 * len(kinds) + 2]
    picks = rest[2 * len(kinds) + 2 : 3 * len(kinds) + 2]
    marks = rest[3 * len(kinds) + 2 :]
    cx, cy, nz = vel.shape[1:]
    nq = rows.shape[1]
    chunks = block // (nz // slots)
    used = (ng - 1) * chunks

    sides = {("gx", True): 0.0, ("gx", False): 0.0, ("gy", True): 0.0, ("gy", False): 0.0}
    for k, (axis, phase, _) in enumerate(kinds):
        above = partner_above(axis, phase)
        nv, count = cleared[k].shape[:2]

        def pick(n):
            cell = halos[k][pl.ds((nv + 3) * count + n * block, block)].astype(jnp.int32)
            cell = cell + cx * cy * nz
            x, y, z = over(cell, nz * cy), rest_of(over(cell, nz), cy), rest_of(cell, nz)
            if axis == "gx":
                at_row = jnp.where(x == jnp.where(above, 0, cx - 1), y, -1)
            else:
                at_row = jnp.where(y == jnp.where(above, 0, cy - 1), x, -1)
            rows[k, pl.ds(n * block, block)] = at_row
            mark(n, at_row, z.T, count, used, chunks, picks[k], marks[k])

        marks[k][...] = jnp.zeros_like(marks[k])
        each(nq // block, pick)
        before = halos[k][: nv * count].reshape(nv, count, nz)
        cleared[k][...] = jnp.where(marks[k][...][None] > 0.5, 0.0, before)
        d = 0 if axis == "gx" else 1
        speed = halos[k][(nv + d) * count : (nv + d + 1) * count]
        sides[axis, True] += jnp.where(above, speed, 0.0)
        sides[axis, False] += jnp.where(above, 0.0, speed)

    coefs[...] = given[...]
    for (axis, high), speed in sides.items():
        if axis == "gx":
            d, edge = 0, (cx - 1 if high else 0,)
        else:
            d, edge = 1, (slice(None), cy - 1 if high else 0)
        mine = vel[(d,) + edge]
        speed = jnp.broadcast_to(speed, mine.shape)
        if high:
            of_low, of_high = face(mine, speed)
            coefs[(2 * d + 1,) + edge] = -of_high
            coefs[(6,) + edge] -= of_low
        else:
            of_low, of_high = face(speed, mine)
            coefs[(2 * d,) + edge] = of_low
            coefs[(6,) + edge] += of_high


def step_kernel(kinds, slots, ng, ngy, vel, aims, base, received, coefs, rows_there, *rest):
    halos, cleared = rest[: len(kinds)], rest[len(kinds) : 2 * len(kinds)]
    picks = rest[2 * len(kinds) : 3 * len(kinds) + 1]
    out, ext, field, acc, result, sems = rest[3 * len(kinds) + 1 :]
    nv, cx, cy, nz = base.shape
    lanes = nz
    nq = received.shape[0] // ng
    per = lanes // slots
    chunks = block // per
    used = (ng - 1) * chunks
    spread = spread_of(cx)
    me = lax.axis_index("grp")
    lane = lax.broadcasted_iota(jnp.int32, (nv, lanes), 1) // slots
    above = [partner_above(axis, phase) for axis, phase, _ in kinds]

    parts = [(cx // spread * cy, spread)]
    parts += [(cy if axis == "gx" else cx, 1) for axis, _, _ in kinds]
    starts = [0]
    for count, groups in parts:
        starts.append(starts[-1] + 2 * nv * count * groups)

    def fill(n):
        for part, (count, groups) in enumerate(parts):
            if part == 0:
                cell = aims[pl.ds(n * block, block)].astype(jnp.int32) + cx * cy * nz
                x, y = over(cell, nz * cy), rest_of(over(cell, nz), cy)
                at_row = over(x, spread) * cy + y
            else:
                at_row = rows_there[part - 1, pl.ds(n * block, block)]
            up = lax.broadcasted_iota(jnp.int32, (count, lanes), 0)
            here = slice(part // per * lanes, (part // per + 1) * lanes)
            lefts = []
            for away in range(1, ng):
                g = (me + away) % ng
                for c in range(chunks):
                    at = (away - 1) * chunks + c
                    value = None
                    for p in range(per):
                        source = n * block + p * chunks + c
                        piece = received[place(ng, nq // ngy, ngy, g, source), :, here]
                        turn = (p - part) % per
                        if turn:
                            piece = pltpu.roll(piece, turn * slots, 1)
                        value = piece if value is None else jnp.where(lane == p, piece, value)
                    high = value.astype(jnp.bfloat16).astype(jnp.float32)
                    low = value - high
                    hit = up == at_row[at : at + 1]
                    pieces = [jnp.where(hit, high[v : v + 1], 0.0) for v in range(nv)]
                    pieces += [jnp.where(hit, low[v : v + 1], 0.0) for v in range(nv)]
                    lefts.append(jnp.concatenate(pieces, axis=0).astype(jnp.bfloat16))
            chosen = picks[part][pl.ds(pl.multiple_of(n * used * lanes, lanes), used * lanes)]
            total = jnp.dot(
                jnp.concatenate(lefts, axis=1), chosen, preferred_element_type=jnp.float32
            )
            if nq == block:
                totals[part] = total
            else:
                rows = total.shape[0]
                for s in range(groups):
                    start = starts[part] + s * rows
                    acc[start : start + rows] += total[:, s * nz : (s + 1) * nz]

    totals = {}
    if nq != block:
        acc[...] = jnp.zeros_like(acc)
    each(nq // block, fill)

    def brought(part, s):
        count = parts[part][0]
        if nq == block:
            new = totals[part][:, s * nz : (s + 1) * nz]
        else:
            start = starts[part] + s * 2 * nv * count
            new = acc[start : start + 2 * nv * count]
        return (new[: nv * count] + new[nv * count :]).reshape(nv, count, nz)

    def crossed(n, speeds, fields):
        a, b = (n + 1) % 3, (n + 2) % 3
        return speeds[b] * fields[a] - speeds[a] * fields[b]

    inside = slice(top, top + cy)
    for s in range(spread):
        new = brought(0, s)
        for n, x in enumerate(range(s, cx, spread)):
            state = base[:, x] + new[:, n * cy : (n + 1) * cy]
            ext[:fluid_count, 1 + x, inside] = state[:fluid_count]
            field[:, x] = state[fluid_count:]
            for d in range(3):
                ext[fluid_count + d, 1 + x, inside] = crossed(d, vel[:, x], state[fluid_count:])

    sides = {("gx", True): 0.0, ("gx", False): 0.0, ("gy", True): 0.0, ("gy", False): 0.0}
    for n, (axis, _, _) in enumerate(kinds):
        count = parts[n + 1][0]
        d = 0 if axis == "gx" else 1
        halo = halos[n][: (nv + 3) * count].reshape(nv + 3, count, nz)
        state = cleared[n][...] + brought(n + 1, 0)
        electric = [crossed(m, halo[nv:], state[fluid_count:])[None] for m in (1 - d, 2)]
        halo = jnp.concatenate([state[:fluid_count]] + electric, axis=0)
        sides[axis, True] += jnp.where(above[n], halo, 0.0)
        sides[axis, False] += jnp.where(above[n], 0.0, halo)

    for (axis, high), halo in sides.items():
        d = 0 if axis == "gx" else 1
        halo = jnp.broadcast_to(halo, (fluid_count + 2, cx if d else cy, nz))
        if d == 0:
            at = (cx + 1 if high else 0, inside)
        else:
            at = (slice(1, cx + 1), top + cy if high else top - 1)
        ext[(slice(0, fluid_count),) + at] = halo[:fluid_count]
        ext[(fluid_count + 1 - d,) + at] = halo[fluid_count]
        ext[(fluid_count + 2,) + at] = halo[fluid_count + 1]

    copies = []

    def finish(v, value):
        result[v] = value
        copies.append(pltpu.make_async_copy(result.at[v], out.at[v], sems.at[v]))
        copies[-1].start()

    def central(n, d):
        v = fluid_count + n
        return shifted(ext, v, cx, cy, d, 1) - shifted(ext, v, cx, cy, d, -1)

    for n in range(3):
        a, b = (n + 1) % 3, (n + 2) % 3
        curl = central(b, a) - central(a, b)
        finish(fluid_count + n, field[n] - (0.5 * courant_number) * curl)
    for v in range(fluid_count):
        total = coefs[6] * window(ext, v, cx, cy)
        for d in range(3):
            total = total + coefs[2 * d] * shifted(ext, v, cx, cy, d, -1)
            total = total + coefs[2 * d + 1] * shifted(ext, v, cx, cy, d, 1)
        finish(v, total)
    for copy in copies:
        copy.wait()


def per_device(ngx, ngy, conserved, velocity, donor_corner, donor_fraction, target_cell):
    kinds = exchanges(ngx, ngy)
    cons = conserved[:, 0]
    vel = velocity[:, 0]
    corner = donor_corner[0, 0, 0]
    fraction = donor_fraction[:, 0, 0, 0]
    target = target_cell[0, 0, 0]
    nv, cx, cy, nz = cons.shape
    ng, nq, slots = corner.shape
    rows = cx * cy
    per = nz // slots
    tiles = -(-(1 + len(kinds)) // per)
    f32 = jnp.float32

    def shape(*dims):
        return jax.ShapeDtypeStruct(dims, f32)

    params = pltpu.CompilerParams(vmem_limit_bytes=(12 + nq // 2) << 20)
    alongs = [cy if axis == "gx" else cx for axis, _, _ in kinds]
    pay_shapes = [((nv + 3) * along + nq, nz) for along in alongs]
    blended = pl.pallas_call(
        functools.partial(blend_kernel, ngy, kinds),
        out_shape=pltpu.VMEM((ng * nq, nv, tiles * nz), f32),
        in_specs=[pl.BlockSpec(memory_space=pl.ANY)] * 3,
        scratch_shapes=[
            pltpu.VMEM(cons.shape, f32),
            pltpu.VMEM(corner.shape, jnp.int32),
            pltpu.VMEM(fraction.shape, f32),
            pltpu.VMEM((nv * rows, 3 * nz), jnp.bfloat16),
            pltpu.VMEM((ng - 1, 3 * nz, block * slots), jnp.bfloat16),
            pltpu.VMEM((ng - 1, rows, block * slots), f32),
            pltpu.VMEM((ng - 1, per, nq // per, nv, nz), f32),
            pltpu.SemaphoreType.DMA((3,)),
        ],
        compiler_params=params,
        name="blend",
    )(*(pltpu.with_memory_space_constraint(value, pltpu.HBM) for value in (cons, corner, fraction)))

    aims, *pays = pl.pallas_call(
        functools.partial(edge_kernel, kinds),
        out_shape=[pltpu.VMEM((nq, nz), f32)] + [pltpu.VMEM(dims, f32) for dims in pay_shapes],
        in_specs=[pl.BlockSpec(memory_space=pltpu.VMEM)] * 3 + [pl.BlockSpec(memory_space=pl.ANY)],
        compiler_params=params,
        name="edge",
    )(cons, vel, target, blended)

    received = lax.all_to_all(
        blended,
        ("grp", "gx", "gy"),
        split_axis=0,
        concat_axis=0,
        tiled=True,
        axis_index_groups=[list(reversed(range(ng * nq)))],
    )
    halos = []
    for (axis, phase, _), pay in zip(kinds, pays):
        count = ngx if axis == "gx" else ngy
        pairs = []
        for low in range(phase, count - 1, 2):
            pairs += [(low, low + 1), (low + 1, low)]
        halos.append(lax.ppermute(pay, axis, pairs))

    spread = spread_of(cx)
    coefs, base, picks = pl.pallas_call(
        functools.partial(prepare_kernel, slots, ng),
        out_shape=[
            pltpu.VMEM((7, cx, cy, nz), f32),
            pltpu.VMEM((nv, cx, cy, nz), f32),
            pltpu.VMEM(((ng - 1) * nq * slots, spread * nz), jnp.bfloat16),
        ],
        scratch_shapes=[pltpu.VMEM((rows // spread, spread * nz), f32)],
        compiler_params=params,
        name="prepare",
    )(cons, vel, aims)
    def kept(values):
        return [pltpu.with_memory_space_constraint(value, pltpu.VMEM) for value in values]

    coefs, base, picks = kept((coefs, base, picks))
    border = pl.pallas_call(
        functools.partial(border_kernel, kinds, slots, ng),
        out_shape=[
            pltpu.VMEM((7, cx, cy, nz), f32),
            pltpu.VMEM((len(kinds), nq, nz), jnp.int32),
        ]
        + [pltpu.VMEM((nv, along, nz), f32) for along in alongs]
        + [pltpu.VMEM(((ng - 1) * nq * slots, nz), jnp.bfloat16) for _ in kinds],
        scratch_shapes=[pltpu.VMEM((along, nz), f32) for along in alongs],
        compiler_params=params,
        name="border",
    )(vel, coefs, *halos)
    coefs, rows_there, *border = kept(border)
    cleared, picks_there = border[: len(kinds)], border[len(kinds) :]

    result = pl.pallas_call(
        functools.partial(step_kernel, kinds, slots, ng, ngy),
        out_shape=shape(nv, cx, cy, nz),
        out_specs=pl.BlockSpec(memory_space=pl.ANY),
        scratch_shapes=[
            pltpu.VMEM((fluid_count + 3, cx + 2, cy + 2 * top, nz), f32),
            pltpu.VMEM((nv - fluid_count, cx, cy, nz), f32),
            pltpu.VMEM((2 * nv * (rows + sum(alongs)), nz), f32),
            pltpu.VMEM((nv, cx, cy, nz), f32),
            pltpu.SemaphoreType.DMA((nv,)),
        ],
        compiler_params=params,
        name="step",
    )(vel, aims, base, received, coefs, rows_there, *halos, *cleared, picks, *picks_there)
    return result[:, None]


def solution(mesh):
    return jax.shard_map(
        functools.partial(per_device, mesh.shape["gx"], mesh.shape["gy"]),
        mesh=mesh,
        in_specs=(
            P(None, "grp", "gx", "gy", None),
            P(None, "grp", "gx", "gy", None),
            P("grp", "gx", "gy", None, None, None),
            P(None, "grp", "gx", "gy", None, None, None),
            P("grp", "gx", "gy", None, None, None),
        ),
        out_specs=P(None, "grp", "gx", "gy", None),
        check_vma=False,
    )
```

```python
import functools

import jax
import jax.numpy as jnp
from jax import lax
from jax.experimental import pallas as pl
from jax.experimental.pallas import tpu as pltpu
from jax.sharding import PartitionSpec as P

signal_speed = 0.5
courant_number = 0.3
fluid_count = 5
block = 8


def exchanges(ngx, ngy):
    def partner(count, phase, n):
        other = n + 1 if (n + phase) % 2 == 0 else n - 1
        return other if 0 <= other < count else n

    kinds = []
    for phase in range(min(ngx - 1, 2)):
        kinds.append(("gx", phase, lambda i, j, phase=phase: (partner(ngx, phase, i), j)))
    for phase in range(min(ngy - 1, 2)):
        kinds.append(("gy", phase, lambda i, j, phase=phase: (i, partner(ngy, phase, j))))
    return kinds


def partner_above(axis, phase):
    return (lax.axis_index(axis) + phase) % 2 == 0


def split(value):
    high = value.astype(jnp.bfloat16)
    low = (value - high.astype(jnp.float32)).astype(jnp.bfloat16)
    return high, low


def spread_of(cx):
    return next(n for n in (4, 2, 1) if cx % n == 0)


def over(value, n):
    return value >> (n.bit_length() - 1) if n & (n - 1) == 0 else value // n


def rest_of(value, n):
    return value & (n - 1) if n & (n - 1) == 0 else value % n


def each(count, body):
    if count == 1:
        body(0)
    else:
        lax.fori_loop(0, count, lambda n, c: (body(n), c)[1], 0)


def block_transpose(value, slots):
    rows, lanes = value.shape
    count = lanes // slots
    each_rows = rows // count
    at_row = lax.broadcasted_iota(jnp.int32, value.shape, 0) // each_rows
    at_lane = lax.broadcasted_iota(jnp.int32, value.shape, 1) // slots
    result = value
    for d in range(1, count):
        turned = pltpu.roll(value, d * each_rows, 0)
        turned = pltpu.roll(turned, lanes - d * slots, 1)
        result = jnp.where((at_row - at_lane) % count == d, turned, result)
    return result


def place(ng, ngx, ngy, grid, q):
    return ng * ngx * ngy - 1 - (grid * ngx * ngy + q)


def packed(tiles, slots):
    empty = jnp.zeros(tiles[0].shape, tiles[0].dtype)
    return block_transpose(jnp.concatenate(tiles + [empty], axis=1), slots)


def blend_kernel(ngy, kinds, cons, corner, fraction, out, *scratch):
    at_cons, at_corner, at_fraction, uhl, wzs, wxys, moved, arrive = scratch
    nv, cx, cy, nz = cons.shape
    ng, nq, slots = corner.shape
    lanes = nz
    per = lanes // slots
    chunks = block // per
    rows = cx * cy
    me = lax.axis_index("grp")

    moves = [(corner, at_corner), (fraction, at_fraction), (cons, at_cons)]
    ins = [pltpu.make_async_copy(a, b, arrive.at[n]) for n, (a, b) in enumerate(moves)]
    for copy in ins:
        copy.start()

    for q in range(nq):
        at = place(ng, nq // ngy, ngy, me, q)
        out[pl.ds(at, 1)] = jnp.zeros((1,) + out.shape[1:], jnp.float32)

    def weight(count, at, upper):
        place = lax.broadcasted_iota(jnp.int32, (count, lanes), 0)
        return jnp.where(place == at, 1.0 - upper, jnp.where(place == at + 1, upper, 0.0))

    def weigh(n):
        here = pl.ds(n * block, block)
        grids = [(me + away) % ng for away in range(1, ng)]
        cell = packed([at_corner[h, here] for h in grids], slots)
        at_x, at_y, at_z = over(cell, nz * cy), rest_of(over(cell, nz), cy), rest_of(cell, nz)
        fx, fy, fz = (packed([at_fraction[d, h, here] for h in grids], slots) for d in range(3))
        for away in range(1, ng):
            for c in range(chunks):
                row = slice((away - 1) * chunks + c, (away - 1) * chunks + c + 1)
                cols = slice(c * lanes, (c + 1) * lanes)
                wx = weight(cx, at_x[row], fx[row])
                wy = weight(cy, at_y[row], fy[row])
                for x in range(cx):
                    wxys[away - 1, x * cy : (x + 1) * cy, cols] = wx[x : x + 1] * wy
                high, low = split(weight(nz, at_z[row], fz[row]))
                wzs[away - 1, :nz, cols] = high
                wzs[away - 1, nz : 2 * nz, cols] = high
                wzs[away - 1, 2 * nz :, cols] = low

    pieces = {}

    def blend(n):
        for away in range(1, ng):
            along = jnp.dot(uhl[...], wzs[away - 1], preferred_element_type=jnp.float32)
            along = along.reshape(nv, rows, chunks * lanes)
            values = jnp.sum(along * wxys[away - 1][None], axis=1)
            for c in range(chunks):
                value = values[:, c * lanes : (c + 1) * lanes]
                for turn in range(per):
                    turned = pltpu.roll(value, turn * slots, 1) if turn else value
                    if nq == block:
                        pieces[away - 1, turn, c] = turned
                    else:
                        moved[away - 1, turn, n * chunks + c] = turned
            if nq == block:
                assemble(away)

    lane = lax.broadcasted_iota(jnp.int32, (nv, lanes), 1) // slots

    def assemble(away):
        for q in range(nq):
            i, j = q // ngy, q % ngy
            owners = [q] + [a * ngy + b for a, b in (of(i, j) for _, _, of in kinds)]
            for t in range(0, len(owners), per):
                tile = None
                for k, owner in enumerate(owners[t : t + per]):
                    chunk = owner // block * chunks + owner % chunks
                    at = (away - 1, (k - owner % block // chunks) % per, chunk)
                    piece = pieces[at] if nq == block else moved[at]
                    tile = piece if tile is None else jnp.where(lane == k, piece, tile)
                cols = slice(t // per * lanes, (t // per + 1) * lanes)
                at = place(ng, nq // ngy, ngy, (me + away) % ng, q)
                out[pl.ds(at, 1), :, cols] = tile[None]

    for copy in ins[:2]:
        copy.wait()
    if nq == block:
        weigh(0)
    ins[2].wait()
    high, low = split(at_cons[...].reshape(nv * rows, nz))
    uhl[:, :nz] = high
    uhl[:, nz : 2 * nz] = low
    uhl[:, 2 * nz :] = high
    if nq == block:
        blend(0)
    else:

        def both(n):
            weigh(n)
            blend(n)

        each(nq // block, both)
        for away in range(1, ng):
            assemble(away)


def edge_kernel(kinds, cons, vel, target, sent, aims, *pays):
    del sent
    nv, cx, cy, nz = cons.shape
    ng, nq, slots = target.shape
    me = lax.axis_index("grp")
    for n in range(nq // block):
        here = slice(n * block, (n + 1) * block)
        tiles = [target[(me + away) % ng, here] - cx * cy * nz for away in range(1, ng)]
        aims[here] = packed(tiles, slots).astype(jnp.float32)
    for (axis, phase, _), pay in zip(kinds, pays):
        above = partner_above(axis, phase)
        along = cy if axis == "gx" else cx
        for count, source, start in ((nv, cons, 0), (3, vel, nv * along)):
            if axis == "gx":
                layer = source[:, pl.ds(jnp.where(above, cx - 1, 0), 1)]
            else:
                layer = source[:, :, pl.ds(jnp.where(above, cy - 1, 0), 1)]
            pay[start : start + count * along] = layer.reshape(count * along, nz)
        pay[(nv + 3) * along :] = aims[...]


top = 8


def window(ext, v, cx, cy, move_x=0, move_y=0):
    return ext[v, 1 + move_x : 1 + move_x + cx, top + move_y : top + move_y + cy]


def along_z(value, by):
    nz = value.shape[-1]
    at = lax.broadcasted_iota(jnp.int32, (1,) + value.shape[1:], 2)
    edge = 0 if by < 0 else nz - 1
    return jnp.where(at == edge, 0.0, pltpu.roll(value, (-by) % nz, 2))


def shifted(ext, v, cx, cy, d, by):
    if d == 2 and by:
        return along_z(window(ext, v, cx, cy), by)
    return window(ext, v, cx, cy, by if d == 0 else 0, by if d == 1 else 0)


def face(low, high):
    wave_low = jnp.minimum(jnp.minimum(low, high) - signal_speed, 0.0)
    wave_high = jnp.maximum(jnp.maximum(low, high) + signal_speed, 0.0)
    scale = courant_number / (wave_high - wave_low)
    return (
        scale * wave_high * (low - wave_low),
        scale * wave_low * (wave_high - high),
    )


def mark(n, at_row, at_column, count, used, chunks, picks, marks):
    lanes = at_row.shape[1]
    up = lax.broadcasted_iota(jnp.int32, (count, lanes), 0)
    along = lax.broadcasted_iota(jnp.int32, (lanes, picks.shape[1]), 1)
    for at in range(0, used, chunks):
        hits = []
        for c in range(chunks):
            hits.append(jnp.where(up == at_row[at + c : at + c + 1], 1.0, 0.0))
            to = pl.ds(pl.multiple_of((n * used + at + c) * lanes, lanes), lanes)
            chosen = at_column[:, at + c : at + c + 1] == along
            picks[to] = jnp.where(chosen, 1.0, 0.0).astype(jnp.bfloat16)
        to = pl.ds(pl.multiple_of((n * used + at) * lanes, lanes), chunks * lanes)
        marks[...] += jnp.dot(
            jnp.concatenate(hits, axis=1).astype(jnp.bfloat16),
            picks[to],
            preferred_element_type=jnp.float32,
        )


def prepare_kernel(slots, ng, cons, vel, aims, coefs, base, picks, marks):
    nv, cx, cy, nz = cons.shape
    per = nz // slots
    chunks = block // per
    spread = spread_of(cx)
    count = cx // spread * cy

    def pick(n):
        cell = aims[pl.ds(n * block, block)].astype(jnp.int32) + cx * cy * nz
        x, y, z = over(cell, nz * cy), rest_of(over(cell, nz), cy), rest_of(cell, nz)
        at_row = over(x, spread) * cy + y
        at_column = (rest_of(x, spread) * nz + z).T
        mark(n, at_row, at_column, count, (ng - 1) * chunks, chunks, picks, marks)

    marks[...] = jnp.zeros_like(marks)
    each(aims.shape[0] // block, pick)
    for x in range(cx):
        rows = slice(x // spread * cy, (x // spread + 1) * cy)
        seen = marks[rows, x % spread * nz : (x % spread + 1) * nz]
        base[:, x] = jnp.where(seen[None] > 0.5, 0.0, cons[:, x])

    centre = jnp.ones((cx, cy, nz), jnp.float32)
    none = jnp.zeros((1, cy, nz), jnp.float32)
    low, high = face(vel[0, : cx - 1], vel[0, 1:])
    coefs[0] = jnp.concatenate([none, low], axis=0)
    coefs[1] = -jnp.concatenate([high, none], axis=0)
    centre += jnp.concatenate([none, high], axis=0) - jnp.concatenate([low, none], axis=0)

    at_y = lax.broadcasted_iota(jnp.int32, (1, cy, nz), 1)
    speed = vel[1]
    low, high = face(speed, pltpu.roll(speed, cy - 1, 1))
    low = jnp.where(at_y == cy - 1, 0.0, low)
    high = jnp.where(at_y == cy - 1, 0.0, high)
    coefs[2] = pltpu.roll(low, 1, 1)
    coefs[3] = -high
    centre += pltpu.roll(high, 1, 1) - low

    speed = vel[2]
    up_low, up_high = face(speed, along_z(speed, 1))
    down_low, down_high = face(along_z(speed, -1), speed)
    coefs[4] = down_low
    coefs[5] = -up_high
    coefs[6] = centre + down_high - up_low


def border_kernel(kinds, slots, ng, vel, given, *rest):
    halos = rest[: len(kinds)]
    coefs, rows = rest[len(kinds) : len(kinds) + 2]
    cleared = rest[len(kinds) + 2 : 2 * len(kinds) + 2]
    picks = rest[2 * len(kinds) + 2 : 3 * len(kinds) + 2]
    marks = rest[3 * len(kinds) + 2 :]
    cx, cy, nz = vel.shape[1:]
    nq = rows.shape[1]
    chunks = block // (nz // slots)
    used = (ng - 1) * chunks

    sides = {("gx", True): 0.0, ("gx", False): 0.0, ("gy", True): 0.0, ("gy", False): 0.0}
    for k, (axis, phase, _) in enumerate(kinds):
        above = partner_above(axis, phase)
        nv, count = cleared[k].shape[:2]

        def pick(n):
            cell = halos[k][pl.ds((nv + 3) * count + n * block, block)].astype(jnp.int32)
            cell = cell + cx * cy * nz
            x, y, z = over(cell, nz * cy), rest_of(over(cell, nz), cy), rest_of(cell, nz)
            if axis == "gx":
                at_row = jnp.where(x == jnp.where(above, 0, cx - 1), y, -1)
            else:
                at_row = jnp.where(y == jnp.where(above, 0, cy - 1), x, -1)
            rows[k, pl.ds(n * block, block)] = at_row
            mark(n, at_row, z.T, count, used, chunks, picks[k], marks[k])

        marks[k][...] = jnp.zeros_like(marks[k])
        each(nq // block, pick)
        before = halos[k][: nv * count].reshape(nv, count, nz)
        cleared[k][...] = jnp.where(marks[k][...][None] > 0.5, 0.0, before)
        d = 0 if axis == "gx" else 1
        speed = halos[k][(nv + d) * count : (nv + d + 1) * count]
        sides[axis, True] += jnp.where(above, speed, 0.0)
        sides[axis, False] += jnp.where(above, 0.0, speed)

    coefs[...] = given[...]
    for (axis, high), speed in sides.items():
        if axis == "gx":
            d, edge = 0, (cx - 1 if high else 0,)
        else:
            d, edge = 1, (slice(None), cy - 1 if high else 0)
        mine = vel[(d,) + edge]
        speed = jnp.broadcast_to(speed, mine.shape)
        if high:
            of_low, of_high = face(mine, speed)
            coefs[(2 * d + 1,) + edge] = -of_high
            coefs[(6,) + edge] -= of_low
        else:
            of_low, of_high = face(speed, mine)
            coefs[(2 * d,) + edge] = of_low
            coefs[(6,) + edge] += of_high


def step_kernel(kinds, slots, ng, ngy, vel, aims, base, received, coefs, rows_there, *rest):
    halos, cleared = rest[: len(kinds)], rest[len(kinds) : 2 * len(kinds)]
    picks = rest[2 * len(kinds) : 3 * len(kinds) + 1]
    out, ext, field, acc, result, sems = rest[3 * len(kinds) + 1 :]
    nv, cx, cy, nz = base.shape
    lanes = nz
    nq = received.shape[0] // ng
    per = lanes // slots
    chunks = block // per
    used = (ng - 1) * chunks
    spread = spread_of(cx)
    me = lax.axis_index("grp")
    lane = lax.broadcasted_iota(jnp.int32, (nv, lanes), 1) // slots
    above = [partner_above(axis, phase) for axis, phase, _ in kinds]

    parts = [(cx // spread * cy, spread)]
    parts += [(cy if axis == "gx" else cx, 1) for axis, _, _ in kinds]
    starts = [0]
    for count, groups in parts:
        starts.append(starts[-1] + 2 * nv * count * groups)

    def fill(n):
        for part, (count, groups) in enumerate(parts):
            if part == 0:
                cell = aims[pl.ds(n * block, block)].astype(jnp.int32) + cx * cy * nz
                x, y = over(cell, nz * cy), rest_of(over(cell, nz), cy)
                at_row = over(x, spread) * cy + y
            else:
                at_row = rows_there[part - 1, pl.ds(n * block, block)]
            up = lax.broadcasted_iota(jnp.int32, (count, lanes), 0)
            here = slice(part // per * lanes, (part // per + 1) * lanes)
            lefts = []
            for away in range(1, ng):
                g = (me + away) % ng
                for c in range(chunks):
                    at = (away - 1) * chunks + c
                    value = None
                    for p in range(per):
                        source = n * block + p * chunks + c
                        piece = received[place(ng, nq // ngy, ngy, g, source), :, here]
                        turn = (p - part) % per
                        if turn:
                            piece = pltpu.roll(piece, turn * slots, 1)
                        value = piece if value is None else jnp.where(lane == p, piece, value)
                    high = value.astype(jnp.bfloat16).astype(jnp.float32)
                    low = value - high
                    hit = up == at_row[at : at + 1]
                    pieces = [jnp.where(hit, high[v : v + 1], 0.0) for v in range(nv)]
                    pieces += [jnp.where(hit, low[v : v + 1], 0.0) for v in range(nv)]
                    lefts.append(jnp.concatenate(pieces, axis=0).astype(jnp.bfloat16))
            chosen = picks[part][pl.ds(pl.multiple_of(n * used * lanes, lanes), used * lanes)]
            total = jnp.dot(
                jnp.concatenate(lefts, axis=1), chosen, preferred_element_type=jnp.float32
            )
            if nq == block:
                totals[part] = total
            else:
                rows = total.shape[0]
                for s in range(groups):
                    start = starts[part] + s * rows
                    acc[start : start + rows] += total[:, s * nz : (s + 1) * nz]

    totals = {}
    if nq != block:
        acc[...] = jnp.zeros_like(acc)
    each(nq // block, fill)

    def brought(part, s):
        count = parts[part][0]
        if nq == block:
            new = totals[part][:, s * nz : (s + 1) * nz]
        else:
            start = starts[part] + s * 2 * nv * count
            new = acc[start : start + 2 * nv * count]
        return (new[: nv * count] + new[nv * count :]).reshape(nv, count, nz)

    def crossed(n, speeds, fields):
        a, b = (n + 1) % 3, (n + 2) % 3
        return speeds[b] * fields[a] - speeds[a] * fields[b]

    inside = slice(top, top + cy)
    for s in range(spread):
        new = brought(0, s)
        for n, x in enumerate(range(s, cx, spread)):
            state = base[:, x] + new[:, n * cy : (n + 1) * cy]
            ext[:fluid_count, 1 + x, inside] = state[:fluid_count]
            field[:, x] = state[fluid_count:]
            for d in range(3):
                ext[fluid_count + d, 1 + x, inside] = crossed(d, vel[:, x], state[fluid_count:])

    sides = {("gx", True): 0.0, ("gx", False): 0.0, ("gy", True): 0.0, ("gy", False): 0.0}
    for n, (axis, _, _) in enumerate(kinds):
        count = parts[n + 1][0]
        d = 0 if axis == "gx" else 1
        halo = halos[n][: (nv + 3) * count].reshape(nv + 3, count, nz)
        state = cleared[n][...] + brought(n + 1, 0)
        electric = [crossed(m, halo[nv:], state[fluid_count:])[None] for m in (1 - d, 2)]
        halo = jnp.concatenate([state[:fluid_count]] + electric, axis=0)
        sides[axis, True] += jnp.where(above[n], halo, 0.0)
        sides[axis, False] += jnp.where(above[n], 0.0, halo)

    for (axis, high), halo in sides.items():
        d = 0 if axis == "gx" else 1
        halo = jnp.broadcast_to(halo, (fluid_count + 2, cx if d else cy, nz))
        if d == 0:
            at = (cx + 1 if high else 0, inside)
        else:
            at = (slice(1, cx + 1), top + cy if high else top - 1)
        ext[(slice(0, fluid_count),) + at] = halo[:fluid_count]
        ext[(fluid_count + 1 - d,) + at] = halo[fluid_count]
        ext[(fluid_count + 2,) + at] = halo[fluid_count + 1]

    copies = []

    def finish(v, value):
        result[v] = value
        copies.append(pltpu.make_async_copy(result.at[v], out.at[v], sems.at[v]))
        copies[-1].start()

    def central(n, d):
        v = fluid_count + n
        return shifted(ext, v, cx, cy, d, 1) - shifted(ext, v, cx, cy, d, -1)

    for n in range(3):
        a, b = (n + 1) % 3, (n + 2) % 3
        curl = central(b, a) - central(a, b)
        finish(fluid_count + n, field[n] - (0.5 * courant_number) * curl)
    for v in range(fluid_count):
        total = coefs[6] * window(ext, v, cx, cy)
        for d in range(3):
            total = total + coefs[2 * d] * shifted(ext, v, cx, cy, d, -1)
            total = total + coefs[2 * d + 1] * shifted(ext, v, cx, cy, d, 1)
        finish(v, total)
    for copy in copies:
        copy.wait()


def per_device(ngx, ngy, conserved, velocity, donor_corner, donor_fraction, target_cell):
    kinds = exchanges(ngx, ngy)
    cons = conserved[:, 0]
    vel = velocity[:, 0]
    corner = donor_corner[0, 0, 0]
    fraction = donor_fraction[:, 0, 0, 0]
    target = target_cell[0, 0, 0]
    nv, cx, cy, nz = cons.shape
    ng, nq, slots = corner.shape
    rows = cx * cy
    per = nz // slots
    tiles = -(-(1 + len(kinds)) // per)
    f32 = jnp.float32

    def shape(*dims):
        return jax.ShapeDtypeStruct(dims, f32)

    params = pltpu.CompilerParams(vmem_limit_bytes=(12 + nq // 2) << 20)
    alongs = [cy if axis == "gx" else cx for axis, _, _ in kinds]
    pay_shapes = [((nv + 3) * along + nq, nz) for along in alongs]
    blended = pl.pallas_call(
        functools.partial(blend_kernel, ngy, kinds),
        out_shape=pltpu.VMEM((ng * nq, nv, tiles * nz), f32),
        in_specs=[pl.BlockSpec(memory_space=pl.ANY)] * 3,
        scratch_shapes=[
            pltpu.VMEM(cons.shape, f32),
            pltpu.VMEM(corner.shape, jnp.int32),
            pltpu.VMEM(fraction.shape, f32),
            pltpu.VMEM((nv * rows, 3 * nz), jnp.bfloat16),
            pltpu.VMEM((ng - 1, 3 * nz, block * slots), jnp.bfloat16),
            pltpu.VMEM((ng - 1, rows, block * slots), f32),
            pltpu.VMEM((ng - 1, per, nq // per, nv, nz), f32),
            pltpu.SemaphoreType.DMA((3,)),
        ],
        compiler_params=params,
        name="blend",
    )(*(pltpu.with_memory_space_constraint(value, pltpu.HBM) for value in (cons, corner, fraction)))

    aims, *pays = pl.pallas_call(
        functools.partial(edge_kernel, kinds),
        out_shape=[pltpu.VMEM((nq, nz), f32)] + [pltpu.VMEM(dims, f32) for dims in pay_shapes],
        in_specs=[pl.BlockSpec(memory_space=pltpu.VMEM)] * 3 + [pl.BlockSpec(memory_space=pl.ANY)],
        compiler_params=params,
        name="edge",
    )(cons, vel, target, blended)

    received = lax.all_to_all(
        blended,
        ("grp", "gx", "gy"),
        split_axis=0,
        concat_axis=0,
        tiled=True,
        axis_index_groups=[list(reversed(range(ng * nq)))],
    )
    halos = []
    for (axis, phase, _), pay in zip(kinds, pays):
        count = ngx if axis == "gx" else ngy
        pairs = []
        for low in range(phase, count - 1, 2):
            pairs += [(low, low + 1), (low + 1, low)]
        halos.append(lax.ppermute(pay, axis, pairs))

    spread = spread_of(cx)
    coefs, base, picks = pl.pallas_call(
        functools.partial(prepare_kernel, slots, ng),
        out_shape=[
            pltpu.VMEM((7, cx, cy, nz), f32),
            pltpu.VMEM((nv, cx, cy, nz), f32),
            pltpu.VMEM(((ng - 1) * nq * slots, spread * nz), jnp.bfloat16),
        ],
        scratch_shapes=[pltpu.VMEM((rows // spread, spread * nz), f32)],
        compiler_params=params,
        name="prepare",
    )(cons, vel, aims)
    def kept(values):
        return [pltpu.with_memory_space_constraint(value, pltpu.VMEM) for value in values]

    coefs, base, picks = kept((coefs, base, picks))
    border = pl.pallas_call(
        functools.partial(border_kernel, kinds, slots, ng),
        out_shape=[
            pltpu.VMEM((7, cx, cy, nz), f32),
            pltpu.VMEM((len(kinds), nq, nz), jnp.int32),
        ]
        + [pltpu.VMEM((nv, along, nz), f32) for along in alongs]
        + [pltpu.VMEM(((ng - 1) * nq * slots, nz), jnp.bfloat16) for _ in kinds],
        scratch_shapes=[pltpu.VMEM((along, nz), f32) for along in alongs],
        compiler_params=params,
        name="border",
    )(vel, coefs, *halos)
    coefs, rows_there, *border = kept(border)
    cleared, picks_there = border[: len(kinds)], border[len(kinds) :]

    result = pl.pallas_call(
        functools.partial(step_kernel, kinds, slots, ng, ngy),
        out_shape=shape(nv, cx, cy, nz),
        out_specs=pl.BlockSpec(memory_space=pl.ANY),
        scratch_shapes=[
            pltpu.VMEM((fluid_count + 3, cx + 2, cy + 2 * top, nz), f32),
            pltpu.VMEM((nv - fluid_count, cx, cy, nz), f32),
            pltpu.VMEM((2 * nv * (rows + sum(alongs)), nz), f32),
            pltpu.VMEM((nv, cx, cy, nz), f32),
            pltpu.SemaphoreType.DMA((nv,)),
        ],
        compiler_params=params,
        name="step",
    )(vel, aims, base, received, coefs, rows_there, *halos, *cleared, picks, *picks_there)
    return result[:, None]


def solution(mesh):
    return jax.shard_map(
        functools.partial(per_device, mesh.shape["gx"], mesh.shape["gy"]),
        mesh=mesh,
        in_specs=(
            P(None, "grp", "gx", "gy", None),
            P(None, "grp", "gx", "gy", None),
            P("grp", "gx", "gy", None, None, None),
            P(None, "grp", "gx", "gy", None, None, None),
            P("grp", "gx", "gy", None, None, None),
        ),
        out_specs=P(None, "grp", "gx", "gy", None),
        check_vma=False,
    )
```
